32 devices in a mesh: dp: 8 (over z, x), ctx: 4 (over y, core).
Axes of the slice: x: 2, y: 2, z: 4, core: 2. Of those that a mesh axis runs over, the one named last changes fastest.
Arguments:
- inputs: bfloat16 [8, 1024, 2048], P('dp', 'ctx'), may hold values from -6 to 6
- segments: int32 [8, 1024], P('dp', 'ctx'), may hold values from 0 to 3, as said below
- ln_gain: bfloat16 [2, 2048], P(None, 'dp'), may hold values from 0.5 to 1.5
- ln_bias: bfloat16 [2, 2048], P(None, 'dp'), may hold values from -1.5 to 1.5
- qkv_weight: bfloat16 [2048, 6144], P('dp'), may hold values from -0.125 to 0.125
- qkv_bias: bfloat16 [6144], P('dp'), may hold values from -2.5 to 2.5
- out_weight: bfloat16 [2048, 2048], P('dp'), may hold values from -1 to 1
- out_bias: bfloat16 [2048], P('dp'), may hold values from -1.5 to 1.5
- up_weight: bfloat16 [2048, 8192], P('dp'), may hold values from -0.125 to 0.125
- up_bias: bfloat16 [8192], P('dp'), may hold values from -2.5 to 2.5
- down_weight: bfloat16 [8192, 2048], P('dp'), may hold values from -0.125 to 0.125
- down_bias: bfloat16 [2048], P('dp'), may hold values from -1.5 to 1.5
- cotangent: bfloat16 [8, 1024, 2048], P('dp', 'ctx'), may hold values from -6 to 6
Outputs:
- result: bfloat16 [8, 1024, 2048], P('dp', 'ctx')
- grad_inputs: bfloat16 [8, 1024, 2048], P('dp', 'ctx')
- grad_ln_gain: float32 [2, 2048], P(None, 'dp')
- grad_ln_bias: float32 [2, 2048], P(None, 'dp')
- grad_qkv_weight: float32 [2048, 6144], P('dp')
- grad_qkv_bias: float32 [6144], P('dp')
- grad_out_weight: float32 [2048, 2048], P('dp')
- grad_out_bias: float32 [2048], P('dp')
- grad_up_weight: float32 [2048, 8192], P('dp')
- grad_up_bias: float32 [8192], P('dp')
- grad_down_weight: float32 [8192, 2048], P('dp')
- grad_down_bias: float32 [2048], P('dp')
The draws below stay inside these ranges and needn't reach their ends.
Inputs may be any that keep to these rules, and one draw needn't show every extreme that they name: `segments`: each sequence holds four documents in order, numbered 0 to 3; document 1 begins within the first 256 tokens and ends within the last 256 tokens.
All inputs are finite; a program needn't handle non-finite values.
Results may differ from the reference program's by a relative error of at most 0.017.
Values may be sent and summed in bfloat16 or wider, within the bound.
A program may use at most 512 MiB of HBM per device.

```python
import jax
import jax.numpy as jnp
from jax import lax

D = 2048
HEADS = 8
HEAD = 256
FF = 8192
ROT = 64
CTX_TOK = 256
SEQ_LEN = 1024
SEQS = 8


def draw_segments(key, part):
    key = jax.random.fold_in(key, 11)
    first_key, second_key, third_key = jax.random.split(key, 3)
    begin = jax.random.randint(first_key, (SEQS, 1), 1, CTX_TOK)
    finish = jax.random.randint(second_key, (SEQS, 1), SEQ_LEN - CTX_TOK + 1, SEQ_LEN - 1)
    offset = jax.random.randint(third_key, (SEQS, 1), 0, 1 << 20) % (SEQ_LEN - 1 - finish)
    latest = finish + 1 + offset
    position = jnp.arange(SEQ_LEN)[None, :]
    numbers = (position >= begin).astype(jnp.int32) + (position >= finish).astype(jnp.int32) + (position >= latest).astype(jnp.int32)
    return numbers.astype(jnp.int32)


def block_scale(key, dims, pieces, low, high):
    def one(axis_at, shards_of):
        draws = jax.random.uniform(jax.random.fold_in(jax.random.fold_in(key, 6), axis_at), (shards_of,), jnp.float32, low / len(pieces), high / len(pieces))
        return jnp.repeat(jnp.exp(draws), dims[axis_at] // shards_of).reshape((-1,) + (1,) * (len(dims) - axis_at - 1))

    loudness = one(*pieces[0])
    for cut in pieces[1:]:
        loudness = loudness * one(*cut)
    return loudness


def scatter_about(rng, shape, width, reach, cuts=(), dtype=jnp.bfloat16):
    values = width * jax.random.normal(rng, shape, jnp.float32)
    if cuts:
        values = values * block_scale(rng, shape, cuts, -0.22, 0.18)
    return jnp.clip(values, -reach, reach).astype(dtype)


def setup_inputs(seed: int = 0) -> dict:
    key_list = jax.random.split(jax.random.key(seed), 14)
    inputs = scatter_about(key_list[0], (SEQS, SEQ_LEN, D), 1.0, 6.0, ((0, 8), (1, 4)))
    segments = draw_segments(jax.random.fold_in(key_list[13], 71), 0)
    ln_gain = jnp.clip(1.0 + 0.1 * jax.random.normal(key_list[2], (2, D), jnp.float32), 0.5, 1.5).astype(jnp.bfloat16)
    ln_bias = scatter_about(key_list[3], (2, D), 0.3, 1.5, ((1, 8),))
    qkv_weight = scatter_about(key_list[4], (D, 3 * D), D ** -0.5, 0.125, ((0, 8),))
    qkv_bias = scatter_about(key_list[5], (3 * D,), 0.5, 2.5, ((0, 8),))
    out_weight = scatter_about(key_list[6], (D, D), (D // 64) ** -0.5, 1.0, ((0, 8),))
    out_bias = scatter_about(key_list[7], (D,), 0.3, 1.5, ((0, 8),))
    up_weight = scatter_about(key_list[8], (D, FF), D ** -0.5, 0.125, ((0, 8),))
    up_bias = scatter_about(key_list[9], (FF,), 0.5, 2.5, ((0, 8),))
    down_weight = scatter_about(key_list[10], (FF, D), (FF // 4) ** -0.5, 0.125, ((0, 8),))
    down_bias = scatter_about(key_list[11], (D,), 0.3, 1.5, ((0, 8),))
    cotangent = scatter_about(key_list[12], (SEQS, SEQ_LEN, D), 1.0, 6.0, ((0, 8), (1, 4)))
    return {"inputs": inputs, "segments": segments, "ln_gain": ln_gain, "ln_bias": ln_bias, "qkv_weight": qkv_weight, "qkv_bias": qkv_bias, "out_weight": out_weight, "out_bias": out_bias, "up_weight": up_weight, "up_bias": up_bias, "down_weight": down_weight, "down_bias": down_bias, "cotangent": cotangent}


EPSILON = 1e-05
MASKED = -1e+30
HIGHEST = lax.Precision.HIGHEST

@jax.custom_vjp
def low(v):
    return lax.optimization_barrier(v.astype(jnp.bfloat16)).astype(jnp.float32)

@jax.custom_vjp
def low_back(v):
    return v

def low_keep(v):
    return (low(v), None)

def low_pass(kept, grad):
    return (grad,)

def back_keep(v):
    return (v, None)

def back_low(kept, grad):
    return (low(grad),)
low.defvjp(low_keep, low_pass)
low_back.defvjp(back_keep, back_low)

def layer_norm(values, gain, offset):
    average = lax.optimization_barrier(jnp.mean(values, -1, keepdims=True))
    centred = values - average
    variance = lax.optimization_barrier(jnp.mean(centred * centred, -1, keepdims=True))
    return centred * lax.rsqrt(variance + EPSILON) * gain + offset

def rotary_tables(positions):
    exponent = jnp.arange(0, ROT, 2).astype(jnp.float32) / ROT
    frequency = 10000.0 ** (-exponent)
    angles = positions[:, None] * frequency[None, :]
    angles = jnp.concatenate([angles, angles], -1)[:, None, :]
    return (jnp.cos(angles), jnp.sin(angles))

def rotate(values, cosine_table, sine_table):
    section = values[..., :ROT]
    half_rot = ROT // 2
    turned = jnp.concatenate([-section[..., half_rot:], section[..., :half_rot]], -1)
    return jnp.concatenate([section * cosine_table + turned * sine_table, values[..., ROT:]], -1)

def sequence_layer(params, values, segment_ids):
    gain_rows, shift_rows, qkv_weight, qkv_bias, out_weight, out_bias, up_weight, up_bias, down_weight, down_bias = params
    length = values.shape[0]
    normed_attn = low(layer_norm(values, gain_rows[0], shift_rows[0]))
    normed_mlp = low(layer_norm(values, gain_rows[1], shift_rows[1]))
    projected = low_back(jnp.dot(normed_attn, qkv_weight, precision=HIGHEST) + qkv_bias)
    queries = projected[:, :D].reshape(length, HEADS, HEAD)
    keys_raw = projected[:, D:2 * D].reshape(length, HEADS, HEAD)
    values_raw = projected[:, 2 * D:].reshape(length, HEADS, HEAD)
    positions = jnp.arange(length).astype(jnp.float32)
    cosine_table, sine_table = rotary_tables(positions)
    queries = low(rotate(queries, cosine_table, sine_table))
    keys_rot = low(rotate(keys_raw, cosine_table, sine_table))
    values_low = low(values_raw)
    scores = low_back(jnp.einsum('qhd,khd->hqk', queries, keys_rot, precision=HIGHEST) * HEAD ** (-0.5))
    index = jnp.arange(length)
    allowed = (index[:, None] >= index[None, :]) & (segment_ids[:, None] == segment_ids[None, :])
    masked_scores = jnp.where(allowed[None], scores, MASKED)
    highest = lax.optimization_barrier(jnp.max(masked_scores, -1, keepdims=True))
    expanded = jnp.exp(masked_scores - highest)
    probs = expanded / lax.optimization_barrier(jnp.sum(expanded, -1, keepdims=True))
    mixed = jnp.einsum('hqk,khd->qhd', low(probs), values_low, precision=HIGHEST).reshape(length, D)
    mixed = low(low_back(mixed))
    attn_branch = jnp.dot(mixed, out_weight, precision=HIGHEST) + out_bias
    hidden = low_back(jnp.dot(normed_mlp, up_weight, precision=HIGHEST) + up_bias)
    activated = low(jax.nn.gelu(hidden, approximate=False))
    mlp_branch = jnp.dot(activated, down_weight, precision=HIGHEST) + down_bias
    return values + attn_branch + mlp_branch

def reference(inputs, segments, ln_gain, ln_bias, qkv_weight, qkv_bias, out_weight, out_bias, up_weight, up_bias, down_weight, down_bias, cotangent):
    params = tuple((array.astype(jnp.float32) for array in (ln_gain, ln_bias, qkv_weight, qkv_bias, out_weight, out_bias, up_weight, up_bias, down_weight, down_bias)))
    layer_step = jax.checkpoint(sequence_layer)

    def forward(weights, batch):

        def scan_step(carried, element):
            return (carried, layer_step(weights, element[0], element[1]))
        _, outputs = lax.scan(scan_step, jnp.zeros((), jnp.float32), (batch, segments))
        return outputs
    outputs, backward = jax.vjp(forward, params, inputs.astype(jnp.float32))
    grad_params, grad_batch = backward(cotangent.astype(jnp.float32))
    return (outputs.astype(jnp.bfloat16), grad_batch.astype(jnp.bfloat16), grad_params[0], grad_params[1], grad_params[2], grad_params[3], grad_params[4], grad_params[5], grad_params[6], grad_params[7], grad_params[8], grad_params[9])
```

```python
from functools import partial

import jax
import jax.numpy as jnp
from jax import lax
from jax.experimental import pallas as pl
from jax.experimental.pallas import tpu as pltpu
from jax.sharding import PartitionSpec as P

HEADS = 8
HEAD = 256
ROT = 64
EPSILON = 1e-05
MASKED = -1e30
F32 = jnp.float32
BF16 = jnp.bfloat16


def dot(left, right):
    return jnp.dot(left, right, preferred_element_type=F32)


def contract_last(left, right):
    return lax.dot_general(left, right, (((1,), (1,)), ((), ())), preferred_element_type=F32)


def contract_first(left, right):
    return lax.dot_general(left, right, (((0,), (0,)), ((), ())), preferred_element_type=F32)


def rotary_tables(positions):
    half = ROT // 2
    exponent = jnp.arange(0, ROT, 2).astype(F32) / ROT
    frequency = 10000.0 ** (-exponent)
    angles = positions[:, None] * frequency[None, :]
    rows = positions.shape[0]
    cosine, sine = jnp.cos(angles), jnp.sin(angles)
    one, nought = jnp.ones((rows, 64), F32), jnp.zeros((rows, 64), F32)
    blank = jnp.zeros((rows, half), F32)
    return (
        jnp.concatenate([cosine, cosine, one], -1),
        jnp.concatenate([-sine, blank, nought], -1),
        jnp.concatenate([blank, sine, nought], -1),
    )


def rotate(values, tables):
    half = ROT // 2
    cosine, above, below = tables
    low = values[..., :128]
    low = low * cosine + jnp.roll(low, -half, -1) * above + jnp.roll(low, half, -1) * below
    return jnp.concatenate([low, values[..., 128:]], -1)


def attention_kernel(
    block, q_ref, k_ref, v_ref, do_ref, col_ref, row_ref, cos_ref, above_ref, below_ref,
    o_ref, dq_ref, dk_ref, dv_ref, dk_sum, dv_sum,
):
    scale = HEAD ** (-0.5)
    half = ROT // 2
    length = q_ref.shape[0]

    def unrotate(grads, rows):
        low = grads[:, :128]
        low = (
            low * cos_ref[rows, :]
            + pltpu.roll(low * below_ref[rows, :], 128 - half, 1)
            + pltpu.roll(low * above_ref[rows, :], half, 1)
        )
        return jnp.concatenate([low, grads[:, 128:]], -1)

    dk_sum[...] = jnp.zeros_like(dk_sum)
    dv_sum[...] = jnp.zeros_like(dv_sum)
    for start in range(0, length, block):
        rows = pl.ds(start, block)
        keys = pl.ds(0, start + block)
        queries, grads = q_ref[rows, :], do_ref[rows, :]
        key_block, value_block = k_ref[keys, :], v_ref[keys, :]
        scores = contract_last(queries, key_block) * scale
        shape = scores.shape
        query_pos = start + lax.broadcasted_iota(jnp.int32, shape, 0)
        key_pos = lax.broadcasted_iota(jnp.int32, shape, 1)
        allowed = (query_pos >= key_pos) & (col_ref[rows, :] == row_ref[:, keys])
        scores = jnp.where(allowed, scores, MASKED)
        expanded = jnp.exp(scores - jnp.max(scores, -1, keepdims=True))
        probs = expanded / jnp.sum(expanded, -1, keepdims=True)
        probs_low = probs.astype(BF16)
        o_ref[rows, :] = dot(probs_low, value_block).astype(BF16)
        grad_probs = contract_last(grads, value_block)
        row_dot = jnp.sum(probs * grad_probs, -1, keepdims=True)
        grad_scores = (probs * (grad_probs - row_dot)).astype(BF16)
        dq_ref[rows, :] = unrotate(dot(grad_scores, key_block) * scale, rows).astype(BF16)
        dk_sum[keys, :] += contract_first(grad_scores, queries)
        dv_sum[keys, :] += contract_first(probs_low, grads)
    dk_ref[...] = unrotate(dk_sum[...] * scale, pl.ds(0, length)).astype(BF16)
    dv_ref[...] = dv_sum[...].astype(BF16)


def attention(queries, keys, values, grads, segments, tables):
    seqs, length, head = queries.shape
    whole = pl.BlockSpec((None, length, head), lambda s: (s, 0, 0))
    table = pl.BlockSpec((length, 128), lambda s: (0, 0))
    shape = jax.ShapeDtypeStruct(queries.shape, BF16)
    return pl.pallas_call(
        partial(attention_kernel, min(256, length)),
        grid=(seqs,),
        in_specs=[whole] * 4
        + [
            pl.BlockSpec((None, length, 1), lambda s: (s, 0, 0)),
            pl.BlockSpec((None, 1, length), lambda s: (s, 0, 0)),
        ]
        + [table] * 3,
        out_specs=[whole] * 4,
        out_shape=[shape] * 4,
        scratch_shapes=[pltpu.VMEM((length, head), F32)] * 2,
        compiler_params=pltpu.CompilerParams(vmem_limit_bytes=48 << 20),
    )(queries, keys, values, grads, segments[:, :, None], segments[:, None, :], *tables)


def normalize(rows):
    average = jnp.mean(rows, -1, keepdims=True)
    centred = rows - average
    variance = jnp.mean(centred * centred, -1, keepdims=True)
    inverse = lax.rsqrt(variance + EPSILON)
    return centred * inverse, inverse


def gelu_exact(values):
    return jax.nn.gelu(values, approximate=False)


def on_device(
    dp,
    ctx,
    inputs,
    segments,
    ln_gain,
    ln_bias,
    qkv_weight,
    qkv_bias,
    out_weight,
    out_bias,
    up_weight,
    up_bias,
    down_weight,
    down_bias,
    cotangent,
):
    team = HEADS
    teams = dp // team
    together = None if teams == 1 else [[g * team + i for i in range(team)] for g in range(teams)]
    across = None if teams == 1 else [[g * team + i for g in range(teams)] for i in range(team)]
    gather = partial(lax.all_gather, axis_name="dp", tiled=True, axis_index_groups=together)
    place = lax.axis_index("dp")
    rank = place % team
    quarter = lax.axis_index("ctx")
    _, tokens, width = inputs.shape
    rows = qkv_weight.shape[0]
    hidden = up_weight.shape[1] // team
    part = rows // ctx

    small = jnp.concatenate(
        [ln_gain.reshape(-1), ln_bias.reshape(-1), qkv_bias, out_bias, up_bias, down_bias]
    )
    small = lax.all_gather(small, "dp", axis=0).astype(F32)
    cuts = [0]
    for size in (2 * rows, 2 * rows, qkv_bias.shape[0], rows, up_bias.shape[0], rows):
        cuts.append(cuts[-1] + size)
    pieces = [small[:, a:b] for a, b in zip(cuts[:-1], cuts[1:])]
    gains = pieces[0].reshape(dp, 2, rows).transpose(1, 0, 2).reshape(2, width)
    shifts = pieces[1].reshape(dp, 2, rows).transpose(1, 0, 2).reshape(2, width)
    b_qkv = lax.dynamic_index_in_dim(pieces[2].reshape(3, HEADS, HEAD), rank, 1, False)
    b_out, b_down = pieces[3].reshape(width), pieces[5].reshape(width)
    b_up = lax.dynamic_index_in_dim(pieces[4].reshape(team, hidden), rank, 0, False)

    my_rows = quarter * part
    columns = jnp.concatenate(
        [
            lax.dynamic_slice_in_dim(qkv_weight, my_rows, part, 0).reshape(part, 3, HEADS, HEAD)
            .transpose(2, 0, 1, 3).reshape(team, part, 3 * HEAD),
            lax.dynamic_slice_in_dim(up_weight, my_rows, part, 0).reshape(part, team, hidden)
            .transpose(1, 0, 2),
        ],
        -1,
    )
    columns = lax.all_to_all(columns, "dp", 0, 0, axis_index_groups=together, tiled=True)
    columns = lax.all_gather(columns, "ctx", axis=1, tiled=True)
    if across is not None:
        columns = lax.all_gather(columns, "dp", axis=0, tiled=True, axis_index_groups=across)
        w_out = lax.all_gather(out_weight, "dp", axis=0, tiled=True)
        w_out = lax.dynamic_slice_in_dim(w_out, rank * HEAD, HEAD, 0)
        w_down = lax.all_gather(down_weight, "dp", axis=0, tiled=True)
        w_down = lax.dynamic_slice_in_dim(w_down, rank * hidden, hidden, 0)
    else:
        w_out, w_down = out_weight, down_weight
    columns = columns.reshape(width, 3 * HEAD + hidden)
    w_qkv, w_up = columns[:, : 3 * HEAD], columns[:, 3 * HEAD :]

    everyone = gather(inputs, axis=0).reshape(team * tokens, width)
    grad_rows = gather(cotangent, axis=0).reshape(team * tokens, width)
    segments_all = lax.all_gather(segments, "ctx", axis=1, tiled=True)
    segments_all = gather(segments_all, axis=0)
    share = team // ctx
    segments_mine = lax.dynamic_slice_in_dim(segments_all, quarter * share, share, 0)

    unit, _ = normalize(everyone.astype(F32))
    attn_input = (unit * gains[0] + shifts[0]).astype(BF16)
    mlp_input = (unit * gains[1] + shifts[1]).astype(BF16)
    positions = (quarter * tokens + jnp.arange(tokens, dtype=jnp.int32)).astype(F32)
    tables = [table[None, :, None, :] for table in rotary_tables(positions)]
    projected = (dot(attn_input, w_qkv) + b_qkv.reshape(-1)).reshape(team, tokens, 3, HEAD)
    turned = rotate(projected[:, :, :2], tables).astype(BF16)
    grad_attended = contract_last(grad_rows, w_out).astype(BF16).reshape(team, tokens, HEAD)
    sent = jnp.stack(
        [turned[:, :, 0], turned[:, :, 1], projected[:, :, 2].astype(BF16), grad_attended]
    )
    whole = lax.all_to_all(sent, "ctx", 1, 2, tiled=True)
    length = tokens * ctx
    outs = attention(
        whole[0], whole[1], whole[2], whole[3], segments_mine,
        rotary_tables(jnp.arange(length).astype(F32)),
    )
    back = lax.all_to_all(jnp.stack(outs), "ctx", 2, 1, tiled=True)
    back = back.reshape(4, team * tokens, HEAD)
    attended = back[0]
    grad_qkv = jnp.concatenate([back[1], back[2], back[3]], -1)

    up_values = dot(mlp_input, w_up) + b_up
    activated, gelu_back = jax.vjp(gelu_exact, up_values)
    activated = activated.astype(BF16)
    grad_up = gelu_back(contract_last(grad_rows, w_down))[0].astype(BF16)

    branches = (dot(attended, w_out) + dot(activated, w_down)).astype(BF16)
    branches = lax.psum_scatter(
        branches, "dp", scatter_dimension=0, axis_index_groups=together, tiled=True
    ).astype(F32)
    mine = inputs.reshape(tokens, width).astype(F32)
    result = (mine + (branches + (b_out + b_down))).astype(BF16)

    grad_attn_in = contract_last(grad_qkv, w_qkv)
    grad_mlp_in = contract_last(grad_up, w_up)
    pulled = (grad_attn_in * gains[0] + grad_mlp_in * gains[1]).astype(BF16)
    pulled = lax.psum_scatter(
        pulled, "dp", scatter_dimension=0, axis_index_groups=together, tiled=True
    ).astype(F32)
    my_unit, my_inverse = normalize(mine)
    grad_inputs = cotangent.reshape(tokens, width).astype(F32) + my_inverse * (
        pulled
        - jnp.mean(pulled, -1, keepdims=True)
        - my_unit * jnp.mean(pulled * my_unit, -1, keepdims=True)
    )

    grad_float = grad_rows.astype(F32)
    qkv_bias_sum = jnp.sum(grad_qkv.astype(F32), 0).reshape(3, 1, HEAD)
    qkv_bias_sum = lax.dynamic_update_slice_in_dim(
        jnp.zeros((3, HEADS, HEAD), F32), qkv_bias_sum, rank, 1
    )
    up_bias_sum = lax.dynamic_update_slice_in_dim(
        jnp.zeros((team, hidden), F32), jnp.sum(grad_up.astype(F32), 0)[None], rank, 0
    )
    dy_sum = jnp.sum(grad_float, 0) * jnp.where(rank == 0, 1.0, 0.0)
    vector = jnp.concatenate(
        [
            jnp.sum(grad_attn_in * unit, 0),
            jnp.sum(grad_mlp_in * unit, 0),
            jnp.sum(grad_attn_in, 0),
            jnp.sum(grad_mlp_in, 0),
            qkv_bias_sum.reshape(-1),
            dy_sum,
            up_bias_sum.reshape(-1),
        ]
    )
    vector = lax.psum(vector, ("dp", "ctx"))

    def own(start, size):
        return lax.dynamic_slice_in_dim(vector, start + place * (size // dp), size // dp, 0)

    grad_gain = jnp.stack([own(0, width), own(width, width)])
    grad_shift = jnp.stack([own(2 * width, width), own(3 * width, width)])
    grad_qkv_b = own(4 * width, 3 * width)
    grad_out_b = own(7 * width, width)
    grad_up_b = own(8 * width, team * hidden)

    term_out = contract_first(attended, grad_rows).astype(BF16)
    term_down = contract_first(activated, grad_rows).astype(BF16)
    term_columns = jnp.concatenate(
        [
            contract_first(attn_input, grad_qkv).astype(BF16),
            contract_first(mlp_input, grad_up).astype(BF16),
        ],
        -1,
    )
    if across is not None:
        full = jnp.zeros((team, HEAD, width), BF16)
        full = lax.dynamic_update_slice_in_dim(full, term_out[None], rank, 0)
        term_out = lax.psum_scatter(
            full.reshape(width, width), "dp", scatter_dimension=0, tiled=True
        )
        full = jnp.zeros((team, hidden, width), BF16)
        full = lax.dynamic_update_slice_in_dim(full, term_down[None], rank, 0)
        term_down = lax.psum_scatter(
            full.reshape(team * hidden, width), "dp", scatter_dimension=0, tiled=True
        )
        term_columns = lax.psum_scatter(
            term_columns, "dp", scatter_dimension=0, axis_index_groups=across, tiled=True
        )
    grad_out_w = lax.psum(term_out, "ctx").astype(F32)
    grad_down_w = lax.psum(term_down, "ctx").astype(F32)
    term_columns = term_columns.reshape(team, rows, 3 * HEAD + hidden)
    term_columns = lax.psum_scatter(term_columns, "ctx", scatter_dimension=1, tiled=True)
    term_columns = lax.all_to_all(
        term_columns, "dp", 0, 0, axis_index_groups=together, tiled=True
    )
    term_columns = lax.all_gather(term_columns, "ctx", axis=1, tiled=True)
    grad_qkv_w = (
        term_columns[:, :, : 3 * HEAD].reshape(team, rows, 3, HEAD).transpose(1, 2, 0, 3)
        .reshape(rows, 3 * width).astype(F32)
    )
    grad_up_w = (
        term_columns[:, :, 3 * HEAD :].transpose(1, 0, 2).reshape(rows, team * hidden).astype(F32)
    )
    return (
        result.reshape(inputs.shape),
        grad_inputs.astype(BF16).reshape(inputs.shape),
        grad_gain,
        grad_shift,
        grad_qkv_w,
        grad_qkv_b,
        grad_out_w,
        grad_out_b,
        grad_up_w,
        grad_up_b,
        grad_down_w,
        grad_out_b,
    )


def solution(mesh):
    placed = (
        P("dp", "ctx", None),
        P("dp", "ctx"),
        P(None, "dp"),
        P(None, "dp"),
        P("dp", None),
        P("dp"),
        P("dp", None),
        P("dp"),
        P("dp", None),
        P("dp"),
        P("dp", None),
        P("dp"),
        P("dp", "ctx", None),
    )
    return jax.shard_map(
        partial(on_device, mesh.shape["dp"], mesh.shape["ctx"]),
        mesh=mesh,
        in_specs=placed,
        out_specs=(
            P("dp", "ctx", None),
            P("dp", "ctx", None),
            P(None, "dp"),
            P(None, "dp"),
            P("dp", None),
            P("dp"),
            P("dp", None),
            P("dp"),
            P("dp", None),
            P("dp"),
            P("dp", None),
            P("dp"),
        ),
        check_vma=False,
    )
```

```python
from functools import partial

import jax
import jax.numpy as jnp
from jax import lax
from jax.experimental import pallas as pl
from jax.experimental.pallas import tpu as pltpu
from jax.sharding import PartitionSpec as P

HEADS = 8
HEAD = 256
ROT = 64
EPSILON = 1e-05
MASKED = -1e30
F32 = jnp.float32
BF16 = jnp.bfloat16
MESH = pl.DeviceIdType.MESH
TEAM = HEADS
PAIRS = TEAM // 2
QUARTERS = 4
RIGHT, LEFT = 0, 1
VECTOR_ROWS = 24


def dot(left, right):
    return jnp.dot(left, right, preferred_element_type=F32)


def contract_last(left, right):
    return lax.dot_general(left, right, (((1,), (1,)), ((), ())), preferred_element_type=F32)


def contract_first(left, right):
    return lax.dot_general(left, right, (((0,), (0,)), ((), ())), preferred_element_type=F32)


def rotary_tables(positions):
    half = ROT // 2
    exponent = jnp.arange(0, ROT, 2).astype(F32) / ROT
    frequency = 10000.0 ** (-exponent)
    angles = positions[:, None] * frequency[None, :]
    rows = positions.shape[0]
    cosine, sine = jnp.cos(angles), jnp.sin(angles)
    one, nought = jnp.ones((rows, 64), F32), jnp.zeros((rows, 64), F32)
    blank = jnp.zeros((rows, half), F32)
    return (
        jnp.concatenate([cosine, cosine, one], -1),
        jnp.concatenate([-sine, blank, nought], -1),
        jnp.concatenate([blank, sine, nought], -1),
    )


def spot():
    place = lax.axis_index("dp")
    rank = lax.rem(place, TEAM)
    return place - rank, lax.div(rank, 2), lax.rem(rank, 2), lax.axis_index("ctx")


def near_first(line):
    second = 1 + lax.rem(line, 2)
    last = 3 * (1 - lax.div(line, 2))
    return (line, second, 6 - line - second - last, last)


def core_peer(quarter):
    return quarter + 1 - 2 * lax.rem(quarter, 2)


def chip_peer(quarter):
    return quarter + 2 - 4 * lax.div(quarter, 2)


def send(src, dst, send_sem, recv_sem, place, quarter):
    return pltpu.make_async_remote_copy(
        src_ref=src, dst_ref=dst, send_sem=send_sem, recv_sem=recv_sem,
        device_id=(place, quarter), device_id_type=MESH,
    )


def greet_line(base, line, side, quarter):
    barrier = pltpu.get_barrier_semaphore()

    def hail(place, quarter):
        pl.semaphore_signal(barrier, inc=1, device_id=(place, quarter), device_id_type=MESH)

    rank = line * 2 + side
    hail(base + line * 2 + 1 - side, quarter)

    pl.when(line < PAIRS - 1)(lambda: hail(base + rank + 2, quarter))
    pl.when(line > 0)(lambda: hail(base + rank - 2, quarter))
    for step in range(1, QUARTERS):
        hail(base + rank, lax.rem(quarter + step, QUARTERS))
    neighbours = 1 + lax.div(line + 2, 3) - lax.div(line, 3)
    pl.semaphore_wait(barrier, neighbours + QUARTERS)


def greet_team(base, line, side, quarter):
    barrier = pltpu.get_barrier_semaphore()
    rank = line * 2 + side
    for step in range(1, TEAM):
        pl.semaphore_signal(
            barrier, inc=1, device_id=(base + lax.rem(rank + step, TEAM), quarter),
            device_id_type=MESH,
        )
    for step in range(1, QUARTERS):
        pl.semaphore_signal(
            barrier, inc=1, device_id=(base + rank, lax.rem(quarter + step, QUARTERS)),
            device_id_type=MESH,
        )
    pl.semaphore_wait(barrier, TEAM + QUARTERS - 2)


class Relay:
    def __init__(self, held, line_send, line_recv, side_send, side_recv):
        self.held = held
        self.sems = line_send, line_recv, side_send, side_recv
        self.base, self.line, self.side, self.quarter = spot()

    def along(self, source, way):
        line_send, line_recv, _, _ = self.sems
        block = self.held.at[source * 2 + self.side]
        place = self.base + self.line * 2 + self.side + (2 if way == RIGHT else -2)
        return send(
            block, block, line_send.at[way, source], line_recv.at[source], place, self.quarter
        )

    def over(self, source, side):
        _, _, side_send, side_recv = self.sems
        block = self.held.at[source * 2 + side]
        place = self.base + self.line * 2 + 1 - self.side
        return send(block, block, side_send.at[source], side_recv.at[source], place, self.quarter)

    def each(self, step, act):
        line = self.line
        if step == 0:
            pl.when(line < PAIRS - 1)(lambda: act(line, RIGHT))
            pl.when(line > 0)(lambda: act(line, LEFT))
            act(line, None)
            return

        @pl.when(line >= step)
        def _():
            source = line - step
            act(source, "arrive")
            pl.when(line < PAIRS - 1)(lambda: act(source, RIGHT))
            act(source, None)

        @pl.when(line + step < PAIRS)
        def _():
            source = line + step
            act(source, "arrive")
            pl.when(line > 0)(lambda: act(source, LEFT))
            act(source, None)

    def start(self, step):
        def act(source, way):
            if way == "arrive":
                self.along(source, RIGHT).wait_recv()
            elif way is None:
                self.over(source, self.side).start()
            else:
                self.along(source, way).start()

        self.each(step, act)

    def finish(self):
        def act(source, way):
            if way is None:
                self.over(source, self.side).wait_send()
            elif way != "arrive":
                self.along(source, way).wait_send()

        for step in range(PAIRS):
            self.each(step, act)

    def wait_over(self, source):
        self.over(source, 1 - self.side).wait_recv()


RELAY_SEMS = [
    pltpu.SemaphoreType.DMA((2, PAIRS)),
    pltpu.SemaphoreType.DMA((PAIRS,)),
    pltpu.SemaphoreType.DMA((PAIRS,)),
    pltpu.SemaphoreType.DMA((PAIRS,)),
]


def normalize(rows):
    average = jnp.mean(rows, -1, keepdims=True)
    centred = rows - average
    variance = jnp.mean(centred * centred, -1, keepdims=True)
    inverse = lax.rsqrt(variance + EPSILON)
    return centred * inverse, inverse


def rotate_low(low, cosine, above, below):
    half = ROT // 2
    return (
        low * cosine + pltpu.roll(low, 128 - half, 1) * above + pltpu.roll(low, half, 1) * below
    )


def unrotate_low(low, cosine, above, below):
    half = ROT // 2
    return (
        low * cosine + pltpu.roll(low * below, 128 - half, 1) + pltpu.roll(low * above, half, 1)
    )


class Spread:
    def __init__(self, pieces, send_sem, recv_sem, own_sem):
        self.pieces, self.sems = pieces, (send_sem, recv_sem, own_sem)
        base, line, side, self.quarter = spot()
        self.place = base + line * 2 + side

    def _remote(self, index, sequence, to, origin):
        src, dst = self.pieces[index]
        send_sem, recv_sem, _ = self.sems
        return send(
            src(sequence), dst(lax.rem(sequence, 2), origin), send_sem.at[index, sequence],
            recv_sem.at[index, origin, lax.rem(sequence, 2)], self.place, to,
        )

    def _own(self, index, sequence):
        src, dst = self.pieces[index]
        return pltpu.make_async_copy(
            src(sequence), dst(lax.rem(sequence, 2), self.quarter),
            self.sems[2].at[index, lax.rem(sequence, 2)],
        )

    def start(self, sequence):
        to = lax.div(sequence, 2)

        @pl.when(to == self.quarter)
        def _():
            for index in range(len(self.pieces)):
                self._own(index, sequence).start()

        @pl.when(to != self.quarter)
        def _():
            for index in range(len(self.pieces)):
                self._remote(index, sequence, to, self.quarter).start()

    def finish(self):
        def sent(sequence, _):
            to = lax.div(sequence, 2)

            @pl.when(to == self.quarter)
            def _():
                for index in range(len(self.pieces)):
                    self._own(index, sequence).wait()

            @pl.when(to != self.quarter)
            def _():
                for index in range(len(self.pieces)):
                    self._remote(index, sequence, to, self.quarter).wait_send()

        lax.fori_loop(0, TEAM, sent, None)

        def landed(step, _):
            origin = lax.rem(self.quarter + 1 + lax.div(step, 2), QUARTERS)
            sequence = lax.rem(step, 2)
            for index in range(len(self.pieces)):
                self._remote(index, sequence, origin, origin).wait_recv()

        lax.fori_loop(0, 2 * (QUARTERS - 1), landed, None)


def spread_sems(count):
    return [
        pltpu.SemaphoreType.DMA((count, TEAM)),
        pltpu.SemaphoreType.DMA((count, QUARTERS, 2)),
        pltpu.SemaphoreType.DMA((count, 2)),
    ]


def first_kernel(
    x_ref, wq_ref, wu_ref, vec_ref, upb_ref, cos_ref, above_ref, below_ref,
    x_out, ha_out, hm_out, u_out, w_out, qkv_out, seg_out, vec_out,
    held, weight, vecs, ha, hm, up, qkv, vectors,
    own_sem, store_sem, w_send, w_recv, w_own, core_send, core_recv, chip_send, chip_recv,
    last_send, last_recv, v_send, v_recv, spread_send, spread_recv, spread_own, *relay_sems,
):
    base, line, side, quarter = spot()
    rank = line * 2 + side
    tokens, width = x_ref.shape
    rows = wq_ref.shape[0]
    part = rows // QUARTERS
    hidden = up.shape[-1]
    core, chip = core_peer(quarter), chip_peer(quarter)
    relay = Relay(held, *relay_sems)
    spread = Spread(
        [
            (
                lambda s: qkv.at[s],
                lambda j, origin: qkv_out.at[j, :, pl.ds(origin * tokens, tokens), :],
            ),
            (lambda s: vecs.at[s, pl.ds(16, 8), :], lambda j, origin: seg_out.at[j, origin]),
        ],
        spread_send, spread_recv, spread_own,
    )
    greet_team(base, line, side, quarter)

    own_x = pltpu.make_async_copy(x_ref, held.at[rank], own_sem.at[0])
    own_x.start()
    own_v = pltpu.make_async_copy(vec_ref, vecs.at[rank], own_sem.at[1])
    own_v.start()

    def band(origin, slice_of):
        return pl.ds(pl.multiple_of(origin * rows + slice_of * part, 16), part)

    def columns(source, target):
        mine = pl.ds(pl.multiple_of(quarter * part, 16), part)
        pieces = []
        for kind in range(3):
            start = pl.multiple_of(kind * width + target * HEAD, HEAD)
            pieces.append(
                (
                    wq_ref.at[mine, pl.ds(start, HEAD)],
                    weight.at[band(source, quarter), pl.ds(kind * HEAD, HEAD)],
                )
            )
        start = pl.multiple_of(target * hidden, hidden)
        pieces.append(
            (
                wu_ref.at[mine, pl.ds(start, hidden)],
                weight.at[band(source, quarter), pl.ds(3 * HEAD, hidden)],
            )
        )
        return pieces

    def column_copies(source, target, peer):
        return [
            send(src, dst, w_send.at[kind, target], w_recv.at[kind, source], base + peer, quarter)
            for kind, (src, dst) in enumerate(columns(source, target))
        ]

    def vector_copy(source, target, peer):
        return send(
            vec_ref, vecs.at[source], v_send.at[target], v_recv.at[source], base + peer, quarter
        )

    def send_columns(step, _):
        target = lax.rem(rank + step, TEAM)
        vector_copy(rank, target, target).start()
        for copy in column_copies(rank, target, target):
            copy.start()

    lax.fori_loop(1, TEAM, send_columns, None)
    own_columns = [
        pltpu.make_async_copy(src, dst, w_own.at[kind])
        for kind, (src, dst) in enumerate(columns(rank, rank))
    ]
    for copy in own_columns:
        copy.start()
    own_x.wait()
    own_v.wait()
    relay.start(0)

    def pass_on(origin, slice_of, sends, recvs, to):
        block = weight.at[band(origin, slice_of), :]
        return send(block, block, sends.at[origin], recvs.at[origin], base + rank, to)

    def to_core(origin):
        return pass_on(origin, quarter, core_send, core_recv, core)

    def to_chip(origin):
        return pass_on(origin, quarter, chip_send, chip_recv, chip)

    def to_last(origin):
        return pass_on(origin, chip, last_send, last_recv, core)

    for copy in own_columns:
        copy.wait()
    to_chip(rank).start()
    to_core(rank).start()

    def forward_columns(step, _):
        origin = lax.rem(rank + TEAM - step, TEAM)
        for copy in column_copies(origin, rank, origin):
            copy.wait_recv()
        to_chip(origin).start()
        to_core(origin).start()

    lax.fori_loop(1, TEAM, forward_columns, None)
    relay.start(1)

    def forward_chip(step, _):
        origin = lax.rem(rank + TEAM - step, TEAM)
        pass_on(origin, chip, chip_send, chip_recv, chip).wait_recv()
        to_last(origin).start()

    lax.fori_loop(0, TEAM, forward_chip, None)
    relay.start(2)

    def take_vectors(step, _):
        origin = lax.rem(rank + TEAM - step, TEAM)
        vector_copy(origin, rank, origin).wait_recv()

    lax.fori_loop(1, TEAM, take_vectors, None)
    for source in range(TEAM):
        for row in range(4):
            vectors[pl.ds(row, 1), pl.ds(source * rows, rows)] = vecs[source, pl.ds(row, 1), :]

    def last_columns(step, _):
        origin = lax.rem(rank + TEAM - step, TEAM)
        pass_on(origin, core, core_send, core_recv, core).wait_recv()
        pass_on(origin, chip_peer(core), last_send, last_recv, core).wait_recv()

    lax.fori_loop(0, TEAM, last_columns, None)
    stores = [
        pltpu.make_async_copy(weight, w_out, store_sem.at[0]),
        pltpu.make_async_copy(vecs, vec_out, store_sem.at[1]),
    ]
    for copy in stores:
        copy.start()

    strip = 32

    def work(which):
        def norm(index, _):
            chunk = pl.ds(pl.multiple_of(index * strip, strip), strip)
            unit, _ = normalize(held[which, chunk, :].astype(F32))
            ha[which, chunk, :] = (unit * vectors[0:1, :] + vectors[2:3, :]).astype(BF16)
            hm[which, chunk, :] = (unit * vectors[1:2, :] + vectors[3:4, :]).astype(BF16)

        lax.fori_loop(0, tokens // strip, norm, None)
        for kind in range(3):
            chunk = kind * TEAM + rank
            bias = vecs[lax.div(chunk, 3), pl.ds(8 + lax.rem(chunk, 3), 1), :]
            made = dot(ha[which], weight[:, pl.ds(kind * HEAD, HEAD)]) + bias
            if kind < 2:
                low = rotate_low(made[:, :128], cos_ref[...], above_ref[...], below_ref[...])
                qkv[which, kind, :, pl.ds(0, 128)] = low.astype(BF16)
                qkv[which, kind, :, pl.ds(128, HEAD - 128)] = made[:, 128:].astype(BF16)
            else:
                qkv[which, kind] = made.astype(BF16)
        spread.start(which)
        for start in range(0, hidden, 256):
            span = pl.ds(start, 256)
            up[which, :, span] = (
                dot(hm[which], weight[:, pl.ds(3 * HEAD + start, 256)]) + upb_ref[:, span]
            )

    for step, place in enumerate(near_first(line)):

        def one(other, _, step=step, place=place):
            @pl.when(other == 1)
            def _():
                if step == 0:
                    relay.start(3)
                relay.wait_over(place)

            work(place * 2 + side + other * (1 - 2 * side))

        lax.fori_loop(0, 2, one, None)

    for index, (src, dst) in enumerate(((held, x_out), (ha, ha_out), (hm, hm_out), (up, u_out))):
        stores.append(pltpu.make_async_copy(src, dst, store_sem.at[2 + index]))
        stores[-1].start()
    relay.finish()
    spread.finish()

    def sent(step, _):
        target = lax.rem(rank + step, TEAM)
        vector_copy(rank, target, target).wait_send()
        for copy in column_copies(rank, target, target):
            copy.wait_send()

    lax.fori_loop(1, TEAM, sent, None)

    def passed(origin, _):
        to_core(origin).wait_send()
        to_chip(origin).wait_send()
        to_last(origin).wait_send()

    lax.fori_loop(0, TEAM, passed, None)
    for copy in stores:
        copy.wait()


ANY = pl.BlockSpec(memory_space=pl.ANY)
VMEM = pl.BlockSpec(memory_space=pltpu.VMEM)
DMA = pltpu.SemaphoreType.DMA
LIMIT = 60 << 20


def first(x, w_qkv, w_up, vec, up_bias, tables):
    tokens, width = x.shape
    hidden = up_bias.shape[-1]
    span = 3 * HEAD + hidden
    shapes = [
        ((TEAM, tokens, width), BF16),
        ((TEAM, tokens, width), BF16),
        ((TEAM, tokens, width), BF16),
        ((TEAM, tokens, hidden), F32),
        ((width, span), BF16),
        ((2, 3, QUARTERS * tokens, HEAD), BF16),
        ((2, QUARTERS, 8, tokens), F32),
        ((TEAM, VECTOR_ROWS, vec.shape[-1]), F32),
    ]
    return pl.pallas_call(
        first_kernel,
        out_shape=[jax.ShapeDtypeStruct(*shape) for shape in shapes],
        in_specs=[VMEM, ANY, ANY, VMEM, VMEM, VMEM, VMEM, VMEM],
        out_specs=[ANY] * len(shapes),
        scratch_shapes=[
            pltpu.VMEM((TEAM, tokens, width), BF16),
            pltpu.VMEM((width, span), BF16),
            pltpu.VMEM((TEAM, VECTOR_ROWS, vec.shape[-1]), F32),
            pltpu.VMEM((TEAM, tokens, width), BF16),
            pltpu.VMEM((TEAM, tokens, width), BF16),
            pltpu.VMEM((TEAM, tokens, hidden), F32),
            pltpu.VMEM((TEAM, 3, tokens, HEAD), BF16),
            pltpu.VMEM((8, width), F32),
            DMA((2,)),
            DMA((6,)),
            DMA((4, TEAM)),
            DMA((4, TEAM)),
            DMA((4,)),
        ]
        + [DMA((TEAM,))] * 8
        + spread_sems(2)
        + RELAY_SEMS,
        compiler_params=pltpu.CompilerParams(
            collective_id=0, has_side_effects=True, vmem_limit_bytes=LIMIT
        ),
        name="gather_x",
    )(x, w_qkv, w_up, vec, up_bias, *tables)


def gelu_terms(values):
    chance = 0.5 * (1.0 + lax.erf(values * (0.5**0.5)))
    density = jnp.exp(-0.5 * values * values) * 0.3989422804014327
    return values * chance, chance + values * density


def second_kernel(
    dy_ref, wo_ref, wd_ref, u_ref, o_ref,
    dy_out, a_out, du_out, do_out, o_out, sum_out,
    held, up, act, grad, attended,
    own_sem, load_sem, store_sem, back_send, back_recv, spread_send, spread_recv, spread_own,
    *relay_sems,
):
    base, line, side, quarter = spot()
    rank = line * 2 + side
    tokens, width = dy_ref.shape
    hidden = up.shape[-1]
    relay = Relay(held, *relay_sems)
    spread = Spread(
        [
            (
                lambda s: attended.at[s],
                lambda j, origin: do_out.at[j, pl.ds(origin * tokens, tokens), :],
            )
        ],
        spread_send, spread_recv, spread_own,
    )
    loads = pltpu.make_async_copy(u_ref, up, load_sem)
    loads.start()
    greet_line(base, line, side, quarter)
    own = pltpu.make_async_copy(dy_ref, held.at[rank], own_sem.at[0])
    own.start()
    own.wait()
    relay.start(0)

    def back(to, origin):
        return send(
            o_ref.at[:, pl.ds(to * tokens, tokens), :], o_out.at[pl.ds(2 * origin, 2)],
            back_send.at[to], back_recv.at[origin], base + rank, to,
        )

    own_back = pltpu.make_async_copy(
        o_ref.at[:, pl.ds(quarter * tokens, tokens), :], o_out.at[pl.ds(2 * quarter, 2)],
        own_sem.at[1],
    )
    own_back.start()
    for step in range(1, QUARTERS):
        back(lax.rem(quarter + step, QUARTERS), quarter).start()
    loads.wait()
    sum_out[...] = jnp.zeros_like(sum_out)

    def work(which):
        attended[which] = contract_last(held[which], wo_ref[...]).astype(BF16)
        spread.start(which)
        for start in range(0, hidden, 256):
            span = pl.ds(start, 256)
            value, slope = gelu_terms(up[which, :, span])
            act[which, :, span] = value.astype(BF16)
            pulled = contract_last(held[which], wd_ref[span, :])
            grad[which, :, span] = (pulled * slope).astype(BF16)
        sum_out[0:1, :] += jnp.sum(held[which].astype(F32), 0, keepdims=True)

    for step, place in enumerate(near_first(line)):

        def one(other, _, step=step, place=place):
            @pl.when(other == 1)
            def _():
                if step < PAIRS - 1:
                    relay.start(step + 1)
                relay.wait_over(place)

            work(place * 2 + side + other * (1 - 2 * side))

        lax.fori_loop(0, 2, one, None)

    stores = []
    for index, (src, dst) in enumerate(((held, dy_out), (act, a_out), (grad, du_out))):
        stores.append(pltpu.make_async_copy(src, dst, store_sem.at[index]))
        stores[-1].start()
    relay.finish()
    spread.finish()
    for step in range(1, QUARTERS):
        back(lax.rem(quarter + step, QUARTERS), quarter).wait_send()
        origin = lax.rem(quarter + step, QUARTERS)
        back(origin, origin).wait_recv()
    own_back.wait()
    for copy in stores:
        copy.wait()


def second(dy, w_out, w_down, up_values, attended):
    tokens, width = dy.shape
    hidden = up_values.shape[-1]
    shapes = [
        ((TEAM, tokens, width), BF16),
        ((TEAM, tokens, hidden), BF16),
        ((TEAM, tokens, hidden), BF16),
        ((2, QUARTERS * tokens, HEAD), BF16),
        ((TEAM, tokens, HEAD), BF16),
        ((8, width), F32),
    ]
    return pl.pallas_call(
        second_kernel,
        out_shape=[jax.ShapeDtypeStruct(*shape) for shape in shapes],
        in_specs=[VMEM, VMEM, VMEM, ANY, ANY],
        out_specs=[ANY] * 5 + [VMEM],
        scratch_shapes=[
            pltpu.VMEM((TEAM, tokens, width), BF16),
            pltpu.VMEM((TEAM, tokens, hidden), F32),
            pltpu.VMEM((TEAM, tokens, hidden), BF16),
            pltpu.VMEM((TEAM, tokens, hidden), BF16),
            pltpu.VMEM((TEAM, tokens, HEAD), BF16),
            DMA((2,)),
            DMA,
            DMA((3,)),
            DMA((QUARTERS,)),
            DMA((QUARTERS,)),
        ]
        + spread_sems(1)
        + RELAY_SEMS,
        compiler_params=pltpu.CompilerParams(
            collective_id=1, has_side_effects=True, vmem_limit_bytes=LIMIT
        ),
        name="gather_dy",
    )(dy, w_out, w_down, up_values, attended)


def probabilities(start, block, q_ref, k_ref, col_ref, row_ref):
    rows, keys = pl.ds(start, block), pl.ds(0, start + block)
    scores = contract_last(q_ref[rows, :], k_ref[keys, :]) * HEAD ** (-0.5)
    shape = scores.shape
    query_pos = start + lax.broadcasted_iota(jnp.int32, shape, 0)
    key_pos = lax.broadcasted_iota(jnp.int32, shape, 1)
    allowed = (query_pos >= key_pos) & (col_ref[rows, :] == row_ref[:, keys])
    scores = jnp.where(allowed, scores, MASKED)
    expanded = jnp.exp(scores - jnp.max(scores, -1, keepdims=True))
    return expanded / jnp.sum(expanded, -1, keepdims=True)


def forward_kernel(block, qkv_ref, col_ref, row_ref, o_ref):
    q_ref, k_ref, v_ref = (qkv_ref.at[kind] for kind in range(3))
    for start in range(0, o_ref.shape[0], block):
        probs = probabilities(start, block, q_ref, k_ref, col_ref, row_ref)
        value_block = v_ref[pl.ds(0, start + block), :]
        o_ref[pl.ds(start, block), :] = dot(probs.astype(BF16), value_block).astype(BF16)


def backward_kernel(
    block, qkv_ref, do_ref, col_ref, row_ref, cos_ref, above_ref, below_ref, d_ref, dk_sum, dv_sum
):
    scale = HEAD ** (-0.5)
    q_ref, k_ref, v_ref = (qkv_ref.at[kind] for kind in range(3))
    length = q_ref.shape[0]

    def put(kind, rows, grads):
        low = unrotate_low(
            grads[:, :128], cos_ref[rows, :], above_ref[rows, :], below_ref[rows, :]
        )
        d_ref[kind, rows, pl.ds(0, 128)] = low.astype(BF16)
        d_ref[kind, rows, pl.ds(128, HEAD - 128)] = grads[:, 128:].astype(BF16)

    dk_sum[...] = jnp.zeros_like(dk_sum)
    dv_sum[...] = jnp.zeros_like(dv_sum)
    for start in range(0, length, block):
        rows, keys = pl.ds(start, block), pl.ds(0, start + block)
        probs = probabilities(start, block, q_ref, k_ref, col_ref, row_ref)
        grads = do_ref[rows, :]
        grad_probs = contract_last(grads, v_ref[keys, :])
        row_dot = jnp.sum(probs * grad_probs, -1, keepdims=True)
        grad_scores = (probs * (grad_probs - row_dot)).astype(BF16)
        put(0, rows, dot(grad_scores, k_ref[keys, :]) * scale)
        dk_sum[keys, :] += contract_first(grad_scores, q_ref[rows, :])
        dv_sum[keys, :] += contract_first(probs.astype(BF16), grads)
    put(1, pl.ds(0, length), dk_sum[...] * scale)
    d_ref[2] = dv_sum[...].astype(BF16)


def attention_specs(seqs, length):
    three = pl.BlockSpec((None, 3, length, HEAD), lambda s: (s, 0, 0, 0))
    one = pl.BlockSpec((None, length, HEAD), lambda s: (s, 0, 0))
    masks = [
        pl.BlockSpec((None, length, 1), lambda s: (s, 0, 0)),
        pl.BlockSpec((None, 1, length), lambda s: (s, 0, 0)),
    ]
    return three, one, masks


def attend(qkv, column, row):
    seqs, _, length, head = qkv.shape
    three, one, masks = attention_specs(seqs, length)
    return pl.pallas_call(
        partial(forward_kernel, min(256, length)),
        grid=(seqs,),
        in_specs=[three] + masks,
        out_specs=one,
        out_shape=jax.ShapeDtypeStruct((seqs, length, head), BF16),
        compiler_params=pltpu.CompilerParams(vmem_limit_bytes=48 << 20),
        name="attend",
    )(qkv, column, row)


def attend_back(qkv, grads, column, row, tables):
    seqs, _, length, head = qkv.shape
    three, one, masks = attention_specs(seqs, length)
    table = pl.BlockSpec((length, 128), lambda s: (0, 0))
    return pl.pallas_call(
        partial(backward_kernel, min(256, length)),
        grid=(seqs,),
        in_specs=[three, one] + masks + [table] * 3,
        out_specs=three,
        out_shape=jax.ShapeDtypeStruct(qkv.shape, BF16),
        scratch_shapes=[pltpu.VMEM((length, head), F32)] * 2,
        compiler_params=pltpu.CompilerParams(vmem_limit_bytes=48 << 20),
        name="attend_back",
    )(qkv, grads, column, row, *tables)


class Reduce:
    def __init__(self, own, side_out, side_in, line_out, line_in, sems):
        self.own, self.side_out, self.side_in = own, side_out, side_in
        self.line_out, self.line_in, self.sems = line_out, line_in, sems
        self.base, self.line, self.side, self.quarter = spot()
        self.order = near_first(self.line)

    def over(self, step):
        side_send, side_recv = self.sems[:2]
        place = self.base + self.line * 2 + 1 - self.side
        return send(
            self.side_out.at[step], self.side_in.at[step], side_send.at[step], side_recv.at[step],
            place, self.quarter,
        )

    def along(self, step, target, way):
        line_send, line_recv = self.sems[2:]
        move = 1 if way == RIGHT else -1
        slot = target if way == RIGHT else jnp.where(target == self.line - 1, PAIRS, target)
        place = self.base + (self.line + move) * 2 + self.side
        return send(
            self.line_out.at[step], self.line_in.at[slot], line_send.at[step], line_recv.at[slot],
            place, self.quarter,
        )

    def arrive(self, slot):
        line_send, line_recv = self.sems[2:]
        return send(
            self.line_out.at[0], self.line_in.at[slot], line_send.at[0], line_recv.at[slot],
            self.base + self.line * 2 + 1 - self.side, self.quarter,
        )

    def begin(self, step):
        self.over(step).start()

    def advance(self, step):
        target = self.order[step]
        self.over(step).wait_recv()

        def forward(way, upstream):
            @pl.when(upstream)
            def _():
                self.arrive(target).wait_recv()

            strip = 64

            def add(index, _):
                chunk = pl.ds(pl.multiple_of(index * strip, strip), strip)
                total = self.own[step, chunk, :] + self.side_in[step, chunk, :].astype(F32)
                held = self.line_in[target, chunk, :].astype(F32)
                total = jnp.where(upstream, total + held, total)
                self.line_out[step, chunk, :] = total.astype(BF16)

            lax.fori_loop(0, self.own.shape[1] // strip, add, None)
            self.along(step, target, way).start()

        @pl.when(target > self.line)
        def _():
            forward(RIGHT, self.line > 0)

        @pl.when(target < self.line)
        def _():
            forward(LEFT, self.line < PAIRS - 1)

    def last(self):
        self.over(0).wait_recv()
        pl.when(self.line > 0)(lambda: self.arrive(self.line).wait_recv())
        pl.when(self.line < PAIRS - 1)(lambda: self.arrive(PAIRS).wait_recv())

    def total(self, chunk):
        total = self.own[0, chunk, :] + self.side_in[0, chunk, :].astype(F32)
        left = self.line_in[self.line, chunk, :].astype(F32)
        right = self.line_in[PAIRS, chunk, :].astype(F32)
        total = jnp.where(self.line > 0, total + left, total)
        return jnp.where(self.line < PAIRS - 1, total + right, total)

    def finish(self):
        for step in range(PAIRS):
            self.over(step).wait_send()
        for step in range(1, PAIRS):
            target = self.order[step]
            pl.when(target > self.line)(lambda: self.along(step, target, RIGHT).wait_send())
            pl.when(target < self.line)(lambda: self.along(step, target, LEFT).wait_send())


def reduce_scratch(tokens, width):
    return [
        pltpu.VMEM((PAIRS, tokens, width), F32),
        pltpu.VMEM((PAIRS, tokens, width), BF16),
        pltpu.VMEM((PAIRS, tokens, width), BF16),
        pltpu.VMEM((PAIRS, tokens, width), BF16),
        pltpu.VMEM((PAIRS + 1, tokens, width), BF16),
        DMA((PAIRS,)),
        DMA((PAIRS,)),
        DMA((PAIRS,)),
        DMA((PAIRS + 1,)),
    ]


def third_kernel(
    x_ref, o_ref, a_ref, wo_ref, wd_ref, bias_ref, d_ref,
    result_ref, back_out,
    own_sem, back_send, back_recv, own, side_out, side_in, line_out, line_in, *sems,
):
    base, line, side, quarter = spot()
    rank = line * 2 + side
    tokens, width = x_ref.shape
    reduce = Reduce(own, side_out, side_in, line_out, line_in, sems)
    greet_line(base, line, side, quarter)

    def pieces(to, origin, kind):
        return (
            d_ref.at[:, kind, pl.ds(to * tokens, tokens), :],
            back_out.at[pl.ds(2 * origin, 2), :, pl.ds(kind * HEAD, HEAD)],
        )

    def back(to, origin, kind):
        src, dst = pieces(to, origin, kind)
        return send(
            src, dst, back_send.at[to, kind], back_recv.at[origin, kind], base + rank, to
        )

    own_back = [
        pltpu.make_async_copy(*pieces(quarter, quarter, kind), own_sem.at[kind])
        for kind in range(3)
    ]

    def make(which, put):
        for start in range(0, width, 512):
            span = pl.ds(start, 512)
            put(
                span,
                dot(o_ref[which], wo_ref[:, span]) + dot(a_ref[which], wd_ref[:, span]),
            )

    for step in reversed(range(PAIRS)):
        place = reduce.order[step]

        def put_out(span, value, step=step):
            side_out[step, :, span] = value.astype(BF16)

        def put_own(span, value, step=step):
            own[step, :, span] = value

        make(place * 2 + 1 - side, put_out)
        reduce.begin(step)
        make(place * 2 + side, put_own)
        if step == PAIRS - 1:
            for kind in range(3):
                own_back[kind].start()
                for hop in range(1, QUARTERS):
                    back(lax.rem(quarter + hop, QUARTERS), quarter, kind).start()

    for step in reversed(range(1, PAIRS)):
        reduce.advance(step)
    reduce.last()
    strip = 64

    def close(index, _):
        chunk = pl.ds(pl.multiple_of(index * strip, strip), strip)
        total = reduce.total(chunk) + bias_ref[0:1, :]
        result_ref[chunk, :] = (x_ref[chunk, :].astype(F32) + total).astype(BF16)

    lax.fori_loop(0, tokens // strip, close, None)
    reduce.finish()
    for kind in range(3):
        own_back[kind].wait()
        for hop in range(1, QUARTERS):
            origin = lax.rem(quarter + hop, QUARTERS)
            back(origin, quarter, kind).wait_send()
            back(origin, origin, kind).wait_recv()


def third(x, attended, activated, w_out, w_down, bias, grads):
    tokens, width = x.shape
    return pl.pallas_call(
        third_kernel,
        out_shape=[
            jax.ShapeDtypeStruct((tokens, width), BF16),
            jax.ShapeDtypeStruct((TEAM, tokens, 3 * HEAD), BF16),
        ],
        in_specs=[VMEM] * 6 + [ANY],
        out_specs=[VMEM, ANY],
        scratch_shapes=[DMA((3,)), DMA((QUARTERS, 3)), DMA((QUARTERS, 3))]
        + reduce_scratch(tokens, width),
        compiler_params=pltpu.CompilerParams(
            collective_id=2, has_side_effects=True, vmem_limit_bytes=LIMIT
        ),
        name="scatter_result",
    )(x, attended, activated, w_out, w_down, bias, grads)


def fourth_kernel(
    x_ref, dy_ref, xs_ref, dqkv_ref, du_ref, w_ref, vec_ref,
    grad_ref, sums_ref,
    weight, xs, load_sem, own, side_out, side_in, line_out, line_in, *sems,
):
    base, line, side, quarter = spot()
    tokens, width = x_ref.shape
    reduce = Reduce(own, side_out, side_in, line_out, line_in, sems)
    loads = [
        pltpu.make_async_copy(w_ref, weight, load_sem.at[0]),
        pltpu.make_async_copy(xs_ref, xs, load_sem.at[1]),
    ]
    for copy in loads:
        copy.start()
    greet_line(base, line, side, quarter)
    sums_ref[...] = jnp.zeros_like(sums_ref)
    for copy in loads:
        copy.wait()

    def make(which, put):
        rows = xs[which].astype(F32)
        average = jnp.mean(rows, -1, keepdims=True)
        variance = jnp.mean(jnp.square(rows - average), -1, keepdims=True)
        inverse = lax.rsqrt(variance + EPSILON)
        for start in range(0, width, 512):
            span = pl.ds(start, 512)
            attn = contract_last(dqkv_ref[which], weight[span, : 3 * HEAD])
            mlp = contract_last(du_ref[which], weight[span, 3 * HEAD :])
            unit = (xs[which, :, span].astype(F32) - average) * inverse
            sums_ref[0:1, span] += jnp.sum(attn * unit, 0, keepdims=True)
            sums_ref[1:2, span] += jnp.sum(mlp * unit, 0, keepdims=True)
            sums_ref[2:3, span] += jnp.sum(attn, 0, keepdims=True)
            sums_ref[3:4, span] += jnp.sum(mlp, 0, keepdims=True)
            put(span, attn * vec_ref[0:1, span] + mlp * vec_ref[1:2, span])

    for step in reversed(range(PAIRS)):
        place = reduce.order[step]

        def put_out(span, value, step=step):
            side_out[step, :, span] = value.astype(BF16)

        def put_own(span, value, step=step):
            own[step, :, span] = value

        make(place * 2 + 1 - side, put_out)
        reduce.begin(step)
        make(place * 2 + side, put_own)

    for step in reversed(range(1, PAIRS)):
        reduce.advance(step)
    reduce.last()
    strip = 64

    def close(index, _):
        chunk = pl.ds(pl.multiple_of(index * strip, strip), strip)
        total = reduce.total(chunk)
        unit, inverse = normalize(x_ref[chunk, :].astype(F32))
        pulled = (
            total
            - jnp.mean(total, -1, keepdims=True)
            - unit * jnp.mean(total * unit, -1, keepdims=True)
        )
        grad_ref[chunk, :] = (dy_ref[chunk, :].astype(F32) + inverse * pulled).astype(BF16)

    lax.fori_loop(0, tokens // strip, close, None)
    reduce.finish()


def fourth(x, dy, everyone, grad_qkv, grad_up, weight, vectors):
    tokens, width = x.shape
    return pl.pallas_call(
        fourth_kernel,
        out_shape=[
            jax.ShapeDtypeStruct((tokens, width), BF16),
            jax.ShapeDtypeStruct((8, width), F32),
        ],
        in_specs=[VMEM, VMEM, ANY, VMEM, VMEM, ANY, VMEM],
        out_specs=[VMEM, VMEM],
        scratch_shapes=[
            pltpu.VMEM(weight.shape, BF16),
            pltpu.VMEM(everyone.shape, BF16),
            DMA((2,)),
        ]
        + reduce_scratch(tokens, width),
        compiler_params=pltpu.CompilerParams(
            collective_id=3, has_side_effects=True, vmem_limit_bytes=LIMIT
        ),
        name="scatter_grad",
    )(x, dy, everyone, grad_qkv, grad_up, weight, vectors)


def on_device(
    dp,
    ctx,
    inputs,
    segments,
    ln_gain,
    ln_bias,
    qkv_weight,
    qkv_bias,
    out_weight,
    out_bias,
    up_weight,
    up_bias,
    down_weight,
    down_bias,
    cotangent,
):
    assert dp % TEAM == 0 and ctx == QUARTERS
    teams = dp // TEAM
    together = None if teams == 1 else [[g * TEAM + i for i in range(TEAM)] for g in range(teams)]
    across = None if teams == 1 else [[g * TEAM + i for g in range(teams)] for i in range(TEAM)]
    place = lax.axis_index("dp")
    rank = place % TEAM
    _, tokens, width = inputs.shape
    hidden = up_weight.shape[1] // TEAM
    shard = width // dp

    def team_order(values):
        if teams == 1:
            return values
        lead = values.shape[:-1]
        return values.reshape(*lead, teams, TEAM, shard).swapaxes(-3, -2).reshape(*lead, width)

    def plain_order(values):
        if teams == 1:
            return values
        lead = values.shape[:-1]
        return values.reshape(*lead, TEAM, teams, shard).swapaxes(-3, -2).reshape(*lead, width)

    if teams == 1:
        w_qkv, w_up, w_out, w_down = qkv_weight, up_weight, out_weight, down_weight
        gain, shift, b_qkv, b_up = ln_gain, ln_bias, qkv_bias, up_bias
        b_rows = [out_bias, down_bias]
    else:
        line_up = partial(lax.all_gather, axis_name="dp", axis_index_groups=across, tiled=True)
        whole = partial(lax.all_gather, axis_name="dp", axis=0, tiled=True)

        def cut(values):
            size = values.shape[0] // TEAM
            return lax.dynamic_slice_in_dim(values, rank * size, size, 0)

        w_qkv, w_up = line_up(qkv_weight, axis=0), line_up(up_weight, axis=0)
        gain, shift = line_up(ln_gain, axis=1), line_up(ln_bias, axis=1)
        w_out, w_down = cut(whole(out_weight)), cut(whole(down_weight))
        b_qkv, b_up = cut(whole(qkv_bias)), cut(whole(up_bias))
        b_rows = [cut(whole(out_bias)), cut(whole(down_bias))]
    rows = w_qkv.shape[0]
    packet = jnp.concatenate(
        [
            gain.astype(F32),
            shift.astype(F32),
            jnp.stack(b_rows).astype(F32),
            jnp.zeros((2, rows), F32),
            b_qkv.astype(F32).reshape(3, rows),
            jnp.zeros((5, rows), F32),
            jnp.broadcast_to(segments.astype(F32), (8, tokens)),
        ]
    )
    mine = inputs.reshape(tokens, width)
    grad_mine = cotangent.reshape(tokens, width)
    mine_team = team_order(mine)
    positions = jnp.arange(ctx * tokens, dtype=jnp.int32)
    tables = rotary_tables(positions.astype(F32))
    own_tables = [
        lax.dynamic_slice_in_dim(table, lax.axis_index("ctx") * tokens, tokens, 0)
        for table in tables
    ]
    everyone, attn_input, mlp_input, up_values, weight, qkv, marks, vectors = first(
        mine_team, w_qkv, w_up, packet, b_up.astype(F32).reshape(1, hidden), own_tables
    )
    marks = marks[:, :, 0, :].reshape(2, ctx * tokens)
    column, row = marks[:, :, None], marks[:, None, :]
    attended = attend(qkv, column, row)
    grad_rows, activated, grad_up, grad_attended, attended, dy_sum = second(
        grad_mine, w_out, w_down, up_values, attended
    )
    grads = attend_back(qkv, grad_attended, column, row, tables)
    branch_bias = (vectors[:, 4] + vectors[:, 5]).reshape(1, width)
    result, grad_qkv = third(
        mine, attended, activated, w_out, w_down, branch_bias, grads
    )
    gains = vectors[:, :2].transpose(1, 0, 2).reshape(2, width)
    grad_inputs, sums = fourth(
        mine_team, team_order(grad_mine), everyone, grad_qkv, grad_up, weight, gains
    )
    grad_inputs = plain_order(grad_inputs)

    flat = (TEAM * tokens, -1)
    attn_input, mlp_input = attn_input.reshape(flat), mlp_input.reshape(flat)
    grad_rows, grad_qkv, grad_up = (
        values.reshape(flat) for values in (grad_rows, grad_qkv, grad_up)
    )
    attended, activated = attended.reshape(flat), activated.reshape(flat)
    qkv_bias_sum = lax.dynamic_update_slice_in_dim(
        jnp.zeros((3, HEADS, HEAD), F32),
        jnp.sum(grad_qkv.astype(F32), 0).reshape(3, 1, HEAD), rank, 1,
    )
    up_bias_sum = lax.dynamic_update_slice_in_dim(
        jnp.zeros((TEAM, hidden), F32), jnp.sum(grad_up.astype(F32), 0)[None], rank, 0
    )
    vector = jnp.concatenate(
        [
            plain_order(sums[:4]).reshape(-1),
            qkv_bias_sum.reshape(-1),
            dy_sum[0] * jnp.where(rank == 0, 1.0, 0.0),
            up_bias_sum.reshape(-1),
        ]
    )
    vector = lax.psum(vector, ("dp", "ctx"))

    def own(start, size):
        return lax.dynamic_slice_in_dim(vector, start + place * (size // dp), size // dp, 0)

    grad_gain = jnp.stack([own(0, width), own(width, width)])
    grad_shift = jnp.stack([own(2 * width, width), own(3 * width, width)])
    grad_qkv_b = own(4 * width, 3 * width)
    grad_out_b = own(7 * width, width)
    grad_up_b = own(8 * width, TEAM * hidden)

    term_out = contract_first(attended, grad_rows).astype(BF16)
    term_down = contract_first(activated, grad_rows).astype(BF16)
    term_columns = jnp.concatenate(
        [
            contract_first(attn_input, grad_qkv).astype(BF16),
            contract_first(mlp_input, grad_up).astype(BF16),
        ],
        -1,
    )
    span = term_columns.shape[-1]
    if teams > 1:
        def scatter_rows(term):
            size = term.shape[0]
            full = jnp.zeros((TEAM, size, width), BF16)
            full = lax.dynamic_update_slice_in_dim(full, term[None], rank, 0)
            return lax.psum_scatter(
                full.reshape(TEAM * size, width), "dp", scatter_dimension=0, tiled=True
            )

        term_out, term_down = scatter_rows(term_out), scatter_rows(term_down)
        term_columns = term_columns.reshape(TEAM, teams, shard, span).swapaxes(0, 1)
        term_columns = lax.psum_scatter(
            term_columns.reshape(width, span), "dp", scatter_dimension=0,
            axis_index_groups=across, tiled=True,
        )
    grad_out_w = lax.psum(term_out, "ctx").astype(F32)
    grad_down_w = lax.psum(term_down, "ctx").astype(F32)
    term_columns = term_columns.reshape(TEAM, shard, span)
    term_columns = lax.psum_scatter(term_columns, "ctx", scatter_dimension=1, tiled=True)
    term_columns = lax.all_to_all(
        term_columns, "dp", 0, 0, axis_index_groups=together, tiled=True
    )
    term_columns = lax.all_gather(term_columns, "ctx", axis=1, tiled=True)
    grad_qkv_w = (
        term_columns[:, :, : 3 * HEAD].reshape(TEAM, shard, 3, HEAD).transpose(1, 2, 0, 3)
        .reshape(shard, 3 * width).astype(F32)
    )
    grad_up_w = (
        term_columns[:, :, 3 * HEAD :].transpose(1, 0, 2).reshape(shard, TEAM * hidden).astype(F32)
    )
    return (
        result.reshape(inputs.shape),
        grad_inputs.reshape(inputs.shape),
        grad_gain,
        grad_shift,
        grad_qkv_w,
        grad_qkv_b,
        grad_out_w,
        grad_out_b,
        grad_up_w,
        grad_up_b,
        grad_down_w,
        grad_out_b,
    )


def solution(mesh):
    placed = (
        P("dp", "ctx", None),
        P("dp", "ctx"),
        P(None, "dp"),
        P(None, "dp"),
        P("dp", None),
        P("dp"),
        P("dp", None),
        P("dp"),
        P("dp", None),
        P("dp"),
        P("dp", None),
        P("dp"),
        P("dp", "ctx", None),
    )
    return jax.shard_map(
        partial(on_device, mesh.shape["dp"], mesh.shape["ctx"]),
        mesh=mesh,
        in_specs=placed,
        out_specs=(
            P("dp", "ctx", None),
            P("dp", "ctx", None),
            P(None, "dp"),
            P(None, "dp"),
            P("dp", None),
            P("dp"),
            P("dp", None),
            P("dp"),
            P("dp", None),
            P("dp"),
            P("dp", None),
            P("dp"),
        ),
        check_vma=False,
    )
```

```python
from functools import partial

import jax
import jax.numpy as jnp
from jax import lax
from jax.experimental import pallas as pl
from jax.experimental.pallas import tpu as pltpu
from jax.sharding import PartitionSpec as P

HEADS = 8
HEAD = 256
ROT = 64
EPSILON = 1e-05
MASKED = -1e30
F32 = jnp.float32
BF16 = jnp.bfloat16
MESH = pl.DeviceIdType.MESH
TEAM = HEADS
PAIRS = TEAM // 2
QUARTERS = 4
RIGHT, LEFT = 0, 1
VECTOR_ROWS = 24


def dot(left, right):
    return jnp.dot(left, right, preferred_element_type=F32)


def contract_last(left, right):
    return lax.dot_general(left, right, (((1,), (1,)), ((), ())), preferred_element_type=F32)


def contract_first(left, right):
    return lax.dot_general(left, right, (((0,), (0,)), ((), ())), preferred_element_type=F32)


def rotary_tables(positions):
    half = ROT // 2
    exponent = jnp.arange(0, ROT, 2).astype(F32) / ROT
    frequency = 10000.0 ** (-exponent)
    angles = positions[:, None] * frequency[None, :]
    rows = positions.shape[0]
    cosine, sine = jnp.cos(angles), jnp.sin(angles)
    one, nought = jnp.ones((rows, 64), F32), jnp.zeros((rows, 64), F32)
    blank = jnp.zeros((rows, half), F32)
    return (
        jnp.concatenate([cosine, cosine, one], -1),
        jnp.concatenate([-sine, blank, nought], -1),
        jnp.concatenate([blank, sine, nought], -1),
    )


def spot():
    place = lax.axis_index("dp")
    rank = lax.rem(place, TEAM)
    return place - rank, lax.div(rank, 2), lax.rem(rank, 2), lax.axis_index("ctx")


def near_first(line):
    second = 1 + lax.rem(line, 2)
    last = 3 * (1 - lax.div(line, 2))
    return (line, second, 6 - line - second - last, last)


def core_peer(quarter):
    return quarter + 1 - 2 * lax.rem(quarter, 2)


def chip_peer(quarter):
    return quarter + 2 - 4 * lax.div(quarter, 2)


def send(src, dst, send_sem, recv_sem, place, quarter):
    return pltpu.make_async_remote_copy(
        src_ref=src, dst_ref=dst, send_sem=send_sem, recv_sem=recv_sem,
        device_id=(place, quarter), device_id_type=MESH,
    )


def greet_line(base, line, side, quarter):
    barrier = pltpu.get_barrier_semaphore()

    def hail(place, quarter):
        pl.semaphore_signal(barrier, inc=1, device_id=(place, quarter), device_id_type=MESH)

    rank = line * 2 + side
    hail(base + line * 2 + 1 - side, quarter)

    pl.when(line < PAIRS - 1)(lambda: hail(base + rank + 2, quarter))
    pl.when(line > 0)(lambda: hail(base + rank - 2, quarter))
    for step in range(1, QUARTERS):
        hail(base + rank, lax.rem(quarter + step, QUARTERS))
    neighbours = 1 + lax.div(line + 2, 3) - lax.div(line, 3)
    pl.semaphore_wait(barrier, neighbours + QUARTERS)


def greet_team(base, line, side, quarter):
    barrier = pltpu.get_barrier_semaphore()
    rank = line * 2 + side
    for step in range(1, TEAM):
        pl.semaphore_signal(
            barrier, inc=1, device_id=(base + lax.rem(rank + step, TEAM), quarter),
            device_id_type=MESH,
        )
    for step in range(1, QUARTERS):
        pl.semaphore_signal(
            barrier, inc=1, device_id=(base + rank, lax.rem(quarter + step, QUARTERS)),
            device_id_type=MESH,
        )
    pl.semaphore_wait(barrier, TEAM + QUARTERS - 2)


class Relay:
    def __init__(self, held, line_send, line_recv, side_send, side_recv):
        self.held = held
        self.sems = line_send, line_recv, side_send, side_recv
        self.base, self.line, self.side, self.quarter = spot()

    def along(self, source, way):
        line_send, line_recv, _, _ = self.sems
        block = self.held.at[source * 2 + self.side]
        place = self.base + self.line * 2 + self.side + (2 if way == RIGHT else -2)
        return send(
            block, block, line_send.at[way, source], line_recv.at[source], place, self.quarter
        )

    def over(self, source, side):
        _, _, side_send, side_recv = self.sems
        block = self.held.at[source * 2 + side]
        place = self.base + self.line * 2 + 1 - self.side
        return send(block, block, side_send.at[source], side_recv.at[source], place, self.quarter)

    def each(self, step, act):
        line = self.line
        if step == 0:
            pl.when(line < PAIRS - 1)(lambda: act(line, RIGHT))
            pl.when(line > 0)(lambda: act(line, LEFT))
            act(line, None)
            return

        @pl.when(line >= step)
        def _():
            source = line - step
            act(source, "arrive")
            pl.when(line < PAIRS - 1)(lambda: act(source, RIGHT))
            act(source, None)

        @pl.when(line + step < PAIRS)
        def _():
            source = line + step
            act(source, "arrive")
            pl.when(line > 0)(lambda: act(source, LEFT))
            act(source, None)

    def start(self, step):
        def act(source, way):
            if way == "arrive":
                self.along(source, RIGHT).wait_recv()
            elif way is None:
                self.over(source, self.side).start()
            else:
                self.along(source, way).start()

        self.each(step, act)

    def finish(self):
        def act(source, way):
            if way is None:
                self.over(source, self.side).wait_send()
            elif way != "arrive":
                self.along(source, way).wait_send()

        for step in range(PAIRS):
            self.each(step, act)

    def wait_over(self, source):
        self.over(source, 1 - self.side).wait_recv()


RELAY_SEMS = [
    pltpu.SemaphoreType.DMA((2, PAIRS)),
    pltpu.SemaphoreType.DMA((PAIRS,)),
    pltpu.SemaphoreType.DMA((PAIRS,)),
    pltpu.SemaphoreType.DMA((PAIRS,)),
]


def normalize(rows):
    average = jnp.mean(rows, -1, keepdims=True)
    centred = rows - average
    variance = jnp.mean(centred * centred, -1, keepdims=True)
    inverse = lax.rsqrt(variance + EPSILON)
    return centred * inverse, inverse


def rotate_low(low, cosine, above, below):
    half = ROT // 2
    return (
        low * cosine + pltpu.roll(low, 128 - half, 1) * above + pltpu.roll(low, half, 1) * below
    )


def unrotate_low(low, cosine, above, below):
    half = ROT // 2
    return (
        low * cosine + pltpu.roll(low * below, 128 - half, 1) + pltpu.roll(low * above, half, 1)
    )


class Spread:
    def __init__(self, pieces, send_sem, recv_sem, own_sem):
        self.pieces, self.sems = pieces, (send_sem, recv_sem, own_sem)
        base, line, side, self.quarter = spot()
        self.place = base + line * 2 + side

    def _remote(self, index, sequence, to, origin):
        src, dst = self.pieces[index]
        send_sem, recv_sem, _ = self.sems
        return send(
            src(sequence), dst(lax.rem(sequence, 2), origin), send_sem.at[index, sequence],
            recv_sem.at[index, origin, lax.rem(sequence, 2)], self.place, to,
        )

    def _own(self, index, sequence):
        src, dst = self.pieces[index]
        return pltpu.make_async_copy(
            src(sequence), dst(lax.rem(sequence, 2), self.quarter),
            self.sems[2].at[index, lax.rem(sequence, 2)],
        )

    def start(self, sequence):
        to = lax.div(sequence, 2)

        @pl.when(to == self.quarter)
        def _():
            for index in range(len(self.pieces)):
                self._own(index, sequence).start()

        @pl.when(to != self.quarter)
        def _():
            for index in range(len(self.pieces)):
                self._remote(index, sequence, to, self.quarter).start()

    def finish(self):
        def sent(sequence, _):
            to = lax.div(sequence, 2)

            @pl.when(to == self.quarter)
            def _():
                for index in range(len(self.pieces)):
                    self._own(index, sequence).wait()

            @pl.when(to != self.quarter)
            def _():
                for index in range(len(self.pieces)):
                    self._remote(index, sequence, to, self.quarter).wait_send()

        lax.fori_loop(0, TEAM, sent, None)

        def landed(step, _):
            origin = lax.rem(self.quarter + 1 + lax.div(step, 2), QUARTERS)
            sequence = lax.rem(step, 2)
            for index in range(len(self.pieces)):
                self._remote(index, sequence, origin, origin).wait_recv()

        lax.fori_loop(0, 2 * (QUARTERS - 1), landed, None)


def spread_sems(count):
    return [
        pltpu.SemaphoreType.DMA((count, TEAM)),
        pltpu.SemaphoreType.DMA((count, QUARTERS, 2)),
        pltpu.SemaphoreType.DMA((count, 2)),
    ]


def first_kernel(
    x_ref, wq_ref, wu_ref, vec_ref, upb_ref, cos_ref, above_ref, below_ref,
    x_out, ha_out, hm_out, u_out, w_out, qkv_out, seg_out, vec_out,
    held, weight, vecs, ha, hm, up, qkv, vectors,
    own_sem, store_sem, w_send, w_recv, w_own, core_send, core_recv, chip_send, chip_recv,
    last_send, last_recv, v_send, v_recv, spread_send, spread_recv, spread_own, *relay_sems,
):
    base, line, side, quarter = spot()
    rank = line * 2 + side
    tokens, width = x_ref.shape
    rows = wq_ref.shape[0]
    part = rows // QUARTERS
    hidden = up.shape[-1]
    core, chip = core_peer(quarter), chip_peer(quarter)
    relay = Relay(held, *relay_sems)
    spread = Spread(
        [
            (
                lambda s: qkv.at[s],
                lambda j, origin: qkv_out.at[j, :, pl.ds(origin * tokens, tokens), :],
            ),
            (lambda s: vecs.at[s, pl.ds(16, 8), :], lambda j, origin: seg_out.at[j, origin]),
        ],
        spread_send, spread_recv, spread_own,
    )
    greet_team(base, line, side, quarter)

    own_x = pltpu.make_async_copy(x_ref, held.at[rank], own_sem.at[0])
    own_x.start()
    own_v = pltpu.make_async_copy(vec_ref, vecs.at[rank], own_sem.at[1])
    own_v.start()

    def band(origin, slice_of):
        return pl.ds(pl.multiple_of(origin * rows + slice_of * part, 16), part)

    def columns(source, target):
        mine = pl.ds(pl.multiple_of(quarter * part, 16), part)
        pieces = []
        for kind in range(3):
            start = pl.multiple_of(kind * width + target * HEAD, HEAD)
            pieces.append(
                (
                    wq_ref.at[mine, pl.ds(start, HEAD)],
                    weight.at[band(source, quarter), pl.ds(kind * HEAD, HEAD)],
                )
            )
        start = pl.multiple_of(target * hidden, hidden)
        pieces.append(
            (
                wu_ref.at[mine, pl.ds(start, hidden)],
                weight.at[band(source, quarter), pl.ds(3 * HEAD, hidden)],
            )
        )
        return pieces

    def column_copies(source, target, peer):
        return [
            send(src, dst, w_send.at[kind, target], w_recv.at[kind, source], base + peer, quarter)
            for kind, (src, dst) in enumerate(columns(source, target))
        ]

    def vector_copy(source, target, peer):
        return send(
            vec_ref, vecs.at[source], v_send.at[target], v_recv.at[source], base + peer, quarter
        )

    def send_columns(step, _):
        target = lax.rem(rank + step, TEAM)
        vector_copy(rank, target, target).start()
        for copy in column_copies(rank, target, target):
            copy.start()

    lax.fori_loop(1, TEAM, send_columns, None)
    own_columns = [
        pltpu.make_async_copy(src, dst, w_own.at[kind])
        for kind, (src, dst) in enumerate(columns(rank, rank))
    ]
    for copy in own_columns:
        copy.start()
    own_x.wait()
    own_v.wait()
    relay.start(0)

    def pass_on(origin, slice_of, sends, recvs, to):
        block = weight.at[band(origin, slice_of), :]
        return send(block, block, sends.at[origin], recvs.at[origin], base + rank, to)

    def to_core(origin):
        return pass_on(origin, quarter, core_send, core_recv, core)

    def to_chip(origin):
        return pass_on(origin, quarter, chip_send, chip_recv, chip)

    def to_last(origin):
        return pass_on(origin, chip, last_send, last_recv, core)

    for copy in own_columns:
        copy.wait()
    to_chip(rank).start()
    to_core(rank).start()

    def forward_columns(step, _):
        origin = lax.rem(rank + TEAM - step, TEAM)
        for copy in column_copies(origin, rank, origin):
            copy.wait_recv()
        to_chip(origin).start()
        to_core(origin).start()

    lax.fori_loop(1, TEAM, forward_columns, None)
    relay.start(1)

    def forward_chip(step, _):
        origin = lax.rem(rank + TEAM - step, TEAM)
        pass_on(origin, chip, chip_send, chip_recv, chip).wait_recv()
        to_last(origin).start()

    lax.fori_loop(0, TEAM, forward_chip, None)
    relay.start(2)

    def take_vectors(step, _):
        origin = lax.rem(rank + TEAM - step, TEAM)
        vector_copy(origin, rank, origin).wait_recv()

    lax.fori_loop(1, TEAM, take_vectors, None)
    for source in range(TEAM):
        for row in range(4):
            vectors[pl.ds(row, 1), pl.ds(source * rows, rows)] = vecs[source, pl.ds(row, 1), :]

    def last_columns(step, _):
        origin = lax.rem(rank + TEAM - step, TEAM)
        pass_on(origin, core, core_send, core_recv, core).wait_recv()
        pass_on(origin, chip_peer(core), last_send, last_recv, core).wait_recv()

    lax.fori_loop(0, TEAM, last_columns, None)
    stores = [
        pltpu.make_async_copy(weight, w_out, store_sem.at[0]),
        pltpu.make_async_copy(vecs, vec_out, store_sem.at[1]),
    ]
    for copy in stores:
        copy.start()

    strip = 32

    def work(which):
        def norm(index, _):
            chunk = pl.ds(pl.multiple_of(index * strip, strip), strip)
            unit, _ = normalize(held[which, chunk, :].astype(F32))
            ha[which, chunk, :] = (unit * vectors[0:1, :] + vectors[2:3, :]).astype(BF16)
            hm[which, chunk, :] = (unit * vectors[1:2, :] + vectors[3:4, :]).astype(BF16)

        lax.fori_loop(0, tokens // strip, norm, None)
        for kind in range(3):
            chunk = kind * TEAM + rank
            bias = vecs[lax.div(chunk, 3), pl.ds(8 + lax.rem(chunk, 3), 1), :]
            made = dot(ha[which], weight[:, pl.ds(kind * HEAD, HEAD)]) + bias
            if kind < 2:
                low = rotate_low(made[:, :128], cos_ref[...], above_ref[...], below_ref[...])
                qkv[which, kind, :, pl.ds(0, 128)] = low.astype(BF16)
                qkv[which, kind, :, pl.ds(128, HEAD - 128)] = made[:, 128:].astype(BF16)
            else:
                qkv[which, kind] = made.astype(BF16)
        spread.start(which)
        for start in range(0, hidden, 256):
            span = pl.ds(start, 256)
            up[which, :, span] = (
                dot(hm[which], weight[:, pl.ds(3 * HEAD + start, 256)]) + upb_ref[:, span]
            )

    for step, place in enumerate(near_first(line)):

        def one(other, _, step=step, place=place):
            @pl.when(other == 1)
            def _():
                if step == 0:
                    relay.start(3)
                relay.wait_over(place)

            work(place * 2 + side + other * (1 - 2 * side))

        lax.fori_loop(0, 2, one, None)

    for index, (src, dst) in enumerate(((held, x_out), (ha, ha_out), (hm, hm_out), (up, u_out))):
        stores.append(pltpu.make_async_copy(src, dst, store_sem.at[2 + index]))
        stores[-1].start()
    relay.finish()
    spread.finish()

    def sent(step, _):
        target = lax.rem(rank + step, TEAM)
        vector_copy(rank, target, target).wait_send()
        for copy in column_copies(rank, target, target):
            copy.wait_send()

    lax.fori_loop(1, TEAM, sent, None)

    def passed(origin, _):
        to_core(origin).wait_send()
        to_chip(origin).wait_send()
        to_last(origin).wait_send()

    lax.fori_loop(0, TEAM, passed, None)
    for copy in stores:
        copy.wait()


ANY = pl.BlockSpec(memory_space=pl.ANY)
VMEM = pl.BlockSpec(memory_space=pltpu.VMEM)
DMA = pltpu.SemaphoreType.DMA
LIMIT = 60 << 20


def first(x, w_qkv, w_up, vec, up_bias, tables):
    tokens, width = x.shape
    hidden = up_bias.shape[-1]
    span = 3 * HEAD + hidden
    shapes = [
        ((TEAM, tokens, width), BF16),
        ((TEAM, tokens, width), BF16),
        ((TEAM, tokens, width), BF16),
        ((TEAM, tokens, hidden), F32),
        ((width, span), BF16),
        ((2, 3, QUARTERS * tokens, HEAD), BF16),
        ((2, QUARTERS, 8, tokens), F32),
        ((TEAM, VECTOR_ROWS, vec.shape[-1]), F32),
    ]
    return pl.pallas_call(
        first_kernel,
        out_shape=[jax.ShapeDtypeStruct(*shape) for shape in shapes],
        in_specs=[VMEM, ANY, ANY, VMEM, VMEM, VMEM, VMEM, VMEM],
        out_specs=[ANY] * len(shapes),
        scratch_shapes=[
            pltpu.VMEM((TEAM, tokens, width), BF16),
            pltpu.VMEM((width, span), BF16),
            pltpu.VMEM((TEAM, VECTOR_ROWS, vec.shape[-1]), F32),
            pltpu.VMEM((TEAM, tokens, width), BF16),
            pltpu.VMEM((TEAM, tokens, width), BF16),
            pltpu.VMEM((TEAM, tokens, hidden), F32),
            pltpu.VMEM((TEAM, 3, tokens, HEAD), BF16),
            pltpu.VMEM((8, width), F32),
            DMA((2,)),
            DMA((6,)),
            DMA((4, TEAM)),
            DMA((4, TEAM)),
            DMA((4,)),
        ]
        + [DMA((TEAM,))] * 8
        + spread_sems(2)
        + RELAY_SEMS,
        compiler_params=pltpu.CompilerParams(
            collective_id=0, has_side_effects=True, vmem_limit_bytes=LIMIT
        ),
        name="gather_x",
    )(x, w_qkv, w_up, vec, up_bias, *tables)


def gelu_terms(values):
    chance = 0.5 * (1.0 + lax.erf(values * (0.5**0.5)))
    density = jnp.exp(-0.5 * values * values) * 0.3989422804014327
    return values * chance, chance + values * density


def second_kernel(
    dy_ref, wo_ref, wd_ref, u_ref, o_ref,
    dy_out, a_out, du_out, do_out, o_out, sum_out,
    held, up, act, grad, attended,
    own_sem, load_sem, store_sem, back_send, back_recv, spread_send, spread_recv, spread_own,
    *relay_sems,
):
    base, line, side, quarter = spot()
    rank = line * 2 + side
    tokens, width = dy_ref.shape
    hidden = up.shape[-1]
    relay = Relay(held, *relay_sems)
    spread = Spread(
        [
            (
                lambda s: attended.at[s],
                lambda j, origin: do_out.at[j, pl.ds(origin * tokens, tokens), :],
            )
        ],
        spread_send, spread_recv, spread_own,
    )
    loads = pltpu.make_async_copy(u_ref, up, load_sem)
    loads.start()
    greet_line(base, line, side, quarter)
    own = pltpu.make_async_copy(dy_ref, held.at[rank], own_sem.at[0])
    own.start()
    own.wait()
    relay.start(0)

    def back(to, origin):
        return send(
            o_ref.at[:, pl.ds(to * tokens, tokens), :], o_out.at[pl.ds(2 * origin, 2)],
            back_send.at[to], back_recv.at[origin], base + rank, to,
        )

    own_back = pltpu.make_async_copy(
        o_ref.at[:, pl.ds(quarter * tokens, tokens), :], o_out.at[pl.ds(2 * quarter, 2)],
        own_sem.at[1],
    )
    own_back.start()
    for step in range(1, QUARTERS):
        back(lax.rem(quarter + step, QUARTERS), quarter).start()
    loads.wait()
    sum_out[...] = jnp.zeros_like(sum_out)

    def work(which):
        attended[which] = contract_last(held[which], wo_ref[...]).astype(BF16)
        spread.start(which)
        for start in range(0, hidden, 256):
            span = pl.ds(start, 256)
            value, slope = gelu_terms(up[which, :, span])
            act[which, :, span] = value.astype(BF16)
            pulled = contract_last(held[which], wd_ref[span, :])
            grad[which, :, span] = (pulled * slope).astype(BF16)
        sum_out[0:1, :] += jnp.sum(held[which].astype(F32), 0, keepdims=True)

    for step, place in enumerate(near_first(line)):

        def one(other, _, step=step, place=place):
            @pl.when(other == 1)
            def _():
                if step < PAIRS - 1:
                    relay.start(step + 1)
                relay.wait_over(place)

            work(place * 2 + side + other * (1 - 2 * side))

        lax.fori_loop(0, 2, one, None)

    stores = []
    for index, (src, dst) in enumerate(((held, dy_out), (act, a_out), (grad, du_out))):
        stores.append(pltpu.make_async_copy(src, dst, store_sem.at[index]))
        stores[-1].start()
    relay.finish()
    spread.finish()
    for step in range(1, QUARTERS):
        back(lax.rem(quarter + step, QUARTERS), quarter).wait_send()
        origin = lax.rem(quarter + step, QUARTERS)
        back(origin, origin).wait_recv()
    own_back.wait()
    for copy in stores:
        copy.wait()


def second(dy, w_out, w_down, up_values, attended):
    tokens, width = dy.shape
    hidden = up_values.shape[-1]
    shapes = [
        ((TEAM, tokens, width), BF16),
        ((TEAM, tokens, hidden), BF16),
        ((TEAM, tokens, hidden), BF16),
        ((2, QUARTERS * tokens, HEAD), BF16),
        ((TEAM, tokens, HEAD), BF16),
        ((8, width), F32),
    ]
    return pl.pallas_call(
        second_kernel,
        out_shape=[jax.ShapeDtypeStruct(*shape) for shape in shapes],
        in_specs=[VMEM, VMEM, VMEM, ANY, ANY],
        out_specs=[ANY] * 5 + [VMEM],
        scratch_shapes=[
            pltpu.VMEM((TEAM, tokens, width), BF16),
            pltpu.VMEM((TEAM, tokens, hidden), F32),
            pltpu.VMEM((TEAM, tokens, hidden), BF16),
            pltpu.VMEM((TEAM, tokens, hidden), BF16),
            pltpu.VMEM((TEAM, tokens, HEAD), BF16),
            DMA((2,)),
            DMA,
            DMA((3,)),
            DMA((QUARTERS,)),
            DMA((QUARTERS,)),
        ]
        + spread_sems(1)
        + RELAY_SEMS,
        compiler_params=pltpu.CompilerParams(
            collective_id=1, has_side_effects=True, vmem_limit_bytes=LIMIT
        ),
        name="gather_dy",
    )(dy, w_out, w_down, up_values, attended)


def probabilities(start, block, q_ref, k_ref, col_ref, row_ref):
    rows, keys = pl.ds(start, block), pl.ds(0, start + block)
    scores = contract_last(q_ref[rows, :], k_ref[keys, :]) * HEAD ** (-0.5)
    shape = scores.shape
    query_pos = start + lax.broadcasted_iota(jnp.int32, shape, 0)
    key_pos = lax.broadcasted_iota(jnp.int32, shape, 1)
    allowed = (query_pos >= key_pos) & (col_ref[rows, :] == row_ref[:, keys])
    scores = jnp.where(allowed, scores, MASKED)
    expanded = jnp.exp(scores - jnp.max(scores, -1, keepdims=True))
    return expanded / jnp.sum(expanded, -1, keepdims=True)


def forward_kernel(block, qkv_ref, col_ref, row_ref, o_ref):
    q_ref, k_ref, v_ref = (qkv_ref.at[kind] for kind in range(3))
    for start in range(0, o_ref.shape[0], block):
        probs = probabilities(start, block, q_ref, k_ref, col_ref, row_ref)
        value_block = v_ref[pl.ds(0, start + block), :]
        o_ref[pl.ds(start, block), :] = dot(probs.astype(BF16), value_block).astype(BF16)


def backward_kernel(
    block, qkv_ref, do_ref, col_ref, row_ref, cos_ref, above_ref, below_ref, d_ref, dk_sum, dv_sum
):
    scale = HEAD ** (-0.5)
    q_ref, k_ref, v_ref = (qkv_ref.at[kind] for kind in range(3))
    length = q_ref.shape[0]

    def put(kind, rows, grads):
        low = unrotate_low(
            grads[:, :128], cos_ref[rows, :], above_ref[rows, :], below_ref[rows, :]
        )
        d_ref[kind, rows, pl.ds(0, 128)] = low.astype(BF16)
        d_ref[kind, rows, pl.ds(128, HEAD - 128)] = grads[:, 128:].astype(BF16)

    dk_sum[...] = jnp.zeros_like(dk_sum)
    dv_sum[...] = jnp.zeros_like(dv_sum)
    for start in range(0, length, block):
        rows, keys = pl.ds(start, block), pl.ds(0, start + block)
        probs = probabilities(start, block, q_ref, k_ref, col_ref, row_ref)
        grads = do_ref[rows, :]
        grad_probs = contract_last(grads, v_ref[keys, :])
        row_dot = jnp.sum(probs * grad_probs, -1, keepdims=True)
        grad_scores = (probs * (grad_probs - row_dot)).astype(BF16)
        put(0, rows, dot(grad_scores, k_ref[keys, :]) * scale)
        dk_sum[keys, :] += contract_first(grad_scores, q_ref[rows, :])
        dv_sum[keys, :] += contract_first(probs.astype(BF16), grads)
    put(1, pl.ds(0, length), dk_sum[...] * scale)
    d_ref[2] = dv_sum[...].astype(BF16)


def attention_specs(seqs, length):
    three = pl.BlockSpec((None, 3, length, HEAD), lambda s: (s, 0, 0, 0))
    one = pl.BlockSpec((None, length, HEAD), lambda s: (s, 0, 0))
    masks = [
        pl.BlockSpec((None, length, 1), lambda s: (s, 0, 0)),
        pl.BlockSpec((None, 1, length), lambda s: (s, 0, 0)),
    ]
    return three, one, masks


def attend(qkv, column, row):
    seqs, _, length, head = qkv.shape
    three, one, masks = attention_specs(seqs, length)
    return pl.pallas_call(
        partial(forward_kernel, min(256, length)),
        grid=(seqs,),
        in_specs=[three] + masks,
        out_specs=one,
        out_shape=jax.ShapeDtypeStruct((seqs, length, head), BF16),
        compiler_params=pltpu.CompilerParams(vmem_limit_bytes=48 << 20),
        name="attend",
    )(qkv, column, row)


def attend_back(qkv, grads, column, row, tables):
    seqs, _, length, head = qkv.shape
    three, one, masks = attention_specs(seqs, length)
    table = pl.BlockSpec((length, 128), lambda s: (0, 0))
    return pl.pallas_call(
        partial(backward_kernel, min(256, length)),
        grid=(seqs,),
        in_specs=[three, one] + masks + [table] * 3,
        out_specs=three,
        out_shape=jax.ShapeDtypeStruct(qkv.shape, BF16),
        scratch_shapes=[pltpu.VMEM((length, head), F32)] * 2,
        compiler_params=pltpu.CompilerParams(vmem_limit_bytes=48 << 20),
        name="attend_back",
    )(qkv, grads, column, row, *tables)


class Reduce:
    def __init__(self, own, side_out, side_in, line_in, sems):
        self.own, self.side_out, self.side_in, self.line_in = own, side_out, side_in, line_in
        self.sems = sems
        self.base, self.line, self.side, self.quarter = spot()
        self.order = near_first(self.line)

    def over(self, step):
        side_send, side_recv = self.sems[:2]
        place = self.base + self.line * 2 + 1 - self.side
        return send(
            self.side_out.at[step], self.side_in.at[step], side_send.at[step], side_recv.at[step],
            place, self.quarter,
        )

    def along(self, step, target, way):
        line_send, line_recv = self.sems[2:]
        move = 1 if way == RIGHT else -1
        slot = target if way == RIGHT else jnp.where(target == self.line - 1, PAIRS, target)
        place = self.base + (self.line + move) * 2 + self.side
        return send(
            self.side_out.at[step], self.line_in.at[slot], line_send.at[step], line_recv.at[slot],
            place, self.quarter,
        )

    def arrive(self, slot):
        line_send, line_recv = self.sems[2:]
        return send(
            self.side_out.at[0], self.line_in.at[slot], line_send.at[0], line_recv.at[slot],
            self.base + self.line * 2 + 1 - self.side, self.quarter,
        )

    def begin(self, step):
        self.over(step).start()

    def mine(self, step, chunk):
        slot = step if self.own.shape[0] > 1 else 0
        return self.own[slot, chunk, :].astype(F32) + self.side_in[step, chunk, :].astype(F32)

    def advance(self, step):
        target = self.order[step]
        self.over(step).wait_recv()
        self.over(step).wait_send()

        def forward(way, upstream):
            pl.when(upstream)(lambda: self.arrive(target).wait_recv())
            strip = 64

            def add(index, _):
                chunk = pl.ds(pl.multiple_of(index * strip, strip), strip)
                total = self.mine(step, chunk)
                passing = self.line_in[target, chunk, :].astype(F32)
                total = jnp.where(upstream, total + passing, total)
                self.side_out[step, chunk, :] = total.astype(BF16)

            lax.fori_loop(0, self.own.shape[1] // strip, add, None)
            self.along(step, target, way).start()

        pl.when(target > self.line)(lambda: forward(RIGHT, self.line > 0))
        pl.when(target < self.line)(lambda: forward(LEFT, self.line < PAIRS - 1))

    def last(self):
        self.over(0).wait_recv()
        self.over(0).wait_send()
        pl.when(self.line > 0)(lambda: self.arrive(self.line).wait_recv())
        pl.when(self.line < PAIRS - 1)(lambda: self.arrive(PAIRS).wait_recv())

    def total(self, chunk):
        total = self.mine(0, chunk)
        left = self.line_in[self.line, chunk, :].astype(F32)
        right = self.line_in[PAIRS, chunk, :].astype(F32)
        total = jnp.where(self.line > 0, total + left, total)
        return jnp.where(self.line < PAIRS - 1, total + right, total)

    def finish(self):
        for step in range(1, PAIRS):
            target = self.order[step]
            pl.when(target > self.line)(lambda: self.along(step, target, RIGHT).wait_send())
            pl.when(target < self.line)(lambda: self.along(step, target, LEFT).wait_send())


def reduce_scratch(tokens, width, slots, dtype):
    return [
        pltpu.VMEM((slots, tokens, width), dtype),
        pltpu.VMEM((PAIRS, tokens, width), BF16),
        pltpu.VMEM((PAIRS, tokens, width), BF16),
        pltpu.VMEM((PAIRS + 1, tokens, width), BF16),
        DMA((PAIRS,)),
        DMA((PAIRS,)),
        DMA((PAIRS,)),
        DMA((PAIRS + 1,)),
    ]


class Quarters:
    def __init__(self, keep, away, came, far, core_send, core_recv, chip_send, chip_recv):
        self.keep, self.away, self.came, self.far = keep, away, came, far
        self.sems = core_send, core_recv, chip_send, chip_recv
        base, line, side, self.quarter = spot()
        self.place = base + line * 2 + side
        self.core, self.chip = lax.rem(self.quarter, 2), lax.div(self.quarter, 2)
        self.tiles = keep.shape[0]

    def to_core(self, tile):
        return send(
            self.away.at[tile], self.came.at[tile], self.sems[0].at[tile], self.sems[1].at[tile],
            self.place, core_peer(self.quarter),
        )

    def to_chip(self, tile):
        return send(
            self.away.at[tile, 0], self.far.at[tile], self.sems[2].at[tile], self.sems[3].at[tile],
            self.place, chip_peer(self.quarter),
        )

    def put(self, tile, quarter_of):
        for chip in range(2):
            self.keep[tile, chip] = quarter_of(2 * chip + self.core).astype(BF16)
            self.away[tile, chip] = quarter_of(2 * chip + 1 - self.core).astype(BF16)
        self.to_core(tile).start()

    def over_cores(self):
        def one(tile, _):
            self.to_core(tile).wait_recv()
            self.to_core(tile).wait_send()
            other = 1 - self.chip
            passed = self.keep[tile, other].astype(F32) + self.came[tile, other].astype(F32)
            self.away[tile, 0] = passed.astype(BF16)
            self.to_chip(tile).start()
            kept = self.keep[tile, self.chip].astype(F32)
            kept = kept + self.came[tile, self.chip].astype(F32)
            self.keep[tile, self.chip] = kept.astype(BF16)

        lax.fori_loop(0, self.tiles, one, None)

    def over_chips(self, then):
        def one(tile, _):
            self.to_chip(tile).wait_recv()
            total = self.keep[tile, self.chip].astype(F32) + self.far[tile].astype(F32)
            self.keep[tile, self.chip] = total.astype(BF16)
            then(tile)

        lax.fori_loop(0, self.tiles, one, None)

    def total(self, tile):
        return self.keep.at[tile, self.chip]

    def finish(self):
        lax.fori_loop(0, self.tiles, lambda tile, _: self.to_chip(tile).wait_send(), None)


def quarters_scratch(tiles, rows, columns):
    return [
        pltpu.VMEM((tiles, 2, rows, columns), BF16),
        pltpu.VMEM((tiles, 2, rows, columns), BF16),
        pltpu.VMEM((tiles, 2, rows, columns), BF16),
        pltpu.VMEM((tiles, rows, columns), BF16),
    ] + [DMA((tiles,))] * 4


class Stream:
    def __init__(self, source, slots, sems):
        self.source, self.slots, self.sems = source, slots, sems

    def copy(self, tile):
        size = self.slots.shape[-1]
        start = pl.multiple_of(tile * size, size)
        slot = lax.rem(tile, 2)
        return pltpu.make_async_copy(
            self.source.at[:, pl.ds(start, size)], self.slots.at[slot], self.sems.at[slot]
        )

    def run(self, tiles, use):
        def one(tile, _):
            self.copy(tile).wait()
            use(tile, self.slots.at[lax.rem(tile, 2)])
            pl.when(tile + 2 < tiles)(lambda: self.copy(tile + 2).start())

        lax.fori_loop(0, tiles, one, None)


def third_kernel(
    x_ref, o_ref, a_ref, wo_ref, wd_ref, bias_ref, du_ref, d_ref, hm_ref, dy_ref,
    result_ref, back_out, up_out, rows_out,
    own_sem, back_send, back_recv, load_sem, store_sem, hm_tiles, tile_sum, dy, *rest,
):
    base, line, side, quarter = spot()
    rank = line * 2 + side
    tokens, width = x_ref.shape
    part = width // TEAM // QUARTERS
    reduce = Reduce(*rest[:4], rest[4:8])
    ups, downs = Quarters(*rest[8:16]), Quarters(*rest[16:24])
    stream = Stream(hm_ref, hm_tiles, load_sem)
    load_dy = pltpu.make_async_copy(dy_ref, dy, own_sem.at[3])
    load_dy.start()
    for tile in range(2):
        stream.copy(tile).start()
    greet_line(base, line, side, quarter)

    def pieces(to, origin, kind):
        return (
            d_ref.at[:, kind, pl.ds(to * tokens, tokens), :],
            back_out.at[pl.ds(2 * origin, 2), :, pl.ds(kind * HEAD, HEAD)],
        )

    def back(to, origin, kind):
        src, dst = pieces(to, origin, kind)
        return send(
            src, dst, back_send.at[to, kind], back_recv.at[origin, kind], base + rank, to
        )

    own_back = [
        pltpu.make_async_copy(*pieces(quarter, quarter, kind), own_sem.at[kind])
        for kind in range(3)
    ]

    def make(which, put):
        rows = pl.ds(pl.multiple_of(which * tokens, tokens), tokens)
        for start in range(0, width, 512):
            span = pl.ds(start, 512)
            put(
                span,
                dot(o_ref[rows, :], wo_ref[:, span]) + dot(a_ref[rows, :], wd_ref[:, span]),
            )

    def put_own(span, value):
        reduce.own[0, :, span] = value

    for step in reversed(range(PAIRS)):

        def put_out(span, value, step=step):
            reduce.side_out[step, :, span] = value.astype(BF16)

        make(reduce.order[step] * 2 + 1 - side, put_out)
        reduce.begin(step)
        if step == PAIRS - 1:
            for kind in range(3):
                own_back[kind].start()
                for hop in range(1, QUARTERS):
                    back(lax.rem(quarter + hop, QUARTERS), quarter, kind).start()

    def up_tile(tile, held):
        for start in range(0, tile_sum.shape[1], 512):
            span = pl.ds(start, 512)
            tile_sum[:, span] = contract_first(held[...], du_ref[:, span])
        ups.put(tile, lambda q: tile_sum[pl.ds(pl.multiple_of(q * part, part), part), :])

    stream.run(TEAM, up_tile)
    make(reduce.order[3] * 2 + side, put_own)
    reduce.advance(3)
    ups.over_cores()
    load_dy.wait()
    share = width // QUARTERS

    def down_tile(source, first, tile, _):
        columns = pl.ds(pl.multiple_of(tile * 128, 128), 128)
        rows = source[:, columns]

        def quarter_of(q):
            span = pl.ds(pl.multiple_of(q * share, share), share)
            return contract_first(rows, dy[:, span])

        downs.put(first + tile, quarter_of)

    hidden = a_ref.shape[1] // 128
    lax.fori_loop(0, hidden, partial(down_tile, a_ref, 0), None)
    lax.fori_loop(0, HEAD // 128, partial(down_tile, o_ref, hidden), None)
    make(reduce.order[2] * 2 + side, put_own)
    reduce.advance(2)
    downs.over_cores()
    make(reduce.order[1] * 2 + side, put_own)
    reduce.advance(1)
    make(rank, put_own)

    def store_up(tile):
        return pltpu.make_async_copy(ups.total(tile), up_out.at[tile], store_sem.at[0])

    def store_down(tile):
        rows = pl.ds(pl.multiple_of(tile * 128, 128), 128)
        return pltpu.make_async_copy(downs.total(tile), rows_out.at[rows, :], store_sem.at[1])

    ups.over_chips(lambda tile: store_up(tile).start())
    reduce.last()
    strip = 64

    def close(index, _):
        chunk = pl.ds(pl.multiple_of(index * strip, strip), strip)
        total = reduce.total(chunk) + bias_ref[0:1, :]
        result_ref[chunk, :] = (x_ref[chunk, :].astype(F32) + total).astype(BF16)

    lax.fori_loop(0, tokens // strip, close, None)
    downs.over_chips(lambda tile: store_down(tile).start())
    reduce.finish()
    for kind in range(3):
        own_back[kind].wait()
        for hop in range(1, QUARTERS):
            origin = lax.rem(quarter + hop, QUARTERS)
            back(origin, quarter, kind).wait_send()
            back(origin, origin, kind).wait_recv()
    ups.finish()
    downs.finish()
    lax.fori_loop(0, ups.tiles, lambda tile, _: store_up(tile).wait(), None)
    lax.fori_loop(0, downs.tiles, lambda tile, _: store_down(tile).wait(), None)


def third(x, attended, activated, w_out, w_down, bias, grad_up, grads, mlp_input, grad_rows):
    tokens, width = x.shape
    hidden = activated.shape[-1]
    part, share = width // TEAM // QUARTERS, width // QUARTERS
    tiles = (hidden + HEAD) // 128
    shapes = [
        (tokens, width),
        (TEAM, tokens, 3 * HEAD),
        (TEAM, part, hidden),
        (tiles * 128, share),
    ]
    return pl.pallas_call(
        third_kernel,
        out_shape=[jax.ShapeDtypeStruct(shape, BF16) for shape in shapes],
        in_specs=[VMEM] * 7 + [ANY] * 3,
        out_specs=[VMEM, ANY, ANY, ANY],
        scratch_shapes=[
            DMA((4,)),
            DMA((QUARTERS, 3)),
            DMA((QUARTERS, 3)),
            DMA((2,)),
            DMA((2,)),
            pltpu.VMEM((2, TEAM * tokens, width // TEAM), BF16),
            pltpu.VMEM((width // TEAM, hidden), F32),
            pltpu.VMEM((TEAM * tokens, width), BF16),
        ]
        + reduce_scratch(tokens, width, 1, F32)
        + quarters_scratch(TEAM, part, hidden)
        + quarters_scratch(tiles, 128, share),
        compiler_params=pltpu.CompilerParams(
            collective_id=2, has_side_effects=True, vmem_limit_bytes=LIMIT
        ),
        name="scatter_result",
    )(x, attended, activated, w_out, w_down, bias, grad_up, grads, mlp_input, grad_rows)


class Columns:
    def __init__(self, kind, source_of, landed, start, size, sems):
        self.kind, self.source_of, self.landed = kind, source_of, landed
        self.start_lane, self.size, self.sems = start, size, sems
        self.base, line, side, self.quarter = spot()
        self.rank = line * 2 + side
        self.part = landed.shape[1] // QUARTERS

    def region(self, source, slice_of):
        rows = pl.ds(pl.multiple_of(slice_of * self.part, 16), self.part)
        return self.landed.at[source, rows, pl.ds(self.start_lane, self.size)]

    def deal(self, source, target, peer):
        sends, recvs = self.sems[:2]
        return send(
            self.source_of(target), self.region(source, self.quarter),
            sends.at[self.kind, target], recvs.at[self.kind, source],
            self.base + peer, self.quarter,
        )

    def own(self):
        return pltpu.make_async_copy(
            self.source_of(self.rank), self.region(self.rank, self.quarter),
            self.sems[8].at[self.kind],
        )

    def start(self):
        self.own().start()

        def one(step, _):
            target = lax.rem(self.rank + step, TEAM)
            self.deal(self.rank, target, target).start()

        lax.fori_loop(1, TEAM, one, None)

    def pass_on(self, which, source, slice_of, to):
        block = self.region(source, slice_of)
        sends, recvs = self.sems[2 + 2 * which : 4 + 2 * which]
        return send(
            block, block, sends.at[self.kind, source], recvs.at[self.kind, source],
            self.base + self.rank, to,
        )

    def to_core(self, source):
        return self.pass_on(0, source, self.quarter, core_peer(self.quarter))

    def to_chip(self, source):
        return self.pass_on(1, source, self.quarter, chip_peer(self.quarter))

    def to_last(self, source):
        return self.pass_on(2, source, chip_peer(self.quarter), core_peer(self.quarter))

    def forward(self):
        self.own().wait()
        self.to_chip(self.rank).start()
        self.to_core(self.rank).start()

        def one(step, _):
            source = lax.rem(self.rank + TEAM - step, TEAM)
            self.deal(source, self.rank, source).wait_recv()
            self.to_chip(source).start()
            self.to_core(source).start()

        lax.fori_loop(1, TEAM, one, None)

    def forward_last(self):
        def one(step, _):
            source = lax.rem(self.rank + TEAM - step, TEAM)
            self.pass_on(
                1, source, chip_peer(self.quarter), chip_peer(self.quarter)
            ).wait_recv()
            self.to_last(source).start()

        lax.fori_loop(0, TEAM, one, None)

    def finish(self):
        core = core_peer(self.quarter)

        def one(source, _):
            self.pass_on(0, source, core, core).wait_recv()
            self.pass_on(2, source, chip_peer(core), core).wait_recv()
            self.to_core(source).wait_send()
            self.to_chip(source).wait_send()
            self.to_last(source).wait_send()

        lax.fori_loop(0, TEAM, one, None)

        def sent(step, _):
            target = lax.rem(self.rank + step, TEAM)
            self.deal(self.rank, target, target).wait_send()

        lax.fori_loop(1, TEAM, sent, None)


COLUMN_SEMS = [DMA((2, TEAM))] * 8 + [DMA((2,))]


def fourth_kernel(
    x_ref, dy_ref, dqkv_ref, du_ref, vec_ref, dy_sum_ref, xs_ref, w_ref, ha_ref, up_ref, rows_ref,
    grad_ref, landed, rows_out, vector_ref,
    weight, xs, load_sem, tile_load, ha_tiles, tile_sum, sums, packets, packets_in, ring, ring_in,
    row_own, row_send, row_recv, pack_send, pack_recv, ring_send, ring_recv, *rest,
):
    base, line, side, quarter = spot()
    rank = line * 2 + side
    tokens, width = x_ref.shape
    hidden = du_ref.shape[1]
    part = width // TEAM // QUARTERS
    block = width // TEAM
    core, chip = core_peer(quarter), chip_peer(quarter)
    reduce = Reduce(*rest[:4], rest[4:8])
    qkvs = Quarters(*rest[8:16])
    sems = rest[16:25]
    up_columns = Columns(0, lambda n: up_ref.at[n], landed, 3 * HEAD, hidden, sems)
    qkv_columns = Columns(1, lambda n: qkvs.total(n), landed, 0, 3 * HEAD, sems)
    stream = Stream(ha_ref, ha_tiles, tile_load)
    loads = [
        pltpu.make_async_copy(w_ref, weight, load_sem.at[0]),
        pltpu.make_async_copy(xs_ref, xs, load_sem.at[1]),
    ]
    for copy in loads:
        copy.start()
    for tile in range(2):
        stream.copy(tile).start()
    greet_team(base, line, side, quarter)

    def rows_copy(which, slice_of, to):
        src = rows_ref if which < 2 else rows_out.at[slice_of]
        return send(
            src, rows_out.at[slice_of], row_send.at[which], row_recv.at[which], base + rank, to
        )

    own_rows = pltpu.make_async_copy(rows_ref, rows_out.at[quarter], row_own)
    own_rows.start()
    rows_copy(0, quarter, core).start()
    rows_copy(1, quarter, chip).start()
    up_columns.start()
    sums[...] = jnp.zeros_like(sums)
    for copy in loads:
        copy.wait()

    def make(which, put):
        rows = pl.ds(pl.multiple_of(which * tokens, tokens), tokens)
        values = xs[which].astype(F32)
        average = jnp.mean(values, -1, keepdims=True)
        variance = jnp.mean(jnp.square(values - average), -1, keepdims=True)
        inverse = lax.rsqrt(variance + EPSILON)
        for start in range(0, width, 512):
            span = pl.ds(start, 512)
            attn = contract_last(dqkv_ref[rows, :], weight[span, : 3 * HEAD])
            mlp = contract_last(du_ref[rows, :], weight[span, 3 * HEAD :])
            unit = (xs[which, :, span].astype(F32) - average) * inverse
            sums[0:1, span] += jnp.sum(attn * unit, 0, keepdims=True)
            sums[1:2, span] += jnp.sum(mlp * unit, 0, keepdims=True)
            sums[2:3, span] += jnp.sum(attn, 0, keepdims=True)
            sums[3:4, span] += jnp.sum(mlp, 0, keepdims=True)
            put(span, attn * vec_ref[0:1, span] + mlp * vec_ref[1:2, span])
        sums[4:5, pl.ds(0, hidden)] += jnp.sum(du_ref[rows, :].astype(F32), 0, keepdims=True)
        sums[5:6, pl.ds(0, 3 * HEAD)] += jnp.sum(
            dqkv_ref[rows, :].astype(F32), 0, keepdims=True
        )

    for step in reversed(range(PAIRS)):

        def put_out(span, value, step=step):
            reduce.side_out[step, :, span] = value.astype(BF16)

        make(reduce.order[step] * 2 + 1 - side, put_out)
        reduce.begin(step)

    def qkv_tile(tile, held):
        tile_sum[...] = contract_first(held[...], dqkv_ref[...])
        qkvs.put(tile, lambda q: tile_sum[pl.ds(pl.multiple_of(q * part, part), part), :])

    stream.run(TEAM, qkv_tile)
    qkvs.over_cores()
    for step in reversed(range(PAIRS)):

        def put_own(span, value, step=step):
            reduce.own[step, :, span] = value.astype(BF16)

        make(reduce.order[step] * 2 + side, put_own)
        if step == PAIRS - 1:
            reduce.advance(step)

    def pack(target, _):
        span = pl.ds(pl.multiple_of(target * block, block), block)
        packets[target, pl.ds(0, 4), :] = sums[pl.ds(0, 4), span]
        packets[target, pl.ds(4, 1), :] = jnp.where(target == rank, dy_sum_ref[0:1, span], 0.0)
        for index in range(3):
            chunk = 3 * target + index
            kind = lax.div(chunk, HEADS)
            lanes = pl.ds(pl.multiple_of(kind * HEAD, HEAD), HEAD)
            packets[target, pl.ds(5 + index, 1), :] = jnp.where(
                lax.rem(chunk, HEADS) == rank, sums[5:6, lanes], 0.0
            )

    lax.fori_loop(0, TEAM, pack, None)

    def pack_copy(source, target, peer):
        return send(
            packets.at[target], packets_in.at[source], pack_send.at[target], pack_recv.at[source],
            base + peer, quarter,
        )

    def deal_packets(step, _):
        target = lax.rem(rank + step, TEAM)
        pack_copy(rank, target, target).start()

    lax.fori_loop(1, TEAM, deal_packets, None)
    packets_in[rank] = packets[rank]

    up_columns.forward()
    reduce.advance(2)
    rows_copy(1, chip, chip).wait_recv()
    rows_copy(2, chip, core).start()
    qkvs.over_chips(lambda tile: None)
    qkv_columns.start()
    up_columns.forward_last()
    reduce.advance(1)

    def take_packets(step, _):
        source = lax.rem(rank + TEAM - step, TEAM)
        pack_copy(source, rank, source).wait_recv()

    lax.fori_loop(1, TEAM, take_packets, None)
    total = packets_in[0]
    for source in range(1, TEAM):
        total = total + packets_in[source]
    ring[pl.ds(0, 8), :] = total
    for index in range(hidden // block):
        ring[pl.ds(8 + index, 1), :] = sums[4:5, pl.ds(index * block, block)]

    def ring_copy(to, origin, peer):
        return send(
            ring, ring_in.at[origin], ring_send.at[to], ring_recv.at[origin], base + rank, peer
        )

    for hop in range(1, QUARTERS):
        to = lax.rem(quarter + hop, QUARTERS)
        ring_copy(to, quarter, to).start()
    ring_in[quarter] = ring[...]
    qkv_columns.forward()
    reduce.last()
    strip = 64

    def close(index, _):
        chunk = pl.ds(pl.multiple_of(index * strip, strip), strip)
        pulled = reduce.total(chunk)
        unit, inverse = normalize(x_ref[chunk, :].astype(F32))
        pulled = (
            pulled
            - jnp.mean(pulled, -1, keepdims=True)
            - unit * jnp.mean(pulled * unit, -1, keepdims=True)
        )
        grad_ref[chunk, :] = (dy_ref[chunk, :].astype(F32) + inverse * pulled).astype(BF16)

    lax.fori_loop(0, tokens // strip, close, None)
    qkv_columns.forward_last()
    for hop in range(1, QUARTERS):
        origin = lax.rem(quarter + hop, QUARTERS)
        ring_copy(quarter, origin, origin).wait_recv()
    vector_ref[...] = (ring_in[0] + ring_in[1]) + (ring_in[2] + ring_in[3])

    reduce.finish()
    qkvs.finish()
    own_rows.wait()
    rows_copy(0, core, core).wait_recv()
    rows_copy(2, chip_peer(core), core).wait_recv()
    rows_copy(0, quarter, core).wait_send()
    rows_copy(1, quarter, chip).wait_send()
    rows_copy(2, chip, core).wait_send()
    up_columns.finish()
    qkv_columns.finish()

    def sent_packets(step, _):
        target = lax.rem(rank + step, TEAM)
        pack_copy(rank, target, target).wait_send()

    lax.fori_loop(1, TEAM, sent_packets, None)
    for hop in range(1, QUARTERS):
        to = lax.rem(quarter + hop, QUARTERS)
        ring_copy(to, quarter, to).wait_send()


def fourth(
    x, dy, grad_qkv, grad_up, gains, dy_sum, everyone, weight, attn_input, up_sums, row_sums
):
    tokens, width = x.shape
    hidden = grad_up.shape[-1]
    part, block = width // TEAM // QUARTERS, width // TEAM
    shapes = [
        ((tokens, width), BF16),
        ((TEAM, block, 3 * HEAD + hidden), BF16),
        ((QUARTERS, *row_sums.shape), BF16),
        ((16, block), F32),
    ]
    return pl.pallas_call(
        fourth_kernel,
        out_shape=[jax.ShapeDtypeStruct(*shape) for shape in shapes],
        in_specs=[VMEM] * 6 + [ANY] * 5,
        out_specs=[VMEM, ANY, ANY, VMEM],
        scratch_shapes=[
            pltpu.VMEM(weight.shape, BF16),
            pltpu.VMEM(everyone.shape, BF16),
            DMA((2,)),
            DMA((2,)),
            pltpu.VMEM((2, TEAM * tokens, block), BF16),
            pltpu.VMEM((block, 3 * HEAD), F32),
            pltpu.VMEM((8, width), F32),
            pltpu.VMEM((TEAM, 8, block), F32),
            pltpu.VMEM((TEAM, 8, block), F32),
            pltpu.VMEM((16, block), F32),
            pltpu.VMEM((QUARTERS, 16, block), F32),
            DMA,
            DMA((3,)),
            DMA((3,)),
            DMA((TEAM,)),
            DMA((TEAM,)),
            DMA((QUARTERS,)),
            DMA((QUARTERS,)),
        ]
        + reduce_scratch(tokens, width, PAIRS, BF16)
        + quarters_scratch(TEAM, part, 3 * HEAD)
        + COLUMN_SEMS,
        compiler_params=pltpu.CompilerParams(
            collective_id=3, has_side_effects=True, vmem_limit_bytes=LIMIT
        ),
        name="scatter_grad",
    )(x, dy, grad_qkv, grad_up, gains, dy_sum, everyone, weight, attn_input, up_sums, row_sums)


def settle_kernel(
    columns_ref, rows_ref, result_ref, grad_ref,
    qkv_out, up_out, down_out, out_out, result_out, grad_out,
    low, wide, low_rows, wide_rows, passing, load_sem, store_sem, rows_load, rows_store, copy_sem,
):
    team, block, span = columns_ref.shape
    quarters, tall, share = rows_ref.shape
    width = team * HEAD
    hidden = span - 3 * HEAD
    plain = [
        (
            pltpu.make_async_copy(src, passing.at[index], copy_sem.at[index, 0]),
            pltpu.make_async_copy(passing.at[index], dst, copy_sem.at[index, 1]),
        )
        for index, (src, dst) in enumerate(((result_ref, result_out), (grad_ref, grad_out)))
    ]
    for load_in, _ in plain:
        load_in.start()

    def load(source):
        slot = lax.rem(source, 2)
        return pltpu.make_async_copy(columns_ref.at[source], low.at[slot], load_sem.at[slot])

    def stores(source):
        slot = lax.rem(source, 2)
        pairs = []
        for kind in range(3):
            start = pl.multiple_of(kind * width + source * HEAD, HEAD)
            pairs.append((pl.ds(kind * HEAD, HEAD), qkv_out.at[:, pl.ds(start, HEAD)]))
        start = pl.multiple_of(source * hidden, hidden)
        pairs.append((pl.ds(3 * HEAD, hidden), up_out.at[:, pl.ds(start, hidden)]))
        return [
            pltpu.make_async_copy(wide.at[slot, :, lanes], dst, store_sem.at[slot, index])
            for index, (lanes, dst) in enumerate(pairs)
        ]

    def load_rows(quarter):
        slot = lax.rem(quarter, 2)
        return pltpu.make_async_copy(rows_ref.at[quarter], low_rows.at[slot], rows_load.at[slot])

    def stores_rows(quarter):
        slot = lax.rem(quarter, 2)
        lanes = pl.ds(pl.multiple_of(quarter * share, share), share)
        size = tall - HEAD
        return [
            pltpu.make_async_copy(
                wide_rows.at[slot, pl.ds(0, size), :], down_out.at[:, lanes], rows_store.at[slot, 0]
            ),
            pltpu.make_async_copy(
                wide_rows.at[slot, pl.ds(size, HEAD), :], out_out.at[:, lanes],
                rows_store.at[slot, 1],
            ),
        ]

    def run(count, load, stores, low, wide, strip):
        def one(index, _):
            slot = lax.rem(index, 2)
            load(index).wait()

            @pl.when(index >= 2)
            def _():
                for copy in stores(index - 2):
                    copy.wait()

            def widen(step, _):
                chunk = pl.ds(pl.multiple_of(step * strip, strip), strip)
                wide[slot, chunk, :] = low[slot, chunk, :].astype(F32)

            lax.fori_loop(0, low.shape[1] // strip, widen, None)
            for copy in stores(index):
                copy.start()
            pl.when(index + 2 < count)(lambda: load(index + 2).start())

        lax.fori_loop(0, count, one, None)

    for index in range(2):
        load_rows(index).start()
        load(index).start()
    for load_in, store_out in plain:
        load_in.wait()
        store_out.start()
    run(quarters, load_rows, stores_rows, low_rows, wide_rows, 64)
    run(team, load, stores, low, wide, min(64, block))
    for index in (quarters - 2, quarters - 1):
        for copy in stores_rows(index):
            copy.wait()
    for index in (team - 2, team - 1):
        for copy in stores(index):
            copy.wait()
    for _, store_out in plain:
        store_out.wait()


def settle(columns, row_sums, result, grad_inputs):
    team, block, span = columns.shape
    quarters, tall, share = row_sums.shape
    shapes = [
        ((block, team * 3 * HEAD), F32),
        ((block, team * (span - 3 * HEAD)), F32),
        ((tall - HEAD, quarters * share), F32),
        ((HEAD, quarters * share), F32),
        (result.shape, BF16),
        (grad_inputs.shape, BF16),
    ]
    return pl.pallas_call(
        settle_kernel,
        out_shape=[jax.ShapeDtypeStruct(*shape) for shape in shapes],
        in_specs=[ANY] * 4,
        out_specs=[ANY] * 6,
        scratch_shapes=[
            pltpu.VMEM((2, block, span), BF16),
            pltpu.VMEM((2, block, span), F32),
            pltpu.VMEM((2, tall, share), BF16),
            pltpu.VMEM((2, tall, share), F32),
            pltpu.VMEM((2, *result.shape), BF16),
            DMA((2,)),
            DMA((2, 4)),
            DMA((2,)),
            DMA((2, 2)),
            DMA((2, 2)),
        ],
        compiler_params=pltpu.CompilerParams(vmem_limit_bytes=LIMIT),
        name="settle",
    )(columns, row_sums, result, grad_inputs)


def on_device(
    dp,
    ctx,
    inputs,
    segments,
    ln_gain,
    ln_bias,
    qkv_weight,
    qkv_bias,
    out_weight,
    out_bias,
    up_weight,
    up_bias,
    down_weight,
    down_bias,
    cotangent,
):
    assert dp % TEAM == 0 and ctx == QUARTERS
    teams = dp // TEAM
    together = None if teams == 1 else [[g * TEAM + i for i in range(TEAM)] for g in range(teams)]
    across = None if teams == 1 else [[g * TEAM + i for g in range(teams)] for i in range(TEAM)]
    place = lax.axis_index("dp")
    rank = place % TEAM
    _, tokens, width = inputs.shape
    hidden = up_weight.shape[1] // TEAM
    shard = width // dp

    def team_order(values):
        if teams == 1:
            return values
        lead = values.shape[:-1]
        return values.reshape(*lead, teams, TEAM, shard).swapaxes(-3, -2).reshape(*lead, width)

    def plain_order(values):
        if teams == 1:
            return values
        lead = values.shape[:-1]
        return values.reshape(*lead, TEAM, teams, shard).swapaxes(-3, -2).reshape(*lead, width)

    if teams == 1:
        w_qkv, w_up, w_out, w_down = qkv_weight, up_weight, out_weight, down_weight
        gain, shift, b_qkv, b_up = ln_gain, ln_bias, qkv_bias, up_bias
        b_rows = [out_bias, down_bias]
    else:
        line_up = partial(lax.all_gather, axis_name="dp", axis_index_groups=across, tiled=True)
        whole = partial(lax.all_gather, axis_name="dp", axis=0, tiled=True)

        def cut(values):
            size = values.shape[0] // TEAM
            return lax.dynamic_slice_in_dim(values, rank * size, size, 0)

        w_qkv, w_up = line_up(qkv_weight, axis=0), line_up(up_weight, axis=0)
        gain, shift = line_up(ln_gain, axis=1), line_up(ln_bias, axis=1)
        w_out, w_down = cut(whole(out_weight)), cut(whole(down_weight))
        b_qkv, b_up = cut(whole(qkv_bias)), cut(whole(up_bias))
        b_rows = [cut(whole(out_bias)), cut(whole(down_bias))]
    rows = w_qkv.shape[0]
    packet = jnp.concatenate(
        [
            gain.astype(F32),
            shift.astype(F32),
            jnp.stack(b_rows).astype(F32),
            jnp.zeros((2, rows), F32),
            b_qkv.astype(F32).reshape(3, rows),
            jnp.zeros((5, rows), F32),
            jnp.broadcast_to(segments.astype(F32), (8, tokens)),
        ]
    )
    mine = inputs.reshape(tokens, width)
    grad_mine = cotangent.reshape(tokens, width)
    mine_team = team_order(mine)
    positions = jnp.arange(ctx * tokens, dtype=jnp.int32)
    tables = rotary_tables(positions.astype(F32))
    own_tables = [
        lax.dynamic_slice_in_dim(table, lax.axis_index("ctx") * tokens, tokens, 0)
        for table in tables
    ]
    everyone, attn_input, mlp_input, up_values, weight, qkv, marks, vectors = first(
        mine_team, w_qkv, w_up, packet, b_up.astype(F32).reshape(1, hidden), own_tables
    )
    marks = marks[:, :, 0, :].reshape(2, ctx * tokens)
    column, row = marks[:, :, None], marks[:, None, :]
    attended = attend(qkv, column, row)
    grad_rows, activated, grad_up, grad_attended, attended, dy_sum = second(
        grad_mine, w_out, w_down, up_values, attended
    )
    grads = attend_back(qkv, grad_attended, column, row, tables)
    flat = (TEAM * tokens, -1)
    attn_input, mlp_input, grad_rows, activated, grad_up, attended = (
        values.reshape(flat)
        for values in (attn_input, mlp_input, grad_rows, activated, grad_up, attended)
    )
    branch_bias = (vectors[:, 4] + vectors[:, 5]).reshape(1, width)
    result, grad_qkv, up_sums, row_sums = third(
        mine, attended, activated, w_out, w_down, branch_bias, grad_up, grads, mlp_input, grad_rows
    )
    gains = vectors[:, :2].transpose(1, 0, 2).reshape(2, width)
    grad_inputs, columns, row_sums, vector = fourth(
        mine_team, team_order(grad_mine), grad_qkv.reshape(flat), grad_up, gains, dy_sum, everyone,
        weight, attn_input, up_sums, row_sums,
    )
    grad_inputs = plain_order(grad_inputs)
    if teams == 1:
        grad_gain, grad_shift, grad_out_b = vector[0:2], vector[2:4], vector[4]
        grad_qkv_b, grad_up_b = vector[5:8].reshape(-1), vector[8 : 8 + hidden // rows].reshape(-1)
    else:
        near = partial(lax.all_gather, axis_name="dp", axis_index_groups=together, tiled=True)

        def own(values):
            size = values.shape[0] // dp
            total = lax.psum(values, "dp", axis_index_groups=across)
            return lax.dynamic_slice_in_dim(total, place * size, size, 0)

        ends = lax.psum_scatter(
            vector[:4], "dp", scatter_dimension=1, axis_index_groups=across, tiled=True
        )
        grad_gain, grad_shift = ends[0:2], ends[2:4]
        grad_out_b = own(near(vector[4], axis=0))
        grad_qkv_b = own(near(vector[5:8].reshape(-1), axis=0))
        grad_up_b = own(near(vector[8 : 8 + hidden // rows].reshape(-1), axis=0))

        def scatter_rows(term):
            size = term.shape[0]
            full = jnp.zeros((TEAM, size, width), BF16)
            full = lax.dynamic_update_slice_in_dim(full, term.astype(BF16)[None], rank, 0)
            return lax.psum_scatter(
                full.reshape(TEAM * size, width), "dp", scatter_dimension=0, tiled=True
            ).astype(F32)

        columns = lax.psum_scatter(
            columns, "dp", scatter_dimension=1, axis_index_groups=across, tiled=True
        )
    grad_qkv_w, grad_up_w, grad_down_w, grad_out_w, result, grad_inputs = settle(
        columns, row_sums, result, grad_inputs
    )
    if teams > 1:
        grad_out_w, grad_down_w = scatter_rows(grad_out_w), scatter_rows(grad_down_w)
    return (
        result.reshape(inputs.shape),
        grad_inputs.reshape(inputs.shape),
        grad_gain,
        grad_shift,
        grad_qkv_w,
        grad_qkv_b,
        grad_out_w,
        grad_out_b,
        grad_up_w,
        grad_up_b,
        grad_down_w,
        grad_out_b,
    )


def solution(mesh):
    placed = (
        P("dp", "ctx", None),
        P("dp", "ctx"),
        P(None, "dp"),
        P(None, "dp"),
        P("dp", None),
        P("dp"),
        P("dp", None),
        P("dp"),
        P("dp", None),
        P("dp"),
        P("dp", None),
        P("dp"),
        P("dp", "ctx", None),
    )
    return jax.shard_map(
        partial(on_device, mesh.shape["dp"], mesh.shape["ctx"]),
        mesh=mesh,
        in_specs=placed,
        out_specs=(
            P("dp", "ctx", None),
            P("dp", "ctx", None),
            P(None, "dp"),
            P(None, "dp"),
            P("dp", None),
            P("dp"),
            P("dp", None),
            P("dp"),
            P("dp", None),
            P("dp"),
            P("dp", None),
            P("dp"),
        ),
        check_vma=False,
    )
```

```python
from functools import partial

import jax
import jax.numpy as jnp
from jax import lax
from jax.experimental import pallas as pl
from jax.experimental.pallas import tpu as pltpu
from jax.sharding import PartitionSpec as P

HEADS = 8
HEAD = 256
ROT = 64
EPSILON = 1e-05
MASKED = -1e30
F32 = jnp.float32
BF16 = jnp.bfloat16
MESH = pl.DeviceIdType.MESH
TEAM = HEADS
PAIRS = TEAM // 2
QUARTERS = 4
RIGHT, LEFT = 0, 1
VECTOR_ROWS = 24


def dot(left, right):
    return jnp.dot(left, right, preferred_element_type=F32)


def contract_last(left, right):
    return lax.dot_general(left, right, (((1,), (1,)), ((), ())), preferred_element_type=F32)


def contract_first(left, right):
    return lax.dot_general(left, right, (((0,), (0,)), ((), ())), preferred_element_type=F32)


def rotary_tables(positions):
    half = ROT // 2
    exponent = jnp.arange(0, ROT, 2).astype(F32) / ROT
    frequency = 10000.0 ** (-exponent)
    angles = positions[:, None] * frequency[None, :]
    rows = positions.shape[0]
    cosine, sine = jnp.cos(angles), jnp.sin(angles)
    one, nought = jnp.ones((rows, 64), F32), jnp.zeros((rows, 64), F32)
    blank = jnp.zeros((rows, half), F32)
    return (
        jnp.concatenate([cosine, cosine, one], -1),
        jnp.concatenate([-sine, blank, nought], -1),
        jnp.concatenate([blank, sine, nought], -1),
    )


def spot():
    place = lax.axis_index("dp")
    rank = lax.rem(place, TEAM)
    return place - rank, lax.div(rank, 2), lax.rem(rank, 2), lax.axis_index("ctx")


def near_first(line):
    second = 1 + lax.rem(line, 2)
    last = 3 * (1 - lax.div(line, 2))
    return (line, second, 6 - line - second - last, last)


def core_peer(quarter):
    return quarter + 1 - 2 * lax.rem(quarter, 2)


def chip_peer(quarter):
    return quarter + 2 - 4 * lax.div(quarter, 2)


def send(src, dst, send_sem, recv_sem, place, quarter):
    return pltpu.make_async_remote_copy(
        src_ref=src, dst_ref=dst, send_sem=send_sem, recv_sem=recv_sem,
        device_id=(place, quarter), device_id_type=MESH,
    )


def greet_line(base, line, side, quarter):
    barrier = pltpu.get_barrier_semaphore()

    def hail(place, quarter):
        pl.semaphore_signal(barrier, inc=1, device_id=(place, quarter), device_id_type=MESH)

    rank = line * 2 + side
    hail(base + line * 2 + 1 - side, quarter)

    pl.when(line < PAIRS - 1)(lambda: hail(base + rank + 2, quarter))
    pl.when(line > 0)(lambda: hail(base + rank - 2, quarter))
    for step in range(1, QUARTERS):
        hail(base + rank, lax.rem(quarter + step, QUARTERS))
    neighbours = 1 + lax.div(line + 2, 3) - lax.div(line, 3)
    pl.semaphore_wait(barrier, neighbours + QUARTERS)


def greet_team(base, line, side, quarter):
    barrier = pltpu.get_barrier_semaphore()
    rank = line * 2 + side
    for step in range(1, TEAM):
        pl.semaphore_signal(
            barrier, inc=1, device_id=(base + lax.rem(rank + step, TEAM), quarter),
            device_id_type=MESH,
        )
    for step in range(1, QUARTERS):
        pl.semaphore_signal(
            barrier, inc=1, device_id=(base + rank, lax.rem(quarter + step, QUARTERS)),
            device_id_type=MESH,
        )
    pl.semaphore_wait(barrier, TEAM + QUARTERS - 2)


class Relay:
    def __init__(self, held, line_send, line_recv, side_send, side_recv, half_send, half_recv):
        self.held = held
        self.sems = line_send, line_recv, side_send, side_recv, half_send, half_recv
        self.base, self.line, self.side, self.quarter = spot()
        self.half = held.shape[1] // 2

    def neighbour(self, way):
        return self.base + self.line * 2 + self.side + (2 if way == RIGHT else -2)

    def along(self, source, way):
        block = self.held.at[source * 2 + self.side]
        return send(
            block, block, self.sems[0].at[way, source], self.sems[1].at[source],
            self.neighbour(way), self.quarter,
        )

    def along_half(self, way):
        source = 0 if way == RIGHT else PAIRS - 1
        block = self.held.at[source * 2 + 1 - self.side, pl.ds(0, self.half)]
        return send(
            block, block, self.sems[4].at[way], self.sems[5].at[way], self.neighbour(way),
            self.quarter,
        )

    def over(self, source, side, low):
        block = self.held.at[source * 2 + side]
        if low:
            block = self.held.at[source * 2 + side, pl.ds(self.half, self.half)]
        place = self.base + self.line * 2 + 1 - self.side
        return send(
            block, block, self.sems[2].at[source], self.sems[3].at[source], place, self.quarter
        )

    def crossing(self, source, side, act):
        parted = (source != self.line) & (lax.rem(source, PAIRS - 1) == 0)
        pl.when(parted)(lambda: act(self.over(source, side, True)))
        pl.when(jnp.logical_not(parted))(lambda: act(self.over(source, side, False)))

    def each(self, step, act):
        line = self.line
        if step == 0:
            pl.when(line < PAIRS - 1)(lambda: act(line, RIGHT))
            pl.when(line > 0)(lambda: act(line, LEFT))
            act(line, None)
            return

        @pl.when(line >= step)
        def _():
            source = line - step
            act(source, "arrive")
            pl.when(line < PAIRS - 1)(lambda: act(source, RIGHT))
            act(source, None)

        @pl.when(line + step < PAIRS)
        def _():
            source = line + step
            act(source, "arrive")
            pl.when(line > 0)(lambda: act(source, LEFT))
            act(source, None)

    def start(self, step):
        def act(source, way):
            if way == "arrive":
                self.along(source, RIGHT).wait_recv()
            elif way is None:
                self.crossing(source, self.side, lambda copy: copy.start())
            else:
                self.along(source, way).start()

        self.each(step, act)

    def start_halves(self):
        for end, way in ((0, RIGHT), (PAIRS - 1, LEFT)):

            @pl.when(self.line == end)
            def _(end=end, way=way):
                self.over(self.line, 1 - self.side, False).wait_recv()
                self.along_half(way).start()

    def pass_halves(self, step):
        for end, way in ((0, RIGHT), (PAIRS - 1, LEFT)):
            here = step if way == RIGHT else PAIRS - 1 - step

            @pl.when(self.line == here)
            def _(way=way):
                self.along_half(way).wait_recv()
                if step < PAIRS - 1:
                    self.along_half(way).start()

    def wait_over(self, step, source):
        def take(copy):
            copy.wait_recv()

        if step == 0:
            inner = (self.line > 0) & (self.line < PAIRS - 1)
            pl.when(inner)(lambda: take(self.over(source, 1 - self.side, False)))
        else:
            self.crossing(source, 1 - self.side, take)

    def finish(self):
        def act(source, way):
            if way is None:
                self.crossing(source, self.side, lambda copy: copy.wait_send())
            elif way != "arrive":
                self.along(source, way).wait_send()

        for step in range(PAIRS):
            self.each(step, act)
        pl.when(self.line < PAIRS - 1)(lambda: self.along_half(RIGHT).wait_send())
        pl.when(self.line > 0)(lambda: self.along_half(LEFT).wait_send())


RELAY_SEMS = [
    pltpu.SemaphoreType.DMA((2, PAIRS)),
    pltpu.SemaphoreType.DMA((PAIRS,)),
    pltpu.SemaphoreType.DMA((PAIRS,)),
    pltpu.SemaphoreType.DMA((PAIRS,)),
    pltpu.SemaphoreType.DMA((2,)),
    pltpu.SemaphoreType.DMA((2,)),
]


def normalize(rows):
    average = jnp.mean(rows, -1, keepdims=True)
    centred = rows - average
    variance = jnp.mean(centred * centred, -1, keepdims=True)
    inverse = lax.rsqrt(variance + EPSILON)
    return centred * inverse, inverse


def rotate_low(low, cosine, above, below):
    half = ROT // 2
    return (
        low * cosine + pltpu.roll(low, 128 - half, 1) * above + pltpu.roll(low, half, 1) * below
    )


def unrotate_low(low, cosine, above, below):
    half = ROT // 2
    return (
        low * cosine + pltpu.roll(low * below, 128 - half, 1) + pltpu.roll(low * above, half, 1)
    )


class Spread:
    def __init__(self, pieces, send_sem, recv_sem, own_sem):
        self.pieces, self.sems = pieces, (send_sem, recv_sem, own_sem)
        base, line, side, self.quarter = spot()
        self.place = base + line * 2 + side

    def _remote(self, index, sequence, to, origin):
        src, dst = self.pieces[index]
        send_sem, recv_sem, _ = self.sems
        return send(
            src(sequence), dst(lax.rem(sequence, 2), origin), send_sem.at[index, sequence],
            recv_sem.at[index, origin, lax.rem(sequence, 2)], self.place, to,
        )

    def _own(self, index, sequence):
        src, dst = self.pieces[index]
        return pltpu.make_async_copy(
            src(sequence), dst(lax.rem(sequence, 2), self.quarter),
            self.sems[2].at[index, lax.rem(sequence, 2)],
        )

    def start(self, sequence):
        to = lax.div(sequence, 2)

        @pl.when(to == self.quarter)
        def _():
            for index in range(len(self.pieces)):
                self._own(index, sequence).start()

        @pl.when(to != self.quarter)
        def _():
            for index in range(len(self.pieces)):
                self._remote(index, sequence, to, self.quarter).start()

    def finish(self):
        def sent(sequence, _):
            to = lax.div(sequence, 2)

            @pl.when(to == self.quarter)
            def _():
                for index in range(len(self.pieces)):
                    self._own(index, sequence).wait()

            @pl.when(to != self.quarter)
            def _():
                for index in range(len(self.pieces)):
                    self._remote(index, sequence, to, self.quarter).wait_send()

        lax.fori_loop(0, TEAM, sent, None)

        def landed(step, _):
            origin = lax.rem(self.quarter + 1 + lax.div(step, 2), QUARTERS)
            sequence = lax.rem(step, 2)
            for index in range(len(self.pieces)):
                self._remote(index, sequence, origin, origin).wait_recv()

        lax.fori_loop(0, 2 * (QUARTERS - 1), landed, None)


def spread_sems(count):
    return [
        pltpu.SemaphoreType.DMA((count, TEAM)),
        pltpu.SemaphoreType.DMA((count, QUARTERS, 2)),
        pltpu.SemaphoreType.DMA((count, 2)),
    ]


class Columns:
    def __init__(self, pieces, place, lane, lanes, sems):
        self.pieces, self.place, self.lane, self.lanes, self.sems = pieces, place, lane, lanes, sems
        self.base, line, side, self.quarter = spot()
        self.rank = line * 2 + side

    def deal(self, source, target, peer):
        sends, recvs = self.sems[:2]
        return [
            send(
                src, self.place(source, self.quarter, lane, lanes),
                sends.at[index, target], recvs.at[index, source], self.base + peer, self.quarter,
            )
            for index, (src, lane, lanes) in enumerate(self.pieces(target))
        ]

    def own(self):
        return [
            pltpu.make_async_copy(
                src, self.place(self.rank, self.quarter, lane, lanes), self.sems[2].at[index]
            )
            for index, (src, lane, lanes) in enumerate(self.pieces(self.rank))
        ]

    def start(self):
        for copy in self.own():
            copy.start()

        def one(step, _):
            target = lax.rem(self.rank + step, TEAM)
            for copy in self.deal(self.rank, target, target):
                copy.start()

        lax.fori_loop(1, TEAM, one, None)

    def pass_on(self, which, source, slice_of, to):
        block = self.place(source, slice_of, self.lane, self.lanes)
        sends, recvs = self.sems[3 + 2 * which : 5 + 2 * which]
        return send(
            block, block, sends.at[source], recvs.at[source], self.base + self.rank, to
        )

    def to_core(self, source):
        return self.pass_on(0, source, self.quarter, core_peer(self.quarter))

    def to_chip(self, source):
        return self.pass_on(1, source, self.quarter, chip_peer(self.quarter))

    def to_last(self, source):
        return self.pass_on(2, source, chip_peer(self.quarter), core_peer(self.quarter))

    def forward(self):
        for copy in self.own():
            copy.wait()
        self.to_chip(self.rank).start()
        self.to_core(self.rank).start()

        def one(step, _):
            source = lax.rem(self.rank + TEAM - step, TEAM)
            for copy in self.deal(source, self.rank, source):
                copy.wait_recv()
            self.to_chip(source).start()
            self.to_core(source).start()

        lax.fori_loop(1, TEAM, one, None)

    def forward_last(self):
        chip = chip_peer(self.quarter)

        def one(step, _):
            source = lax.rem(self.rank + TEAM - step, TEAM)
            self.pass_on(1, source, chip, chip).wait_recv()
            self.to_last(source).start()

        lax.fori_loop(0, TEAM, one, None)

    def arrive(self):
        core = core_peer(self.quarter)

        def one(source, _):
            self.pass_on(0, source, core, core).wait_recv()
            self.pass_on(2, source, chip_peer(core), core).wait_recv()

        lax.fori_loop(0, TEAM, one, None)

    def finish(self):
        def one(source, _):
            self.to_core(source).wait_send()
            self.to_chip(source).wait_send()
            self.to_last(source).wait_send()

        lax.fori_loop(0, TEAM, one, None)

        def sent(step, _):
            target = lax.rem(self.rank + step, TEAM)
            for copy in self.deal(self.rank, target, target):
                copy.wait_send()

        lax.fori_loop(1, TEAM, sent, None)


def column_sems(count):
    dma = pltpu.SemaphoreType.DMA
    return [dma((count, TEAM))] * 2 + [dma((count,))] + [dma((TEAM,))] * 6


def first_kernel(
    x_ref, wq_ref, vec_ref, cos_ref, above_ref, below_ref,
    x_out, ha_out, hm_out, w_out, qkv_out, seg_out, vec_out,
    held, weight, vecs, ha, hm, qkv, vectors,
    own_sem, store_sem, last_store, v_send, v_recv, spread_send, spread_recv, spread_own, *sems,
):
    base, line, side, quarter = spot()
    rank = line * 2 + side
    tokens, width = x_ref.shape
    rows = wq_ref.shape[0]
    part = rows // QUARTERS
    relay = Relay(held, *sems[:6])
    spread = Spread(
        [
            (
                lambda s: qkv.at[s],
                lambda j, origin: qkv_out.at[j, :, pl.ds(origin * tokens, tokens), :],
            ),
            (lambda s: vecs.at[s, pl.ds(16, 8), :], lambda j, origin: seg_out.at[j, origin]),
        ],
        spread_send, spread_recv, spread_own,
    )
    columns = Columns(
        lambda target: [
            (
                wq_ref.at[
                    pl.ds(pl.multiple_of(quarter * part, 16), part),
                    pl.ds(pl.multiple_of(kind * width + target * HEAD, HEAD), HEAD),
                ],
                kind * HEAD,
                HEAD,
            )
            for kind in range(3)
        ],
        lambda source, slice_of, lane, lanes: weight.at[
            pl.ds(pl.multiple_of(source * rows + slice_of * part, 16), part), pl.ds(lane, lanes)
        ],
        0, 3 * HEAD, sems[6:15],
    )
    greet_team(base, line, side, quarter)

    def vector_copy(source, target, peer):
        return send(
            vec_ref, vecs.at[source], v_send.at[target], v_recv.at[source], base + peer, quarter
        )

    own_x = pltpu.make_async_copy(x_ref, held.at[rank], own_sem.at[0])
    own_x.start()
    own_v = pltpu.make_async_copy(vec_ref, vecs.at[rank], own_sem.at[1])
    own_v.start()

    def send_vector(step, _):
        target = lax.rem(rank + step, TEAM)
        vector_copy(rank, target, target).start()

    lax.fori_loop(1, TEAM, send_vector, None)
    columns.start()
    own_x.wait()
    own_v.wait()
    relay.start(0)
    columns.forward()
    relay.start_halves()
    relay.start(1)
    columns.forward_last()

    def take_vector(step, _):
        origin = lax.rem(rank + TEAM - step, TEAM)
        vector_copy(origin, rank, origin).wait_recv()

    lax.fori_loop(1, TEAM, take_vector, None)
    for source in range(TEAM):
        for row in range(4):
            vectors[pl.ds(row, 1), pl.ds(source * rows, rows)] = vecs[source, pl.ds(row, 1), :]
    columns.arrive()
    last_stores = [
        pltpu.make_async_copy(weight, w_out, last_store.at[0]),
        pltpu.make_async_copy(vecs, vec_out, last_store.at[1]),
    ]
    for copy in last_stores:
        copy.start()

    strip = 32
    own_rows = pl.ds(pl.multiple_of(quarter * tokens, tokens), tokens)

    def stores(which):
        return [
            pltpu.make_async_copy(src.at[which], dst.at[which], store_sem.at[index, which])
            for index, (src, dst) in enumerate(((held, x_out), (ha, ha_out), (hm, hm_out)))
        ]

    def work(which):
        def norm(index, _):
            chunk = pl.ds(pl.multiple_of(index * strip, strip), strip)
            unit, _ = normalize(held[which, chunk, :].astype(F32))
            ha[which, chunk, :] = (unit * vectors[0:1, :] + vectors[2:3, :]).astype(BF16)
            hm[which, chunk, :] = (unit * vectors[1:2, :] + vectors[3:4, :]).astype(BF16)

        lax.fori_loop(0, tokens // strip, norm, None)
        for kind in range(3):
            chunk = kind * TEAM + rank
            bias = vecs[lax.div(chunk, 3), pl.ds(8 + lax.rem(chunk, 3), 1), :]
            made = dot(ha[which], weight[:, pl.ds(kind * HEAD, HEAD)]) + bias
            if kind < 2:
                low = rotate_low(
                    made[:, :128], cos_ref[own_rows, :], above_ref[own_rows, :],
                    below_ref[own_rows, :],
                )
                qkv[which, kind, :, pl.ds(0, 128)] = low.astype(BF16)
                qkv[which, kind, :, pl.ds(128, HEAD - 128)] = made[:, 128:].astype(BF16)
            else:
                qkv[which, kind] = made.astype(BF16)
        spread.start(which)
        for copy in stores(which):
            copy.start()

    for step, place in enumerate(near_first(line)):

        def one(other, _, step=step, place=place):
            @pl.when(other == 1)
            def _():
                if 0 < step < PAIRS - 1:
                    relay.start(step + 1)
                if step > 0:
                    relay.pass_halves(step)
                relay.wait_over(step, place)

            work(place * 2 + side + other * (1 - 2 * side))

        lax.fori_loop(0, 2, one, None)

    relay.finish()
    spread.finish()
    columns.finish()

    def sent(step, _):
        target = lax.rem(rank + step, TEAM)
        vector_copy(rank, target, target).wait_send()

    lax.fori_loop(1, TEAM, sent, None)

    def stored(which, _):
        for copy in stores(which):
            copy.wait()

    lax.fori_loop(0, TEAM, stored, None)
    for copy in last_stores:
        copy.wait()


ANY = pl.BlockSpec(memory_space=pl.ANY)
VMEM = pl.BlockSpec(memory_space=pltpu.VMEM)
DMA = pltpu.SemaphoreType.DMA
LIMIT = 60 << 20


def first(x, w_qkv, vec, tables):
    tokens, width = x.shape
    shapes = [
        ((TEAM, tokens, width), BF16),
        ((TEAM, tokens, width), BF16),
        ((TEAM, tokens, width), BF16),
        ((width, 3 * HEAD), BF16),
        ((2, 3, QUARTERS * tokens, HEAD), BF16),
        ((2, QUARTERS, 8, tokens), F32),
        ((TEAM, VECTOR_ROWS, vec.shape[-1]), F32),
    ]
    return pl.pallas_call(
        first_kernel,
        out_shape=[jax.ShapeDtypeStruct(*shape) for shape in shapes],
        in_specs=[VMEM, ANY, VMEM, VMEM, VMEM, VMEM],
        out_specs=[ANY] * len(shapes),
        scratch_shapes=[
            pltpu.VMEM((TEAM, tokens, width), BF16),
            pltpu.VMEM((width, 3 * HEAD), BF16),
            pltpu.VMEM((TEAM, VECTOR_ROWS, vec.shape[-1]), F32),
            pltpu.VMEM((TEAM, tokens, width), BF16),
            pltpu.VMEM((TEAM, tokens, width), BF16),
            pltpu.VMEM((TEAM, 3, tokens, HEAD), BF16),
            pltpu.VMEM((8, width), F32),
            DMA((2,)),
            DMA((3, TEAM)),
            DMA((2,)),
            DMA((TEAM,)),
            DMA((TEAM,)),
        ]
        + spread_sems(2)
        + RELAY_SEMS
        + column_sems(3),
        compiler_params=pltpu.CompilerParams(
            collective_id=0, has_side_effects=True, vmem_limit_bytes=LIMIT
        ),
        name="gather_x",
    )(x, w_qkv, vec, *tables)


def gelu_terms(values):
    chance = 0.5 * (1.0 + lax.erf(values * (0.5**0.5)))
    density = jnp.exp(-0.5 * values * values) * 0.3989422804014327
    return values * chance, chance + values * density


def probabilities(start, block, q_ref, k_ref, col_ref, row_ref):
    rows, keys = pl.ds(start, block), pl.ds(0, start + block)
    scores = contract_last(q_ref[rows, :], k_ref[keys, :]) * HEAD ** (-0.5)
    shape = scores.shape
    query_pos = start + lax.broadcasted_iota(jnp.int32, shape, 0)
    key_pos = lax.broadcasted_iota(jnp.int32, shape, 1)
    allowed = (query_pos >= key_pos) & (col_ref[rows, :] == row_ref[:, keys])
    scores = jnp.where(allowed, scores, MASKED)
    expanded = jnp.exp(scores - jnp.max(scores, -1, keepdims=True))
    return expanded / jnp.sum(expanded, -1, keepdims=True)


def second_kernel(
    dy_ref, wo_ref, wd_ref, upb_ref, col_ref, row_ref, wu_ref, hm_ref, qkv_ref,
    dy_out, a_out, du_out, do_out, o_out, w_out, sum_out,
    held, hm, weight, qkv, mixed, act, grad, attended,
    own_sem, load_sem, store_sem, w_store, back_send, back_recv,
    spread_send, spread_recv, spread_own, *sems,
):
    base, line, side, quarter = spot()
    rank = line * 2 + side
    tokens, width = dy_ref.shape
    hidden = act.shape[-1]
    rows = wu_ref.shape[0]
    part = rows // QUARTERS
    relay = Relay(held, *sems[:6])
    spread = Spread(
        [
            (
                lambda s: attended.at[s],
                lambda j, origin: do_out.at[j, pl.ds(origin * tokens, tokens), :],
            )
        ],
        spread_send, spread_recv, spread_own,
    )
    columns = Columns(
        lambda target: [
            (
                wu_ref.at[
                    pl.ds(pl.multiple_of(quarter * part, 16), part),
                    pl.ds(pl.multiple_of(target * hidden, hidden), hidden),
                ],
                0,
                hidden,
            )
        ],
        lambda source, slice_of, lane, lanes: weight.at[
            pl.ds(pl.multiple_of(source * rows + slice_of * part, 16), part), pl.ds(lane, lanes)
        ],
        0, hidden, sems[6:15],
    )
    load_qkv = pltpu.make_async_copy(qkv_ref, qkv, load_sem.at[0])
    load_hm = pltpu.make_async_copy(hm_ref, hm, load_sem.at[1])
    load_qkv.start()
    load_hm.start()
    greet_team(base, line, side, quarter)
    own = pltpu.make_async_copy(dy_ref, held.at[rank], own_sem.at[0])
    own.start()
    columns.start()
    own.wait()
    relay.start(0)

    load_qkv.wait()
    length = QUARTERS * tokens

    def attend(sequence, _):
        q, k, v = (qkv.at[sequence, kind] for kind in range(3))
        for start in range(0, length, tokens):
            probs = probabilities(
                start, tokens, q, k, col_ref.at[sequence], row_ref.at[sequence]
            )
            value_block = v[pl.ds(0, start + tokens), :]
            mixed[sequence, pl.ds(start, tokens), :] = dot(
                probs.astype(BF16), value_block
            ).astype(BF16)

    lax.fori_loop(0, 2, attend, None)

    def back(to, origin):
        return send(
            mixed.at[:, pl.ds(to * tokens, tokens), :], o_out.at[pl.ds(2 * origin, 2)],
            back_send.at[to], back_recv.at[origin], base + rank, to,
        )

    own_back = pltpu.make_async_copy(
        mixed.at[:, pl.ds(quarter * tokens, tokens), :], o_out.at[pl.ds(2 * quarter, 2)],
        own_sem.at[1],
    )
    own_back.start()
    for step in range(1, QUARTERS):
        to = lax.rem(quarter + step, QUARTERS)
        back(to, quarter).start()
    columns.forward()
    sum_out[...] = jnp.zeros_like(sum_out)
    relay.start_halves()
    relay.start(1)
    columns.forward_last()
    columns.arrive()
    store_weight = pltpu.make_async_copy(weight, w_out, w_store)
    store_weight.start()
    load_hm.wait()

    def stores(which):
        return [
            pltpu.make_async_copy(src.at[which], dst.at[which], store_sem.at[index, which])
            for index, (src, dst) in enumerate(((held, dy_out), (act, a_out), (grad, du_out)))
        ]

    def work(which):
        attended[which] = contract_last(held[which], wo_ref[...]).astype(BF16)
        spread.start(which)
        for start in range(0, hidden, 256):
            span = pl.ds(start, 256)
            up = dot(hm[which], weight[:, span]) + upb_ref[:, span]
            value, slope = gelu_terms(up)
            act[which, :, span] = value.astype(BF16)
            pulled = contract_last(held[which], wd_ref[span, :])
            grad[which, :, span] = (pulled * slope).astype(BF16)
        for copy in stores(which):
            copy.start()
        sum_out[0:1, :] += jnp.sum(held[which].astype(F32), 0, keepdims=True)

    for step, place in enumerate(near_first(line)):

        def one(other, _, step=step, place=place):
            @pl.when(other == 1)
            def _():
                if 0 < step < PAIRS - 1:
                    relay.start(step + 1)
                if step > 0:
                    relay.pass_halves(step)
                relay.wait_over(step, place)

            work(place * 2 + side + other * (1 - 2 * side))

        lax.fori_loop(0, 2, one, None)

    relay.finish()
    spread.finish()
    columns.finish()
    for step in range(1, QUARTERS):
        other = lax.rem(quarter + step, QUARTERS)
        back(other, quarter).wait_send()
        back(other, other).wait_recv()
    own_back.wait()
    store_weight.wait()

    def stored(which, _):
        for copy in stores(which):
            copy.wait()

    lax.fori_loop(0, TEAM, stored, None)


def second(dy, w_out, w_down, up_bias, column, row, w_up, mlp_input, qkv):
    tokens, width = dy.shape
    hidden = up_bias.shape[-1]
    shapes = [
        ((TEAM, tokens, width), BF16),
        ((TEAM, tokens, hidden), BF16),
        ((TEAM, tokens, hidden), BF16),
        ((2, QUARTERS * tokens, HEAD), BF16),
        ((TEAM, tokens, HEAD), BF16),
        ((width, hidden), BF16),
        ((8, width), F32),
    ]
    return pl.pallas_call(
        second_kernel,
        out_shape=[jax.ShapeDtypeStruct(*shape) for shape in shapes],
        in_specs=[VMEM] * 6 + [ANY] * 3,
        out_specs=[ANY] * 6 + [VMEM],
        scratch_shapes=[
            pltpu.VMEM((TEAM, tokens, width), BF16),
            pltpu.VMEM((TEAM, tokens, width), BF16),
            pltpu.VMEM((width, hidden), BF16),
            pltpu.VMEM(qkv.shape, BF16),
            pltpu.VMEM((2, QUARTERS * tokens, HEAD), BF16),
            pltpu.VMEM((TEAM, tokens, hidden), BF16),
            pltpu.VMEM((TEAM, tokens, hidden), BF16),
            pltpu.VMEM((TEAM, tokens, HEAD), BF16),
            DMA((2,)),
            DMA((2,)),
            DMA((3, TEAM)),
            DMA,
            DMA((QUARTERS,)),
            DMA((QUARTERS,)),
        ]
        + spread_sems(1)
        + RELAY_SEMS
        + column_sems(1),
        compiler_params=pltpu.CompilerParams(
            collective_id=1, has_side_effects=True, vmem_limit_bytes=LIMIT
        ),
        name="gather_dy",
    )(dy, w_out, w_down, up_bias, column, row, w_up, mlp_input, qkv)


def backward_kernel(
    block, qkv_ref, do_ref, col_ref, row_ref, cos_ref, above_ref, below_ref, d_ref, dk_sum, dv_sum
):
    scale = HEAD ** (-0.5)
    q_ref, k_ref, v_ref = (qkv_ref.at[kind] for kind in range(3))
    length = q_ref.shape[0]

    def put(kind, rows, grads):
        low = unrotate_low(
            grads[:, :128], cos_ref[rows, :], above_ref[rows, :], below_ref[rows, :]
        )
        d_ref[kind, rows, pl.ds(0, 128)] = low.astype(BF16)
        d_ref[kind, rows, pl.ds(128, HEAD - 128)] = grads[:, 128:].astype(BF16)

    dk_sum[...] = jnp.zeros_like(dk_sum)
    dv_sum[...] = jnp.zeros_like(dv_sum)
    for start in range(0, length, block):
        rows, keys = pl.ds(start, block), pl.ds(0, start + block)
        probs = probabilities(start, block, q_ref, k_ref, col_ref, row_ref)
        grads = do_ref[rows, :]
        grad_probs = contract_last(grads, v_ref[keys, :])
        row_dot = jnp.sum(probs * grad_probs, -1, keepdims=True)
        grad_scores = (probs * (grad_probs - row_dot)).astype(BF16)
        put(0, rows, dot(grad_scores, k_ref[keys, :]) * scale)
        dk_sum[keys, :] += contract_first(grad_scores, q_ref[rows, :])
        dv_sum[keys, :] += contract_first(probs.astype(BF16), grads)
    put(1, pl.ds(0, length), dk_sum[...] * scale)
    d_ref[2] = dv_sum[...].astype(BF16)


def attention_specs(seqs, length):
    three = pl.BlockSpec((None, 3, length, HEAD), lambda s: (s, 0, 0, 0))
    one = pl.BlockSpec((None, length, HEAD), lambda s: (s, 0, 0))
    masks = [
        pl.BlockSpec((None, length, 1), lambda s: (s, 0, 0)),
        pl.BlockSpec((None, 1, length), lambda s: (s, 0, 0)),
    ]
    return three, one, masks


def attend_back(qkv, grads, column, row, tables):
    seqs, _, length, head = qkv.shape
    three, one, masks = attention_specs(seqs, length)
    table = pl.BlockSpec((length, 128), lambda s: (0, 0))
    return pl.pallas_call(
        partial(backward_kernel, min(256, length)),
        grid=(seqs,),
        in_specs=[three, one] + masks + [table] * 3,
        out_specs=three,
        out_shape=jax.ShapeDtypeStruct(qkv.shape, BF16),
        scratch_shapes=[pltpu.VMEM((length, head), F32)] * 2,
        compiler_params=pltpu.CompilerParams(vmem_limit_bytes=48 << 20),
        name="attend_back",
    )(qkv, grads, column, row, *tables)


class Reduce:
    def __init__(self, own, side_out, side_in, line_in, sems):
        self.own, self.side_out, self.side_in, self.line_in = own, side_out, side_in, line_in
        self.sems = sems
        self.base, self.line, self.side, self.quarter = spot()
        self.order = near_first(self.line)

    def over(self, step):
        side_send, side_recv = self.sems[:2]
        place = self.base + self.line * 2 + 1 - self.side
        return send(
            self.side_out.at[step], self.side_in.at[step], side_send.at[step], side_recv.at[step],
            place, self.quarter,
        )

    def along(self, step, target, way):
        line_send, line_recv = self.sems[2:]
        move = 1 if way == RIGHT else -1
        slot = target if way == RIGHT else jnp.where(target == self.line - 1, PAIRS, target)
        place = self.base + (self.line + move) * 2 + self.side
        return send(
            self.side_out.at[step], self.line_in.at[slot], line_send.at[step], line_recv.at[slot],
            place, self.quarter,
        )

    def arrive(self, slot):
        line_send, line_recv = self.sems[2:]
        return send(
            self.side_out.at[0], self.line_in.at[slot], line_send.at[0], line_recv.at[slot],
            self.base + self.line * 2 + 1 - self.side, self.quarter,
        )

    def begin(self, step):
        self.over(step).start()

    def mine(self, step, chunk):
        slot = step if self.own.shape[0] > 1 else 0
        return self.own[slot, chunk, :].astype(F32) + self.side_in[step, chunk, :].astype(F32)

    def advance(self, step):
        target = self.order[step]
        self.over(step).wait_recv()
        self.over(step).wait_send()

        def forward(way, upstream):
            pl.when(upstream)(lambda: self.arrive(target).wait_recv())
            strip = 64

            def add(index, _):
                chunk = pl.ds(pl.multiple_of(index * strip, strip), strip)
                total = self.mine(step, chunk)
                passing = self.line_in[target, chunk, :].astype(F32)
                total = jnp.where(upstream, total + passing, total)
                self.side_out[step, chunk, :] = total.astype(BF16)

            lax.fori_loop(0, self.own.shape[1] // strip, add, None)
            self.along(step, target, way).start()

        pl.when(target > self.line)(lambda: forward(RIGHT, self.line > 0))
        pl.when(target < self.line)(lambda: forward(LEFT, self.line < PAIRS - 1))

    def last(self):
        self.over(0).wait_recv()
        self.over(0).wait_send()
        pl.when(self.line > 0)(lambda: self.arrive(self.line).wait_recv())
        pl.when(self.line < PAIRS - 1)(lambda: self.arrive(PAIRS).wait_recv())

    def total(self, chunk):
        total = self.mine(0, chunk)
        left = self.line_in[self.line, chunk, :].astype(F32)
        right = self.line_in[PAIRS, chunk, :].astype(F32)
        total = jnp.where(self.line > 0, total + left, total)
        return jnp.where(self.line < PAIRS - 1, total + right, total)

    def finish(self):
        for step in range(1, PAIRS):
            target = self.order[step]
            pl.when(target > self.line)(lambda: self.along(step, target, RIGHT).wait_send())
            pl.when(target < self.line)(lambda: self.along(step, target, LEFT).wait_send())


def reduce_scratch(tokens, width, slots, dtype):
    return [
        pltpu.VMEM((slots, tokens, width), dtype),
        pltpu.VMEM((PAIRS, tokens, width), BF16),
        pltpu.VMEM((PAIRS, tokens, width), BF16),
        pltpu.VMEM((PAIRS + 1, tokens, width), BF16),
        DMA((PAIRS,)),
        DMA((PAIRS,)),
        DMA((PAIRS,)),
        DMA((PAIRS + 1,)),
    ]


class Quarters:
    def __init__(self, keep, away, came, far, core_send, core_recv, chip_send, chip_recv):
        self.keep, self.away, self.came, self.far = keep, away, came, far
        self.sems = core_send, core_recv, chip_send, chip_recv
        base, line, side, self.quarter = spot()
        self.place = base + line * 2 + side
        self.core, self.chip = lax.rem(self.quarter, 2), lax.div(self.quarter, 2)
        self.tiles = keep.shape[0]

    def to_core(self, tile):
        return send(
            self.away.at[tile], self.came.at[tile], self.sems[0].at[tile], self.sems[1].at[tile],
            self.place, core_peer(self.quarter),
        )

    def to_chip(self, tile):
        return send(
            self.away.at[tile, 0], self.far.at[tile], self.sems[2].at[tile], self.sems[3].at[tile],
            self.place, chip_peer(self.quarter),
        )

    def put(self, tile, quarter_of):
        for chip in range(2):
            self.keep[tile, chip] = quarter_of(2 * chip + self.core).astype(BF16)
            self.away[tile, chip] = quarter_of(2 * chip + 1 - self.core).astype(BF16)
        self.to_core(tile).start()

    def over_cores(self):
        def one(tile, _):
            self.to_core(tile).wait_recv()
            self.to_core(tile).wait_send()
            other = 1 - self.chip
            passed = self.keep[tile, other].astype(F32) + self.came[tile, other].astype(F32)
            self.away[tile, 0] = passed.astype(BF16)
            self.to_chip(tile).start()
            kept = self.keep[tile, self.chip].astype(F32)
            kept = kept + self.came[tile, self.chip].astype(F32)
            self.keep[tile, self.chip] = kept.astype(BF16)

        lax.fori_loop(0, self.tiles, one, None)

    def over_chips(self, then):
        def one(tile, _):
            self.to_chip(tile).wait_recv()
            total = self.keep[tile, self.chip].astype(F32) + self.far[tile].astype(F32)
            self.keep[tile, self.chip] = total.astype(BF16)
            then(tile)

        lax.fori_loop(0, self.tiles, one, None)

    def total(self, tile):
        return self.keep.at[tile, self.chip]

    def finish(self):
        lax.fori_loop(0, self.tiles, lambda tile, _: self.to_chip(tile).wait_send(), None)


def quarters_scratch(tiles, rows, columns):
    return [
        pltpu.VMEM((tiles, 2, rows, columns), BF16),
        pltpu.VMEM((tiles, 2, rows, columns), BF16),
        pltpu.VMEM((tiles, 2, rows, columns), BF16),
        pltpu.VMEM((tiles, rows, columns), BF16),
    ] + [DMA((tiles,))] * 4


class Stream:
    def __init__(self, source, slots, sems):
        self.source, self.slots, self.sems = source, slots, sems

    def copy(self, tile):
        size = self.slots.shape[-1]
        start = pl.multiple_of(tile * size, size)
        slot = lax.rem(tile, 2)
        return pltpu.make_async_copy(
            self.source.at[:, pl.ds(start, size)], self.slots.at[slot], self.sems.at[slot]
        )

    def run(self, tiles, use):
        def one(tile, _):
            self.copy(tile).wait()
            use(tile, self.slots.at[lax.rem(tile, 2)])
            pl.when(tile + 2 < tiles)(lambda: self.copy(tile + 2).start())

        lax.fori_loop(0, tiles, one, None)


def third_kernel(
    x_ref, o_ref, a_ref, wo_ref, wd_ref, vec_ref, du_ref, d_ref, hm_ref, dy_ref,
    result_ref, back_out, up_out, rows_out,
    own_sem, back_send, back_recv, load_sem, store_sem, hm_tiles, tile_sum, dy, bias, *rest,
):
    base, line, side, quarter = spot()
    rank = line * 2 + side
    tokens, width = x_ref.shape
    part = width // TEAM // QUARTERS
    reduce = Reduce(*rest[:4], rest[4:8])
    ups, downs = Quarters(*rest[8:16]), Quarters(*rest[16:24])
    stream = Stream(hm_ref, hm_tiles, load_sem)
    load_dy = pltpu.make_async_copy(dy_ref, dy, own_sem.at[3])
    load_dy.start()
    for tile in range(2):
        stream.copy(tile).start()
    greet_line(base, line, side, quarter)

    def pieces(to, origin, kind):
        return (
            d_ref.at[:, kind, pl.ds(to * tokens, tokens), :],
            back_out.at[pl.ds(2 * origin, 2), :, pl.ds(kind * HEAD, HEAD)],
        )

    def back(to, origin, kind):
        src, dst = pieces(to, origin, kind)
        return send(
            src, dst, back_send.at[to, kind], back_recv.at[origin, kind], base + rank, to
        )

    own_back = [
        pltpu.make_async_copy(*pieces(quarter, quarter, kind), own_sem.at[kind])
        for kind in range(3)
    ]

    def make(which, put):
        rows = pl.ds(pl.multiple_of(which * tokens, tokens), tokens)
        for start in range(0, width, 512):
            span = pl.ds(start, 512)
            put(
                span,
                dot(o_ref[rows, :], wo_ref[:, span]) + dot(a_ref[rows, :], wd_ref[:, span]),
            )

    def put_own(span, value):
        reduce.own[0, :, span] = value

    for step in reversed(range(PAIRS)):

        def put_out(span, value, step=step):
            reduce.side_out[step, :, span] = value.astype(BF16)

        make(reduce.order[step] * 2 + 1 - side, put_out)
        reduce.begin(step)
        if step == PAIRS - 1:
            for kind in range(3):
                own_back[kind].start()
                for hop in range(1, QUARTERS):
                    back(lax.rem(quarter + hop, QUARTERS), quarter, kind).start()

    def up_tile(tile, held):
        for start in range(0, tile_sum.shape[1], 512):
            span = pl.ds(start, 512)
            tile_sum[:, span] = contract_first(held[...], du_ref[:, span])
        ups.put(tile, lambda q: tile_sum[pl.ds(pl.multiple_of(q * part, part), part), :])

    stream.run(TEAM, up_tile)
    make(reduce.order[3] * 2 + side, put_own)
    reduce.advance(3)
    ups.over_cores()
    load_dy.wait()
    share = width // QUARTERS

    def down_tile(source, first, tile, _):
        columns = pl.ds(pl.multiple_of(tile * 128, 128), 128)
        rows = source[:, columns]

        def quarter_of(q):
            span = pl.ds(pl.multiple_of(q * share, share), share)
            return contract_first(rows, dy[:, span])

        downs.put(first + tile, quarter_of)

    hidden = a_ref.shape[1] // 128
    lax.fori_loop(0, hidden, partial(down_tile, a_ref, 0), None)
    lax.fori_loop(0, HEAD // 128, partial(down_tile, o_ref, hidden), None)
    make(reduce.order[2] * 2 + side, put_own)
    reduce.advance(2)
    downs.over_cores()
    make(reduce.order[1] * 2 + side, put_own)
    reduce.advance(1)
    make(rank, put_own)

    def store_up(tile):
        return pltpu.make_async_copy(ups.total(tile), up_out.at[tile], store_sem.at[0])

    def store_down(tile):
        rows = pl.ds(pl.multiple_of(tile * 128, 128), 128)
        return pltpu.make_async_copy(downs.total(tile), rows_out.at[rows, :], store_sem.at[1])

    ups.over_chips(lambda tile: store_up(tile).start())
    block = width // TEAM
    for source in range(TEAM):
        bias[0:1, pl.ds(source * block, block)] = vec_ref[source, 4:5, :] + vec_ref[source, 5:6, :]
    reduce.last()
    strip = 64

    def close(index, _):
        chunk = pl.ds(pl.multiple_of(index * strip, strip), strip)
        total = reduce.total(chunk) + bias[0:1, :]
        result_ref[chunk, :] = (x_ref[chunk, :].astype(F32) + total).astype(BF16)

    lax.fori_loop(0, tokens // strip, close, None)
    downs.over_chips(lambda tile: store_down(tile).start())
    reduce.finish()
    for kind in range(3):
        own_back[kind].wait()
        for hop in range(1, QUARTERS):
            origin = lax.rem(quarter + hop, QUARTERS)
            back(origin, quarter, kind).wait_send()
            back(origin, origin, kind).wait_recv()
    ups.finish()
    downs.finish()
    lax.fori_loop(0, ups.tiles, lambda tile, _: store_up(tile).wait(), None)
    lax.fori_loop(0, downs.tiles, lambda tile, _: store_down(tile).wait(), None)


def third(x, attended, activated, w_out, w_down, vectors, grad_up, grads, mlp_input, grad_rows):
    tokens, width = x.shape
    hidden = activated.shape[-1]
    part, share = width // TEAM // QUARTERS, width // QUARTERS
    tiles = (hidden + HEAD) // 128
    shapes = [
        (tokens, width),
        (TEAM, tokens, 3 * HEAD),
        (TEAM, part, hidden),
        (tiles * 128, share),
    ]
    return pl.pallas_call(
        third_kernel,
        out_shape=[jax.ShapeDtypeStruct(shape, BF16) for shape in shapes],
        in_specs=[VMEM] * 7 + [ANY] * 3,
        out_specs=[VMEM, ANY, ANY, ANY],
        scratch_shapes=[
            DMA((4,)),
            DMA((QUARTERS, 3)),
            DMA((QUARTERS, 3)),
            DMA((2,)),
            DMA((2,)),
            pltpu.VMEM((2, TEAM * tokens, width // TEAM), BF16),
            pltpu.VMEM((width // TEAM, hidden), F32),
            pltpu.VMEM((TEAM * tokens, width), BF16),
            pltpu.VMEM((8, width), F32),
        ]
        + reduce_scratch(tokens, width, 1, F32)
        + quarters_scratch(TEAM, part, hidden)
        + quarters_scratch(tiles, 128, share),
        compiler_params=pltpu.CompilerParams(
            collective_id=2, has_side_effects=True, vmem_limit_bytes=LIMIT
        ),
        name="scatter_result",
    )(x, attended, activated, w_out, w_down, vectors, grad_up, grads, mlp_input, grad_rows)


def fourth_kernel(
    x_ref, dy_ref, dqkv_ref, du_ref, vec_ref, dy_sum_ref, xs_ref, wq_ref, wu_ref, ha_ref, up_ref, rows_ref,
    grad_ref, landed, rows_out, vector_ref,
    wq, wu, xs, gains, load_sem, tile_load, ha_tiles, tile_sum, sums, packets, packets_in, ring, ring_in,
    row_own, row_send, row_recv, pack_send, pack_recv, ring_send, ring_recv, *rest,
):
    base, line, side, quarter = spot()
    rank = line * 2 + side
    tokens, width = x_ref.shape
    hidden = du_ref.shape[1]
    part = width // TEAM // QUARTERS
    block = width // TEAM
    core, chip = core_peer(quarter), chip_peer(quarter)
    reduce = Reduce(*rest[:4], rest[4:8])
    qkvs = Quarters(*rest[8:16])

    def place(source, slice_of, lane, lanes):
        rows = pl.ds(pl.multiple_of(slice_of * part, 16), part)
        return landed.at[source, rows, pl.ds(lane, lanes)]

    up_columns = Columns(
        lambda n: [(up_ref.at[n], 3 * HEAD, hidden)], place, 3 * HEAD, hidden, rest[16:25]
    )
    qkv_columns = Columns(
        lambda n: [(qkvs.total(n), 0, 3 * HEAD)], place, 0, 3 * HEAD, rest[25:34]
    )
    stream = Stream(ha_ref, ha_tiles, tile_load)
    loads = [
        pltpu.make_async_copy(wq_ref, wq, load_sem.at[0]),
        pltpu.make_async_copy(wu_ref, wu, load_sem.at[1]),
        pltpu.make_async_copy(xs_ref, xs, load_sem.at[2]),
    ]
    for copy in loads:
        copy.start()
    for tile in range(2):
        stream.copy(tile).start()
    greet_team(base, line, side, quarter)

    def rows_copy(which, slice_of, to):
        src = rows_ref if which < 2 else rows_out.at[slice_of]
        return send(
            src, rows_out.at[slice_of], row_send.at[which], row_recv.at[which], base + rank, to
        )

    own_rows = pltpu.make_async_copy(rows_ref, rows_out.at[quarter], row_own)
    own_rows.start()
    rows_copy(0, quarter, core).start()
    rows_copy(1, quarter, chip).start()
    up_columns.start()
    sums[...] = jnp.zeros_like(sums)
    for source in range(TEAM):
        gains[0:2, pl.ds(source * block, block)] = vec_ref[source, 0:2, :]
    for copy in loads:
        copy.wait()

    def make(which, put):
        rows = pl.ds(pl.multiple_of(which * tokens, tokens), tokens)
        values = xs[which].astype(F32)
        average = jnp.mean(values, -1, keepdims=True)
        variance = jnp.mean(jnp.square(values - average), -1, keepdims=True)
        inverse = lax.rsqrt(variance + EPSILON)
        for start in range(0, width, 512):
            span = pl.ds(start, 512)
            attn = contract_last(dqkv_ref[rows, :], wq[span, :])
            mlp = contract_last(du_ref[rows, :], wu[span, :])
            unit = (xs[which, :, span].astype(F32) - average) * inverse
            sums[0:1, span] += jnp.sum(attn * unit, 0, keepdims=True)
            sums[1:2, span] += jnp.sum(mlp * unit, 0, keepdims=True)
            sums[2:3, span] += jnp.sum(attn, 0, keepdims=True)
            sums[3:4, span] += jnp.sum(mlp, 0, keepdims=True)
            put(span, attn * gains[0:1, span] + mlp * gains[1:2, span])
        sums[4:5, pl.ds(0, hidden)] += jnp.sum(du_ref[rows, :].astype(F32), 0, keepdims=True)
        sums[5:6, pl.ds(0, 3 * HEAD)] += jnp.sum(
            dqkv_ref[rows, :].astype(F32), 0, keepdims=True
        )

    for step in reversed(range(PAIRS)):

        def put_out(span, value, step=step):
            reduce.side_out[step, :, span] = value.astype(BF16)

        make(reduce.order[step] * 2 + 1 - side, put_out)
        reduce.begin(step)

    def qkv_tile(tile, held):
        tile_sum[...] = contract_first(held[...], dqkv_ref[...])
        qkvs.put(tile, lambda q: tile_sum[pl.ds(pl.multiple_of(q * part, part), part), :])

    stream.run(TEAM, qkv_tile)
    qkvs.over_cores()
    for step in reversed(range(PAIRS)):

        def put_own(span, value, step=step):
            reduce.own[step, :, span] = value.astype(BF16)

        make(reduce.order[step] * 2 + side, put_own)
        if step == PAIRS - 1:
            reduce.advance(step)

    def pack(target, _):
        span = pl.ds(pl.multiple_of(target * block, block), block)
        packets[target, pl.ds(0, 4), :] = sums[pl.ds(0, 4), span]
        packets[target, pl.ds(4, 1), :] = jnp.where(target == rank, dy_sum_ref[0:1, span], 0.0)
        for index in range(3):
            chunk = 3 * target + index
            kind = lax.div(chunk, HEADS)
            lanes = pl.ds(pl.multiple_of(kind * HEAD, HEAD), HEAD)
            packets[target, pl.ds(5 + index, 1), :] = jnp.where(
                lax.rem(chunk, HEADS) == rank, sums[5:6, lanes], 0.0
            )

    lax.fori_loop(0, TEAM, pack, None)

    def pack_copy(source, target, peer):
        return send(
            packets.at[target], packets_in.at[source], pack_send.at[target], pack_recv.at[source],
            base + peer, quarter,
        )

    def deal_packets(step, _):
        target = lax.rem(rank + step, TEAM)
        pack_copy(rank, target, target).start()

    lax.fori_loop(1, TEAM, deal_packets, None)
    packets_in[rank] = packets[rank]

    up_columns.forward()
    reduce.advance(2)
    rows_copy(1, chip, chip).wait_recv()
    rows_copy(2, chip, core).start()
    qkvs.over_chips(lambda tile: None)
    qkv_columns.start()
    up_columns.forward_last()
    reduce.advance(1)

    def take_packets(step, _):
        source = lax.rem(rank + TEAM - step, TEAM)
        pack_copy(source, rank, source).wait_recv()

    lax.fori_loop(1, TEAM, take_packets, None)
    total = packets_in[0]
    for source in range(1, TEAM):
        total = total + packets_in[source]
    ring[pl.ds(0, 8), :] = total
    for index in range(hidden // block):
        ring[pl.ds(8 + index, 1), :] = sums[4:5, pl.ds(index * block, block)]

    def ring_copy(to, origin, peer):
        return send(
            ring, ring_in.at[origin], ring_send.at[to], ring_recv.at[origin], base + rank, peer
        )

    for hop in range(1, QUARTERS):
        to = lax.rem(quarter + hop, QUARTERS)
        ring_copy(to, quarter, to).start()
    ring_in[quarter] = ring[...]
    qkv_columns.forward()
    reduce.last()
    strip = 64

    def close(index, _):
        chunk = pl.ds(pl.multiple_of(index * strip, strip), strip)
        pulled = reduce.total(chunk)
        unit, inverse = normalize(x_ref[chunk, :].astype(F32))
        pulled = (
            pulled
            - jnp.mean(pulled, -1, keepdims=True)
            - unit * jnp.mean(pulled * unit, -1, keepdims=True)
        )
        grad_ref[chunk, :] = (dy_ref[chunk, :].astype(F32) + inverse * pulled).astype(BF16)

    lax.fori_loop(0, tokens // strip, close, None)
    qkv_columns.forward_last()
    for hop in range(1, QUARTERS):
        origin = lax.rem(quarter + hop, QUARTERS)
        ring_copy(quarter, origin, origin).wait_recv()
    vector_ref[...] = (ring_in[0] + ring_in[1]) + (ring_in[2] + ring_in[3])

    reduce.finish()
    qkvs.finish()
    own_rows.wait()
    rows_copy(0, core, core).wait_recv()
    rows_copy(2, chip_peer(core), core).wait_recv()
    rows_copy(0, quarter, core).wait_send()
    rows_copy(1, quarter, chip).wait_send()
    rows_copy(2, chip, core).wait_send()
    for columns in (up_columns, qkv_columns):
        columns.arrive()
        columns.finish()

    def sent_packets(step, _):
        target = lax.rem(rank + step, TEAM)
        pack_copy(rank, target, target).wait_send()

    lax.fori_loop(1, TEAM, sent_packets, None)
    for hop in range(1, QUARTERS):
        to = lax.rem(quarter + hop, QUARTERS)
        ring_copy(to, quarter, to).wait_send()


def fourth(
    x, dy, grad_qkv, grad_up, vectors, dy_sum, everyone, w_qkv, w_up, attn_input, up_sums, row_sums
):
    tokens, width = x.shape
    hidden = grad_up.shape[-1]
    part, block = width // TEAM // QUARTERS, width // TEAM
    shapes = [
        ((tokens, width), BF16),
        ((TEAM, block, 3 * HEAD + hidden), BF16),
        ((QUARTERS, *row_sums.shape), BF16),
        ((16, block), F32),
    ]
    return pl.pallas_call(
        fourth_kernel,
        out_shape=[jax.ShapeDtypeStruct(*shape) for shape in shapes],
        in_specs=[VMEM] * 6 + [ANY] * 6,
        out_specs=[VMEM, ANY, ANY, VMEM],
        scratch_shapes=[
            pltpu.VMEM(w_qkv.shape, BF16),
            pltpu.VMEM(w_up.shape, BF16),
            pltpu.VMEM(everyone.shape, BF16),
            pltpu.VMEM((8, width), F32),
            DMA((3,)),
            DMA((2,)),
            pltpu.VMEM((2, TEAM * tokens, block), BF16),
            pltpu.VMEM((block, 3 * HEAD), F32),
            pltpu.VMEM((8, width), F32),
            pltpu.VMEM((TEAM, 8, block), F32),
            pltpu.VMEM((TEAM, 8, block), F32),
            pltpu.VMEM((16, block), F32),
            pltpu.VMEM((QUARTERS, 16, block), F32),
            DMA,
            DMA((3,)),
            DMA((3,)),
            DMA((TEAM,)),
            DMA((TEAM,)),
            DMA((QUARTERS,)),
            DMA((QUARTERS,)),
        ]
        + reduce_scratch(tokens, width, PAIRS, BF16)
        + quarters_scratch(TEAM, part, 3 * HEAD)
        + column_sems(1) * 2,
        compiler_params=pltpu.CompilerParams(
            collective_id=3, has_side_effects=True, vmem_limit_bytes=LIMIT
        ),
        name="scatter_grad",
    )(
        x, dy, grad_qkv, grad_up, vectors, dy_sum, everyone, w_qkv, w_up, attn_input, up_sums,
        row_sums,
    )


def settle_kernel(
    columns_ref, rows_ref, result_ref, grad_ref,
    qkv_out, up_out, down_out, out_out, result_out, grad_out,
    low, wide, low_rows, wide_rows, passing, load_sem, store_sem, rows_load, rows_store, copy_sem,
):
    team, block, span = columns_ref.shape
    quarters, tall, share = rows_ref.shape
    width = team * HEAD
    hidden = span - 3 * HEAD
    plain = [
        (
            pltpu.make_async_copy(src, passing.at[index], copy_sem.at[index, 0]),
            pltpu.make_async_copy(passing.at[index], dst, copy_sem.at[index, 1]),
        )
        for index, (src, dst) in enumerate(((result_ref, result_out), (grad_ref, grad_out)))
    ]
    for load_in, _ in plain:
        load_in.start()

    def load(source):
        slot = lax.rem(source, 2)
        return pltpu.make_async_copy(columns_ref.at[source], low.at[slot], load_sem.at[slot])

    def stores(source):
        slot = lax.rem(source, 2)
        pairs = []
        for kind in range(3):
            start = pl.multiple_of(kind * width + source * HEAD, HEAD)
            pairs.append((pl.ds(kind * HEAD, HEAD), qkv_out.at[:, pl.ds(start, HEAD)]))
        start = pl.multiple_of(source * hidden, hidden)
        pairs.append((pl.ds(3 * HEAD, hidden), up_out.at[:, pl.ds(start, hidden)]))
        return [
            pltpu.make_async_copy(wide.at[slot, :, lanes], dst, store_sem.at[slot, index])
            for index, (lanes, dst) in enumerate(pairs)
        ]

    def load_rows(quarter):
        slot = lax.rem(quarter, 2)
        return pltpu.make_async_copy(rows_ref.at[quarter], low_rows.at[slot], rows_load.at[slot])

    def stores_rows(quarter):
        slot = lax.rem(quarter, 2)
        lanes = pl.ds(pl.multiple_of(quarter * share, share), share)
        size = tall - HEAD
        return [
            pltpu.make_async_copy(
                wide_rows.at[slot, pl.ds(0, size), :], down_out.at[:, lanes], rows_store.at[slot, 0]
            ),
            pltpu.make_async_copy(
                wide_rows.at[slot, pl.ds(size, HEAD), :], out_out.at[:, lanes],
                rows_store.at[slot, 1],
            ),
        ]

    def run(count, load, stores, low, wide, strip):
        def one(index, _):
            slot = lax.rem(index, 2)
            load(index).wait()

            @pl.when(index >= 2)
            def _():
                for copy in stores(index - 2):
                    copy.wait()

            def widen(step, _):
                chunk = pl.ds(pl.multiple_of(step * strip, strip), strip)
                wide[slot, chunk, :] = low[slot, chunk, :].astype(F32)

            lax.fori_loop(0, low.shape[1] // strip, widen, None)
            for copy in stores(index):
                copy.start()
            pl.when(index + 2 < count)(lambda: load(index + 2).start())

        lax.fori_loop(0, count, one, None)

    for index in range(2):
        load_rows(index).start()
        load(index).start()
    for load_in, store_out in plain:
        load_in.wait()
        store_out.start()
    run(quarters, load_rows, stores_rows, low_rows, wide_rows, 64)
    run(team, load, stores, low, wide, min(64, block))
    for index in (quarters - 2, quarters - 1):
        for copy in stores_rows(index):
            copy.wait()
    for index in (team - 2, team - 1):
        for copy in stores(index):
            copy.wait()
    for _, store_out in plain:
        store_out.wait()


def settle(columns, row_sums, result, grad_inputs):
    team, block, span = columns.shape
    quarters, tall, share = row_sums.shape
    shapes = [
        ((block, team * 3 * HEAD), F32),
        ((block, team * (span - 3 * HEAD)), F32),
        ((tall - HEAD, quarters * share), F32),
        ((HEAD, quarters * share), F32),
        (result.shape, BF16),
        (grad_inputs.shape, BF16),
    ]
    return pl.pallas_call(
        settle_kernel,
        out_shape=[jax.ShapeDtypeStruct(*shape) for shape in shapes],
        in_specs=[ANY] * 4,
        out_specs=[ANY] * 6,
        scratch_shapes=[
            pltpu.VMEM((2, block, span), BF16),
            pltpu.VMEM((2, block, span), F32),
            pltpu.VMEM((2, tall, share), BF16),
            pltpu.VMEM((2, tall, share), F32),
            pltpu.VMEM((2, *result.shape), BF16),
            DMA((2,)),
            DMA((2, 4)),
            DMA((2,)),
            DMA((2, 2)),
            DMA((2, 2)),
        ],
        compiler_params=pltpu.CompilerParams(vmem_limit_bytes=LIMIT),
        name="settle",
    )(columns, row_sums, result, grad_inputs)


def on_device(
    dp,
    ctx,
    inputs,
    segments,
    ln_gain,
    ln_bias,
    qkv_weight,
    qkv_bias,
    out_weight,
    out_bias,
    up_weight,
    up_bias,
    down_weight,
    down_bias,
    cotangent,
):
    assert dp % TEAM == 0 and ctx == QUARTERS
    teams = dp // TEAM
    together = None if teams == 1 else [[g * TEAM + i for i in range(TEAM)] for g in range(teams)]
    across = None if teams == 1 else [[g * TEAM + i for g in range(teams)] for i in range(TEAM)]
    place = lax.axis_index("dp")
    rank = place % TEAM
    _, tokens, width = inputs.shape
    hidden = up_weight.shape[1] // TEAM
    shard = width // dp

    def team_order(values):
        if teams == 1:
            return values
        lead = values.shape[:-1]
        return values.reshape(*lead, teams, TEAM, shard).swapaxes(-3, -2).reshape(*lead, width)

    def plain_order(values):
        if teams == 1:
            return values
        lead = values.shape[:-1]
        return values.reshape(*lead, TEAM, teams, shard).swapaxes(-3, -2).reshape(*lead, width)

    if teams == 1:
        w_qkv, w_up, w_out, w_down = qkv_weight, up_weight, out_weight, down_weight
        gain, shift, b_qkv, b_up = ln_gain, ln_bias, qkv_bias, up_bias
        b_rows = [out_bias, down_bias]
    else:
        line_up = partial(lax.all_gather, axis_name="dp", axis_index_groups=across, tiled=True)
        whole = partial(lax.all_gather, axis_name="dp", axis=0, tiled=True)

        def cut(values):
            size = values.shape[0] // TEAM
            return lax.dynamic_slice_in_dim(values, rank * size, size, 0)

        w_qkv, w_up = line_up(qkv_weight, axis=0), line_up(up_weight, axis=0)
        gain, shift = line_up(ln_gain, axis=1), line_up(ln_bias, axis=1)
        w_out, w_down = cut(whole(out_weight)), cut(whole(down_weight))
        b_qkv, b_up = cut(whole(qkv_bias)), cut(whole(up_bias))
        b_rows = [cut(whole(out_bias)), cut(whole(down_bias))]
    rows = w_qkv.shape[0]
    packet = jnp.concatenate(
        [
            gain.astype(F32),
            shift.astype(F32),
            jnp.stack(b_rows).astype(F32),
            jnp.zeros((2, rows), F32),
            b_qkv.astype(F32).reshape(3, rows),
            jnp.zeros((5, rows), F32),
            jnp.broadcast_to(segments.astype(F32), (8, tokens)),
        ]
    )
    mine = inputs.reshape(tokens, width)
    grad_mine = cotangent.reshape(tokens, width)
    mine_team = team_order(mine)
    positions = jnp.arange(ctx * tokens, dtype=jnp.int32)
    tables = rotary_tables(positions.astype(F32))
    everyone, attn_input, mlp_input, w_head, qkv, marks, vectors = first(
        mine_team, w_qkv, packet, tables
    )
    marks = marks[:, :, 0, :].reshape(2, ctx * tokens)
    column, row = marks[:, :, None], marks[:, None, :]
    grad_rows, activated, grad_up, grad_attended, attended, w_units, dy_sum = second(
        grad_mine, w_out, w_down, b_up.astype(F32).reshape(1, hidden), column, row, w_up, mlp_input,
        qkv,
    )
    grads = attend_back(qkv, grad_attended, column, row, tables)
    flat = (TEAM * tokens, -1)
    attn_input, mlp_input, grad_rows, activated, grad_up, attended = (
        values.reshape(flat)
        for values in (attn_input, mlp_input, grad_rows, activated, grad_up, attended)
    )
    result, grad_qkv, up_sums, row_sums = third(
        mine, attended, activated, w_out, w_down, vectors, grad_up, grads, mlp_input, grad_rows
    )
    grad_inputs, columns, row_sums, vector = fourth(
        mine_team, team_order(grad_mine), grad_qkv.reshape(flat), grad_up, vectors, dy_sum, everyone,
        w_head, w_units, attn_input, up_sums, row_sums,
    )
    grad_inputs = plain_order(grad_inputs)
    if teams == 1:
        grad_gain, grad_shift, grad_out_b = vector[0:2], vector[2:4], vector[4]
        grad_qkv_b, grad_up_b = vector[5:8].reshape(-1), vector[8 : 8 + hidden // rows].reshape(-1)
    else:
        near = partial(lax.all_gather, axis_name="dp", axis_index_groups=together, tiled=True)

        def own(values):
            size = values.shape[0] // dp
            total = lax.psum(values, "dp", axis_index_groups=across)
            return lax.dynamic_slice_in_dim(total, place * size, size, 0)

        ends = lax.psum_scatter(
            vector[:4], "dp", scatter_dimension=1, axis_index_groups=across, tiled=True
        )
        grad_gain, grad_shift = ends[0:2], ends[2:4]
        grad_out_b = own(near(vector[4], axis=0))
        grad_qkv_b = own(near(vector[5:8].reshape(-1), axis=0))
        grad_up_b = own(near(vector[8 : 8 + hidden // rows].reshape(-1), axis=0))

        def scatter_rows(term):
            size = term.shape[0]
            full = jnp.zeros((TEAM, size, width), BF16)
            full = lax.dynamic_update_slice_in_dim(full, term.astype(BF16)[None], rank, 0)
            return lax.psum_scatter(
                full.reshape(TEAM * size, width), "dp", scatter_dimension=0, tiled=True
            ).astype(F32)

        columns = lax.psum_scatter(
            columns, "dp", scatter_dimension=1, axis_index_groups=across, tiled=True
        )
    grad_qkv_w, grad_up_w, grad_down_w, grad_out_w, result, grad_inputs = settle(
        columns, row_sums, result, grad_inputs
    )
    if teams > 1:
        grad_out_w, grad_down_w = scatter_rows(grad_out_w), scatter_rows(grad_down_w)
    return (
        result.reshape(inputs.shape),
        grad_inputs.reshape(inputs.shape),
        grad_gain,
        grad_shift,
        grad_qkv_w,
        grad_qkv_b,
        grad_out_w,
        grad_out_b,
        grad_up_w,
        grad_up_b,
        grad_down_w,
        grad_out_b,
    )


def solution(mesh):
    placed = (
        P("dp", "ctx", None),
        P("dp", "ctx"),
        P(None, "dp"),
        P(None, "dp"),
        P("dp", None),
        P("dp"),
        P("dp", None),
        P("dp"),
        P("dp", None),
        P("dp"),
        P("dp", None),
        P("dp"),
        P("dp", "ctx", None),
    )
    return jax.shard_map(
        partial(on_device, mesh.shape["dp"], mesh.shape["ctx"]),
        mesh=mesh,
        in_specs=placed,
        out_specs=(
            P("dp", "ctx", None),
            P("dp", "ctx", None),
            P(None, "dp"),
            P(None, "dp"),
            P("dp", None),
            P("dp"),
            P("dp", None),
            P("dp"),
            P("dp", None),
            P("dp"),
            P("dp", None),
            P("dp"),
        ),
        check_vma=False,
    )
```

```python
from functools import partial

import jax
import jax.numpy as jnp
from jax import lax
from jax.experimental import pallas as pl
from jax.experimental.pallas import tpu as pltpu
from jax.sharding import PartitionSpec as P

HEADS = 8
HEAD = 256
ROT = 64
EPSILON = 1e-05
MASKED = -1e30
F32 = jnp.float32
BF16 = jnp.bfloat16
MESH = pl.DeviceIdType.MESH
TEAM = HEADS
PAIRS = TEAM // 2
QUARTERS = 4
RIGHT, LEFT = 0, 1
VECTOR_ROWS = 24


def dot(left, right):
    return jnp.dot(left, right, preferred_element_type=F32)


def contract_last(left, right):
    return lax.dot_general(left, right, (((1,), (1,)), ((), ())), preferred_element_type=F32)


def contract_first(left, right):
    return lax.dot_general(left, right, (((0,), (0,)), ((), ())), preferred_element_type=F32)


def rotary_tables(positions):
    half = ROT // 2
    exponent = jnp.arange(0, ROT, 2).astype(F32) / ROT
    frequency = 10000.0 ** (-exponent)
    angles = positions[:, None] * frequency[None, :]
    rows = positions.shape[0]
    cosine, sine = jnp.cos(angles), jnp.sin(angles)
    one, nought = jnp.ones((rows, 64), F32), jnp.zeros((rows, 64), F32)
    blank = jnp.zeros((rows, half), F32)
    return (
        jnp.concatenate([cosine, cosine, one], -1),
        jnp.concatenate([-sine, blank, nought], -1),
        jnp.concatenate([blank, sine, nought], -1),
    )


def spot():
    place = lax.axis_index("dp")
    rank = lax.rem(place, TEAM)
    return place - rank, lax.div(rank, 2), lax.rem(rank, 2), lax.axis_index("ctx")


def near_first(line):
    second = 1 + lax.rem(line, 2)
    last = 3 * (1 - lax.div(line, 2))
    return (line, second, 6 - line - second - last, last)


def core_peer(quarter):
    return quarter + 1 - 2 * lax.rem(quarter, 2)


def chip_peer(quarter):
    return quarter + 2 - 4 * lax.div(quarter, 2)


def send(src, dst, send_sem, recv_sem, place, quarter):
    return pltpu.make_async_remote_copy(
        src_ref=src, dst_ref=dst, send_sem=send_sem, recv_sem=recv_sem,
        device_id=(place, quarter), device_id_type=MESH,
    )


def greet_line(base, line, side, quarter):
    barrier = pltpu.get_barrier_semaphore()

    def hail(place, quarter):
        pl.semaphore_signal(barrier, inc=1, device_id=(place, quarter), device_id_type=MESH)

    rank = line * 2 + side
    hail(base + line * 2 + 1 - side, quarter)

    pl.when(line < PAIRS - 1)(lambda: hail(base + rank + 2, quarter))
    pl.when(line > 0)(lambda: hail(base + rank - 2, quarter))
    for step in range(1, QUARTERS):
        hail(base + rank, lax.rem(quarter + step, QUARTERS))
    neighbours = 1 + lax.div(line + 2, 3) - lax.div(line, 3)
    pl.semaphore_wait(barrier, neighbours + QUARTERS)


def greet_team(base, line, side, quarter):
    barrier = pltpu.get_barrier_semaphore()
    rank = line * 2 + side
    for step in range(1, TEAM):
        pl.semaphore_signal(
            barrier, inc=1, device_id=(base + lax.rem(rank + step, TEAM), quarter),
            device_id_type=MESH,
        )
    for step in range(1, QUARTERS):
        pl.semaphore_signal(
            barrier, inc=1, device_id=(base + rank, lax.rem(quarter + step, QUARTERS)),
            device_id_type=MESH,
        )
    pl.semaphore_wait(barrier, TEAM + QUARTERS - 2)


class Relay:
    def __init__(self, held, line_send, line_recv, side_send, side_recv, half_send, half_recv):
        self.held = held
        self.sems = line_send, line_recv, side_send, side_recv, half_send, half_recv
        self.base, self.line, self.side, self.quarter = spot()
        self.half = held.shape[1] * 3 // 8

    def neighbour(self, way):
        return self.base + self.line * 2 + self.side + (2 if way == RIGHT else -2)

    def along(self, source, way):
        block = self.held.at[source * 2 + self.side]
        return send(
            block, block, self.sems[0].at[way, source], self.sems[1].at[source],
            self.neighbour(way), self.quarter,
        )

    def along_half(self, way):
        source = 0 if way == RIGHT else PAIRS - 1
        block = self.held.at[source * 2 + 1 - self.side, pl.ds(0, self.half)]
        return send(
            block, block, self.sems[4].at[way], self.sems[5].at[way], self.neighbour(way),
            self.quarter,
        )

    def over(self, source, side, low):
        block = self.held.at[source * 2 + side]
        if low:
            block = self.held.at[source * 2 + side, pl.ds(self.half, self.held.shape[1] - self.half)]
        place = self.base + self.line * 2 + 1 - self.side
        return send(
            block, block, self.sems[2].at[source], self.sems[3].at[source], place, self.quarter
        )

    def crossing(self, source, side, act):
        parted = (source != self.line) & (lax.rem(source, PAIRS - 1) == 0)
        pl.when(parted)(lambda: act(self.over(source, side, True)))
        pl.when(jnp.logical_not(parted))(lambda: act(self.over(source, side, False)))

    def each(self, step, act):
        line = self.line
        if step == 0:
            pl.when(line < PAIRS - 1)(lambda: act(line, RIGHT))
            pl.when(line > 0)(lambda: act(line, LEFT))
            act(line, None)
            return

        @pl.when(line >= step)
        def _():
            source = line - step
            act(source, "arrive")
            pl.when(line < PAIRS - 1)(lambda: act(source, RIGHT))
            act(source, None)

        @pl.when(line + step < PAIRS)
        def _():
            source = line + step
            act(source, "arrive")
            pl.when(line > 0)(lambda: act(source, LEFT))
            act(source, None)

    def start(self, step):
        def act(source, way):
            if way == "arrive":
                self.along(source, RIGHT).wait_recv()
            elif way is None:
                self.crossing(source, self.side, lambda copy: copy.start())
            else:
                self.along(source, way).start()

        self.each(step, act)

    def start_halves(self):
        for end, way in ((0, RIGHT), (PAIRS - 1, LEFT)):

            @pl.when(self.line == end)
            def _(end=end, way=way):
                self.over(self.line, 1 - self.side, False).wait_recv()
                self.along_half(way).start()

    def pass_halves(self, step):
        for end, way in ((0, RIGHT), (PAIRS - 1, LEFT)):
            here = step if way == RIGHT else PAIRS - 1 - step

            @pl.when(self.line == here)
            def _(way=way):
                self.along_half(way).wait_recv()
                if step < PAIRS - 1:
                    self.along_half(way).start()

    def wait_over(self, step, source):
        def take(copy):
            copy.wait_recv()

        if step == 0:
            inner = (self.line > 0) & (self.line < PAIRS - 1)
            pl.when(inner)(lambda: take(self.over(source, 1 - self.side, False)))
        else:
            self.crossing(source, 1 - self.side, take)

    def finish(self):
        def act(source, way):
            if way is None:
                self.crossing(source, self.side, lambda copy: copy.wait_send())
            elif way != "arrive":
                self.along(source, way).wait_send()

        for step in range(PAIRS):
            self.each(step, act)
        pl.when(self.line < PAIRS - 1)(lambda: self.along_half(RIGHT).wait_send())
        pl.when(self.line > 0)(lambda: self.along_half(LEFT).wait_send())


RELAY_SEMS = [
    pltpu.SemaphoreType.DMA((2, PAIRS)),
    pltpu.SemaphoreType.DMA((PAIRS,)),
    pltpu.SemaphoreType.DMA((PAIRS,)),
    pltpu.SemaphoreType.DMA((PAIRS,)),
    pltpu.SemaphoreType.DMA((2,)),
    pltpu.SemaphoreType.DMA((2,)),
]


def normalize(rows):
    average = jnp.mean(rows, -1, keepdims=True)
    centred = rows - average
    variance = jnp.mean(centred * centred, -1, keepdims=True)
    inverse = lax.rsqrt(variance + EPSILON)
    return centred * inverse, inverse


def rotate_low(low, cosine, above, below):
    half = ROT // 2
    return (
        low * cosine + pltpu.roll(low, 128 - half, 1) * above + pltpu.roll(low, half, 1) * below
    )


def unrotate_low(low, cosine, above, below):
    half = ROT // 2
    return (
        low * cosine + pltpu.roll(low * below, 128 - half, 1) + pltpu.roll(low * above, half, 1)
    )


def reader(sequence):
    return 2 * lax.rem(sequence, 2) + lax.rem(lax.div(sequence, 2), 2)


def reader_slot(sequence):
    return lax.div(sequence, QUARTERS)


def among(quarter):
    return 2 * lax.rem(quarter, 2) + lax.div(quarter, 2)


class Spread:
    def __init__(self, pieces, send_sem, recv_sem, own_sem):
        self.pieces, self.sems = pieces, (send_sem, recv_sem, own_sem)
        base, line, side, self.quarter = spot()
        self.place = base + line * 2 + side

    def _remote(self, index, sequence, slot, to, origin):
        src, dst = self.pieces[index]
        send_sem, recv_sem, _ = self.sems
        return send(
            src(sequence), dst(slot, origin), send_sem.at[index, sequence],
            recv_sem.at[index, origin, slot], self.place, to,
        )

    def _own(self, index, sequence):
        src, dst = self.pieces[index]
        slot = reader_slot(sequence)
        return pltpu.make_async_copy(
            src(sequence), dst(slot, self.quarter), self.sems[2].at[index, slot]
        )

    def each(self, sequence, own, other):
        to, slot = reader(sequence), reader_slot(sequence)

        @pl.when(to == self.quarter)
        def _():
            for index in range(len(self.pieces)):
                own(self._own(index, sequence))

        @pl.when(to != self.quarter)
        def _():
            for index in range(len(self.pieces)):
                other(self._remote(index, sequence, slot, to, self.quarter))

    def start(self, sequence):
        self.each(sequence, lambda copy: copy.start(), lambda copy: copy.start())

    def finish(self):
        def sent(sequence, _):
            self.each(sequence, lambda copy: copy.wait(), lambda copy: copy.wait_send())

        lax.fori_loop(0, TEAM, sent, None)

        def landed(step, _):
            origin = lax.rem(self.quarter + 1 + lax.div(step, 2), QUARTERS)
            slot = lax.rem(step, 2)
            for index in range(len(self.pieces)):
                self._remote(index, 0, slot, origin, origin).wait_recv()

        lax.fori_loop(0, 2 * (QUARTERS - 1), landed, None)


def spread_sems(count):
    return [
        pltpu.SemaphoreType.DMA((count, TEAM)),
        pltpu.SemaphoreType.DMA((count, QUARTERS, 2)),
        pltpu.SemaphoreType.DMA((count, 2)),
    ]


class Columns:
    def __init__(self, pieces, place, lane, lanes, sems):
        self.pieces, self.place, self.lane, self.lanes, self.sems = pieces, place, lane, lanes, sems
        self.base, line, side, self.quarter = spot()
        self.rank = line * 2 + side

    def deal(self, source, target, peer):
        sends, recvs = self.sems[:2]
        return [
            send(
                src, self.place(source, self.quarter, lane, lanes),
                sends.at[index, target], recvs.at[index, source], self.base + peer, self.quarter,
            )
            for index, (src, lane, lanes) in enumerate(self.pieces(target))
        ]

    def own(self):
        return [
            pltpu.make_async_copy(
                src, self.place(self.rank, self.quarter, lane, lanes), self.sems[2].at[index]
            )
            for index, (src, lane, lanes) in enumerate(self.pieces(self.rank))
        ]

    def start(self):
        for copy in self.own():
            copy.start()

        def one(step, _):
            target = lax.rem(self.rank + step, TEAM)
            for copy in self.deal(self.rank, target, target):
                copy.start()

        lax.fori_loop(1, TEAM, one, None)

    def pass_on(self, which, source, slice_of, to):
        block = self.place(source, slice_of, self.lane, self.lanes)
        sends, recvs = self.sems[3 + 2 * which : 5 + 2 * which]
        return send(
            block, block, sends.at[source], recvs.at[source], self.base + self.rank, to
        )

    def to_core(self, source):
        return self.pass_on(0, source, self.quarter, core_peer(self.quarter))

    def to_chip(self, source):
        return self.pass_on(1, source, self.quarter, chip_peer(self.quarter))

    def to_last(self, source):
        return self.pass_on(2, source, chip_peer(self.quarter), core_peer(self.quarter))

    def forward(self):
        for copy in self.own():
            copy.wait()
        self.to_chip(self.rank).start()
        self.to_core(self.rank).start()

        def one(step, _):
            source = lax.rem(self.rank + TEAM - step, TEAM)
            for copy in self.deal(source, self.rank, source):
                copy.wait_recv()
            self.to_chip(source).start()
            self.to_core(source).start()

        lax.fori_loop(1, TEAM, one, None)

    def forward_last(self):
        chip = chip_peer(self.quarter)

        def one(step, _):
            source = lax.rem(self.rank + TEAM - step, TEAM)
            self.pass_on(1, source, chip, chip).wait_recv()
            self.to_last(source).start()

        lax.fori_loop(0, TEAM, one, None)

    def arrive(self):
        core = core_peer(self.quarter)

        def one(source, _):
            self.pass_on(0, source, core, core).wait_recv()
            self.pass_on(2, source, chip_peer(core), core).wait_recv()

        lax.fori_loop(0, TEAM, one, None)

    def finish(self):
        def one(source, _):
            self.to_core(source).wait_send()
            self.to_chip(source).wait_send()
            self.to_last(source).wait_send()

        lax.fori_loop(0, TEAM, one, None)

        def sent(step, _):
            target = lax.rem(self.rank + step, TEAM)
            for copy in self.deal(self.rank, target, target):
                copy.wait_send()

        lax.fori_loop(1, TEAM, sent, None)


def column_sems(count):
    dma = pltpu.SemaphoreType.DMA
    return [dma((count, TEAM))] * 2 + [dma((count,))] + [dma((TEAM,))] * 6


def same_document(query_marks, key_marks):
    def one_hot(marks):
        number = lax.broadcasted_iota(jnp.int32, marks.shape, 0).astype(F32)
        return jnp.where(marks == number, 1.0, 0.0).astype(BF16)

    return contract_first(one_hot(query_marks), one_hot(key_marks)) > 0.5


def probabilities(block, size, q_ref, k_ref, marks_ref):
    start = block * size
    rows, keys = pl.ds(start, size), pl.ds(0, start + size)
    scores = contract_last(q_ref[rows, :], k_ref[keys, :]) * HEAD ** (-0.5)
    shape = scores.shape
    query_pos = start + lax.broadcasted_iota(jnp.int32, shape, 0)
    key_pos = lax.broadcasted_iota(jnp.int32, shape, 1)
    key_marks = jnp.concatenate([marks_ref[index] for index in range(block + 1)], -1)
    allowed = (query_pos >= key_pos) & same_document(marks_ref[block], key_marks)
    scores = jnp.where(allowed, scores, MASKED)
    expanded = jnp.exp(scores - jnp.max(scores, -1, keepdims=True))
    return expanded / jnp.sum(expanded, -1, keepdims=True)


def gelu_terms(values):
    chance = 0.5 * (1.0 + lax.erf(values * (0.5**0.5)))
    density = jnp.exp(-0.5 * values * values) * 0.3989422804014327
    return values * chance, chance + values * density


ANY = pl.BlockSpec(memory_space=pl.ANY)
VMEM = pl.BlockSpec(memory_space=pltpu.VMEM)
DMA = pltpu.SemaphoreType.DMA
LIMIT = 60 << 20


def gather_kernel(
    x_ref, dy_ref, vec_ref, wo_ref, wd_ref, upb_ref, cos_ref, above_ref, below_ref, wq_ref, wu_ref,
    x_out, ha_out, hm_out, wq_out, wu_out, qkv_out, marks_out, vec_out,
    dy_out, a_out, du_out, do_out, o_out, sum_out,
    xs, dys, hm, head, units, vecs, vectors, ha, qkv, whole, marks, mixed, act, grad, attended,
    table, own_sem, x_store, ha_store, du_store, dy_store, late_store, v_send, v_recv, back_send, back_recv,
    *sems,
):
    base, line, side, quarter = spot()
    rank = line * 2 + side
    tokens, width = x_ref.shape
    hidden = act.shape[-1]
    rows = wq_ref.shape[0]
    part = rows // QUARTERS
    take = iter(range(0, len(sems)))

    def some(count):
        return [sems[next(take)] for _ in range(count)]

    relay_x, relay_dy = Relay(xs, *some(6)), Relay(dys, *some(6))
    head_columns, unit_columns = some(9), some(9)
    spread_x = Spread(
        [
            (
                lambda s: qkv.at[s],
                lambda j, origin: whole.at[j, :, pl.ds(origin * tokens, tokens), :],
            ),
            (lambda s: vecs.at[s, pl.ds(16, 8), :], lambda j, origin: marks.at[j, origin]),
        ],
        *some(3),
    )
    spread_do = Spread(
        [
            (
                lambda s: attended.at[s],
                lambda j, origin: do_out.at[j, pl.ds(origin * tokens, tokens), :],
            )
        ],
        *some(3),
    )
    mine = pl.ds(pl.multiple_of(quarter * part, 16), part)

    def landing(weight):
        def place(source, slice_of, lane, lanes):
            band = pl.ds(pl.multiple_of(source * rows + slice_of * part, 16), part)
            return weight.at[band, pl.ds(lane, lanes)]

        return place

    head_columns = Columns(
        lambda target: [
            (
                wq_ref.at[mine, pl.ds(pl.multiple_of(kind * width + target * HEAD, HEAD), HEAD)],
                kind * HEAD,
                HEAD,
            )
            for kind in range(3)
        ],
        landing(head), 0, 3 * HEAD, head_columns,
    )
    unit_columns = Columns(
        lambda target: [
            (wu_ref.at[mine, pl.ds(pl.multiple_of(target * hidden, hidden), hidden)], 0, hidden)
        ],
        landing(units), 0, hidden, unit_columns,
    )
    own_rows = pl.ds(pl.multiple_of(quarter * tokens, tokens), tokens)
    greet_team(base, line, side, quarter)

    def vector_copy(source, target, peer):
        return send(
            vec_ref, vecs.at[source], v_send.at[target], v_recv.at[source], base + peer, quarter
        )

    owns = [
        pltpu.make_async_copy(src, dst, own_sem.at[index])
        for index, (src, dst) in enumerate(
            (
                (x_ref, xs.at[rank]),
                (vec_ref, vecs.at[rank]),
                (dy_ref, dys.at[rank]),
                (cos_ref.at[own_rows, :], table.at[0]),
                (above_ref.at[own_rows, :], table.at[1]),
                (below_ref.at[own_rows, :], table.at[2]),
            )
        )
    ]
    for copy in owns:
        copy.start()

    def send_vector(step, _):
        target = lax.rem(rank + step, TEAM)
        vector_copy(rank, target, target).start()

    lax.fori_loop(1, TEAM, send_vector, None)
    head_columns.start()
    for copy in owns:
        copy.wait()
    relay_x.start(0)
    head_columns.forward()
    relay_x.start_halves()
    relay_x.start(1)
    head_columns.forward_last()

    def take_vector(step, _):
        origin = lax.rem(rank + TEAM - step, TEAM)
        vector_copy(origin, rank, origin).wait_recv()

    lax.fori_loop(1, TEAM, take_vector, None)
    for source in range(TEAM):
        for row in range(4):
            vectors[pl.ds(row, 1), pl.ds(source * rows, rows)] = vecs[source, pl.ds(row, 1), :]
    head_columns.arrive()
    late = [
        pltpu.make_async_copy(src, dst, late_store.at[index])
        for index, (src, dst) in enumerate(
            ((head, wq_out), (vecs, vec_out), (units, wu_out), (whole, qkv_out), (marks, marks_out))
        )
    ]
    late[0].start()
    late[1].start()

    strip = 128
    order = near_first(line)

    def member(step, other):
        return order[step] * 2 + side + other * (1 - 2 * side)

    def store_x(which):
        return [
            pltpu.make_async_copy(xs.at[which], x_out.at[which], x_store.at[0, which]),
            pltpu.make_async_copy(hm.at[which], hm_out.at[which], x_store.at[1, which]),
        ]

    def store_ha(slot, which):
        return pltpu.make_async_copy(ha.at[slot], ha_out.at[which], ha_store.at[slot])

    def project(slot, which):
        def norm(index, _):
            chunk = pl.ds(pl.multiple_of(index * strip, strip), strip)
            unit, _ = normalize(xs[which, chunk, :].astype(F32))
            ha[slot, chunk, :] = (unit * vectors[0:1, :] + vectors[2:3, :]).astype(BF16)
            hm[which, chunk, :] = (unit * vectors[1:2, :] + vectors[3:4, :]).astype(BF16)

        lax.fori_loop(0, tokens // strip, norm, None)
        for kind in range(3):
            chunk = kind * TEAM + rank
            bias = vecs[lax.div(chunk, 3), pl.ds(8 + lax.rem(chunk, 3), 1), :]
            made = dot(ha[slot], head[:, pl.ds(kind * HEAD, HEAD)]) + bias
            if kind < 2:
                low = rotate_low(made[:, :128], table[0], table[1], table[2])
                qkv[which, kind, :, pl.ds(0, 128)] = low.astype(BF16)
                qkv[which, kind, :, pl.ds(128, HEAD - 128)] = made[:, 128:].astype(BF16)
            else:
                qkv[which, kind] = made.astype(BF16)
        spread_x.start(which)
        store_ha(slot, which).start()
        for copy in store_x(which):
            copy.start()

    for step, place in enumerate(order):

        def one(other, _, step=step, place=place):
            @pl.when(other == 1)
            def _():
                if 0 < step < PAIRS - 1:
                    relay_x.start(step + 1)
                if step > 0:
                    relay_x.pass_halves(step)
                if step == 2:
                    unit_columns.start()
                    relay_dy.start(0)
                relay_x.wait_over(step, place)

            if step > 0:
                store_ha(other, member(step - 1, other)).wait()
            project(other, member(step, other))

        lax.fori_loop(0, 2, one, None)

    unit_columns.forward()
    sum_out[...] = jnp.zeros_like(sum_out)
    relay_dy.start_halves()
    relay_dy.start(1)
    unit_columns.forward_last()
    spread_x.finish()
    late[3].start()
    late[4].start()

    def attend(sequence, _):
        q, k, v = (whole.at[sequence, kind] for kind in range(3))
        for block in range(QUARTERS):
            probs = probabilities(block, tokens, q, k, marks.at[sequence])
            value_block = v[pl.ds(0, (block + 1) * tokens), :]
            mixed[sequence, pl.ds(block * tokens, tokens), :] = dot(
                probs.astype(BF16), value_block
            ).astype(BF16)

    lax.fori_loop(0, 2, attend, None)

    def back(to, origin):
        return send(
            mixed.at[:, pl.ds(to * tokens, tokens), :], o_out.at[:, among(origin)],
            back_send.at[to], back_recv.at[origin], base + rank, to,
        )

    own_back = pltpu.make_async_copy(
        mixed.at[:, pl.ds(quarter * tokens, tokens), :], o_out.at[:, among(quarter)],
        own_sem.at[6],
    )
    own_back.start()
    for step in range(1, QUARTERS):
        to = lax.rem(quarter + step, QUARTERS)
        back(to, quarter).start()
    unit_columns.arrive()
    late[2].start()

    def store_dy(which):
        return pltpu.make_async_copy(dys.at[which], dy_out.at[which], dy_store.at[which])

    def store_du(slot, which):
        return [
            pltpu.make_async_copy(act.at[slot], a_out.at[which], du_store.at[0, slot]),
            pltpu.make_async_copy(grad.at[slot], du_out.at[which], du_store.at[1, slot]),
        ]

    def pull(slot, which):
        attended[which] = contract_last(dys[which], wo_ref[...]).astype(BF16)
        spread_do.start(which)
        for start in range(0, hidden, 256):
            span = pl.ds(start, 256)
            up = dot(hm[which], units[:, span]) + upb_ref[:, span]
            value, slope = gelu_terms(up)
            act[slot, :, span] = value.astype(BF16)
            pulled = contract_last(dys[which], wd_ref[span, :])
            grad[slot, :, span] = (pulled * slope).astype(BF16)
        for copy in store_du(slot, which):
            copy.start()
        store_dy(which).start()
        sum_out[0:1, :] += jnp.sum(dys[which].astype(F32), 0, keepdims=True)

    for step, place in enumerate(order):

        def one(other, _, step=step, place=place):
            @pl.when(other == 1)
            def _():
                if 0 < step < PAIRS - 1:
                    relay_dy.start(step + 1)
                if step > 0:
                    relay_dy.pass_halves(step)
                relay_dy.wait_over(step, place)

            if step > 0:
                for copy in store_du(other, member(step - 1, other)):
                    copy.wait()
            pull(other, member(step, other))

        lax.fori_loop(0, 2, one, None)

    relay_x.finish()
    relay_dy.finish()
    spread_do.finish()
    head_columns.finish()
    unit_columns.finish()
    for step in range(1, QUARTERS):
        other = lax.rem(quarter + step, QUARTERS)
        back(other, quarter).wait_send()
        back(other, other).wait_recv()
    own_back.wait()

    def sent(step, _):
        target = lax.rem(rank + step, TEAM)
        vector_copy(rank, target, target).wait_send()

    lax.fori_loop(1, TEAM, sent, None)

    def stored(which, _):
        for copy in store_x(which):
            copy.wait()
        store_dy(which).wait()

    lax.fori_loop(0, TEAM, stored, None)
    for other in range(2):
        store_ha(other, member(PAIRS - 1, other)).wait()
        for copy in store_du(other, member(PAIRS - 1, other)):
            copy.wait()
    for copy in late:
        copy.wait()


def gather(x, dy, vec, w_out, w_down, up_bias, tables, w_qkv, w_up):
    tokens, width = x.shape
    hidden = up_bias.shape[-1]
    all_tokens = (TEAM, tokens, width)
    whole = (2, 3, QUARTERS * tokens, HEAD)
    marks = ((2, QUARTERS, 8, tokens), F32)
    vecs = ((TEAM, VECTOR_ROWS, vec.shape[-1]), F32)
    units = ((TEAM, tokens, hidden), BF16)
    shapes = [
        (all_tokens, BF16),
        (all_tokens, BF16),
        (all_tokens, BF16),
        ((width, 3 * HEAD), BF16),
        ((width, hidden), BF16),
        (whole, BF16),
        marks,
        vecs,
        (all_tokens, BF16),
        units,
        units,
        ((2, QUARTERS * tokens, HEAD), BF16),
        ((2, QUARTERS, tokens, HEAD), BF16),
        ((8, width), F32),
    ]
    return pl.pallas_call(
        gather_kernel,
        out_shape=[jax.ShapeDtypeStruct(*shape) for shape in shapes],
        in_specs=[ANY] * 2 + [VMEM] * 4 + [ANY] * 5,
        out_specs=[ANY] * 13 + [VMEM],
        scratch_shapes=[
            pltpu.VMEM(all_tokens, BF16),
            pltpu.VMEM(all_tokens, BF16),
            pltpu.VMEM(all_tokens, BF16),
            pltpu.VMEM((width, 3 * HEAD), BF16),
            pltpu.VMEM((width, hidden), BF16),
            pltpu.VMEM(*vecs),
            pltpu.VMEM((8, width), F32),
            pltpu.VMEM((2, tokens, width), BF16),
            pltpu.VMEM((TEAM, 3, tokens, HEAD), BF16),
            pltpu.VMEM(whole, BF16),
            pltpu.VMEM(*marks),
            pltpu.VMEM((2, QUARTERS * tokens, HEAD), BF16),
            pltpu.VMEM((2, tokens, hidden), BF16),
            pltpu.VMEM((2, tokens, hidden), BF16),
            pltpu.VMEM((TEAM, tokens, HEAD), BF16),
            pltpu.VMEM((3, tokens, 128), F32),
            DMA((7,)),
            DMA((2, TEAM)),
            DMA((2,)),
            DMA((2, 2)),
            DMA((TEAM,)),
            DMA((5,)),
            DMA((TEAM,)),
            DMA((TEAM,)),
            DMA((QUARTERS,)),
            DMA((QUARTERS,)),
        ]
        + RELAY_SEMS * 2
        + column_sems(3)
        + column_sems(1)
        + spread_sems(2)
        + spread_sems(1),
        compiler_params=pltpu.CompilerParams(
            collective_id=0, has_side_effects=True, vmem_limit_bytes=LIMIT
        ),
        name="gather",
    )(x, dy, vec, w_out, w_down, up_bias, *tables, w_qkv, w_up)


def backward_kernel(
    qkv_ref, do_ref, marks_ref, cos_ref, above_ref, below_ref, d_ref, dk_sum, dv_sum
):
    scale = HEAD ** (-0.5)
    q_ref, k_ref, v_ref = (qkv_ref.at[kind] for kind in range(3))
    length = q_ref.shape[0]
    size = marks_ref.shape[-1]

    def put(kind, rows, grads):
        low = unrotate_low(
            grads[:, :128], cos_ref[rows, :], above_ref[rows, :], below_ref[rows, :]
        )
        d_ref[kind, rows, pl.ds(0, 128)] = low.astype(BF16)
        d_ref[kind, rows, pl.ds(128, HEAD - 128)] = grads[:, 128:].astype(BF16)

    dk_sum[...] = jnp.zeros_like(dk_sum)
    dv_sum[...] = jnp.zeros_like(dv_sum)
    for block in range(length // size):
        start = block * size
        rows, keys = pl.ds(start, size), pl.ds(0, start + size)
        probs = probabilities(block, size, q_ref, k_ref, marks_ref)
        grads = do_ref[rows, :]
        grad_probs = contract_last(grads, v_ref[keys, :])
        row_dot = jnp.sum(probs * grad_probs, -1, keepdims=True)
        grad_scores = (probs * (grad_probs - row_dot)).astype(BF16)
        put(0, rows, dot(grad_scores, k_ref[keys, :]) * scale)
        dk_sum[keys, :] += contract_first(grad_scores, q_ref[rows, :])
        dv_sum[keys, :] += contract_first(probs.astype(BF16), grads)
    put(1, pl.ds(0, length), dk_sum[...] * scale)
    d_ref[2] = dv_sum[...].astype(BF16)


def attend_back(qkv, grads, marks, tables):
    seqs, _, length, head = qkv.shape
    three = pl.BlockSpec((None, 3, length, HEAD), lambda s: (s, 0, 0, 0))
    one = pl.BlockSpec((None, length, HEAD), lambda s: (s, 0, 0))
    table = pl.BlockSpec((length, 128), lambda s: (0, 0))
    return pl.pallas_call(
        backward_kernel,
        grid=(seqs,),
        in_specs=[three, one, pl.BlockSpec((None, *marks.shape[1:]), lambda s: (s, 0, 0, 0))]
        + [table] * 3,
        out_specs=three,
        out_shape=jax.ShapeDtypeStruct(qkv.shape, BF16),
        scratch_shapes=[pltpu.VMEM((length, head), F32)] * 2,
        compiler_params=pltpu.CompilerParams(vmem_limit_bytes=48 << 20),
        name="attend_back",
    )(qkv, grads, marks, *tables)


class Reduce:
    def __init__(self, cut, own, side_out, side_in, line_in, half_in, sems):
        self.cut = cut
        self.own, self.side_out, self.side_in = own, side_out, side_in
        self.line_in, self.half_in, self.sems = line_in, half_in, sems
        self.base, self.line, self.side, self.quarter = spot()
        self.order = near_first(self.line)
        self.inner = (self.line > 0) & (self.line < PAIRS - 1)
        self.tokens = own.shape[1]

    def over(self, step, low):
        side_send, side_recv = self.sems[:2]
        place = self.base + self.line * 2 + 1 - self.side
        rows = pl.ds(self.cut, self.tokens - self.cut) if low else pl.ds(0, self.tokens)
        return send(
            self.side_out.at[step, rows], self.side_in.at[step, rows],
            side_send.at[step], side_recv.at[step], place, self.quarter,
        )

    def crossing(self, step, act):
        if step == PAIRS - 1:
            act(self.over(step, True))
        elif step == 1:
            act(self.over(step, False))
        else:
            first, second = (True, False) if step == PAIRS - 2 else (False, True)
            pl.when(self.inner)(lambda: act(self.over(step, first)))
            pl.when(jnp.logical_not(self.inner))(lambda: act(self.over(step, second)))

    def along(self, step, target, way):
        line_send, line_recv = self.sems[2:4]
        move = 1 if way == RIGHT else -1
        slot = target if way == RIGHT else jnp.where(target == self.line - 1, PAIRS, target)
        place = self.base + (self.line + move) * 2 + self.side
        return send(
            self.side_out.at[step], self.line_in.at[slot], line_send.at[step], line_recv.at[slot],
            place, self.quarter,
        )

    def arrive(self, slot):
        line_send, line_recv = self.sems[2:4]
        return send(
            self.side_out.at[0], self.line_in.at[slot], line_send.at[0], line_recv.at[slot],
            self.base + self.line * 2 + 1 - self.side, self.quarter,
        )

    def upper(self, step, way):
        half_send, half_recv = self.sems[4:6]
        move = 1 if way == RIGHT else -1
        rows = pl.ds(0, self.cut)
        place = self.base + (self.line + move) * 2 + self.side
        return send(
            self.side_out.at[step, rows], self.half_in.at[way], half_send.at[way],
            half_recv.at[way], place, self.quarter,
        )

    def upper_over(self):
        cross_send, cross_recv = self.sems[6:8]
        rows = pl.ds(0, self.cut)
        place = self.base + self.line * 2 + 1 - self.side
        return send(
            self.side_out.at[0, rows], self.side_in.at[0, rows], cross_send, cross_recv, place,
            self.quarter,
        )

    def begin(self, step):
        self.crossing(step, lambda copy: copy.start())

    def launch(self):
        pl.when(self.line == 0)(lambda: self.upper(PAIRS - 1, RIGHT).start())
        pl.when(self.line == PAIRS - 1)(lambda: self.upper(PAIRS - 1, LEFT).start())

    def hop(self, count):
        for way in (RIGHT, LEFT):
            here = count if way == RIGHT else PAIRS - 1 - count
            step = (None, PAIRS - 1, PAIRS - 2, 0)[count]

            @pl.when(self.line == here)
            def _(way=way, step=step):
                self.upper(step, way).wait_recv()
                rows = pl.ds(0, self.cut)
                total = self.side_out[step, rows].astype(F32) + self.half_in[way].astype(F32)
                self.side_out[step, rows] = total.astype(BF16)
                if count < PAIRS - 1:
                    self.upper(step, way).start()
                else:
                    self.upper_over().start()

    def upper_sent(self, step):
        first, second = (RIGHT, LEFT) if step == PAIRS - 1 else (LEFT, RIGHT)
        low_line = self.line < PAIRS // 2

        def wait():
            pl.when(low_line)(lambda: self.upper(step, first).wait_send())
            pl.when(jnp.logical_not(low_line))(lambda: self.upper(step, second).wait_send())

        if step == PAIRS - 1:
            wait()
        elif step == PAIRS - 2:
            pl.when(self.inner)(wait)

    def mine(self, step, index, strip):
        chunk = pl.ds(pl.multiple_of(index * strip, strip), strip)
        slot = step if self.own.shape[0] > 1 else 0
        own = self.own[slot, chunk, :].astype(F32)
        other = self.side_in[step, chunk, :].astype(F32)
        if step == PAIRS - 1:
            return jnp.where(index * strip >= self.cut, own + other, own)
        if step == PAIRS - 2:
            whole = (index * strip >= self.cut) | jnp.logical_not(self.inner)
            return jnp.where(whole, own + other, own)
        return own + other

    def advance(self, step):
        target = self.order[step]
        self.crossing(step, lambda copy: copy.wait_recv())
        self.crossing(step, lambda copy: copy.wait_send())
        self.upper_sent(step)

        def forward(way, upstream):
            pl.when(upstream)(lambda: self.arrive(target).wait_recv())
            strip = 64

            def add(index, _):
                chunk = pl.ds(pl.multiple_of(index * strip, strip), strip)
                total = self.mine(step, index, strip)
                passing = self.line_in[target, chunk, :].astype(F32)
                total = jnp.where(upstream, total + passing, total)
                self.side_out[step, chunk, :] = total.astype(BF16)

            lax.fori_loop(0, self.tokens // strip, add, None)
            self.along(step, target, way).start()

        pl.when(target > self.line)(lambda: forward(RIGHT, self.line > 0))
        pl.when(target < self.line)(lambda: forward(LEFT, self.line < PAIRS - 1))

    def last(self):
        self.crossing(0, lambda copy: copy.wait_recv())
        self.crossing(0, lambda copy: copy.wait_send())

        @pl.when(jnp.logical_not(self.inner))
        def _():
            self.upper_over().wait_recv()
            self.upper_over().wait_send()

        pl.when(self.line > 0)(lambda: self.arrive(self.line).wait_recv())
        pl.when(self.line < PAIRS - 1)(lambda: self.arrive(PAIRS).wait_recv())

    def total(self, index, strip):
        chunk = pl.ds(pl.multiple_of(index * strip, strip), strip)
        total = self.mine(0, index, strip)
        left = self.line_in[self.line, chunk, :].astype(F32)
        right = self.line_in[PAIRS, chunk, :].astype(F32)
        total = jnp.where(self.line > 0, total + left, total)
        return jnp.where(self.line < PAIRS - 1, total + right, total)

    def finish(self):
        for step in range(1, PAIRS):
            target = self.order[step]
            pl.when(target > self.line)(lambda: self.along(step, target, RIGHT).wait_send())
            pl.when(target < self.line)(lambda: self.along(step, target, LEFT).wait_send())


REDUCE = 13


def reduce_scratch(tokens, width, slots, dtype, cut):
    return [
        pltpu.VMEM((slots, tokens, width), dtype),
        pltpu.VMEM((PAIRS, tokens, width), BF16),
        pltpu.VMEM((PAIRS, tokens, width), BF16),
        pltpu.VMEM((PAIRS + 1, tokens, width), BF16),
        pltpu.VMEM((2, cut, width), BF16),
        DMA((PAIRS,)),
        DMA((PAIRS,)),
        DMA((PAIRS,)),
        DMA((PAIRS + 1,)),
        DMA((2,)),
        DMA((2,)),
        DMA,
        DMA,
    ]


class Quarters:
    def __init__(self, keep, away, came, far, core_send, core_recv, chip_send, chip_recv):
        self.keep, self.away, self.came, self.far = keep, away, came, far
        self.sems = core_send, core_recv, chip_send, chip_recv
        base, line, side, self.quarter = spot()
        self.place = base + line * 2 + side
        self.core, self.chip = lax.rem(self.quarter, 2), lax.div(self.quarter, 2)
        self.tiles = keep.shape[0]

    def to_core(self, tile):
        return send(
            self.away.at[tile], self.came.at[tile], self.sems[0].at[tile], self.sems[1].at[tile],
            self.place, core_peer(self.quarter),
        )

    def to_chip(self, tile):
        return send(
            self.away.at[tile, 0], self.far.at[tile], self.sems[2].at[tile], self.sems[3].at[tile],
            self.place, chip_peer(self.quarter),
        )

    def put(self, tile, quarter_of):
        for chip in range(2):
            self.keep[tile, chip] = quarter_of(2 * chip + self.core).astype(BF16)
            self.away[tile, chip] = quarter_of(2 * chip + 1 - self.core).astype(BF16)
        self.to_core(tile).start()

    def over_cores(self):
        def one(tile, _):
            self.to_core(tile).wait_recv()
            self.to_core(tile).wait_send()
            other = 1 - self.chip
            passed = self.keep[tile, other].astype(F32) + self.came[tile, other].astype(F32)
            self.away[tile, 0] = passed.astype(BF16)
            self.to_chip(tile).start()
            kept = self.keep[tile, self.chip].astype(F32)
            kept = kept + self.came[tile, self.chip].astype(F32)
            self.keep[tile, self.chip] = kept.astype(BF16)

        lax.fori_loop(0, self.tiles, one, None)

    def over_chips(self, then):
        def one(tile, _):
            self.to_chip(tile).wait_recv()
            total = self.keep[tile, self.chip].astype(F32) + self.far[tile].astype(F32)
            self.keep[tile, self.chip] = total.astype(BF16)
            then(tile)

        lax.fori_loop(0, self.tiles, one, None)

    def total(self, tile):
        return self.keep.at[tile, self.chip]

    def finish(self):
        lax.fori_loop(0, self.tiles, lambda tile, _: self.to_chip(tile).wait_send(), None)


def quarters_scratch(tiles, rows, columns):
    return [
        pltpu.VMEM((tiles, 2, rows, columns), BF16),
        pltpu.VMEM((tiles, 2, rows, columns), BF16),
        pltpu.VMEM((tiles, 2, rows, columns), BF16),
        pltpu.VMEM((tiles, rows, columns), BF16),
    ] + [DMA((tiles,))] * 4


class Stream:
    def __init__(self, source, slots, sems):
        self.source, self.slots, self.sems = source, slots, sems

    def copy(self, tile):
        size = self.slots.shape[-1]
        start = pl.multiple_of(tile * size, size)
        slot = lax.rem(tile, 2)
        return pltpu.make_async_copy(
            self.source.at[:, pl.ds(start, size)], self.slots.at[slot], self.sems.at[slot]
        )

    def run(self, tiles, use):
        def one(tile, _):
            self.copy(tile).wait()
            use(tile, self.slots.at[lax.rem(tile, 2)])
            pl.when(tile + 2 < tiles)(lambda: self.copy(tile + 2).start())

        lax.fori_loop(0, tiles, one, None)


def third_kernel(
    x_ref, o_ref, a_ref, wo_ref, wd_ref, vec_ref, du_ref, d_ref, hm_ref, dy_ref,
    result_out, back_out, up_out, rows_out,
    own_sem, back_send, back_recv, load_sem, store_sem, hm_tiles, tile_sum, dy, bias, *rest,
):
    base, line, side, quarter = spot()
    rank = line * 2 + side
    tokens, width = x_ref.shape
    part = width // TEAM // QUARTERS
    reduce = Reduce(tokens // 2, *rest[:5], rest[5:REDUCE])
    rest = rest[REDUCE:]
    ups, downs = Quarters(*rest[:8]), Quarters(*rest[8:16])
    stream = Stream(hm_ref, hm_tiles, load_sem)
    load_dy = pltpu.make_async_copy(dy_ref, dy, own_sem.at[3])
    load_dy.start()
    for tile in range(2):
        stream.copy(tile).start()
    greet_line(base, line, side, quarter)

    def pieces(to, origin, kind):
        return (
            d_ref.at[:, kind, pl.ds(to * tokens, tokens), :],
            back_out.at[:, among(origin), :, pl.ds(kind * HEAD, HEAD)],
        )

    def back(to, origin, kind):
        src, dst = pieces(to, origin, kind)
        return send(
            src, dst, back_send.at[to, kind], back_recv.at[origin, kind], base + rank, to
        )

    own_back = [
        pltpu.make_async_copy(*pieces(quarter, quarter, kind), own_sem.at[kind])
        for kind in range(3)
    ]

    def make(which, put):
        rows = pl.ds(pl.multiple_of(which * tokens, tokens), tokens)
        for start in range(0, width, 512):
            span = pl.ds(start, 512)
            put(
                span,
                dot(o_ref[rows, :], wo_ref[:, span]) + dot(a_ref[rows, :], wd_ref[:, span]),
            )

    def put_own(span, value):
        reduce.own[0, :, span] = value.astype(BF16)

    for step in reversed(range(PAIRS)):

        def put_out(span, value, step=step):
            reduce.side_out[step, :, span] = value.astype(BF16)

        make(reduce.order[step] * 2 + 1 - side, put_out)
        reduce.begin(step)
        if step == PAIRS - 1:
            reduce.launch()
            for kind in range(3):
                own_back[kind].start()
                for hop in range(1, QUARTERS):
                    back(lax.rem(quarter + hop, QUARTERS), quarter, kind).start()

    def up_tile(tile, held):
        for start in range(0, tile_sum.shape[1], 512):
            span = pl.ds(start, 512)
            tile_sum[:, span] = contract_first(held[...], du_ref[:, span])
        ups.put(tile, lambda q: tile_sum[pl.ds(pl.multiple_of(q * part, part), part), :])

    stream.run(TEAM, up_tile)
    reduce.hop(1)
    ups.over_cores()
    make(reduce.order[3] * 2 + side, put_own)
    reduce.advance(3)
    reduce.hop(2)
    load_dy.wait()
    share = width // QUARTERS

    def down_tile(source, first, tile, _):
        columns = pl.ds(pl.multiple_of(tile * 128, 128), 128)
        rows = source[:, columns]

        def quarter_of(q):
            span = pl.ds(pl.multiple_of(q * share, share), share)
            return contract_first(rows, dy[:, span])

        downs.put(first + tile, quarter_of)

    hidden = a_ref.shape[1] // 128
    lax.fori_loop(0, hidden, partial(down_tile, a_ref, 0), None)
    lax.fori_loop(0, HEAD // 128, partial(down_tile, o_ref, hidden), None)
    make(reduce.order[2] * 2 + side, put_own)
    reduce.advance(2)
    reduce.hop(3)
    downs.over_cores()
    make(reduce.order[1] * 2 + side, put_own)
    reduce.advance(1)
    make(rank, put_own)

    def store_up(tile):
        return pltpu.make_async_copy(ups.total(tile), up_out.at[tile], store_sem.at[0])

    def store_down(tile):
        rows = pl.ds(pl.multiple_of(tile * 128, 128), 128)
        return pltpu.make_async_copy(downs.total(tile), rows_out.at[rows, :], store_sem.at[1])

    ups.over_chips(lambda tile: store_up(tile).start())
    block = width // TEAM
    for source in range(TEAM):
        bias[0:1, pl.ds(source * block, block)] = vec_ref[source, 4:5, :] + vec_ref[source, 5:6, :]
    reduce.last()
    strip = 64

    def close(index, _):
        chunk = pl.ds(pl.multiple_of(index * strip, strip), strip)
        total = reduce.total(index, strip) + bias[0:1, :]
        reduce.own[0, chunk, :] = (x_ref[chunk, :].astype(F32) + total).astype(BF16)

    lax.fori_loop(0, tokens // strip, close, None)
    store_result = pltpu.make_async_copy(reduce.own.at[0], result_out, store_sem.at[2])
    store_result.start()
    downs.over_chips(lambda tile: store_down(tile).start())
    reduce.finish()
    for kind in range(3):
        own_back[kind].wait()
        for hop in range(1, QUARTERS):
            origin = lax.rem(quarter + hop, QUARTERS)
            back(origin, quarter, kind).wait_send()
            back(origin, origin, kind).wait_recv()
    store_result.wait()
    ups.finish()
    downs.finish()
    lax.fori_loop(0, ups.tiles, lambda tile, _: store_up(tile).wait(), None)
    lax.fori_loop(0, downs.tiles, lambda tile, _: store_down(tile).wait(), None)


def third(x, attended, activated, w_out, w_down, vectors, grad_up, grads, mlp_input, grad_rows):
    tokens, width = x.shape
    hidden = activated.shape[-1]
    part, share = width // TEAM // QUARTERS, width // QUARTERS
    tiles = (hidden + HEAD) // 128
    shapes = [
        (tokens, width),
        (2, QUARTERS, tokens, 3 * HEAD),
        (TEAM, part, hidden),
        (tiles * 128, share),
    ]
    return pl.pallas_call(
        third_kernel,
        out_shape=[jax.ShapeDtypeStruct(shape, BF16) for shape in shapes],
        in_specs=[VMEM] * 7 + [ANY] * 3,
        out_specs=[ANY] * 4,
        scratch_shapes=[
            DMA((4,)),
            DMA((QUARTERS, 3)),
            DMA((QUARTERS, 3)),
            DMA((2,)),
            DMA((3,)),
            pltpu.VMEM((2, TEAM * tokens, width // TEAM), BF16),
            pltpu.VMEM((width // TEAM, hidden), F32),
            pltpu.VMEM((TEAM * tokens, width), BF16),
            pltpu.VMEM((8, width), F32),
        ]
        + reduce_scratch(tokens, width, 1, BF16, tokens // 2)
        + quarters_scratch(TEAM, part, hidden)
        + quarters_scratch(tiles, 128, share),
        compiler_params=pltpu.CompilerParams(
            collective_id=2, has_side_effects=True, vmem_limit_bytes=LIMIT
        ),
        name="scatter_result",
    )(x, attended, activated, w_out, w_down, vectors, grad_up, grads, mlp_input, grad_rows)


def fourth_kernel(
    x_ref, dy_ref, dqkv_ref, du_ref, vec_ref, dy_sum_ref, xs_ref, wq_ref, wu_ref, ha_ref, up_ref, rows_ref,
    grad_ref, landed, rows_out, vector_ref,
    wq, wu, xs, gains, load_sem, tile_load, ha_tiles, tile_sum, sums, packets, packets_in, ring, ring_in,
    row_own, row_send, row_recv, pack_send, pack_recv, ring_send, ring_recv, *rest,
):
    base, line, side, quarter = spot()
    rank = line * 2 + side
    tokens, width = x_ref.shape
    hidden = du_ref.shape[1]
    part = width // TEAM // QUARTERS
    block = width // TEAM
    core, chip = core_peer(quarter), chip_peer(quarter)
    reduce = Reduce(tokens // 4, *rest[:5], rest[5:REDUCE])
    rest = rest[REDUCE:]
    qkvs = Quarters(*rest[:8])

    def place(source, slice_of, lane, lanes):
        rows = pl.ds(pl.multiple_of(slice_of * part, 16), part)
        return landed.at[source, rows, pl.ds(lane, lanes)]

    up_columns = Columns(
        lambda n: [(up_ref.at[n], 3 * HEAD, hidden)], place, 3 * HEAD, hidden, rest[8:17]
    )
    qkv_columns = Columns(
        lambda n: [(qkvs.total(n), 0, 3 * HEAD)], place, 0, 3 * HEAD, rest[17:26]
    )
    stream = Stream(ha_ref, ha_tiles, tile_load)
    loads = [
        pltpu.make_async_copy(wq_ref, wq, load_sem.at[0]),
        pltpu.make_async_copy(wu_ref, wu, load_sem.at[1]),
        pltpu.make_async_copy(xs_ref, xs, load_sem.at[2]),
    ]
    for copy in loads:
        copy.start()
    for tile in range(2):
        stream.copy(tile).start()
    greet_team(base, line, side, quarter)

    def rows_copy(which, slice_of, to):
        src = rows_ref if which < 2 else rows_out.at[slice_of]
        return send(
            src, rows_out.at[slice_of], row_send.at[which], row_recv.at[which], base + rank, to
        )

    own_rows = pltpu.make_async_copy(rows_ref, rows_out.at[quarter], row_own)
    own_rows.start()
    rows_copy(0, quarter, core).start()
    up_columns.start()
    sums[...] = jnp.zeros_like(sums)
    for source in range(TEAM):
        gains[0:2, pl.ds(source * block, block)] = vec_ref[source, 0:2, :]
    for copy in loads:
        copy.wait()

    def make(which, put):
        rows = pl.ds(pl.multiple_of(which * tokens, tokens), tokens)
        values = xs[which].astype(F32)
        average = jnp.mean(values, -1, keepdims=True)
        variance = jnp.mean(jnp.square(values - average), -1, keepdims=True)
        inverse = lax.rsqrt(variance + EPSILON)
        for start in range(0, width, 512):
            span = pl.ds(start, 512)
            attn = contract_last(dqkv_ref[rows, :], wq[span, :])
            mlp = contract_last(du_ref[rows, :], wu[span, :])
            unit = (xs[which, :, span].astype(F32) - average) * inverse
            sums[0:1, span] += jnp.sum(attn * unit, 0, keepdims=True)
            sums[1:2, span] += jnp.sum(mlp * unit, 0, keepdims=True)
            sums[2:3, span] += jnp.sum(attn, 0, keepdims=True)
            sums[3:4, span] += jnp.sum(mlp, 0, keepdims=True)
            put(span, attn * gains[0:1, span] + mlp * gains[1:2, span])
        sums[4:5, pl.ds(0, hidden)] += jnp.sum(du_ref[rows, :].astype(F32), 0, keepdims=True)
        sums[5:6, pl.ds(0, 3 * HEAD)] += jnp.sum(
            dqkv_ref[rows, :].astype(F32), 0, keepdims=True
        )

    for step in reversed(range(PAIRS)):

        def put_out(span, value, step=step):
            reduce.side_out[step, :, span] = value.astype(BF16)

        make(reduce.order[step] * 2 + 1 - side, put_out)
        reduce.begin(step)
        if step == PAIRS - 1:
            reduce.launch()

    def qkv_tile(tile, held):
        tile_sum[...] = contract_first(held[...], dqkv_ref[...])
        qkvs.put(tile, lambda q: tile_sum[pl.ds(pl.multiple_of(q * part, part), part), :])

    stream.run(TEAM, qkv_tile)
    qkvs.over_cores()
    rows_copy(1, quarter, chip).start()
    reduce.hop(1)
    for step in reversed(range(PAIRS)):

        def put_own(span, value, step=step):
            reduce.own[step, :, span] = value.astype(BF16)

        make(reduce.order[step] * 2 + side, put_own)
        if step == PAIRS - 1:
            reduce.advance(step)

    reduce.hop(2)

    def pack(target, _):
        span = pl.ds(pl.multiple_of(target * block, block), block)
        packets[target, pl.ds(0, 4), :] = sums[pl.ds(0, 4), span]
        packets[target, pl.ds(4, 1), :] = jnp.where(target == rank, dy_sum_ref[0:1, span], 0.0)
        for index in range(3):
            chunk = 3 * target + index
            kind = lax.div(chunk, HEADS)
            lanes = pl.ds(pl.multiple_of(kind * HEAD, HEAD), HEAD)
            packets[target, pl.ds(5 + index, 1), :] = jnp.where(
                lax.rem(chunk, HEADS) == rank, sums[5:6, lanes], 0.0
            )

    lax.fori_loop(0, TEAM, pack, None)

    def pack_copy(source, target, peer):
        return send(
            packets.at[target], packets_in.at[source], pack_send.at[target], pack_recv.at[source],
            base + peer, quarter,
        )

    def deal_packets(step, _):
        target = lax.rem(rank + step, TEAM)
        pack_copy(rank, target, target).start()

    lax.fori_loop(1, TEAM, deal_packets, None)
    packets_in[rank] = packets[rank]

    up_columns.forward()
    reduce.advance(2)
    reduce.hop(3)
    qkvs.over_chips(lambda tile: None)
    qkv_columns.start()
    reduce.advance(1)
    rows_copy(1, chip, chip).wait_recv()
    rows_copy(2, chip, core).start()
    up_columns.forward_last()

    def take_packets(step, _):
        source = lax.rem(rank + TEAM - step, TEAM)
        pack_copy(source, rank, source).wait_recv()

    lax.fori_loop(1, TEAM, take_packets, None)
    total = packets_in[0]
    for source in range(1, TEAM):
        total = total + packets_in[source]
    ring[pl.ds(0, 8), :] = total
    for index in range(hidden // block):
        ring[pl.ds(8 + index, 1), :] = sums[4:5, pl.ds(index * block, block)]

    def ring_copy(to, origin, peer):
        return send(
            ring, ring_in.at[origin], ring_send.at[to], ring_recv.at[origin], base + rank, peer
        )

    for hop in range(1, QUARTERS):
        to = lax.rem(quarter + hop, QUARTERS)
        ring_copy(to, quarter, to).start()
    ring_in[quarter] = ring[...]
    qkv_columns.forward()
    reduce.last()
    strip = 64

    def close(index, _):
        chunk = pl.ds(pl.multiple_of(index * strip, strip), strip)
        pulled = reduce.total(index, strip)
        unit, inverse = normalize(x_ref[chunk, :].astype(F32))
        pulled = (
            pulled
            - jnp.mean(pulled, -1, keepdims=True)
            - unit * jnp.mean(pulled * unit, -1, keepdims=True)
        )
        grad_ref[chunk, :] = (dy_ref[chunk, :].astype(F32) + inverse * pulled).astype(BF16)

    lax.fori_loop(0, tokens // strip, close, None)
    qkv_columns.forward_last()
    for hop in range(1, QUARTERS):
        origin = lax.rem(quarter + hop, QUARTERS)
        ring_copy(quarter, origin, origin).wait_recv()
    vector_ref[...] = (ring_in[0] + ring_in[1]) + (ring_in[2] + ring_in[3])

    reduce.finish()
    qkvs.finish()
    own_rows.wait()
    rows_copy(0, core, core).wait_recv()
    rows_copy(2, chip_peer(core), core).wait_recv()
    rows_copy(0, quarter, core).wait_send()
    rows_copy(1, quarter, chip).wait_send()
    rows_copy(2, chip, core).wait_send()
    for columns in (up_columns, qkv_columns):
        columns.arrive()
        columns.finish()

    def sent_packets(step, _):
        target = lax.rem(rank + step, TEAM)
        pack_copy(rank, target, target).wait_send()

    lax.fori_loop(1, TEAM, sent_packets, None)
    for hop in range(1, QUARTERS):
        to = lax.rem(quarter + hop, QUARTERS)
        ring_copy(to, quarter, to).wait_send()


def fourth(
    x, dy, grad_qkv, grad_up, vectors, dy_sum, everyone, w_qkv, w_up, attn_input, up_sums, row_sums
):
    tokens, width = x.shape
    hidden = grad_up.shape[-1]
    part, block = width // TEAM // QUARTERS, width // TEAM
    shapes = [
        ((tokens, width), BF16),
        ((TEAM, block, 3 * HEAD + hidden), BF16),
        ((QUARTERS, *row_sums.shape), BF16),
        ((16, block), F32),
    ]
    return pl.pallas_call(
        fourth_kernel,
        out_shape=[jax.ShapeDtypeStruct(*shape) for shape in shapes],
        in_specs=[VMEM] * 6 + [ANY] * 6,
        out_specs=[VMEM, ANY, ANY, VMEM],
        scratch_shapes=[
            pltpu.VMEM(w_qkv.shape, BF16),
            pltpu.VMEM(w_up.shape, BF16),
            pltpu.VMEM(everyone.shape, BF16),
            pltpu.VMEM((8, width), F32),
            DMA((3,)),
            DMA((2,)),
            pltpu.VMEM((2, TEAM * tokens, block), BF16),
            pltpu.VMEM((block, 3 * HEAD), F32),
            pltpu.VMEM((8, width), F32),
            pltpu.VMEM((TEAM, 8, block), F32),
            pltpu.VMEM((TEAM, 8, block), F32),
            pltpu.VMEM((16, block), F32),
            pltpu.VMEM((QUARTERS, 16, block), F32),
            DMA,
            DMA((3,)),
            DMA((3,)),
            DMA((TEAM,)),
            DMA((TEAM,)),
            DMA((QUARTERS,)),
            DMA((QUARTERS,)),
        ]
        + reduce_scratch(tokens, width, PAIRS, BF16, tokens // 4)
        + quarters_scratch(TEAM, part, 3 * HEAD)
        + column_sems(1) * 2,
        compiler_params=pltpu.CompilerParams(
            collective_id=3, has_side_effects=True, vmem_limit_bytes=LIMIT
        ),
        name="scatter_grad",
    )(
        x, dy, grad_qkv, grad_up, vectors, dy_sum, everyone, w_qkv, w_up, attn_input, up_sums,
        row_sums,
    )


def settle_kernel(
    columns_ref, rows_ref, result_ref, grad_ref,
    qkv_out, up_out, down_out, out_out, result_out, grad_out,
    low, wide, low_rows, wide_rows, passing, load_sem, store_sem, rows_load, rows_store, copy_sem,
):
    team, block, span = columns_ref.shape
    quarters, tall, share = rows_ref.shape
    width = team * HEAD
    hidden = span - 3 * HEAD
    plain = [
        (
            pltpu.make_async_copy(src, passing.at[index], copy_sem.at[index, 0]),
            pltpu.make_async_copy(passing.at[index], dst, copy_sem.at[index, 1]),
        )
        for index, (src, dst) in enumerate(((result_ref, result_out), (grad_ref, grad_out)))
    ]
    for load_in, _ in plain:
        load_in.start()

    def load(source):
        slot = lax.rem(source, 2)
        return pltpu.make_async_copy(columns_ref.at[source], low.at[slot], load_sem.at[slot])

    def stores(source):
        slot = lax.rem(source, 2)
        pairs = []
        for kind in range(3):
            start = pl.multiple_of(kind * width + source * HEAD, HEAD)
            pairs.append((pl.ds(kind * HEAD, HEAD), qkv_out.at[:, pl.ds(start, HEAD)]))
        start = pl.multiple_of(source * hidden, hidden)
        pairs.append((pl.ds(3 * HEAD, hidden), up_out.at[:, pl.ds(start, hidden)]))
        return [
            pltpu.make_async_copy(wide.at[slot, :, lanes], dst, store_sem.at[slot, index])
            for index, (lanes, dst) in enumerate(pairs)
        ]

    def load_rows(quarter):
        slot = lax.rem(quarter, 2)
        return pltpu.make_async_copy(rows_ref.at[quarter], low_rows.at[slot], rows_load.at[slot])

    def stores_rows(quarter):
        slot = lax.rem(quarter, 2)
        lanes = pl.ds(pl.multiple_of(quarter * share, share), share)
        size = tall - HEAD
        return [
            pltpu.make_async_copy(
                wide_rows.at[slot, pl.ds(0, size), :], down_out.at[:, lanes], rows_store.at[slot, 0]
            ),
            pltpu.make_async_copy(
                wide_rows.at[slot, pl.ds(size, HEAD), :], out_out.at[:, lanes],
                rows_store.at[slot, 1],
            ),
        ]

    def run(count, load, stores, low, wide, strip):
        def one(index, _):
            slot = lax.rem(index, 2)
            load(index).wait()

            @pl.when(index >= 2)
            def _():
                for copy in stores(index - 2):
                    copy.wait()

            def widen(step, _):
                chunk = pl.ds(pl.multiple_of(step * strip, strip), strip)
                wide[slot, chunk, :] = low[slot, chunk, :].astype(F32)

            lax.fori_loop(0, low.shape[1] // strip, widen, None)
            for copy in stores(index):
                copy.start()
            pl.when(index + 2 < count)(lambda: load(index + 2).start())

        lax.fori_loop(0, count, one, None)

    for index in range(2):
        load_rows(index).start()
        load(index).start()
    for load_in, store_out in plain:
        load_in.wait()
        store_out.start()
    run(quarters, load_rows, stores_rows, low_rows, wide_rows, 64)
    run(team, load, stores, low, wide, min(64, block))
    for index in (quarters - 2, quarters - 1):
        for copy in stores_rows(index):
            copy.wait()
    for index in (team - 2, team - 1):
        for copy in stores(index):
            copy.wait()
    for _, store_out in plain:
        store_out.wait()


def settle(columns, row_sums, result, grad_inputs):
    team, block, span = columns.shape
    quarters, tall, share = row_sums.shape
    shapes = [
        ((block, team * 3 * HEAD), F32),
        ((block, team * (span - 3 * HEAD)), F32),
        ((tall - HEAD, quarters * share), F32),
        ((HEAD, quarters * share), F32),
        (result.shape, BF16),
        (grad_inputs.shape, BF16),
    ]
    return pl.pallas_call(
        settle_kernel,
        out_shape=[jax.ShapeDtypeStruct(*shape) for shape in shapes],
        in_specs=[ANY] * 4,
        out_specs=[ANY] * 6,
        scratch_shapes=[
            pltpu.VMEM((2, block, span), BF16),
            pltpu.VMEM((2, block, span), F32),
            pltpu.VMEM((2, tall, share), BF16),
            pltpu.VMEM((2, tall, share), F32),
            pltpu.VMEM((2, *result.shape), BF16),
            DMA((2,)),
            DMA((2, 4)),
            DMA((2,)),
            DMA((2, 2)),
            DMA((2, 2)),
        ],
        compiler_params=pltpu.CompilerParams(vmem_limit_bytes=LIMIT),
        name="settle",
    )(columns, row_sums, result, grad_inputs)


def on_device(
    dp,
    ctx,
    inputs,
    segments,
    ln_gain,
    ln_bias,
    qkv_weight,
    qkv_bias,
    out_weight,
    out_bias,
    up_weight,
    up_bias,
    down_weight,
    down_bias,
    cotangent,
):
    assert dp % TEAM == 0 and ctx == QUARTERS
    teams = dp // TEAM
    together = None if teams == 1 else [[g * TEAM + i for i in range(TEAM)] for g in range(teams)]
    across = None if teams == 1 else [[g * TEAM + i for g in range(teams)] for i in range(TEAM)]
    place = lax.axis_index("dp")
    rank = place % TEAM
    _, tokens, width = inputs.shape
    hidden = up_weight.shape[1] // TEAM
    shard = width // dp

    def team_order(values):
        if teams == 1:
            return values
        lead = values.shape[:-1]
        return values.reshape(*lead, teams, TEAM, shard).swapaxes(-3, -2).reshape(*lead, width)

    def plain_order(values):
        if teams == 1:
            return values
        lead = values.shape[:-1]
        return values.reshape(*lead, TEAM, teams, shard).swapaxes(-3, -2).reshape(*lead, width)

    if teams == 1:
        w_qkv, w_up, w_out, w_down = qkv_weight, up_weight, out_weight, down_weight
        gain, shift, b_qkv, b_up = ln_gain, ln_bias, qkv_bias, up_bias
        b_rows = [out_bias, down_bias]
    else:
        line_up = partial(lax.all_gather, axis_name="dp", axis_index_groups=across, tiled=True)
        whole = partial(lax.all_gather, axis_name="dp", axis=0, tiled=True)

        def cut(values):
            size = values.shape[0] // TEAM
            return lax.dynamic_slice_in_dim(values, rank * size, size, 0)

        w_qkv, w_up = line_up(qkv_weight, axis=0), line_up(up_weight, axis=0)
        gain, shift = line_up(ln_gain, axis=1), line_up(ln_bias, axis=1)
        w_out, w_down = cut(whole(out_weight)), cut(whole(down_weight))
        b_qkv, b_up = cut(whole(qkv_bias)), cut(whole(up_bias))
        b_rows = [cut(whole(out_bias)), cut(whole(down_bias))]
    rows = w_qkv.shape[0]
    packet = jnp.concatenate(
        [
            gain.astype(F32),
            shift.astype(F32),
            jnp.stack(b_rows).astype(F32),
            jnp.zeros((2, rows), F32),
            b_qkv.astype(F32).reshape(3, rows),
            jnp.zeros((5, rows), F32),
            jnp.broadcast_to(segments.astype(F32), (8, tokens)),
        ]
    )
    mine = inputs.reshape(tokens, width)
    grad_mine = cotangent.reshape(tokens, width)
    mine_team = team_order(mine)
    positions = jnp.arange(ctx * tokens, dtype=jnp.int32)
    tables = rotary_tables(positions.astype(F32))
    (
        everyone, attn_input, mlp_input, w_head, w_units, qkv, marks, vectors,
        grad_rows, activated, grad_up, grad_attended, attended, dy_sum,
    ) = gather(
        mine_team, grad_mine, packet, w_out, w_down, b_up.astype(F32).reshape(1, hidden), tables,
        w_qkv, w_up,
    )
    grads = attend_back(qkv, grad_attended, marks, tables)
    flat = (TEAM * tokens, -1)
    attn_input, mlp_input, grad_rows, activated, grad_up, attended = (
        values.reshape(flat)
        for values in (attn_input, mlp_input, grad_rows, activated, grad_up, attended)
    )
    result, grad_qkv, up_sums, row_sums = third(
        mine, attended, activated, w_out, w_down, vectors, grad_up, grads, mlp_input, grad_rows
    )
    grad_inputs, columns, row_sums, vector = fourth(
        mine_team, team_order(grad_mine), grad_qkv.reshape(flat), grad_up, vectors, dy_sum, everyone,
        w_head, w_units, attn_input, up_sums, row_sums,
    )
    grad_inputs = plain_order(grad_inputs)
    if teams == 1:
        grad_gain, grad_shift, grad_out_b = vector[0:2], vector[2:4], vector[4]
        grad_qkv_b, grad_up_b = vector[5:8].reshape(-1), vector[8 : 8 + hidden // rows].reshape(-1)
    else:
        near = partial(lax.all_gather, axis_name="dp", axis_index_groups=together, tiled=True)

        def own(values):
            size = values.shape[0] // dp
            total = lax.psum(values, "dp", axis_index_groups=across)
            return lax.dynamic_slice_in_dim(total, place * size, size, 0)

        ends = lax.psum_scatter(
            vector[:4], "dp", scatter_dimension=1, axis_index_groups=across, tiled=True
        )
        grad_gain, grad_shift = ends[0:2], ends[2:4]
        grad_out_b = own(near(vector[4], axis=0))
        grad_qkv_b = own(near(vector[5:8].reshape(-1), axis=0))
        grad_up_b = own(near(vector[8 : 8 + hidden // rows].reshape(-1), axis=0))

        def scatter_rows(term):
            size = term.shape[0]
            full = jnp.zeros((TEAM, size, width), BF16)
            full = lax.dynamic_update_slice_in_dim(full, term.astype(BF16)[None], rank, 0)
            return lax.psum_scatter(
                full.reshape(TEAM * size, width), "dp", scatter_dimension=0, tiled=True
            ).astype(F32)

        columns = lax.psum_scatter(
            columns, "dp", scatter_dimension=1, axis_index_groups=across, tiled=True
        )
    grad_qkv_w, grad_up_w, grad_down_w, grad_out_w, result, grad_inputs = settle(
        columns, row_sums, result, grad_inputs
    )
    if teams > 1:
        grad_out_w, grad_down_w = scatter_rows(grad_out_w), scatter_rows(grad_down_w)
    return (
        result.reshape(inputs.shape),
        grad_inputs.reshape(inputs.shape),
        grad_gain,
        grad_shift,
        grad_qkv_w,
        grad_qkv_b,
        grad_out_w,
        grad_out_b,
        grad_up_w,
        grad_up_b,
        grad_down_w,
        grad_out_b,
    )


def solution(mesh):
    placed = (
        P("dp", "ctx", None),
        P("dp", "ctx"),
        P(None, "dp"),
        P(None, "dp"),
        P("dp", None),
        P("dp"),
        P("dp", None),
        P("dp"),
        P("dp", None),
        P("dp"),
        P("dp", None),
        P("dp"),
        P("dp", "ctx", None),
    )
    return jax.shard_map(
        partial(on_device, mesh.shape["dp"], mesh.shape["ctx"]),
        mesh=mesh,
        in_specs=placed,
        out_specs=(
            P("dp", "ctx", None),
            P("dp", "ctx", None),
            P(None, "dp"),
            P(None, "dp"),
            P("dp", None),
            P("dp"),
            P("dp", None),
            P("dp"),
            P("dp", None),
            P("dp"),
            P("dp", None),
            P("dp"),
        ),
        check_vma=False,
    )
```

```python
from functools import partial

import jax
import jax.numpy as jnp
import numpy as np
from jax import lax
from jax.experimental import pallas as pl
from jax.experimental.pallas import tpu as pltpu
from jax.sharding import PartitionSpec as P

HEADS = 8
HEAD = 256
ROT = 64
EPSILON = 1e-05
MASKED = -1e30
F32 = jnp.float32
BF16 = jnp.bfloat16
MESH = pl.DeviceIdType.MESH
TEAM = HEADS
PAIRS = TEAM // 2
QUARTERS = 4
RIGHT, LEFT = 0, 1
VECTOR_ROWS = 24


def dot(left, right):
    return jnp.dot(left, right, preferred_element_type=F32)


def contract_last(left, right):
    return lax.dot_general(left, right, (((1,), (1,)), ((), ())), preferred_element_type=F32)


def contract_first(left, right):
    return lax.dot_general(left, right, (((0,), (0,)), ((), ())), preferred_element_type=F32)


def rotary_tables(length):
    half = ROT // 2
    exponent = np.arange(0, ROT, 2).astype(np.float32) / np.float32(ROT)
    frequency = np.float32(10000.0) ** (-exponent)
    angles = np.arange(length, dtype=np.float32)[:, None] * frequency[None, :]
    cosine, sine = np.cos(angles), np.sin(angles)
    one, nought = np.ones((length, 64), np.float32), np.zeros((length, 64), np.float32)
    blank = np.zeros((length, half), np.float32)
    tables = ([cosine, cosine, one], [-sine, blank, nought], [blank, sine, nought])
    return [jnp.asarray(np.concatenate(table, -1)) for table in tables]


def spot():
    place = lax.axis_index("dp")
    rank = lax.rem(place, TEAM)
    return place - rank, lax.div(rank, 2), lax.rem(rank, 2), lax.axis_index("ctx")


def near_first(line):
    second = 1 + lax.rem(line, 2)
    last = 3 * (1 - lax.div(line, 2))
    return (line, second, 6 - line - second - last, last)


def core_peer(quarter):
    return quarter + 1 - 2 * lax.rem(quarter, 2)


def chip_peer(quarter):
    return quarter + 2 - 4 * lax.div(quarter, 2)


def send(src, dst, send_sem, recv_sem, place, quarter):
    return pltpu.make_async_remote_copy(
        src_ref=src, dst_ref=dst, send_sem=send_sem, recv_sem=recv_sem,
        device_id=(place, quarter), device_id_type=MESH,
    )


def greet_line(base, line, side, quarter):
    barrier = pltpu.get_barrier_semaphore()

    def hail(place, quarter):
        pl.semaphore_signal(barrier, inc=1, device_id=(place, quarter), device_id_type=MESH)

    rank = line * 2 + side
    hail(base + line * 2 + 1 - side, quarter)

    pl.when(line < PAIRS - 1)(lambda: hail(base + rank + 2, quarter))
    pl.when(line > 0)(lambda: hail(base + rank - 2, quarter))
    for step in range(1, QUARTERS):
        hail(base + rank, lax.rem(quarter + step, QUARTERS))
    neighbours = 1 + lax.div(line + 2, 3) - lax.div(line, 3)
    pl.semaphore_wait(barrier, neighbours + QUARTERS)


def greet_team(base, line, side, quarter):
    barrier = pltpu.get_barrier_semaphore()
    rank = line * 2 + side
    for step in range(1, TEAM):
        pl.semaphore_signal(
            barrier, inc=1, device_id=(base + lax.rem(rank + step, TEAM), quarter),
            device_id_type=MESH,
        )
    for step in range(1, QUARTERS):
        pl.semaphore_signal(
            barrier, inc=1, device_id=(base + rank, lax.rem(quarter + step, QUARTERS)),
            device_id_type=MESH,
        )
    pl.semaphore_wait(barrier, TEAM + QUARTERS - 2)


class Relay:
    def __init__(self, held, line_send, line_recv, side_send, side_recv, half_send, half_recv):
        self.held = held
        self.sems = line_send, line_recv, side_send, side_recv, half_send, half_recv
        self.base, self.line, self.side, self.quarter = spot()
        self.half = held.shape[1] * 3 // 8

    def neighbour(self, way):
        return self.base + self.line * 2 + self.side + (2 if way == RIGHT else -2)

    def along(self, source, way):
        block = self.held.at[source * 2 + self.side]
        return send(
            block, block, self.sems[0].at[way, source], self.sems[1].at[source],
            self.neighbour(way), self.quarter,
        )

    def along_half(self, way):
        source = 0 if way == RIGHT else PAIRS - 1
        block = self.held.at[source * 2 + 1 - self.side, pl.ds(0, self.half)]
        return send(
            block, block, self.sems[4].at[way], self.sems[5].at[way], self.neighbour(way),
            self.quarter,
        )

    def over(self, source, side, low):
        block = self.held.at[source * 2 + side]
        if low:
            block = self.held.at[source * 2 + side, pl.ds(self.half, self.held.shape[1] - self.half)]
        place = self.base + self.line * 2 + 1 - self.side
        return send(
            block, block, self.sems[2].at[source], self.sems[3].at[source], place, self.quarter
        )

    def crossing(self, source, side, act):
        parted = (source != self.line) & (lax.rem(source, PAIRS - 1) == 0)
        pl.when(parted)(lambda: act(self.over(source, side, True)))
        pl.when(jnp.logical_not(parted))(lambda: act(self.over(source, side, False)))

    def each(self, step, act):
        line = self.line
        if step == 0:
            pl.when(line < PAIRS - 1)(lambda: act(line, RIGHT))
            pl.when(line > 0)(lambda: act(line, LEFT))
            act(line, None)
            return

        @pl.when(line >= step)
        def _():
            source = line - step
            act(source, "arrive")
            pl.when(line < PAIRS - 1)(lambda: act(source, RIGHT))
            act(source, None)

        @pl.when(line + step < PAIRS)
        def _():
            source = line + step
            act(source, "arrive")
            pl.when(line > 0)(lambda: act(source, LEFT))
            act(source, None)

    def start(self, step):
        def act(source, way):
            if way == "arrive":
                self.along(source, RIGHT).wait_recv()
            elif way is None:
                self.crossing(source, self.side, lambda copy: copy.start())
            else:
                self.along(source, way).start()

        self.each(step, act)

    def start_halves(self):
        for end, way in ((0, RIGHT), (PAIRS - 1, LEFT)):

            @pl.when(self.line == end)
            def _(end=end, way=way):
                self.over(self.line, 1 - self.side, False).wait_recv()
                self.along_half(way).start()

    def pass_halves(self, step):
        for end, way in ((0, RIGHT), (PAIRS - 1, LEFT)):
            here = step if way == RIGHT else PAIRS - 1 - step

            @pl.when(self.line == here)
            def _(way=way):
                self.along_half(way).wait_recv()
                if step < PAIRS - 1:
                    self.along_half(way).start()

    def wait_over(self, step, source):
        def take(copy):
            copy.wait_recv()

        if step == 0:
            inner = (self.line > 0) & (self.line < PAIRS - 1)
            pl.when(inner)(lambda: take(self.over(source, 1 - self.side, False)))
        else:
            self.crossing(source, 1 - self.side, take)

    def finish(self):
        def act(source, way):
            if way is None:
                self.crossing(source, self.side, lambda copy: copy.wait_send())
            elif way != "arrive":
                self.along(source, way).wait_send()

        for step in range(PAIRS):
            self.each(step, act)
        pl.when(self.line < PAIRS - 1)(lambda: self.along_half(RIGHT).wait_send())
        pl.when(self.line > 0)(lambda: self.along_half(LEFT).wait_send())


RELAY_SEMS = [
    pltpu.SemaphoreType.DMA((2, PAIRS)),
    pltpu.SemaphoreType.DMA((PAIRS,)),
    pltpu.SemaphoreType.DMA((PAIRS,)),
    pltpu.SemaphoreType.DMA((PAIRS,)),
    pltpu.SemaphoreType.DMA((2,)),
    pltpu.SemaphoreType.DMA((2,)),
]


def normalize(rows):
    average = jnp.mean(rows, -1, keepdims=True)
    centred = rows - average
    variance = jnp.mean(centred * centred, -1, keepdims=True)
    inverse = lax.rsqrt(variance + EPSILON)
    return centred * inverse, inverse


def rotate_low(low, cosine, above, below):
    half = ROT // 2
    return (
        low * cosine + pltpu.roll(low, 128 - half, 1) * above + pltpu.roll(low, half, 1) * below
    )


def unrotate_low(low, cosine, above, below):
    half = ROT // 2
    return (
        low * cosine + pltpu.roll(low * below, 128 - half, 1) + pltpu.roll(low * above, half, 1)
    )


def reader(sequence):
    return 2 * lax.rem(sequence, 2) + lax.rem(lax.div(sequence, 2), 2)


def reader_slot(sequence):
    return lax.div(sequence, QUARTERS)


def among(quarter):
    return 2 * lax.rem(quarter, 2) + lax.div(quarter, 2)


class Spread:
    def __init__(self, pieces, send_sem, recv_sem, own_sem):
        self.pieces, self.sems = pieces, (send_sem, recv_sem, own_sem)
        base, line, side, self.quarter = spot()
        self.place = base + line * 2 + side

    def _remote(self, index, sequence, slot, to, origin):
        src, dst = self.pieces[index]
        send_sem, recv_sem, _ = self.sems
        return send(
            src(sequence), dst(slot, origin), send_sem.at[index, sequence],
            recv_sem.at[index, origin, slot], self.place, to,
        )

    def _own(self, index, sequence):
        src, dst = self.pieces[index]
        slot = reader_slot(sequence)
        return pltpu.make_async_copy(
            src(sequence), dst(slot, self.quarter), self.sems[2].at[index, slot]
        )

    def each(self, sequence, own, other):
        to, slot = reader(sequence), reader_slot(sequence)

        @pl.when(to == self.quarter)
        def _():
            for index in range(len(self.pieces)):
                own(self._own(index, sequence))

        @pl.when(to != self.quarter)
        def _():
            for index in range(len(self.pieces)):
                other(self._remote(index, sequence, slot, to, self.quarter))

    def start(self, sequence):
        self.each(sequence, lambda copy: copy.start(), lambda copy: copy.start())

    def finish(self):
        def sent(sequence, _):
            self.each(sequence, lambda copy: copy.wait(), lambda copy: copy.wait_send())

        lax.fori_loop(0, TEAM, sent, None)

        def landed(step, _):
            origin = lax.rem(self.quarter + 1 + lax.div(step, 2), QUARTERS)
            slot = lax.rem(step, 2)
            for index in range(len(self.pieces)):
                self._remote(index, 0, slot, origin, origin).wait_recv()

        lax.fori_loop(0, 2 * (QUARTERS - 1), landed, None)


def spread_sems(count):
    return [
        pltpu.SemaphoreType.DMA((count, TEAM)),
        pltpu.SemaphoreType.DMA((count, QUARTERS, 2)),
        pltpu.SemaphoreType.DMA((count, 2)),
    ]


class Columns:
    def __init__(self, pieces, place, lane, lanes, sems):
        self.pieces, self.place, self.lane, self.lanes, self.sems = pieces, place, lane, lanes, sems
        self.base, line, side, self.quarter = spot()
        self.rank = line * 2 + side

    def deal(self, source, target, peer):
        sends, recvs = self.sems[:2]
        return [
            send(
                src, self.place(source, self.quarter, lane, lanes),
                sends.at[index, target], recvs.at[index, source], self.base + peer, self.quarter,
            )
            for index, (src, lane, lanes) in enumerate(self.pieces(target))
        ]

    def own(self):
        return [
            pltpu.make_async_copy(
                src, self.place(self.rank, self.quarter, lane, lanes), self.sems[2].at[index]
            )
            for index, (src, lane, lanes) in enumerate(self.pieces(self.rank))
        ]

    def start(self):
        for copy in self.own():
            copy.start()

        def one(step, _):
            target = lax.rem(self.rank + step, TEAM)
            for copy in self.deal(self.rank, target, target):
                copy.start()

        lax.fori_loop(1, TEAM, one, None)

    def pass_on(self, which, source, slice_of, to):
        block = self.place(source, slice_of, self.lane, self.lanes)
        sends, recvs = self.sems[3 + 2 * which : 5 + 2 * which]
        return send(
            block, block, sends.at[source], recvs.at[source], self.base + self.rank, to
        )

    def to_core(self, source):
        return self.pass_on(0, source, self.quarter, core_peer(self.quarter))

    def to_chip(self, source):
        return self.pass_on(1, source, self.quarter, chip_peer(self.quarter))

    def to_last(self, source):
        return self.pass_on(2, source, chip_peer(self.quarter), core_peer(self.quarter))

    def forward(self):
        for copy in self.own():
            copy.wait()
        self.to_chip(self.rank).start()
        self.to_core(self.rank).start()

        def one(step, _):
            source = lax.rem(self.rank + TEAM - step, TEAM)
            for copy in self.deal(source, self.rank, source):
                copy.wait_recv()
            self.to_chip(source).start()
            self.to_core(source).start()

        lax.fori_loop(1, TEAM, one, None)

    def forward_last(self):
        chip = chip_peer(self.quarter)

        def one(step, _):
            source = lax.rem(self.rank + TEAM - step, TEAM)
            self.pass_on(1, source, chip, chip).wait_recv()
            self.to_last(source).start()

        lax.fori_loop(0, TEAM, one, None)

    def arrive(self):
        core = core_peer(self.quarter)

        def one(source, _):
            self.pass_on(0, source, core, core).wait_recv()
            self.pass_on(2, source, chip_peer(core), core).wait_recv()

        lax.fori_loop(0, TEAM, one, None)

    def finish(self):
        def one(source, _):
            self.to_core(source).wait_send()
            self.to_chip(source).wait_send()
            self.to_last(source).wait_send()

        lax.fori_loop(0, TEAM, one, None)

        def sent(step, _):
            target = lax.rem(self.rank + step, TEAM)
            for copy in self.deal(self.rank, target, target):
                copy.wait_send()

        lax.fori_loop(1, TEAM, sent, None)


def column_sems(count):
    dma = pltpu.SemaphoreType.DMA
    return [dma((count, TEAM))] * 2 + [dma((count,))] + [dma((TEAM,))] * 6


def same_document(query_marks, key_marks):
    def one_hot(marks):
        number = lax.broadcasted_iota(jnp.int32, marks.shape, 0).astype(F32)
        return jnp.where(marks == number, 1.0, 0.0).astype(BF16)

    return contract_first(one_hot(query_marks), one_hot(key_marks)) > 0.5


def probabilities(block, size, q_ref, k_ref, marks_ref):
    start = block * size
    rows, keys = pl.ds(start, size), pl.ds(0, start + size)
    scores = contract_last(q_ref[rows, :], k_ref[keys, :]) * HEAD ** (-0.5)
    shape = scores.shape
    query_pos = start + lax.broadcasted_iota(jnp.int32, shape, 0)
    key_pos = lax.broadcasted_iota(jnp.int32, shape, 1)
    key_marks = jnp.concatenate([marks_ref[index] for index in range(block + 1)], -1)
    allowed = (query_pos >= key_pos) & same_document(marks_ref[block], key_marks)
    scores = jnp.where(allowed, scores, MASKED)
    expanded = jnp.exp(scores - jnp.max(scores, -1, keepdims=True))
    return expanded / jnp.sum(expanded, -1, keepdims=True)


def gelu_terms(values):
    chance = 0.5 * (1.0 + lax.erf(values * (0.5**0.5)))
    density = jnp.exp(-0.5 * values * values) * 0.3989422804014327
    return values * chance, chance + values * density


ANY = pl.BlockSpec(memory_space=pl.ANY)
VMEM = pl.BlockSpec(memory_space=pltpu.VMEM)
DMA = pltpu.SemaphoreType.DMA
LIMIT = 60 << 20


def gather_kernel(
    x_ref, dy_ref, gain_ref, shift_ref, out_b_ref, down_b_ref, qkv_b_ref, up_b_ref, marks_ref,
    wo_in, wd_in, cos_ref, above_ref, below_ref, wq_ref, wu_ref,
    x_out, ha_out, hm_out, wq_out, wu_out, qkv_out, marks_out, vec_out,
    dy_out, a_out, du_out, do_out, o_out, sum_out,
    xs, dys, hm, head, units, vec_ref, vecs, vectors, ha, qkv, whole, marks, mixed, act, grad, attended,
    table, wo_ref, wd_ref, late_load, own_sem, x_store, ha_store, du_store, dy_store, late_store, v_send, v_recv, back_send, back_recv,
    *sems,
):
    base, line, side, quarter = spot()
    rank = line * 2 + side
    tokens, width = x_ref.shape
    hidden = act.shape[-1]
    rows = wq_ref.shape[0]
    part = rows // QUARTERS
    take = iter(range(0, len(sems)))

    def some(count):
        return [sems[next(take)] for _ in range(count)]

    relay_x, relay_dy = Relay(xs, *some(6)), Relay(dys, *some(6))
    head_columns, unit_columns = some(9), some(9)
    spread_x = Spread(
        [
            (
                lambda s: qkv.at[s],
                lambda j, origin: whole.at[j, :, pl.ds(origin * tokens, tokens), :],
            ),
            (lambda s: vecs.at[s, pl.ds(16, 8), :], lambda j, origin: marks.at[j, origin]),
        ],
        *some(3),
    )
    spread_do = Spread(
        [
            (
                lambda s: attended.at[s],
                lambda j, origin: do_out.at[j, pl.ds(origin * tokens, tokens), :],
            )
        ],
        *some(3),
    )
    mine = pl.ds(pl.multiple_of(quarter * part, 16), part)

    def landing(weight):
        def place(source, slice_of, lane, lanes):
            band = pl.ds(pl.multiple_of(source * rows + slice_of * part, 16), part)
            return weight.at[band, pl.ds(lane, lanes)]

        return place

    head_columns = Columns(
        lambda target: [
            (
                wq_ref.at[mine, pl.ds(pl.multiple_of(kind * width + target * HEAD, HEAD), HEAD)],
                kind * HEAD,
                HEAD,
            )
            for kind in range(3)
        ],
        landing(head), 0, 3 * HEAD, head_columns,
    )
    unit_columns = Columns(
        lambda target: [
            (wu_ref.at[mine, pl.ds(pl.multiple_of(target * hidden, hidden), hidden)], 0, hidden)
        ],
        landing(units), 0, hidden, unit_columns,
    )
    own_rows = pl.ds(pl.multiple_of(quarter * tokens, tokens), tokens)

    def put_row(row, values):
        vec_ref[row : row + 1, :] = values.astype(F32).reshape(1, rows)

    vec_ref[...] = jnp.zeros_like(vec_ref)
    vec_ref[0:2, :] = gain_ref[...].astype(F32)
    vec_ref[2:4, :] = shift_ref[...].astype(F32)
    put_row(4, out_b_ref[...])
    put_row(5, down_b_ref[...])
    for index in range(3):
        put_row(8 + index, qkv_b_ref[pl.ds(index * rows, rows)])
    vec_ref[16:24, :] = jnp.broadcast_to(marks_ref[...].astype(F32), (8, tokens))
    for start in range(0, hidden, 256):
        values = up_b_ref[pl.ds(start, 256)].astype(F32)
        vectors[4:5, pl.ds(start, 256)] = values.reshape(1, 256)
    greet_team(base, line, side, quarter)

    def vector_copy(source, target, peer):
        return send(
            vec_ref, vecs.at[source], v_send.at[target], v_recv.at[source], base + peer, quarter
        )

    owns = [
        pltpu.make_async_copy(src, dst, own_sem.at[index])
        for index, (src, dst) in enumerate(
            (
                (x_ref, xs.at[rank]),
                (vec_ref, vecs.at[rank]),
                (dy_ref, dys.at[rank]),
                (cos_ref.at[own_rows, :], table.at[0]),
                (above_ref.at[own_rows, :], table.at[1]),
                (below_ref.at[own_rows, :], table.at[2]),
            )
        )
    ]
    for copy in owns:
        copy.start()
    load_out = pltpu.make_async_copy(wo_in, wo_ref, late_load.at[0])
    load_down = pltpu.make_async_copy(wd_in, wd_ref, late_load.at[1])
    load_out.start()
    load_down.start()

    def send_vector(step, _):
        target = lax.rem(rank + step, TEAM)
        vector_copy(rank, target, target).start()

    lax.fori_loop(1, TEAM, send_vector, None)
    head_columns.start()
    for copy in owns:
        copy.wait()
    relay_x.start(0)
    head_columns.forward()
    relay_x.start_halves()
    relay_x.start(1)
    head_columns.forward_last()

    def take_vector(step, _):
        origin = lax.rem(rank + TEAM - step, TEAM)
        vector_copy(origin, rank, origin).wait_recv()

    lax.fori_loop(1, TEAM, take_vector, None)
    for source in range(TEAM):
        for row in range(4):
            vectors[pl.ds(row, 1), pl.ds(source * rows, rows)] = vecs[source, pl.ds(row, 1), :]
    head_columns.arrive()
    late = [
        pltpu.make_async_copy(src, dst, late_store.at[index])
        for index, (src, dst) in enumerate(
            ((head, wq_out), (vecs, vec_out), (units, wu_out), (whole, qkv_out), (marks, marks_out))
        )
    ]
    late[0].start()
    late[1].start()

    strip = 128
    order = near_first(line)

    def member(step, other):
        return order[step] * 2 + side + other * (1 - 2 * side)

    def store_x(which):
        return [
            pltpu.make_async_copy(xs.at[which], x_out.at[which], x_store.at[0, which]),
            pltpu.make_async_copy(hm.at[which], hm_out.at[which], x_store.at[1, which]),
        ]

    def store_ha(slot, which):
        return pltpu.make_async_copy(ha.at[slot], ha_out.at[which], ha_store.at[slot])

    def project(slot, which):
        def norm(index, _):
            chunk = pl.ds(pl.multiple_of(index * strip, strip), strip)
            unit, _ = normalize(xs[which, chunk, :].astype(F32))
            ha[slot, chunk, :] = (unit * vectors[0:1, :] + vectors[2:3, :]).astype(BF16)
            hm[which, chunk, :] = (unit * vectors[1:2, :] + vectors[3:4, :]).astype(BF16)

        lax.fori_loop(0, tokens // strip, norm, None)
        for kind in range(3):
            chunk = kind * TEAM + rank
            bias = vecs[lax.div(chunk, 3), pl.ds(8 + lax.rem(chunk, 3), 1), :]
            made = dot(ha[slot], head[:, pl.ds(kind * HEAD, HEAD)]) + bias
            if kind < 2:
                low = rotate_low(made[:, :128], table[0], table[1], table[2])
                qkv[which, kind, :, pl.ds(0, 128)] = low.astype(BF16)
                qkv[which, kind, :, pl.ds(128, HEAD - 128)] = made[:, 128:].astype(BF16)
            else:
                qkv[which, kind] = made.astype(BF16)
        spread_x.start(which)
        store_ha(slot, which).start()
        for copy in store_x(which):
            copy.start()

    for step, place in enumerate(order):

        def one(other, _, step=step, place=place):
            @pl.when(other == 1)
            def _():
                if 0 < step < PAIRS - 1:
                    relay_x.start(step + 1)
                if step > 0:
                    relay_x.pass_halves(step)
                if step == 2:
                    unit_columns.start()
                    relay_dy.start(0)
                relay_x.wait_over(step, place)

            if step > 0:
                store_ha(other, member(step - 1, other)).wait()
            project(other, member(step, other))

        lax.fori_loop(0, 2, one, None)

    unit_columns.forward()
    sum_out[...] = jnp.zeros_like(sum_out)
    relay_dy.start_halves()
    relay_dy.start(1)
    unit_columns.forward_last()
    spread_x.finish()
    late[3].start()
    late[4].start()

    def attend(sequence, _):
        q, k, v = (whole.at[sequence, kind] for kind in range(3))
        for block in range(QUARTERS):
            probs = probabilities(block, tokens, q, k, marks.at[sequence])
            value_block = v[pl.ds(0, (block + 1) * tokens), :]
            mixed[sequence, pl.ds(block * tokens, tokens), :] = dot(
                probs.astype(BF16), value_block
            ).astype(BF16)

    lax.fori_loop(0, 2, attend, None)

    def back(to, origin):
        return send(
            mixed.at[:, pl.ds(to * tokens, tokens), :], o_out.at[:, among(origin)],
            back_send.at[to], back_recv.at[origin], base + rank, to,
        )

    own_back = pltpu.make_async_copy(
        mixed.at[:, pl.ds(quarter * tokens, tokens), :], o_out.at[:, among(quarter)],
        own_sem.at[6],
    )
    own_back.start()
    for step in range(1, QUARTERS):
        to = lax.rem(quarter + step, QUARTERS)
        back(to, quarter).start()
    unit_columns.arrive()
    late[2].start()
    load_out.wait()
    load_down.wait()

    def store_dy(which):
        return pltpu.make_async_copy(dys.at[which], dy_out.at[which], dy_store.at[which])

    def store_du(slot, which):
        return [
            pltpu.make_async_copy(act.at[slot], a_out.at[which], du_store.at[0, slot]),
            pltpu.make_async_copy(grad.at[slot], du_out.at[which], du_store.at[1, slot]),
        ]

    def pull(slot, which):
        attended[which] = contract_last(dys[which], wo_ref[...]).astype(BF16)
        spread_do.start(which)
        for start in range(0, hidden, 256):
            span = pl.ds(start, 256)
            up = dot(hm[which], units[:, span]) + vectors[4:5, span]
            value, slope = gelu_terms(up)
            act[slot, :, span] = value.astype(BF16)
            pulled = contract_last(dys[which], wd_ref[span, :])
            grad[slot, :, span] = (pulled * slope).astype(BF16)
        for copy in store_du(slot, which):
            copy.start()
        store_dy(which).start()
        sum_out[0:1, :] += jnp.sum(dys[which].astype(F32), 0, keepdims=True)

    for step, place in enumerate(order):

        def one(other, _, step=step, place=place):
            @pl.when(other == 1)
            def _():
                if 0 < step < PAIRS - 1:
                    relay_dy.start(step + 1)
                if step > 0:
                    relay_dy.pass_halves(step)
                relay_dy.wait_over(step, place)

            if step > 0:
                for copy in store_du(other, member(step - 1, other)):
                    copy.wait()
            pull(other, member(step, other))

        lax.fori_loop(0, 2, one, None)

    relay_x.finish()
    relay_dy.finish()
    spread_do.finish()
    head_columns.finish()
    unit_columns.finish()
    for step in range(1, QUARTERS):
        other = lax.rem(quarter + step, QUARTERS)
        back(other, quarter).wait_send()
        back(other, other).wait_recv()
    own_back.wait()

    def sent(step, _):
        target = lax.rem(rank + step, TEAM)
        vector_copy(rank, target, target).wait_send()

    lax.fori_loop(1, TEAM, sent, None)

    def stored(which, _):
        for copy in store_x(which):
            copy.wait()
        store_dy(which).wait()

    lax.fori_loop(0, TEAM, stored, None)
    for other in range(2):
        store_ha(other, member(PAIRS - 1, other)).wait()
        for copy in store_du(other, member(PAIRS - 1, other)):
            copy.wait()
    for copy in late:
        copy.wait()


def gather(x, dy, parameters, w_out, w_down, tables, w_qkv, w_up):
    tokens, width = x.shape
    hidden, rows = w_down.shape[0], w_qkv.shape[0]
    all_tokens = (TEAM, tokens, width)
    whole = (2, 3, QUARTERS * tokens, HEAD)
    marks = ((2, QUARTERS, 8, tokens), F32)
    vec = (VECTOR_ROWS, rows)
    vecs = ((TEAM, *vec), F32)
    units = ((TEAM, tokens, hidden), BF16)
    shapes = [
        (all_tokens, BF16),
        (all_tokens, BF16),
        (all_tokens, BF16),
        ((width, 3 * HEAD), BF16),
        ((width, hidden), BF16),
        (whole, BF16),
        marks,
        vecs,
        (all_tokens, BF16),
        units,
        units,
        ((2, QUARTERS * tokens, HEAD), BF16),
        ((2, QUARTERS, tokens, HEAD), BF16),
        ((8, width), F32),
    ]
    return pl.pallas_call(
        gather_kernel,
        out_shape=[jax.ShapeDtypeStruct(*shape) for shape in shapes],
        in_specs=[ANY] * 2 + [VMEM] * 7 + [ANY] * 7,
        out_specs=[ANY] * 13 + [VMEM],
        scratch_shapes=[
            pltpu.VMEM(all_tokens, BF16),
            pltpu.VMEM(all_tokens, BF16),
            pltpu.VMEM(all_tokens, BF16),
            pltpu.VMEM((width, 3 * HEAD), BF16),
            pltpu.VMEM((width, hidden), BF16),
            pltpu.VMEM(vec, F32),
            pltpu.VMEM(*vecs),
            pltpu.VMEM((8, width), F32),
            pltpu.VMEM((2, tokens, width), BF16),
            pltpu.VMEM((TEAM, 3, tokens, HEAD), BF16),
            pltpu.VMEM(whole, BF16),
            pltpu.VMEM(*marks),
            pltpu.VMEM((2, QUARTERS * tokens, HEAD), BF16),
            pltpu.VMEM((2, tokens, hidden), BF16),
            pltpu.VMEM((2, tokens, hidden), BF16),
            pltpu.VMEM((TEAM, tokens, HEAD), BF16),
            pltpu.VMEM((3, tokens, 128), F32),
            pltpu.VMEM(w_out.shape, BF16),
            pltpu.VMEM(w_down.shape, BF16),
            DMA((2,)),
            DMA((7,)),
            DMA((2, TEAM)),
            DMA((2,)),
            DMA((2, 2)),
            DMA((TEAM,)),
            DMA((5,)),
            DMA((TEAM,)),
            DMA((TEAM,)),
            DMA((QUARTERS,)),
            DMA((QUARTERS,)),
        ]
        + RELAY_SEMS * 2
        + column_sems(3)
        + column_sems(1)
        + spread_sems(2)
        + spread_sems(1),
        compiler_params=pltpu.CompilerParams(
            collective_id=0, has_side_effects=True, vmem_limit_bytes=LIMIT
        ),
        name="gather",
    )(x, dy, *parameters, w_out, w_down, *tables, w_qkv, w_up)


def backward_kernel(
    qkv_ref, do_ref, marks_ref, cos_ref, above_ref, below_ref, d_ref, dk_sum, dv_sum
):
    scale = HEAD ** (-0.5)
    q_ref, k_ref, v_ref = (qkv_ref.at[kind] for kind in range(3))
    length = q_ref.shape[0]
    size = marks_ref.shape[-1]

    def put(kind, rows, grads):
        low = unrotate_low(
            grads[:, :128], cos_ref[rows, :], above_ref[rows, :], below_ref[rows, :]
        )
        d_ref[kind, rows, pl.ds(0, 128)] = low.astype(BF16)
        d_ref[kind, rows, pl.ds(128, HEAD - 128)] = grads[:, 128:].astype(BF16)

    dk_sum[...] = jnp.zeros_like(dk_sum)
    dv_sum[...] = jnp.zeros_like(dv_sum)
    for block in range(length // size):
        start = block * size
        rows, keys = pl.ds(start, size), pl.ds(0, start + size)
        probs = probabilities(block, size, q_ref, k_ref, marks_ref)
        grads = do_ref[rows, :]
        grad_probs = contract_last(grads, v_ref[keys, :])
        row_dot = jnp.sum(probs * grad_probs, -1, keepdims=True)
        grad_scores = (probs * (grad_probs - row_dot)).astype(BF16)
        put(0, rows, dot(grad_scores, k_ref[keys, :]) * scale)
        dk_sum[keys, :] += contract_first(grad_scores, q_ref[rows, :])
        dv_sum[keys, :] += contract_first(probs.astype(BF16), grads)
    put(1, pl.ds(0, length), dk_sum[...] * scale)
    d_ref[2] = dv_sum[...].astype(BF16)


def attend_back(qkv, grads, marks, tables):
    seqs, _, length, head = qkv.shape
    three = pl.BlockSpec((None, 3, length, HEAD), lambda s: (s, 0, 0, 0))
    one = pl.BlockSpec((None, length, HEAD), lambda s: (s, 0, 0))
    table = pl.BlockSpec((length, 128), lambda s: (0, 0))
    return pl.pallas_call(
        backward_kernel,
        grid=(seqs,),
        in_specs=[three, one, pl.BlockSpec((None, *marks.shape[1:]), lambda s: (s, 0, 0, 0))]
        + [table] * 3,
        out_specs=three,
        out_shape=jax.ShapeDtypeStruct(qkv.shape, BF16),
        scratch_shapes=[pltpu.VMEM((length, head), F32)] * 2,
        compiler_params=pltpu.CompilerParams(vmem_limit_bytes=48 << 20),
        name="attend_back",
    )(qkv, grads, marks, *tables)


class Reduce:
    def __init__(self, cut, own, side_out, side_in, line_in, half_in, sems):
        self.cut = cut
        self.own, self.side_out, self.side_in = own, side_out, side_in
        self.line_in, self.half_in, self.sems = line_in, half_in, sems
        self.base, self.line, self.side, self.quarter = spot()
        self.order = near_first(self.line)
        self.inner = (self.line > 0) & (self.line < PAIRS - 1)
        self.tokens = own.shape[1]

    def over(self, step, low):
        side_send, side_recv = self.sems[:2]
        place = self.base + self.line * 2 + 1 - self.side
        rows = pl.ds(self.cut, self.tokens - self.cut) if low else pl.ds(0, self.tokens)
        return send(
            self.side_out.at[step, rows], self.side_in.at[step, rows],
            side_send.at[step], side_recv.at[step], place, self.quarter,
        )

    def crossing(self, step, act):
        if step == PAIRS - 1:
            act(self.over(step, True))
        elif step == 1:
            act(self.over(step, False))
        else:
            first, second = (True, False) if step == PAIRS - 2 else (False, True)
            pl.when(self.inner)(lambda: act(self.over(step, first)))
            pl.when(jnp.logical_not(self.inner))(lambda: act(self.over(step, second)))

    def along(self, step, target, way):
        line_send, line_recv = self.sems[2:4]
        move = 1 if way == RIGHT else -1
        slot = target if way == RIGHT else jnp.where(target == self.line - 1, PAIRS, target)
        place = self.base + (self.line + move) * 2 + self.side
        return send(
            self.side_out.at[step], self.line_in.at[slot], line_send.at[step], line_recv.at[slot],
            place, self.quarter,
        )

    def arrive(self, slot):
        line_send, line_recv = self.sems[2:4]
        return send(
            self.side_out.at[0], self.line_in.at[slot], line_send.at[0], line_recv.at[slot],
            self.base + self.line * 2 + 1 - self.side, self.quarter,
        )

    def upper(self, step, way):
        half_send, half_recv = self.sems[4:6]
        move = 1 if way == RIGHT else -1
        rows = pl.ds(0, self.cut)
        place = self.base + (self.line + move) * 2 + self.side
        return send(
            self.side_out.at[step, rows], self.half_in.at[way], half_send.at[way],
            half_recv.at[way], place, self.quarter,
        )

    def upper_over(self):
        cross_send, cross_recv = self.sems[6:8]
        rows = pl.ds(0, self.cut)
        place = self.base + self.line * 2 + 1 - self.side
        return send(
            self.side_out.at[0, rows], self.side_in.at[0, rows], cross_send, cross_recv, place,
            self.quarter,
        )

    def begin(self, step):
        self.crossing(step, lambda copy: copy.start())

    def launch(self):
        pl.when(self.line == 0)(lambda: self.upper(PAIRS - 1, RIGHT).start())
        pl.when(self.line == PAIRS - 1)(lambda: self.upper(PAIRS - 1, LEFT).start())

    def hop(self, count):
        for way in (RIGHT, LEFT):
            here = count if way == RIGHT else PAIRS - 1 - count
            step = (None, PAIRS - 1, PAIRS - 2, 0)[count]

            @pl.when(self.line == here)
            def _(way=way, step=step):
                self.upper(step, way).wait_recv()
                rows = pl.ds(0, self.cut)
                total = self.side_out[step, rows].astype(F32) + self.half_in[way].astype(F32)
                self.side_out[step, rows] = total.astype(BF16)
                if count < PAIRS - 1:
                    self.upper(step, way).start()
                else:
                    self.upper_over().start()

    def upper_sent(self, step):
        first, second = (RIGHT, LEFT) if step == PAIRS - 1 else (LEFT, RIGHT)
        low_line = self.line < PAIRS // 2

        def wait():
            pl.when(low_line)(lambda: self.upper(step, first).wait_send())
            pl.when(jnp.logical_not(low_line))(lambda: self.upper(step, second).wait_send())

        if step == PAIRS - 1:
            wait()
        elif step == PAIRS - 2:
            pl.when(self.inner)(wait)

    def mine(self, step, index, strip):
        chunk = pl.ds(pl.multiple_of(index * strip, strip), strip)
        slot = step if self.own.shape[0] > 1 else 0
        own = self.own[slot, chunk, :].astype(F32)
        other = self.side_in[step, chunk, :].astype(F32)
        if step == PAIRS - 1:
            return jnp.where(index * strip >= self.cut, own + other, own)
        if step == PAIRS - 2:
            whole = (index * strip >= self.cut) | jnp.logical_not(self.inner)
            return jnp.where(whole, own + other, own)
        return own + other

    def advance(self, step):
        target = self.order[step]
        self.crossing(step, lambda copy: copy.wait_recv())
        self.crossing(step, lambda copy: copy.wait_send())
        self.upper_sent(step)

        def forward(way, upstream):
            pl.when(upstream)(lambda: self.arrive(target).wait_recv())
            strip = 64

            def add(index, _):
                chunk = pl.ds(pl.multiple_of(index * strip, strip), strip)
                total = self.mine(step, index, strip)
                passing = self.line_in[target, chunk, :].astype(F32)
                total = jnp.where(upstream, total + passing, total)
                self.side_out[step, chunk, :] = total.astype(BF16)

            lax.fori_loop(0, self.tokens // strip, add, None)
            self.along(step, target, way).start()

        pl.when(target > self.line)(lambda: forward(RIGHT, self.line > 0))
        pl.when(target < self.line)(lambda: forward(LEFT, self.line < PAIRS - 1))

    def last(self):
        self.crossing(0, lambda copy: copy.wait_recv())
        self.crossing(0, lambda copy: copy.wait_send())

        @pl.when(jnp.logical_not(self.inner))
        def _():
            self.upper_over().wait_recv()
            self.upper_over().wait_send()

        pl.when(self.line > 0)(lambda: self.arrive(self.line).wait_recv())
        pl.when(self.line < PAIRS - 1)(lambda: self.arrive(PAIRS).wait_recv())

    def total(self, index, strip):
        chunk = pl.ds(pl.multiple_of(index * strip, strip), strip)
        total = self.mine(0, index, strip)
        left = self.line_in[self.line, chunk, :].astype(F32)
        right = self.line_in[PAIRS, chunk, :].astype(F32)
        total = jnp.where(self.line > 0, total + left, total)
        return jnp.where(self.line < PAIRS - 1, total + right, total)

    def finish(self):
        for step in range(1, PAIRS):
            target = self.order[step]
            pl.when(target > self.line)(lambda: self.along(step, target, RIGHT).wait_send())
            pl.when(target < self.line)(lambda: self.along(step, target, LEFT).wait_send())


REDUCE = 13


def reduce_scratch(tokens, width, slots, dtype, cut):
    return [
        pltpu.VMEM((slots, tokens, width), dtype),
        pltpu.VMEM((PAIRS, tokens, width), BF16),
        pltpu.VMEM((PAIRS, tokens, width), BF16),
        pltpu.VMEM((PAIRS + 1, tokens, width), BF16),
        pltpu.VMEM((2, cut, width), BF16),
        DMA((PAIRS,)),
        DMA((PAIRS,)),
        DMA((PAIRS,)),
        DMA((PAIRS + 1,)),
        DMA((2,)),
        DMA((2,)),
        DMA,
        DMA,
    ]


class Quarters:
    def __init__(self, keep, away, came, far, core_send, core_recv, chip_send, chip_recv):
        self.keep, self.away, self.came, self.far = keep, away, came, far
        self.sems = core_send, core_recv, chip_send, chip_recv
        base, line, side, self.quarter = spot()
        self.place = base + line * 2 + side
        self.core, self.chip = lax.rem(self.quarter, 2), lax.div(self.quarter, 2)
        self.tiles = keep.shape[0]

    def to_core(self, tile):
        return send(
            self.away.at[tile], self.came.at[tile], self.sems[0].at[tile], self.sems[1].at[tile],
            self.place, core_peer(self.quarter),
        )

    def to_chip(self, tile):
        return send(
            self.away.at[tile, 0], self.far.at[tile], self.sems[2].at[tile], self.sems[3].at[tile],
            self.place, chip_peer(self.quarter),
        )

    def put(self, tile, quarter_of):
        for chip in range(2):
            self.keep[tile, chip] = quarter_of(2 * chip + self.core).astype(BF16)
            self.away[tile, chip] = quarter_of(2 * chip + 1 - self.core).astype(BF16)
        self.to_core(tile).start()

    def over_cores(self):
        def one(tile, _):
            self.to_core(tile).wait_recv()
            self.to_core(tile).wait_send()
            other = 1 - self.chip
            passed = self.keep[tile, other].astype(F32) + self.came[tile, other].astype(F32)
            self.away[tile, 0] = passed.astype(BF16)
            self.to_chip(tile).start()
            kept = self.keep[tile, self.chip].astype(F32)
            kept = kept + self.came[tile, self.chip].astype(F32)
            self.keep[tile, self.chip] = kept.astype(BF16)

        lax.fori_loop(0, self.tiles, one, None)

    def over_chips(self, then):
        def one(tile, _):
            self.to_chip(tile).wait_recv()
            total = self.keep[tile, self.chip].astype(F32) + self.far[tile].astype(F32)
            self.keep[tile, self.chip] = total.astype(BF16)
            then(tile)

        lax.fori_loop(0, self.tiles, one, None)

    def total(self, tile):
        return self.keep.at[tile, self.chip]

    def finish(self):
        lax.fori_loop(0, self.tiles, lambda tile, _: self.to_chip(tile).wait_send(), None)


def quarters_scratch(tiles, rows, columns):
    return [
        pltpu.VMEM((tiles, 2, rows, columns), BF16),
        pltpu.VMEM((tiles, 2, rows, columns), BF16),
        pltpu.VMEM((tiles, 2, rows, columns), BF16),
        pltpu.VMEM((tiles, rows, columns), BF16),
    ] + [DMA((tiles,))] * 4


class Stream:
    def __init__(self, source, slots, sems):
        self.source, self.slots, self.sems = source, slots, sems

    def copy(self, tile):
        size = self.slots.shape[-1]
        start = pl.multiple_of(tile * size, size)
        slot = lax.rem(tile, 2)
        return pltpu.make_async_copy(
            self.source.at[:, pl.ds(start, size)], self.slots.at[slot], self.sems.at[slot]
        )

    def run(self, tiles, use):
        def one(tile, _):
            self.copy(tile).wait()
            use(tile, self.slots.at[lax.rem(tile, 2)])
            pl.when(tile + 2 < tiles)(lambda: self.copy(tile + 2).start())

        lax.fori_loop(0, tiles, one, None)


def third_kernel(
    vec_ref, x_in, o_in, a_in, wo_in, wd_in, du_in, d_ref, hm_ref, dy_ref,
    result_out, back_out, up_out, rows_out,
    x_ref, o_ref, a_ref, wo_ref, wd_ref, du_ref, in_sem, own_sem, back_send, back_recv, load_sem, store_sem, hm_tiles, tile_sum, dy, bias, *rest,
):
    base, line, side, quarter = spot()
    rank = line * 2 + side
    tokens, width = x_ref.shape
    part = width // TEAM // QUARTERS
    reduce = Reduce(tokens // 2, *rest[:5], rest[5:REDUCE])
    rest = rest[REDUCE:]
    ups, downs = Quarters(*rest[:8]), Quarters(*rest[8:16])
    stream = Stream(hm_ref, hm_tiles, load_sem)
    loads = [
        pltpu.make_async_copy(src, dst, in_sem.at[index])
        for index, (src, dst) in enumerate(
            (
                (o_in, o_ref), (wo_in, wo_ref), (a_in, a_ref), (wd_in, wd_ref), (du_in, du_ref),
                (x_in, x_ref),
            )
        )
    ]
    for copy in loads:
        copy.start()
    load_dy = pltpu.make_async_copy(dy_ref, dy, own_sem.at[3])
    load_dy.start()
    for tile in range(2):
        stream.copy(tile).start()
    greet_line(base, line, side, quarter)

    def pieces(to, origin, kind):
        return (
            d_ref.at[:, kind, pl.ds(to * tokens, tokens), :],
            back_out.at[:, among(origin), :, pl.ds(kind * HEAD, HEAD)],
        )

    def back(to, origin, kind):
        src, dst = pieces(to, origin, kind)
        return send(
            src, dst, back_send.at[to, kind], back_recv.at[origin, kind], base + rank, to
        )

    own_back = [
        pltpu.make_async_copy(*pieces(quarter, quarter, kind), own_sem.at[kind])
        for kind in range(3)
    ]

    def make(which, put):
        rows = pl.ds(pl.multiple_of(which * tokens, tokens), tokens)
        for start in range(0, width, 512):
            span = pl.ds(start, 512)
            put(
                span,
                dot(o_ref[rows, :], wo_ref[:, span]) + dot(a_ref[rows, :], wd_ref[:, span]),
            )

    def put_own(span, value):
        reduce.own[0, :, span] = value.astype(BF16)

    for copy in loads:
        copy.wait()
    for step in reversed(range(PAIRS)):

        def put_out(span, value, step=step):
            reduce.side_out[step, :, span] = value.astype(BF16)

        make(reduce.order[step] * 2 + 1 - side, put_out)
        reduce.begin(step)
        if step == PAIRS - 1:
            reduce.launch()
            for kind in range(3):
                own_back[kind].start()
                for hop in range(1, QUARTERS):
                    back(lax.rem(quarter + hop, QUARTERS), quarter, kind).start()

    def up_tile(tile, held):
        for start in range(0, tile_sum.shape[1], 512):
            span = pl.ds(start, 512)
            tile_sum[:, span] = contract_first(held[...], du_ref[:, span])
        ups.put(tile, lambda q: tile_sum[pl.ds(pl.multiple_of(q * part, part), part), :])

    stream.run(TEAM, up_tile)
    reduce.hop(1)
    ups.over_cores()
    make(reduce.order[3] * 2 + side, put_own)
    reduce.advance(3)
    reduce.hop(2)
    load_dy.wait()
    share = width // QUARTERS

    def down_tile(source, first, tile, _):
        columns = pl.ds(pl.multiple_of(tile * 128, 128), 128)
        rows = source[:, columns]

        def quarter_of(q):
            span = pl.ds(pl.multiple_of(q * share, share), share)
            return contract_first(rows, dy[:, span])

        downs.put(first + tile, quarter_of)

    hidden = a_ref.shape[1] // 128
    lax.fori_loop(0, hidden, partial(down_tile, a_ref, 0), None)
    lax.fori_loop(0, HEAD // 128, partial(down_tile, o_ref, hidden), None)
    make(reduce.order[2] * 2 + side, put_own)
    reduce.advance(2)
    reduce.hop(3)
    downs.over_cores()
    make(reduce.order[1] * 2 + side, put_own)
    reduce.advance(1)
    make(rank, put_own)

    def store_up(tile):
        return pltpu.make_async_copy(ups.total(tile), up_out.at[tile], store_sem.at[0])

    def store_down(tile):
        rows = pl.ds(pl.multiple_of(tile * 128, 128), 128)
        return pltpu.make_async_copy(downs.total(tile), rows_out.at[rows, :], store_sem.at[1])

    ups.over_chips(lambda tile: store_up(tile).start())
    block = width // TEAM
    for source in range(TEAM):
        bias[0:1, pl.ds(source * block, block)] = vec_ref[source, 4:5, :] + vec_ref[source, 5:6, :]
    reduce.last()
    strip = 64

    def close(index, _):
        chunk = pl.ds(pl.multiple_of(index * strip, strip), strip)
        total = reduce.total(index, strip) + bias[0:1, :]
        reduce.own[0, chunk, :] = (x_ref[chunk, :].astype(F32) + total).astype(BF16)

    lax.fori_loop(0, tokens // strip, close, None)
    store_result = pltpu.make_async_copy(reduce.own.at[0], result_out, store_sem.at[2])
    store_result.start()
    downs.over_chips(lambda tile: store_down(tile).start())
    reduce.finish()
    for kind in range(3):
        own_back[kind].wait()
        for hop in range(1, QUARTERS):
            origin = lax.rem(quarter + hop, QUARTERS)
            back(origin, quarter, kind).wait_send()
            back(origin, origin, kind).wait_recv()
    store_result.wait()
    ups.finish()
    downs.finish()
    lax.fori_loop(0, ups.tiles, lambda tile, _: store_up(tile).wait(), None)
    lax.fori_loop(0, downs.tiles, lambda tile, _: store_down(tile).wait(), None)


def third(x, attended, activated, w_out, w_down, vectors, grad_up, grads, mlp_input, grad_rows):
    tokens, width = x.shape
    hidden = activated.shape[-1]
    part, share = width // TEAM // QUARTERS, width // QUARTERS
    tiles = (hidden + HEAD) // 128
    shapes = [
        (tokens, width),
        (2, QUARTERS, tokens, 3 * HEAD),
        (TEAM, part, hidden),
        (tiles * 128, share),
    ]
    return pl.pallas_call(
        third_kernel,
        out_shape=[jax.ShapeDtypeStruct(shape, BF16) for shape in shapes],
        in_specs=[VMEM] + [ANY] * 9,
        out_specs=[ANY] * 4,
        scratch_shapes=[
            pltpu.VMEM(values.shape, BF16)
            for values in (x, attended, activated, w_out, w_down, grad_up)
        ]
        + [
            DMA((6,)),
            DMA((4,)),
            DMA((QUARTERS, 3)),
            DMA((QUARTERS, 3)),
            DMA((2,)),
            DMA((3,)),
            pltpu.VMEM((2, TEAM * tokens, width // TEAM), BF16),
            pltpu.VMEM((width // TEAM, hidden), F32),
            pltpu.VMEM((TEAM * tokens, width), BF16),
            pltpu.VMEM((8, width), F32),
        ]
        + reduce_scratch(tokens, width, 1, BF16, tokens // 2)
        + quarters_scratch(TEAM, part, hidden)
        + quarters_scratch(tiles, 128, share),
        compiler_params=pltpu.CompilerParams(
            collective_id=2, has_side_effects=True, vmem_limit_bytes=LIMIT
        ),
        name="scatter_result",
    )(vectors, x, attended, activated, w_out, w_down, grad_up, grads, mlp_input, grad_rows)


def fourth_kernel(
    vec_ref, dy_sum_ref, x_in, dy_in, dqkv_in, du_in, xs_ref, wq_ref, wu_ref, ha_ref, up_ref, rows_ref,
    grad_ref, landed, rows_out, vector_ref,
    x_ref, dy_ref, dqkv_ref, du_ref, wq, wu, xs, gains, load_sem, xs_sem, tile_load, ha_tiles, tile_sum, sums, packets, packets_in, ring, ring_in,
    row_own, row_send, row_recv, pack_send, pack_recv, ring_send, ring_recv, *rest,
):
    base, line, side, quarter = spot()
    rank = line * 2 + side
    tokens, width = x_ref.shape
    hidden = du_ref.shape[1]
    part = width // TEAM // QUARTERS
    block = width // TEAM
    core, chip = core_peer(quarter), chip_peer(quarter)
    reduce = Reduce(tokens // 4, *rest[:5], rest[5:REDUCE])
    rest = rest[REDUCE:]
    qkvs = Quarters(*rest[:8])

    def place(source, slice_of, lane, lanes):
        rows = pl.ds(pl.multiple_of(slice_of * part, 16), part)
        return landed.at[source, rows, pl.ds(lane, lanes)]

    up_columns = Columns(
        lambda n: [(up_ref.at[n], 3 * HEAD, hidden)], place, 3 * HEAD, hidden, rest[8:17]
    )
    qkv_columns = Columns(
        lambda n: [(qkvs.total(n), 0, 3 * HEAD)], place, 0, 3 * HEAD, rest[17:26]
    )
    stream = Stream(ha_ref, ha_tiles, tile_load)
    loads = [
        pltpu.make_async_copy(src, dst, load_sem.at[index])
        for index, (src, dst) in enumerate(
            (
                (dqkv_in, dqkv_ref), (wq_ref, wq), (du_in, du_ref), (wu_ref, wu), (x_in, x_ref),
                (dy_in, dy_ref),
            )
        )
    ]
    for copy in loads:
        copy.start()

    def load_x(which):
        return pltpu.make_async_copy(xs_ref.at[which], xs.at[which], xs_sem.at[which])

    for other in (1 - side, side):
        for step in reversed(range(PAIRS)):
            load_x(reduce.order[step] * 2 + other).start()
    for tile in range(2):
        stream.copy(tile).start()
    greet_team(base, line, side, quarter)

    def rows_copy(which, slice_of, to):
        src = rows_ref if which < 2 else rows_out.at[slice_of]
        return send(
            src, rows_out.at[slice_of], row_send.at[which], row_recv.at[which], base + rank, to
        )

    own_rows = pltpu.make_async_copy(rows_ref, rows_out.at[quarter], row_own)
    own_rows.start()
    rows_copy(0, quarter, core).start()
    sums[...] = jnp.zeros_like(sums)
    for source in range(TEAM):
        gains[0:2, pl.ds(source * block, block)] = vec_ref[source, 0:2, :]
    for copy in loads:
        copy.wait()

    def make(which, put):
        rows = pl.ds(pl.multiple_of(which * tokens, tokens), tokens)
        load_x(which).wait()
        values = xs[which].astype(F32)
        average = jnp.mean(values, -1, keepdims=True)
        variance = jnp.mean(jnp.square(values - average), -1, keepdims=True)
        inverse = lax.rsqrt(variance + EPSILON)
        for start in range(0, width, 512):
            span = pl.ds(start, 512)
            attn = contract_last(dqkv_ref[rows, :], wq[span, :])
            mlp = contract_last(du_ref[rows, :], wu[span, :])
            unit = (xs[which, :, span].astype(F32) - average) * inverse
            sums[0:1, span] += jnp.sum(attn * unit, 0, keepdims=True)
            sums[1:2, span] += jnp.sum(mlp * unit, 0, keepdims=True)
            sums[2:3, span] += jnp.sum(attn, 0, keepdims=True)
            sums[3:4, span] += jnp.sum(mlp, 0, keepdims=True)
            put(span, attn * gains[0:1, span] + mlp * gains[1:2, span])
        sums[4:5, pl.ds(0, hidden)] += jnp.sum(du_ref[rows, :].astype(F32), 0, keepdims=True)
        sums[5:6, pl.ds(0, 3 * HEAD)] += jnp.sum(
            dqkv_ref[rows, :].astype(F32), 0, keepdims=True
        )

    for step in reversed(range(PAIRS)):

        def put_out(span, value, step=step):
            reduce.side_out[step, :, span] = value.astype(BF16)

        make(reduce.order[step] * 2 + 1 - side, put_out)
        reduce.begin(step)
        if step == PAIRS - 1:
            reduce.launch()
            up_columns.start()

    def qkv_tile(tile, held):
        tile_sum[...] = contract_first(held[...], dqkv_ref[...])
        qkvs.put(tile, lambda q: tile_sum[pl.ds(pl.multiple_of(q * part, part), part), :])

    stream.run(TEAM, qkv_tile)
    qkvs.over_cores()
    rows_copy(1, quarter, chip).start()
    reduce.hop(1)
    for step in reversed(range(PAIRS)):

        def put_own(span, value, step=step):
            reduce.own[step, :, span] = value.astype(BF16)

        make(reduce.order[step] * 2 + side, put_own)
        if step == PAIRS - 1:
            reduce.advance(step)

    reduce.hop(2)

    def pack(target, _):
        span = pl.ds(pl.multiple_of(target * block, block), block)
        packets[target, pl.ds(0, 4), :] = sums[pl.ds(0, 4), span]
        packets[target, pl.ds(4, 1), :] = jnp.where(target == rank, dy_sum_ref[0:1, span], 0.0)
        for index in range(3):
            chunk = 3 * target + index
            kind = lax.div(chunk, HEADS)
            lanes = pl.ds(pl.multiple_of(kind * HEAD, HEAD), HEAD)
            packets[target, pl.ds(5 + index, 1), :] = jnp.where(
                lax.rem(chunk, HEADS) == rank, sums[5:6, lanes], 0.0
            )

    lax.fori_loop(0, TEAM, pack, None)

    def pack_copy(source, target, peer):
        return send(
            packets.at[target], packets_in.at[source], pack_send.at[target], pack_recv.at[source],
            base + peer, quarter,
        )

    def deal_packets(step, _):
        target = lax.rem(rank + step, TEAM)
        pack_copy(rank, target, target).start()

    lax.fori_loop(1, TEAM, deal_packets, None)
    packets_in[rank] = packets[rank]

    up_columns.forward()
    reduce.advance(2)
    reduce.hop(3)
    qkvs.over_chips(lambda tile: None)
    qkv_columns.start()
    reduce.advance(1)
    rows_copy(1, chip, chip).wait_recv()
    rows_copy(2, chip, core).start()
    up_columns.forward_last()

    def take_packets(step, _):
        source = lax.rem(rank + TEAM - step, TEAM)
        pack_copy(source, rank, source).wait_recv()

    lax.fori_loop(1, TEAM, take_packets, None)
    total = packets_in[0]
    for source in range(1, TEAM):
        total = total + packets_in[source]
    ring[pl.ds(0, 8), :] = total
    for index in range(hidden // block):
        ring[pl.ds(8 + index, 1), :] = sums[4:5, pl.ds(index * block, block)]

    def ring_copy(to, origin, peer):
        return send(
            ring, ring_in.at[origin], ring_send.at[to], ring_recv.at[origin], base + rank, peer
        )

    for hop in range(1, QUARTERS):
        to = lax.rem(quarter + hop, QUARTERS)
        ring_copy(to, quarter, to).start()
    ring_in[quarter] = ring[...]
    qkv_columns.forward()
    reduce.last()
    strip = 64

    def close(index, _):
        chunk = pl.ds(pl.multiple_of(index * strip, strip), strip)
        pulled = reduce.total(index, strip)
        unit, inverse = normalize(x_ref[chunk, :].astype(F32))
        pulled = (
            pulled
            - jnp.mean(pulled, -1, keepdims=True)
            - unit * jnp.mean(pulled * unit, -1, keepdims=True)
        )
        grad_ref[chunk, :] = (dy_ref[chunk, :].astype(F32) + inverse * pulled).astype(BF16)

    lax.fori_loop(0, tokens // strip, close, None)
    qkv_columns.forward_last()
    for hop in range(1, QUARTERS):
        origin = lax.rem(quarter + hop, QUARTERS)
        ring_copy(quarter, origin, origin).wait_recv()
    vector_ref[...] = (ring_in[0] + ring_in[1]) + (ring_in[2] + ring_in[3])

    reduce.finish()
    qkvs.finish()
    own_rows.wait()
    rows_copy(0, core, core).wait_recv()
    rows_copy(2, chip_peer(core), core).wait_recv()
    rows_copy(0, quarter, core).wait_send()
    rows_copy(1, quarter, chip).wait_send()
    rows_copy(2, chip, core).wait_send()
    for columns in (up_columns, qkv_columns):
        columns.arrive()
        columns.finish()

    def sent_packets(step, _):
        target = lax.rem(rank + step, TEAM)
        pack_copy(rank, target, target).wait_send()

    lax.fori_loop(1, TEAM, sent_packets, None)
    for hop in range(1, QUARTERS):
        to = lax.rem(quarter + hop, QUARTERS)
        ring_copy(to, quarter, to).wait_send()


def fourth(
    x, dy, grad_qkv, grad_up, vectors, dy_sum, everyone, w_qkv, w_up, attn_input, up_sums, row_sums
):
    tokens, width = x.shape
    hidden = grad_up.shape[-1]
    part, block = width // TEAM // QUARTERS, width // TEAM
    shapes = [
        ((tokens, width), BF16),
        ((TEAM, block, 3 * HEAD + hidden), BF16),
        ((QUARTERS, *row_sums.shape), BF16),
        ((16, block), F32),
    ]
    return pl.pallas_call(
        fourth_kernel,
        out_shape=[jax.ShapeDtypeStruct(*shape) for shape in shapes],
        in_specs=[VMEM] * 2 + [ANY] * 10,
        out_specs=[VMEM, ANY, ANY, VMEM],
        scratch_shapes=[
            pltpu.VMEM(x.shape, BF16),
            pltpu.VMEM(dy.shape, BF16),
            pltpu.VMEM(grad_qkv.shape, BF16),
            pltpu.VMEM(grad_up.shape, BF16),
            pltpu.VMEM(w_qkv.shape, BF16),
            pltpu.VMEM(w_up.shape, BF16),
            pltpu.VMEM(everyone.shape, BF16),
            pltpu.VMEM((8, width), F32),
            DMA((6,)),
            DMA((TEAM,)),
            DMA((2,)),
            pltpu.VMEM((2, TEAM * tokens, block), BF16),
            pltpu.VMEM((block, 3 * HEAD), F32),
            pltpu.VMEM((8, width), F32),
            pltpu.VMEM((TEAM, 8, block), F32),
            pltpu.VMEM((TEAM, 8, block), F32),
            pltpu.VMEM((16, block), F32),
            pltpu.VMEM((QUARTERS, 16, block), F32),
            DMA,
            DMA((3,)),
            DMA((3,)),
            DMA((TEAM,)),
            DMA((TEAM,)),
            DMA((QUARTERS,)),
            DMA((QUARTERS,)),
        ]
        + reduce_scratch(tokens, width, PAIRS, BF16, tokens // 4)
        + quarters_scratch(TEAM, part, 3 * HEAD)
        + column_sems(1) * 2,
        compiler_params=pltpu.CompilerParams(
            collective_id=3, has_side_effects=True, vmem_limit_bytes=LIMIT
        ),
        name="scatter_grad",
    )(
        vectors, dy_sum, x, dy, grad_qkv, grad_up, everyone, w_qkv, w_up, attn_input, up_sums,
        row_sums,
    )


def settle_kernel(
    vector_ref, columns_ref, rows_ref, result_ref, grad_ref,
    gain_out, shift_out, bias_out, bias_again, qkv_bias_out, up_bias_out,
    qkv_out, up_out, down_out, out_out, result_out, grad_out,
    low, wide, low_rows, wide_rows, passing, load_sem, store_sem, rows_load, rows_store, copy_sem,
):
    team, block, span = columns_ref.shape
    quarters, tall, share = rows_ref.shape
    width = team * HEAD
    hidden = span - 3 * HEAD
    plain = [
        (
            pltpu.make_async_copy(src, passing.at[index], copy_sem.at[index, 0]),
            pltpu.make_async_copy(passing.at[index], dst, copy_sem.at[index, 1]),
        )
        for index, (src, dst) in enumerate(((result_ref, result_out), (grad_ref, grad_out)))
    ]
    for load_in, _ in plain:
        load_in.start()
    size = vector_ref.shape[1]
    gain_out[...] = vector_ref[0:2, :]
    shift_out[...] = vector_ref[2:4, :]
    bias_out[...] = vector_ref[4:5, :].reshape(size)
    bias_again[...] = vector_ref[4:5, :].reshape(size)
    for index in range(3):
        row = vector_ref[5 + index : 6 + index, :]
        qkv_bias_out[pl.ds(index * size, size)] = row.reshape(size)
    for index in range(hidden // size):
        row = vector_ref[8 + index : 9 + index, :]
        up_bias_out[pl.ds(index * size, size)] = row.reshape(size)

    def load(source):
        slot = lax.rem(source, 2)
        return pltpu.make_async_copy(columns_ref.at[source], low.at[slot], load_sem.at[slot])

    def stores(source):
        slot = lax.rem(source, 2)
        pairs = []
        for kind in range(3):
            start = pl.multiple_of(kind * width + source * HEAD, HEAD)
            pairs.append((pl.ds(kind * HEAD, HEAD), qkv_out.at[:, pl.ds(start, HEAD)]))
        start = pl.multiple_of(source * hidden, hidden)
        pairs.append((pl.ds(3 * HEAD, hidden), up_out.at[:, pl.ds(start, hidden)]))
        return [
            pltpu.make_async_copy(wide.at[slot, :, lanes], dst, store_sem.at[slot, index])
            for index, (lanes, dst) in enumerate(pairs)
        ]

    def load_rows(quarter):
        slot = lax.rem(quarter, 2)
        return pltpu.make_async_copy(rows_ref.at[quarter], low_rows.at[slot], rows_load.at[slot])

    def stores_rows(quarter):
        slot = lax.rem(quarter, 2)
        lanes = pl.ds(pl.multiple_of(quarter * share, share), share)
        size = tall - HEAD
        return [
            pltpu.make_async_copy(
                wide_rows.at[slot, pl.ds(0, size), :], down_out.at[:, lanes], rows_store.at[slot, 0]
            ),
            pltpu.make_async_copy(
                wide_rows.at[slot, pl.ds(size, HEAD), :], out_out.at[:, lanes],
                rows_store.at[slot, 1],
            ),
        ]

    def run(count, load, stores, low, wide, strip):
        def one(index, _):
            slot = lax.rem(index, 2)
            load(index).wait()

            @pl.when(index >= 2)
            def _():
                for copy in stores(index - 2):
                    copy.wait()

            def widen(step, _):
                chunk = pl.ds(pl.multiple_of(step * strip, strip), strip)
                wide[slot, chunk, :] = low[slot, chunk, :].astype(F32)

            lax.fori_loop(0, low.shape[1] // strip, widen, None)
            for copy in stores(index):
                copy.start()
            pl.when(index + 2 < count)(lambda: load(index + 2).start())

        lax.fori_loop(0, count, one, None)

    for index in range(2):
        load_rows(index).start()
        load(index).start()
    for load_in, store_out in plain:
        load_in.wait()
        store_out.start()
    run(quarters, load_rows, stores_rows, low_rows, wide_rows, 64)
    run(team, load, stores, low, wide, min(64, block))
    for index in (quarters - 2, quarters - 1):
        for copy in stores_rows(index):
            copy.wait()
    for index in (team - 2, team - 1):
        for copy in stores(index):
            copy.wait()
    for _, store_out in plain:
        store_out.wait()


def settle(vector, columns, row_sums, result, grad_inputs):
    team, block, span = columns.shape
    quarters, tall, share = row_sums.shape
    size = vector.shape[1]
    shapes = [
        ((2, size), F32),
        ((2, size), F32),
        ((size,), F32),
        ((size,), F32),
        ((3 * size,), F32),
        ((tall - HEAD,), F32),
        ((block, team * 3 * HEAD), F32),
        ((block, team * (span - 3 * HEAD)), F32),
        ((tall - HEAD, quarters * share), F32),
        ((HEAD, quarters * share), F32),
        (result.shape, BF16),
        (grad_inputs.shape, BF16),
    ]
    return pl.pallas_call(
        settle_kernel,
        out_shape=[jax.ShapeDtypeStruct(*shape) for shape in shapes],
        in_specs=[VMEM] + [ANY] * 4,
        out_specs=[VMEM] * 6 + [ANY] * 6,
        scratch_shapes=[
            pltpu.VMEM((2, block, span), BF16),
            pltpu.VMEM((2, block, span), F32),
            pltpu.VMEM((2, tall, share), BF16),
            pltpu.VMEM((2, tall, share), F32),
            pltpu.VMEM((2, *result.shape), BF16),
            DMA((2,)),
            DMA((2, 4)),
            DMA((2,)),
            DMA((2, 2)),
            DMA((2, 2)),
        ],
        compiler_params=pltpu.CompilerParams(vmem_limit_bytes=LIMIT),
        name="settle",
    )(vector, columns, row_sums, result, grad_inputs)


def on_device(
    dp,
    ctx,
    inputs,
    segments,
    ln_gain,
    ln_bias,
    qkv_weight,
    qkv_bias,
    out_weight,
    out_bias,
    up_weight,
    up_bias,
    down_weight,
    down_bias,
    cotangent,
):
    assert dp % TEAM == 0 and ctx == QUARTERS
    teams = dp // TEAM
    together = None if teams == 1 else [[g * TEAM + i for i in range(TEAM)] for g in range(teams)]
    across = None if teams == 1 else [[g * TEAM + i for g in range(teams)] for i in range(TEAM)]
    place = lax.axis_index("dp")
    rank = place % TEAM
    _, tokens, width = inputs.shape
    hidden = up_weight.shape[1] // TEAM
    shard = width // dp

    def team_order(values):
        if teams == 1:
            return values
        lead = values.shape[:-1]
        return values.reshape(*lead, teams, TEAM, shard).swapaxes(-3, -2).reshape(*lead, width)

    def plain_order(values):
        if teams == 1:
            return values
        lead = values.shape[:-1]
        return values.reshape(*lead, TEAM, teams, shard).swapaxes(-3, -2).reshape(*lead, width)

    if teams == 1:
        w_qkv, w_up, w_out, w_down = qkv_weight, up_weight, out_weight, down_weight
        gain, shift, b_qkv, b_up = ln_gain, ln_bias, qkv_bias, up_bias
        b_rows = [out_bias, down_bias]
    else:
        line_up = partial(lax.all_gather, axis_name="dp", axis_index_groups=across, tiled=True)
        whole = partial(lax.all_gather, axis_name="dp", axis=0, tiled=True)

        def cut(values):
            size = values.shape[0] // TEAM
            return lax.dynamic_slice_in_dim(values, rank * size, size, 0)

        w_qkv, w_up = line_up(qkv_weight, axis=0), line_up(up_weight, axis=0)
        gain, shift = line_up(ln_gain, axis=1), line_up(ln_bias, axis=1)
        w_out, w_down = cut(whole(out_weight)), cut(whole(down_weight))
        b_qkv, b_up = cut(whole(qkv_bias)), cut(whole(up_bias))
        b_rows = [cut(whole(out_bias)), cut(whole(down_bias))]
    rows = w_qkv.shape[0]
    mine = inputs.reshape(tokens, width)
    grad_mine = cotangent.reshape(tokens, width)
    mine_team = team_order(mine)
    tables = rotary_tables(ctx * tokens)
    (
        everyone, attn_input, mlp_input, w_head, w_units, qkv, marks, vectors,
        grad_rows, activated, grad_up, grad_attended, attended, dy_sum,
    ) = gather(
        mine_team, grad_mine, (gain, shift, *b_rows, b_qkv, b_up, segments), w_out, w_down, tables,
        w_qkv, w_up,
    )
    grads = attend_back(qkv, grad_attended, marks, tables)
    flat = (TEAM * tokens, -1)
    attn_input, mlp_input, grad_rows, activated, grad_up, attended = (
        values.reshape(flat)
        for values in (attn_input, mlp_input, grad_rows, activated, grad_up, attended)
    )
    result, grad_qkv, up_sums, row_sums = third(
        mine, attended, activated, w_out, w_down, vectors, grad_up, grads, mlp_input, grad_rows
    )
    grad_inputs, columns, row_sums, vector = fourth(
        mine_team, team_order(grad_mine), grad_qkv.reshape(flat), grad_up, vectors, dy_sum, everyone,
        w_head, w_units, attn_input, up_sums, row_sums,
    )
    grad_inputs = plain_order(grad_inputs)
    if teams > 1:
        columns = lax.psum_scatter(
            columns, "dp", scatter_dimension=1, axis_index_groups=across, tiled=True
        )
    (
        grad_gain, grad_shift, grad_out_b, grad_down_b, grad_qkv_b, grad_up_b,
        grad_qkv_w, grad_up_w, grad_down_w, grad_out_w, result, grad_inputs,
    ) = settle(vector, columns, row_sums, result, grad_inputs)
    if teams > 1:
        near = partial(lax.all_gather, axis_name="dp", axis_index_groups=together, tiled=True)

        def own(values):
            size = values.shape[0] // dp
            total = lax.psum(near(values, axis=0), "dp", axis_index_groups=across)
            return lax.dynamic_slice_in_dim(total, place * (TEAM * size), TEAM * size, 0)

        def own_end(values):
            return lax.psum_scatter(
                values, "dp", scatter_dimension=1, axis_index_groups=across, tiled=True
            )

        def scatter_rows(term):
            size = term.shape[0]
            full = jnp.zeros((TEAM, size, width), BF16)
            full = lax.dynamic_update_slice_in_dim(full, term.astype(BF16)[None], rank, 0)
            return lax.psum_scatter(
                full.reshape(TEAM * size, width), "dp", scatter_dimension=0, tiled=True
            ).astype(F32)

        grad_gain, grad_shift = own_end(grad_gain), own_end(grad_shift)
        grad_out_b, grad_down_b = own(grad_out_b), own(grad_down_b)
        grad_qkv_b, grad_up_b = own(grad_qkv_b), own(grad_up_b)
        grad_out_w, grad_down_w = scatter_rows(grad_out_w), scatter_rows(grad_down_w)
    return (
        result.reshape(inputs.shape),
        grad_inputs.reshape(inputs.shape),
        grad_gain,
        grad_shift,
        grad_qkv_w,
        grad_qkv_b,
        grad_out_w,
        grad_out_b,
        grad_up_w,
        grad_up_b,
        grad_down_w,
        grad_down_b,
    )


def solution(mesh):
    placed = (
        P("dp", "ctx", None),
        P("dp", "ctx"),
        P(None, "dp"),
        P(None, "dp"),
        P("dp", None),
        P("dp"),
        P("dp", None),
        P("dp"),
        P("dp", None),
        P("dp"),
        P("dp", None),
        P("dp"),
        P("dp", "ctx", None),
    )
    return jax.shard_map(
        partial(on_device, mesh.shape["dp"], mesh.shape["ctx"]),
        mesh=mesh,
        in_specs=placed,
        out_specs=(
            P("dp", "ctx", None),
            P("dp", "ctx", None),
            P(None, "dp"),
            P(None, "dp"),
            P("dp", None),
            P("dp"),
            P("dp", None),
            P("dp"),
            P("dp", None),
            P("dp"),
            P("dp", None),
            P("dp"),
        ),
        check_vma=False,
    )
```

```python
from functools import partial

import jax
import jax.numpy as jnp
import numpy as np
from jax import lax
from jax.experimental import pallas as pl
from jax.experimental.pallas import tpu as pltpu
from jax.sharding import PartitionSpec as P

HEADS = 8
HEAD = 256
ROT = 64
EPSILON = 1e-05
MASKED = -1e30
F32 = jnp.float32
BF16 = jnp.bfloat16
MESH = pl.DeviceIdType.MESH
TEAM = HEADS
PAIRS = TEAM // 2
QUARTERS = 4
RIGHT, LEFT = 0, 1
VECTOR_ROWS = 24


def dot(left, right):
    return jnp.dot(left, right, preferred_element_type=F32)


def contract_last(left, right):
    return lax.dot_general(left, right, (((1,), (1,)), ((), ())), preferred_element_type=F32)


def contract_first(left, right):
    return lax.dot_general(left, right, (((0,), (0,)), ((), ())), preferred_element_type=F32)


def rotary_tables(length):
    half = ROT // 2
    exponent = np.arange(0, ROT, 2).astype(np.float32) / np.float32(ROT)
    frequency = np.float32(10000.0) ** (-exponent)
    angles = np.arange(length, dtype=np.float32)[:, None] * frequency[None, :]
    cosine, sine = np.cos(angles), np.sin(angles)
    one, nought = np.ones((length, 64), np.float32), np.zeros((length, 64), np.float32)
    blank = np.zeros((length, half), np.float32)
    tables = ([cosine, cosine, one], [-sine, blank, nought], [blank, sine, nought])
    return [jnp.asarray(np.concatenate(table, -1)) for table in tables]


def spot():
    place = lax.axis_index("dp")
    rank = lax.rem(place, TEAM)
    return place - rank, lax.div(rank, 2), lax.rem(rank, 2), lax.axis_index("ctx")


def near_first(line):
    second = 1 + lax.rem(line, 2)
    last = 3 * (1 - lax.div(line, 2))
    return (line, second, 6 - line - second - last, last)


def core_peer(quarter):
    return quarter + 1 - 2 * lax.rem(quarter, 2)


def chip_peer(quarter):
    return quarter + 2 - 4 * lax.div(quarter, 2)


def send(src, dst, send_sem, recv_sem, place, quarter):
    return pltpu.make_async_remote_copy(
        src_ref=src, dst_ref=dst, send_sem=send_sem, recv_sem=recv_sem,
        device_id=(place, quarter), device_id_type=MESH,
    )


def greet_line(base, line, side, quarter):
    barrier = pltpu.get_barrier_semaphore()

    def hail(place, quarter):
        pl.semaphore_signal(barrier, inc=1, device_id=(place, quarter), device_id_type=MESH)

    rank = line * 2 + side
    hail(base + line * 2 + 1 - side, quarter)

    pl.when(line < PAIRS - 1)(lambda: hail(base + rank + 2, quarter))
    pl.when(line > 0)(lambda: hail(base + rank - 2, quarter))
    for step in range(1, QUARTERS):
        hail(base + rank, lax.rem(quarter + step, QUARTERS))
    neighbours = 1 + lax.div(line + 2, 3) - lax.div(line, 3)
    pl.semaphore_wait(barrier, neighbours + QUARTERS)


def greet_team(base, line, side, quarter):
    barrier = pltpu.get_barrier_semaphore()
    rank = line * 2 + side
    for step in range(1, TEAM):
        pl.semaphore_signal(
            barrier, inc=1, device_id=(base + lax.rem(rank + step, TEAM), quarter),
            device_id_type=MESH,
        )
    for step in range(1, QUARTERS):
        pl.semaphore_signal(
            barrier, inc=1, device_id=(base + rank, lax.rem(quarter + step, QUARTERS)),
            device_id_type=MESH,
        )
    pl.semaphore_wait(barrier, TEAM + QUARTERS - 2)


class Relay:
    def __init__(self, held, line_send, line_recv, side_send, side_recv, half_send, half_recv):
        self.held = held
        self.sems = line_send, line_recv, side_send, side_recv, half_send, half_recv
        self.base, self.line, self.side, self.quarter = spot()
        self.half = held.shape[1] * 3 // 8

    def neighbour(self, way):
        return self.base + self.line * 2 + self.side + (2 if way == RIGHT else -2)

    def along(self, source, way):
        block = self.held.at[source * 2 + self.side]
        return send(
            block, block, self.sems[0].at[way, source], self.sems[1].at[source],
            self.neighbour(way), self.quarter,
        )

    def along_half(self, way):
        source = 0 if way == RIGHT else PAIRS - 1
        block = self.held.at[source * 2 + 1 - self.side, pl.ds(0, self.half)]
        return send(
            block, block, self.sems[4].at[way], self.sems[5].at[way], self.neighbour(way),
            self.quarter,
        )

    def over(self, source, side, low):
        block = self.held.at[source * 2 + side]
        if low:
            block = self.held.at[source * 2 + side, pl.ds(self.half, self.held.shape[1] - self.half)]
        place = self.base + self.line * 2 + 1 - self.side
        return send(
            block, block, self.sems[2].at[source], self.sems[3].at[source], place, self.quarter
        )

    def crossing(self, source, side, act):
        parted = (source != self.line) & (lax.rem(source, PAIRS - 1) == 0)
        pl.when(parted)(lambda: act(self.over(source, side, True)))
        pl.when(jnp.logical_not(parted))(lambda: act(self.over(source, side, False)))

    def each(self, step, act):
        line = self.line
        if step == 0:
            pl.when(line < PAIRS - 1)(lambda: act(line, RIGHT))
            pl.when(line > 0)(lambda: act(line, LEFT))
            act(line, None)
            return

        @pl.when(line >= step)
        def _():
            source = line - step
            act(source, "arrive")
            pl.when(line < PAIRS - 1)(lambda: act(source, RIGHT))
            act(source, None)

        @pl.when(line + step < PAIRS)
        def _():
            source = line + step
            act(source, "arrive")
            pl.when(line > 0)(lambda: act(source, LEFT))
            act(source, None)

    def start(self, step):
        def act(source, way):
            if way == "arrive":
                self.along(source, RIGHT).wait_recv()
            elif way is None:
                self.crossing(source, self.side, lambda copy: copy.start())
            else:
                self.along(source, way).start()

        self.each(step, act)

    def start_halves(self):
        for end, way in ((0, RIGHT), (PAIRS - 1, LEFT)):

            @pl.when(self.line == end)
            def _(end=end, way=way):
                self.over(self.line, 1 - self.side, False).wait_recv()
                self.along_half(way).start()

    def pass_halves(self, step):
        for end, way in ((0, RIGHT), (PAIRS - 1, LEFT)):
            here = step if way == RIGHT else PAIRS - 1 - step

            @pl.when(self.line == here)
            def _(way=way):
                self.along_half(way).wait_recv()
                if step < PAIRS - 1:
                    self.along_half(way).start()

    def wait_over(self, step, source):
        def take(copy):
            copy.wait_recv()

        if step == 0:
            inner = (self.line > 0) & (self.line < PAIRS - 1)
            pl.when(inner)(lambda: take(self.over(source, 1 - self.side, False)))
        else:
            self.crossing(source, 1 - self.side, take)

    def finish(self):
        def act(source, way):
            if way is None:
                self.crossing(source, self.side, lambda copy: copy.wait_send())
            elif way != "arrive":
                self.along(source, way).wait_send()

        for step in range(PAIRS):
            self.each(step, act)
        pl.when(self.line < PAIRS - 1)(lambda: self.along_half(RIGHT).wait_send())
        pl.when(self.line > 0)(lambda: self.along_half(LEFT).wait_send())


RELAY_SEMS = [
    pltpu.SemaphoreType.DMA((2, PAIRS)),
    pltpu.SemaphoreType.DMA((PAIRS,)),
    pltpu.SemaphoreType.DMA((PAIRS,)),
    pltpu.SemaphoreType.DMA((PAIRS,)),
    pltpu.SemaphoreType.DMA((2,)),
    pltpu.SemaphoreType.DMA((2,)),
]


def normalize(rows):
    average = jnp.mean(rows, -1, keepdims=True)
    centred = rows - average
    variance = jnp.mean(centred * centred, -1, keepdims=True)
    inverse = lax.rsqrt(variance + EPSILON)
    return centred * inverse, inverse


def rotate_low(low, cosine, above, below):
    half = ROT // 2
    return (
        low * cosine + pltpu.roll(low, 128 - half, 1) * above + pltpu.roll(low, half, 1) * below
    )


def unrotate_low(low, cosine, above, below):
    half = ROT // 2
    return (
        low * cosine + pltpu.roll(low * below, 128 - half, 1) + pltpu.roll(low * above, half, 1)
    )


def reader(sequence):
    return 2 * lax.rem(sequence, 2) + lax.rem(lax.div(sequence, 2), 2)


def reader_slot(sequence):
    return lax.div(sequence, QUARTERS)


def among(quarter):
    return 2 * lax.rem(quarter, 2) + lax.div(quarter, 2)


class Spread:
    def __init__(self, pieces, send_sem, recv_sem, own_sem):
        self.pieces, self.sems = pieces, (send_sem, recv_sem, own_sem)
        base, line, side, self.quarter = spot()
        self.place = base + line * 2 + side

    def _remote(self, index, sequence, slot, to, origin):
        src, dst = self.pieces[index]
        send_sem, recv_sem, _ = self.sems
        return send(
            src(sequence), dst(slot, origin), send_sem.at[index, sequence],
            recv_sem.at[index, origin, slot], self.place, to,
        )

    def _own(self, index, sequence):
        src, dst = self.pieces[index]
        slot = reader_slot(sequence)
        return pltpu.make_async_copy(
            src(sequence), dst(slot, self.quarter), self.sems[2].at[index, slot]
        )

    def each(self, sequence, own, other):
        to, slot = reader(sequence), reader_slot(sequence)

        @pl.when(to == self.quarter)
        def _():
            for index in range(len(self.pieces)):
                own(self._own(index, sequence))

        @pl.when(to != self.quarter)
        def _():
            for index in range(len(self.pieces)):
                other(self._remote(index, sequence, slot, to, self.quarter))

    def start(self, sequence):
        self.each(sequence, lambda copy: copy.start(), lambda copy: copy.start())

    def finish(self):
        def sent(sequence, _):
            self.each(sequence, lambda copy: copy.wait(), lambda copy: copy.wait_send())

        lax.fori_loop(0, TEAM, sent, None)

        def landed(step, _):
            origin = lax.rem(self.quarter + 1 + lax.div(step, 2), QUARTERS)
            slot = lax.rem(step, 2)
            for index in range(len(self.pieces)):
                self._remote(index, 0, slot, origin, origin).wait_recv()

        lax.fori_loop(0, 2 * (QUARTERS - 1), landed, None)


def spread_sems(count):
    return [
        pltpu.SemaphoreType.DMA((count, TEAM)),
        pltpu.SemaphoreType.DMA((count, QUARTERS, 2)),
        pltpu.SemaphoreType.DMA((count, 2)),
    ]


class Columns:
    def __init__(self, pieces, place, lane, lanes, sems):
        self.pieces, self.place, self.lane, self.lanes, self.sems = pieces, place, lane, lanes, sems
        self.base, line, side, self.quarter = spot()
        self.rank = line * 2 + side

    def deal(self, source, target, peer):
        sends, recvs = self.sems[:2]
        return [
            send(
                src, self.place(source, self.quarter, lane, lanes),
                sends.at[index, target], recvs.at[index, source], self.base + peer, self.quarter,
            )
            for index, (src, lane, lanes) in enumerate(self.pieces(target))
        ]

    def own(self):
        return [
            pltpu.make_async_copy(
                src, self.place(self.rank, self.quarter, lane, lanes), self.sems[2].at[index]
            )
            for index, (src, lane, lanes) in enumerate(self.pieces(self.rank))
        ]

    def start(self):
        for copy in self.own():
            copy.start()

        def one(step, _):
            target = lax.rem(self.rank + step, TEAM)
            for copy in self.deal(self.rank, target, target):
                copy.start()

        lax.fori_loop(1, TEAM, one, None)

    def pass_on(self, which, source, slice_of, to):
        block = self.place(source, slice_of, self.lane, self.lanes)
        sends, recvs = self.sems[3 + 2 * which : 5 + 2 * which]
        return send(
            block, block, sends.at[source], recvs.at[source], self.base + self.rank, to
        )

    def to_core(self, source):
        return self.pass_on(0, source, self.quarter, core_peer(self.quarter))

    def to_chip(self, source):
        return self.pass_on(1, source, self.quarter, chip_peer(self.quarter))

    def to_last(self, source):
        return self.pass_on(2, source, chip_peer(self.quarter), core_peer(self.quarter))

    def forward(self):
        for copy in self.own():
            copy.wait()
        self.to_chip(self.rank).start()
        self.to_core(self.rank).start()

        def one(step, _):
            source = lax.rem(self.rank + TEAM - step, TEAM)
            for copy in self.deal(source, self.rank, source):
                copy.wait_recv()
            self.to_chip(source).start()
            self.to_core(source).start()

        lax.fori_loop(1, TEAM, one, None)

    def forward_last(self):
        chip = chip_peer(self.quarter)

        def one(step, _):
            source = lax.rem(self.rank + TEAM - step, TEAM)
            self.pass_on(1, source, chip, chip).wait_recv()
            self.to_last(source).start()

        lax.fori_loop(0, TEAM, one, None)

    def arrive(self):
        core = core_peer(self.quarter)

        def one(source, _):
            self.pass_on(0, source, core, core).wait_recv()
            self.pass_on(2, source, chip_peer(core), core).wait_recv()

        lax.fori_loop(0, TEAM, one, None)

    def finish(self):
        def one(source, _):
            self.to_core(source).wait_send()
            self.to_chip(source).wait_send()
            self.to_last(source).wait_send()

        lax.fori_loop(0, TEAM, one, None)

        def sent(step, _):
            target = lax.rem(self.rank + step, TEAM)
            for copy in self.deal(self.rank, target, target):
                copy.wait_send()

        lax.fori_loop(1, TEAM, sent, None)


def column_sems(count):
    dma = pltpu.SemaphoreType.DMA
    return [dma((count, TEAM))] * 2 + [dma((count,))] + [dma((TEAM,))] * 6


def same_document(query_marks, key_marks):
    def one_hot(marks):
        number = lax.broadcasted_iota(jnp.int32, marks.shape, 0).astype(F32)
        return jnp.where(marks == number, 1.0, 0.0).astype(BF16)

    return contract_first(one_hot(query_marks), one_hot(key_marks)) > 0.5


def probabilities(block, size, q_ref, k_ref, marks_ref):
    start = block * size
    rows, keys = pl.ds(start, size), pl.ds(0, start + size)
    scores = contract_last(q_ref[rows, :], k_ref[keys, :]) * HEAD ** (-0.5)
    shape = scores.shape
    query_pos = start + lax.broadcasted_iota(jnp.int32, shape, 0)
    key_pos = lax.broadcasted_iota(jnp.int32, shape, 1)
    key_marks = jnp.concatenate([marks_ref[index] for index in range(block + 1)], -1)
    allowed = (query_pos >= key_pos) & same_document(marks_ref[block], key_marks)
    scores = jnp.where(allowed, scores, MASKED)
    expanded = jnp.exp(scores - jnp.max(scores, -1, keepdims=True))
    return expanded / jnp.sum(expanded, -1, keepdims=True)


def gelu_terms(values):
    chance = 0.5 * (1.0 + lax.erf(values * (0.5**0.5)))
    density = jnp.exp(-0.5 * values * values) * 0.3989422804014327
    return values * chance, chance + values * density


ANY = pl.BlockSpec(memory_space=pl.ANY)
VMEM = pl.BlockSpec(memory_space=pltpu.VMEM)
DMA = pltpu.SemaphoreType.DMA
LIMIT = 60 << 20


def gather_kernel(
    x_ref, dy_ref, gain_ref, shift_ref, out_b_ref, down_b_ref, qkv_b_ref, up_b_ref, marks_ref,
    wo_in, wd_in, cos_ref, above_ref, below_ref, wq_ref, wu_ref,
    x_out, ha_out, hm_out, wq_out, wu_out, qkv_out, marks_out, vec_out,
    dy_out, a_out, du_out, do_out, o_out, sum_out,
    xs, dys, hm, head, units, vec_ref, vecs, vectors, ha, qkv, whole, marks, mixed, act, grad, attended,
    table, wo_ref, wd_ref, late_load, own_sem, x_store, ha_store, du_store, dy_store, late_store, v_send, v_recv, back_send, back_recv,
    *sems,
):
    base, line, side, quarter = spot()
    rank = line * 2 + side
    tokens, width = x_ref.shape
    hidden = act.shape[-1]
    rows = wq_ref.shape[0]
    part = rows // QUARTERS
    take = iter(range(0, len(sems)))

    def some(count):
        return [sems[next(take)] for _ in range(count)]

    relay_x, relay_dy = Relay(xs, *some(6)), Relay(dys, *some(6))
    head_columns, unit_columns = some(9), some(9)
    spread_x = Spread(
        [
            (
                lambda s: qkv.at[s],
                lambda j, origin: whole.at[j, :, pl.ds(origin * tokens, tokens), :],
            ),
            (lambda s: vecs.at[s, pl.ds(16, 8), :], lambda j, origin: marks.at[j, origin]),
        ],
        *some(3),
    )
    spread_do = Spread(
        [
            (
                lambda s: attended.at[s],
                lambda j, origin: do_out.at[j, pl.ds(origin * tokens, tokens), :],
            )
        ],
        *some(3),
    )
    mine = pl.ds(pl.multiple_of(quarter * part, 16), part)

    def landing(weight):
        def place(source, slice_of, lane, lanes):
            band = pl.ds(pl.multiple_of(source * rows + slice_of * part, 16), part)
            return weight.at[band, pl.ds(lane, lanes)]

        return place

    head_columns = Columns(
        lambda target: [
            (
                wq_ref.at[mine, pl.ds(pl.multiple_of(kind * width + target * HEAD, HEAD), HEAD)],
                kind * HEAD,
                HEAD,
            )
            for kind in range(3)
        ],
        landing(head), 0, 3 * HEAD, head_columns,
    )
    unit_columns = Columns(
        lambda target: [
            (wu_ref.at[mine, pl.ds(pl.multiple_of(target * hidden, hidden), hidden)], 0, hidden)
        ],
        landing(units), 0, hidden, unit_columns,
    )
    own_rows = pl.ds(pl.multiple_of(quarter * tokens, tokens), tokens)

    def put_row(row, values):
        vec_ref[row : row + 1, :] = values.astype(F32).reshape(1, rows)

    vec_ref[...] = jnp.zeros_like(vec_ref)
    vec_ref[0:2, :] = gain_ref[...].astype(F32)
    vec_ref[2:4, :] = shift_ref[...].astype(F32)
    put_row(4, out_b_ref[...])
    put_row(5, down_b_ref[...])
    for index in range(3):
        put_row(8 + index, qkv_b_ref[pl.ds(index * rows, rows)])
    vec_ref[16:24, :] = jnp.broadcast_to(marks_ref[...].astype(F32), (8, tokens))
    for start in range(0, hidden, 256):
        values = up_b_ref[pl.ds(start, 256)].astype(F32)
        vectors[4:5, pl.ds(start, 256)] = values.reshape(1, 256)
    greet_team(base, line, side, quarter)

    def vector_copy(source, target, peer):
        return send(
            vec_ref, vecs.at[source], v_send.at[target], v_recv.at[source], base + peer, quarter
        )

    owns = [
        pltpu.make_async_copy(src, dst, own_sem.at[index])
        for index, (src, dst) in enumerate(
            (
                (x_ref, xs.at[rank]),
                (vec_ref, vecs.at[rank]),
                (dy_ref, dys.at[rank]),
                (cos_ref.at[own_rows, :], table.at[0]),
                (above_ref.at[own_rows, :], table.at[1]),
                (below_ref.at[own_rows, :], table.at[2]),
            )
        )
    ]
    for copy in owns:
        copy.start()
    load_out = pltpu.make_async_copy(wo_in, wo_ref, late_load.at[0])
    load_down = pltpu.make_async_copy(wd_in, wd_ref, late_load.at[1])
    load_out.start()
    load_down.start()

    def send_vector(step, _):
        target = lax.rem(rank + step, TEAM)
        vector_copy(rank, target, target).start()

    lax.fori_loop(1, TEAM, send_vector, None)
    head_columns.start()
    for copy in owns:
        copy.wait()
    relay_x.start(0)
    head_columns.forward()
    relay_x.start_halves()
    relay_x.start(1)
    head_columns.forward_last()

    def take_vector(step, _):
        origin = lax.rem(rank + TEAM - step, TEAM)
        vector_copy(origin, rank, origin).wait_recv()

    lax.fori_loop(1, TEAM, take_vector, None)
    for source in range(TEAM):
        for row in range(4):
            vectors[pl.ds(row, 1), pl.ds(source * rows, rows)] = vecs[source, pl.ds(row, 1), :]
    head_columns.arrive()
    late = [
        pltpu.make_async_copy(src, dst, late_store.at[index])
        for index, (src, dst) in enumerate(
            ((head, wq_out), (vecs, vec_out), (units, wu_out), (whole, qkv_out), (marks, marks_out))
        )
    ]
    late[0].start()
    late[1].start()

    strip = 128
    order = near_first(line)

    def member(step, other):
        return order[step] * 2 + side + other * (1 - 2 * side)

    def store_x(which):
        return [
            pltpu.make_async_copy(xs.at[which], x_out.at[which], x_store.at[0, which]),
            pltpu.make_async_copy(hm.at[which], hm_out.at[which], x_store.at[1, which]),
        ]

    def store_ha(slot, which):
        return pltpu.make_async_copy(ha.at[slot], ha_out.at[which], ha_store.at[slot])

    def project(slot, which):
        def norm(index, _):
            chunk = pl.ds(pl.multiple_of(index * strip, strip), strip)
            unit, _ = normalize(xs[which, chunk, :].astype(F32))
            ha[slot, chunk, :] = (unit * vectors[0:1, :] + vectors[2:3, :]).astype(BF16)
            hm[which, chunk, :] = (unit * vectors[1:2, :] + vectors[3:4, :]).astype(BF16)

        lax.fori_loop(0, tokens // strip, norm, None)
        for kind in range(3):
            chunk = kind * TEAM + rank
            bias = vecs[lax.div(chunk, 3), pl.ds(8 + lax.rem(chunk, 3), 1), :]
            made = dot(ha[slot], head[:, pl.ds(kind * HEAD, HEAD)]) + bias
            if kind < 2:
                low = rotate_low(made[:, :128], table[0], table[1], table[2])
                qkv[which, kind, :, pl.ds(0, 128)] = low.astype(BF16)
                qkv[which, kind, :, pl.ds(128, HEAD - 128)] = made[:, 128:].astype(BF16)
            else:
                qkv[which, kind] = made.astype(BF16)
        spread_x.start(which)
        store_ha(slot, which).start()
        for copy in store_x(which):
            copy.start()

    for step, place in enumerate(order):

        def one(other, _, step=step, place=place):
            @pl.when(other == 1)
            def _():
                if 0 < step < PAIRS - 1:
                    relay_x.start(step + 1)
                if step > 0:
                    relay_x.pass_halves(step)
                if step == 2:
                    unit_columns.start()
                    relay_dy.start(0)
                relay_x.wait_over(step, place)

            if step > 0:
                store_ha(other, member(step - 1, other)).wait()
            project(other, member(step, other))

        lax.fori_loop(0, 2, one, None)

    unit_columns.forward()
    sum_out[...] = jnp.zeros_like(sum_out)
    relay_dy.start_halves()
    relay_dy.start(1)
    unit_columns.forward_last()
    spread_x.finish()
    late[3].start()
    late[4].start()

    def attend(sequence, _):
        q, k, v = (whole.at[sequence, kind] for kind in range(3))
        for block in range(QUARTERS):
            probs = probabilities(block, tokens, q, k, marks.at[sequence])
            value_block = v[pl.ds(0, (block + 1) * tokens), :]
            mixed[sequence, pl.ds(block * tokens, tokens), :] = dot(
                probs.astype(BF16), value_block
            ).astype(BF16)

    lax.fori_loop(0, 2, attend, None)

    def back(to, origin):
        return send(
            mixed.at[:, pl.ds(to * tokens, tokens), :], o_out.at[:, among(origin)],
            back_send.at[to], back_recv.at[origin], base + rank, to,
        )

    own_back = pltpu.make_async_copy(
        mixed.at[:, pl.ds(quarter * tokens, tokens), :], o_out.at[:, among(quarter)],
        own_sem.at[6],
    )
    own_back.start()
    for step in range(1, QUARTERS):
        to = lax.rem(quarter + step, QUARTERS)
        back(to, quarter).start()
    unit_columns.arrive()
    late[2].start()
    load_out.wait()
    load_down.wait()

    def store_dy(which):
        return pltpu.make_async_copy(dys.at[which], dy_out.at[which], dy_store.at[which])

    def store_du(slot, which):
        return [
            pltpu.make_async_copy(act.at[slot], a_out.at[which], du_store.at[0, slot]),
            pltpu.make_async_copy(grad.at[slot], du_out.at[which], du_store.at[1, slot]),
        ]

    def pull(slot, which):
        attended[which] = contract_last(dys[which], wo_ref[...]).astype(BF16)
        spread_do.start(which)
        for start in range(0, hidden, 256):
            span = pl.ds(start, 256)
            up = dot(hm[which], units[:, span]) + vectors[4:5, span]
            value, slope = gelu_terms(up)
            act[slot, :, span] = value.astype(BF16)
            pulled = contract_last(dys[which], wd_ref[span, :])
            grad[slot, :, span] = (pulled * slope).astype(BF16)
        for copy in store_du(slot, which):
            copy.start()
        store_dy(which).start()
        sum_out[0:1, :] += jnp.sum(dys[which].astype(F32), 0, keepdims=True)

    for step, place in enumerate(order):

        def one(other, _, step=step, place=place):
            @pl.when(other == 1)
            def _():
                if 0 < step < PAIRS - 1:
                    relay_dy.start(step + 1)
                if step > 0:
                    relay_dy.pass_halves(step)
                relay_dy.wait_over(step, place)

            if step > 0:
                for copy in store_du(other, member(step - 1, other)):
                    copy.wait()
            pull(other, member(step, other))

        lax.fori_loop(0, 2, one, None)

    relay_x.finish()
    relay_dy.finish()
    spread_do.finish()
    head_columns.finish()
    unit_columns.finish()
    for step in range(1, QUARTERS):
        other = lax.rem(quarter + step, QUARTERS)
        back(other, quarter).wait_send()
        back(other, other).wait_recv()
    own_back.wait()

    def sent(step, _):
        target = lax.rem(rank + step, TEAM)
        vector_copy(rank, target, target).wait_send()

    lax.fori_loop(1, TEAM, sent, None)

    def stored(which, _):
        for copy in store_x(which):
            copy.wait()
        store_dy(which).wait()

    lax.fori_loop(0, TEAM, stored, None)
    for other in range(2):
        store_ha(other, member(PAIRS - 1, other)).wait()
        for copy in store_du(other, member(PAIRS - 1, other)):
            copy.wait()
    for copy in late:
        copy.wait()


def gather(x, dy, parameters, w_out, w_down, tables, w_qkv, w_up):
    tokens, width = x.shape
    hidden, rows = w_down.shape[0], w_qkv.shape[0]
    all_tokens = (TEAM, tokens, width)
    whole = (2, 3, QUARTERS * tokens, HEAD)
    marks = ((2, QUARTERS, 8, tokens), F32)
    vec = (VECTOR_ROWS, rows)
    vecs = ((TEAM, *vec), F32)
    units = ((TEAM, tokens, hidden), BF16)
    shapes = [
        (all_tokens, BF16),
        (all_tokens, BF16),
        (all_tokens, BF16),
        ((width, 3 * HEAD), BF16),
        ((width, hidden), BF16),
        (whole, BF16),
        marks,
        vecs,
        (all_tokens, BF16),
        units,
        units,
        ((2, QUARTERS * tokens, HEAD), BF16),
        ((2, QUARTERS, tokens, HEAD), BF16),
        ((8, width), F32),
    ]
    return pl.pallas_call(
        gather_kernel,
        out_shape=[jax.ShapeDtypeStruct(*shape) for shape in shapes],
        in_specs=[ANY] * 2 + [VMEM] * 7 + [ANY] * 7,
        out_specs=[ANY] * 13 + [VMEM],
        scratch_shapes=[
            pltpu.VMEM(all_tokens, BF16),
            pltpu.VMEM(all_tokens, BF16),
            pltpu.VMEM(all_tokens, BF16),
            pltpu.VMEM((width, 3 * HEAD), BF16),
            pltpu.VMEM((width, hidden), BF16),
            pltpu.VMEM(vec, F32),
            pltpu.VMEM(*vecs),
            pltpu.VMEM((8, width), F32),
            pltpu.VMEM((2, tokens, width), BF16),
            pltpu.VMEM((TEAM, 3, tokens, HEAD), BF16),
            pltpu.VMEM(whole, BF16),
            pltpu.VMEM(*marks),
            pltpu.VMEM((2, QUARTERS * tokens, HEAD), BF16),
            pltpu.VMEM((2, tokens, hidden), BF16),
            pltpu.VMEM((2, tokens, hidden), BF16),
            pltpu.VMEM((TEAM, tokens, HEAD), BF16),
            pltpu.VMEM((3, tokens, 128), F32),
            pltpu.VMEM(w_out.shape, BF16),
            pltpu.VMEM(w_down.shape, BF16),
            DMA((2,)),
            DMA((7,)),
            DMA((2, TEAM)),
            DMA((2,)),
            DMA((2, 2)),
            DMA((TEAM,)),
            DMA((5,)),
            DMA((TEAM,)),
            DMA((TEAM,)),
            DMA((QUARTERS,)),
            DMA((QUARTERS,)),
        ]
        + RELAY_SEMS * 2
        + column_sems(3)
        + column_sems(1)
        + spread_sems(2)
        + spread_sems(1),
        compiler_params=pltpu.CompilerParams(
            collective_id=0, has_side_effects=True, vmem_limit_bytes=LIMIT
        ),
        name="gather",
    )(x, dy, *parameters, w_out, w_down, *tables, w_qkv, w_up)


def backward_kernel(
    qkv_ref, do_ref, marks_ref, cos_ref, above_ref, below_ref, d_ref, dk_sum, dv_sum
):
    scale = HEAD ** (-0.5)
    q_ref, k_ref, v_ref = (qkv_ref.at[kind] for kind in range(3))
    length = q_ref.shape[0]
    size = marks_ref.shape[-1]

    def put(kind, rows, grads):
        low = unrotate_low(
            grads[:, :128], cos_ref[rows, :], above_ref[rows, :], below_ref[rows, :]
        )
        d_ref[kind, rows, pl.ds(0, 128)] = low.astype(BF16)
        d_ref[kind, rows, pl.ds(128, HEAD - 128)] = grads[:, 128:].astype(BF16)

    dk_sum[...] = jnp.zeros_like(dk_sum)
    dv_sum[...] = jnp.zeros_like(dv_sum)
    for block in range(length // size):
        start = block * size
        rows, keys = pl.ds(start, size), pl.ds(0, start + size)
        probs = probabilities(block, size, q_ref, k_ref, marks_ref)
        grads = do_ref[rows, :]
        grad_probs = contract_last(grads, v_ref[keys, :])
        row_dot = jnp.sum(probs * grad_probs, -1, keepdims=True)
        grad_scores = (probs * (grad_probs - row_dot)).astype(BF16)
        put(0, rows, dot(grad_scores, k_ref[keys, :]) * scale)
        dk_sum[keys, :] += contract_first(grad_scores, q_ref[rows, :])
        dv_sum[keys, :] += contract_first(probs.astype(BF16), grads)
    put(1, pl.ds(0, length), dk_sum[...] * scale)
    d_ref[2] = dv_sum[...].astype(BF16)


def attend_back(qkv, grads, marks, tables):
    seqs, _, length, head = qkv.shape
    three = pl.BlockSpec((None, 3, length, HEAD), lambda s: (s, 0, 0, 0))
    one = pl.BlockSpec((None, length, HEAD), lambda s: (s, 0, 0))
    table = pl.BlockSpec((length, 128), lambda s: (0, 0))
    return pl.pallas_call(
        backward_kernel,
        grid=(seqs,),
        in_specs=[three, one, pl.BlockSpec((None, *marks.shape[1:]), lambda s: (s, 0, 0, 0))]
        + [table] * 3,
        out_specs=three,
        out_shape=jax.ShapeDtypeStruct(qkv.shape, BF16),
        scratch_shapes=[pltpu.VMEM((length, head), F32)] * 2,
        compiler_params=pltpu.CompilerParams(vmem_limit_bytes=48 << 20),
        name="attend_back",
    )(qkv, grads, marks, *tables)


class Reduce:
    def __init__(self, cut, own, side_out, side_in, line_in, half_in, sems):
        self.cut = cut
        self.own, self.side_out, self.side_in = own, side_out, side_in
        self.line_in, self.half_in, self.sems = line_in, half_in, sems
        self.base, self.line, self.side, self.quarter = spot()
        self.order = near_first(self.line)
        self.inner = (self.line > 0) & (self.line < PAIRS - 1)
        self.tokens = own.shape[1]

    def over(self, step, low):
        side_send, side_recv = self.sems[:2]
        place = self.base + self.line * 2 + 1 - self.side
        rows = pl.ds(self.cut, self.tokens - self.cut) if low else pl.ds(0, self.tokens)
        return send(
            self.side_out.at[step, rows], self.side_in.at[step, rows],
            side_send.at[step], side_recv.at[step], place, self.quarter,
        )

    def crossing(self, step, act):
        if step == PAIRS - 1:
            act(self.over(step, True))
        elif step == 1:
            act(self.over(step, False))
        else:
            first, second = (True, False) if step == PAIRS - 2 else (False, True)
            pl.when(self.inner)(lambda: act(self.over(step, first)))
            pl.when(jnp.logical_not(self.inner))(lambda: act(self.over(step, second)))

    def along(self, step, target, way):
        line_send, line_recv = self.sems[2:4]
        move = 1 if way == RIGHT else -1
        slot = target if way == RIGHT else jnp.where(target == self.line - 1, PAIRS, target)
        place = self.base + (self.line + move) * 2 + self.side
        return send(
            self.side_out.at[step], self.line_in.at[slot], line_send.at[step], line_recv.at[slot],
            place, self.quarter,
        )

    def arrive(self, slot):
        line_send, line_recv = self.sems[2:4]
        return send(
            self.side_out.at[0], self.line_in.at[slot], line_send.at[0], line_recv.at[slot],
            self.base + self.line * 2 + 1 - self.side, self.quarter,
        )

    def upper(self, step, way):
        half_send, half_recv = self.sems[4:6]
        move = 1 if way == RIGHT else -1
        rows = pl.ds(0, self.cut)
        place = self.base + (self.line + move) * 2 + self.side
        return send(
            self.side_out.at[step, rows], self.half_in.at[way], half_send.at[way],
            half_recv.at[way], place, self.quarter,
        )

    def upper_over(self):
        cross_send, cross_recv = self.sems[6:8]
        rows = pl.ds(0, self.cut)
        place = self.base + self.line * 2 + 1 - self.side
        return send(
            self.side_out.at[0, rows], self.side_in.at[0, rows], cross_send, cross_recv, place,
            self.quarter,
        )

    def begin(self, step):
        self.crossing(step, lambda copy: copy.start())

    def launch(self):
        pl.when(self.line == 0)(lambda: self.upper(PAIRS - 1, RIGHT).start())
        pl.when(self.line == PAIRS - 1)(lambda: self.upper(PAIRS - 1, LEFT).start())

    def hop(self, count):
        for way in (RIGHT, LEFT):
            here = count if way == RIGHT else PAIRS - 1 - count
            step = (None, PAIRS - 1, PAIRS - 2, 0)[count]

            @pl.when(self.line == here)
            def _(way=way, step=step):
                self.upper(step, way).wait_recv()
                rows = pl.ds(0, self.cut)
                total = self.side_out[step, rows].astype(F32) + self.half_in[way].astype(F32)
                self.side_out[step, rows] = total.astype(BF16)
                if count < PAIRS - 1:
                    self.upper(step, way).start()
                else:
                    self.upper_over().start()

    def upper_sent(self, step):
        first, second = (RIGHT, LEFT) if step == PAIRS - 1 else (LEFT, RIGHT)
        low_line = self.line < PAIRS // 2

        def wait():
            pl.when(low_line)(lambda: self.upper(step, first).wait_send())
            pl.when(jnp.logical_not(low_line))(lambda: self.upper(step, second).wait_send())

        if step == PAIRS - 1:
            wait()
        elif step == PAIRS - 2:
            pl.when(self.inner)(wait)

    def mine(self, step, index, strip):
        chunk = pl.ds(pl.multiple_of(index * strip, strip), strip)
        slot = step if self.own.shape[0] > 1 else 0
        own = self.own[slot, chunk, :].astype(F32)
        other = self.side_in[step, chunk, :].astype(F32)
        if step == PAIRS - 1:
            return jnp.where(index * strip >= self.cut, own + other, own)
        if step == PAIRS - 2:
            whole = (index * strip >= self.cut) | jnp.logical_not(self.inner)
            return jnp.where(whole, own + other, own)
        return own + other

    def advance(self, step):
        target = self.order[step]
        self.crossing(step, lambda copy: copy.wait_recv())
        self.crossing(step, lambda copy: copy.wait_send())
        self.upper_sent(step)

        def forward(way, upstream):
            pl.when(upstream)(lambda: self.arrive(target).wait_recv())
            strip = 64

            def add(index, _):
                chunk = pl.ds(pl.multiple_of(index * strip, strip), strip)
                total = self.mine(step, index, strip)
                passing = self.line_in[target, chunk, :].astype(F32)
                total = jnp.where(upstream, total + passing, total)
                self.side_out[step, chunk, :] = total.astype(BF16)

            lax.fori_loop(0, self.tokens // strip, add, None)
            self.along(step, target, way).start()

        pl.when(target > self.line)(lambda: forward(RIGHT, self.line > 0))
        pl.when(target < self.line)(lambda: forward(LEFT, self.line < PAIRS - 1))

    def last(self):
        self.crossing(0, lambda copy: copy.wait_recv())
        self.crossing(0, lambda copy: copy.wait_send())

        @pl.when(jnp.logical_not(self.inner))
        def _():
            self.upper_over().wait_recv()
            self.upper_over().wait_send()

        pl.when(self.line > 0)(lambda: self.arrive(self.line).wait_recv())
        pl.when(self.line < PAIRS - 1)(lambda: self.arrive(PAIRS).wait_recv())

    def total(self, index, strip):
        chunk = pl.ds(pl.multiple_of(index * strip, strip), strip)
        total = self.mine(0, index, strip)
        left = self.line_in[self.line, chunk, :].astype(F32)
        right = self.line_in[PAIRS, chunk, :].astype(F32)
        total = jnp.where(self.line > 0, total + left, total)
        return jnp.where(self.line < PAIRS - 1, total + right, total)

    def finish(self):
        for step in range(1, PAIRS):
            target = self.order[step]
            pl.when(target > self.line)(lambda: self.along(step, target, RIGHT).wait_send())
            pl.when(target < self.line)(lambda: self.along(step, target, LEFT).wait_send())


REDUCE = 13


def reduce_scratch(tokens, width, slots, dtype, cut):
    return [
        pltpu.VMEM((slots, tokens, width), dtype),
        pltpu.VMEM((PAIRS, tokens, width), BF16),
        pltpu.VMEM((PAIRS, tokens, width), BF16),
        pltpu.VMEM((PAIRS + 1, tokens, width), BF16),
        pltpu.VMEM((2, cut, width), BF16),
        DMA((PAIRS,)),
        DMA((PAIRS,)),
        DMA((PAIRS,)),
        DMA((PAIRS + 1,)),
        DMA((2,)),
        DMA((2,)),
        DMA,
        DMA,
    ]


class Quarters:
    def __init__(self, keep, away, came, far, core_send, core_recv, chip_send, chip_recv):
        self.keep, self.away, self.came, self.far = keep, away, came, far
        self.sems = core_send, core_recv, chip_send, chip_recv
        base, line, side, self.quarter = spot()
        self.place = base + line * 2 + side
        self.core, self.chip = lax.rem(self.quarter, 2), lax.div(self.quarter, 2)
        self.tiles = keep.shape[0]

    def to_core(self, tile):
        return send(
            self.away.at[tile], self.came.at[tile], self.sems[0].at[tile], self.sems[1].at[tile],
            self.place, core_peer(self.quarter),
        )

    def to_chip(self, tile):
        return send(
            self.away.at[tile, 0], self.far.at[tile], self.sems[2].at[tile], self.sems[3].at[tile],
            self.place, chip_peer(self.quarter),
        )

    def put(self, tile, quarter_of):
        for chip in range(2):
            self.keep[tile, chip] = quarter_of(2 * chip + self.core).astype(BF16)
            self.away[tile, chip] = quarter_of(2 * chip + 1 - self.core).astype(BF16)
        self.to_core(tile).start()

    def over_cores(self):
        def one(tile, _):
            self.to_core(tile).wait_recv()
            self.to_core(tile).wait_send()
            other = 1 - self.chip
            passed = self.keep[tile, other].astype(F32) + self.came[tile, other].astype(F32)
            self.away[tile, 0] = passed.astype(BF16)
            self.to_chip(tile).start()
            kept = self.keep[tile, self.chip].astype(F32)
            kept = kept + self.came[tile, self.chip].astype(F32)
            self.keep[tile, self.chip] = kept.astype(BF16)

        lax.fori_loop(0, self.tiles, one, None)

    def over_chips(self, then):
        def one(tile, _):
            self.to_chip(tile).wait_recv()
            total = self.keep[tile, self.chip].astype(F32) + self.far[tile].astype(F32)
            self.keep[tile, self.chip] = total.astype(BF16)
            then(tile)

        lax.fori_loop(0, self.tiles, one, None)

    def total(self, tile):
        return self.keep.at[tile, self.chip]

    def finish(self):
        lax.fori_loop(0, self.tiles, lambda tile, _: self.to_chip(tile).wait_send(), None)


def quarters_scratch(tiles, rows, columns):
    return [
        pltpu.VMEM((tiles, 2, rows, columns), BF16),
        pltpu.VMEM((tiles, 2, rows, columns), BF16),
        pltpu.VMEM((tiles, 2, rows, columns), BF16),
        pltpu.VMEM((tiles, rows, columns), BF16),
    ] + [DMA((tiles,))] * 4


class Stream:
    def __init__(self, source, slots, sems):
        self.source, self.slots, self.sems = source, slots, sems

    def copy(self, tile):
        size = self.slots.shape[-1]
        start = pl.multiple_of(tile * size, size)
        slot = lax.rem(tile, 2)
        return pltpu.make_async_copy(
            self.source.at[:, pl.ds(start, size)], self.slots.at[slot], self.sems.at[slot]
        )

    def run(self, tiles, use):
        def one(tile, _):
            self.copy(tile).wait()
            use(tile, self.slots.at[lax.rem(tile, 2)])
            pl.when(tile + 2 < tiles)(lambda: self.copy(tile + 2).start())

        lax.fori_loop(0, tiles, one, None)


def third_kernel(
    vec_ref, x_in, o_in, a_in, wo_in, wd_in, du_in, d_ref, hm_ref, dy_ref,
    result_out, back_out, up_out, rows_out,
    x_ref, o_ref, a_ref, wo_ref, wd_ref, du_ref, in_sem, own_sem, back_send, back_recv, load_sem, store_sem, hm_tiles, tile_sum, dy, bias, *rest,
):
    base, line, side, quarter = spot()
    rank = line * 2 + side
    tokens, width = x_ref.shape
    part = width // TEAM // QUARTERS
    reduce = Reduce(tokens // 2, *rest[:5], rest[5:REDUCE])
    rest = rest[REDUCE:]
    ups, downs = Quarters(*rest[:8]), Quarters(*rest[8:16])
    stream = Stream(hm_ref, hm_tiles, load_sem)
    loads = [
        pltpu.make_async_copy(src, dst, in_sem.at[index])
        for index, (src, dst) in enumerate(
            (
                (o_in, o_ref), (wo_in, wo_ref), (a_in, a_ref), (wd_in, wd_ref), (du_in, du_ref),
                (x_in, x_ref),
            )
        )
    ]
    for copy in loads:
        copy.start()
    load_dy = pltpu.make_async_copy(dy_ref, dy, own_sem.at[3])
    load_dy.start()
    for tile in range(2):
        stream.copy(tile).start()
    greet_line(base, line, side, quarter)

    def pieces(to, origin, kind):
        return (
            d_ref.at[:, kind, pl.ds(to * tokens, tokens), :],
            back_out.at[:, among(origin), :, pl.ds(kind * HEAD, HEAD)],
        )

    def back(to, origin, kind):
        src, dst = pieces(to, origin, kind)
        return send(
            src, dst, back_send.at[to, kind], back_recv.at[origin, kind], base + rank, to
        )

    own_back = [
        pltpu.make_async_copy(*pieces(quarter, quarter, kind), own_sem.at[kind])
        for kind in range(3)
    ]

    def make(which, put):
        rows = pl.ds(pl.multiple_of(which * tokens, tokens), tokens)
        for start in range(0, width, 512):
            span = pl.ds(start, 512)
            put(
                span,
                dot(o_ref[rows, :], wo_ref[:, span]) + dot(a_ref[rows, :], wd_ref[:, span]),
            )

    def put_own(span, value):
        reduce.own[0, :, span] = value.astype(BF16)

    for copy in loads:
        copy.wait()
    for step in reversed(range(PAIRS)):

        def put_out(span, value, step=step):
            reduce.side_out[step, :, span] = value.astype(BF16)

        make(reduce.order[step] * 2 + 1 - side, put_out)
        reduce.begin(step)
        if step == PAIRS - 1:
            reduce.launch()
            for kind in range(3):
                own_back[kind].start()
                for hop in range(1, QUARTERS):
                    back(lax.rem(quarter + hop, QUARTERS), quarter, kind).start()

    def up_tile(tile, held):
        for start in range(0, tile_sum.shape[1], 512):
            span = pl.ds(start, 512)
            tile_sum[:, span] = contract_first(held[...], du_ref[:, span])
        ups.put(tile, lambda q: tile_sum[pl.ds(pl.multiple_of(q * part, part), part), :])

    stream.run(TEAM, up_tile)
    reduce.hop(1)
    ups.over_cores()
    make(reduce.order[3] * 2 + side, put_own)
    reduce.advance(3)
    reduce.hop(2)
    load_dy.wait()
    share = width // QUARTERS

    def down_tile(source, first, tile, _):
        columns = pl.ds(pl.multiple_of(tile * 128, 128), 128)
        rows = source[:, columns]

        def quarter_of(q):
            span = pl.ds(pl.multiple_of(q * share, share), share)
            return contract_first(rows, dy[:, span])

        downs.put(first + tile, quarter_of)

    hidden = a_ref.shape[1] // 128
    lax.fori_loop(0, hidden, partial(down_tile, a_ref, 0), None)
    lax.fori_loop(0, HEAD // 128, partial(down_tile, o_ref, hidden), None)
    make(reduce.order[2] * 2 + side, put_own)
    reduce.advance(2)
    reduce.hop(3)
    downs.over_cores()
    make(reduce.order[1] * 2 + side, put_own)
    reduce.advance(1)
    make(rank, put_own)

    def store_up(tile):
        return pltpu.make_async_copy(ups.total(tile), up_out.at[tile], store_sem.at[0])

    def store_down(tile):
        rows = pl.ds(pl.multiple_of(tile * 128, 128), 128)
        return pltpu.make_async_copy(downs.total(tile), rows_out.at[rows, :], store_sem.at[1])

    ups.over_chips(lambda tile: store_up(tile).start())
    block = width // TEAM
    for source in range(TEAM):
        bias[0:1, pl.ds(source * block, block)] = vec_ref[source, 4:5, :] + vec_ref[source, 5:6, :]
    reduce.last()
    strip = 128

    def close(index, _):
        chunk = pl.ds(pl.multiple_of(index * strip, strip), strip)
        total = reduce.total(index, strip) + bias[0:1, :]
        reduce.own[0, chunk, :] = (x_ref[chunk, :].astype(F32) + total).astype(BF16)

    lax.fori_loop(0, tokens // strip, close, None)
    store_result = pltpu.make_async_copy(reduce.own.at[0], result_out, store_sem.at[2])
    store_result.start()
    downs.over_chips(lambda tile: store_down(tile).start())
    reduce.finish()
    for kind in range(3):
        own_back[kind].wait()
        for hop in range(1, QUARTERS):
            origin = lax.rem(quarter + hop, QUARTERS)
            back(origin, quarter, kind).wait_send()
            back(origin, origin, kind).wait_recv()
    store_result.wait()
    ups.finish()
    downs.finish()
    lax.fori_loop(0, ups.tiles, lambda tile, _: store_up(tile).wait(), None)
    lax.fori_loop(0, downs.tiles, lambda tile, _: store_down(tile).wait(), None)


def third(x, attended, activated, w_out, w_down, vectors, grad_up, grads, mlp_input, grad_rows):
    tokens, width = x.shape
    hidden = activated.shape[-1]
    part, share = width // TEAM // QUARTERS, width // QUARTERS
    tiles = (hidden + HEAD) // 128
    shapes = [
        (tokens, width),
        (2, QUARTERS, tokens, 3 * HEAD),
        (TEAM, part, hidden),
        (tiles * 128, share),
    ]
    return pl.pallas_call(
        third_kernel,
        out_shape=[jax.ShapeDtypeStruct(shape, BF16) for shape in shapes],
        in_specs=[VMEM] + [ANY] * 9,
        out_specs=[ANY] * 4,
        scratch_shapes=[
            pltpu.VMEM(values.shape, BF16)
            for values in (x, attended, activated, w_out, w_down, grad_up)
        ]
        + [
            DMA((6,)),
            DMA((4,)),
            DMA((QUARTERS, 3)),
            DMA((QUARTERS, 3)),
            DMA((2,)),
            DMA((3,)),
            pltpu.VMEM((2, TEAM * tokens, width // TEAM), BF16),
            pltpu.VMEM((width // TEAM, hidden), F32),
            pltpu.VMEM((TEAM * tokens, width), BF16),
            pltpu.VMEM((8, width), F32),
        ]
        + reduce_scratch(tokens, width, 1, BF16, tokens // 2)
        + quarters_scratch(TEAM, part, hidden)
        + quarters_scratch(tiles, 128, share),
        compiler_params=pltpu.CompilerParams(
            collective_id=2, has_side_effects=True, vmem_limit_bytes=LIMIT
        ),
        name="scatter_result",
    )(vectors, x, attended, activated, w_out, w_down, grad_up, grads, mlp_input, grad_rows)


def fourth_kernel(
    vec_ref, dy_sum_ref, x_in, dy_in, dqkv_in, du_in, xs_ref, wq_ref, wu_ref, ha_ref, up_ref, rows_ref,
    grad_ref, landed, rows_out, vector_ref,
    x_ref, dy_ref, dqkv_ref, du_ref, wq, wu, xs, gains, load_sem, xs_sem, tile_load, ha_tiles, tile_sum, sums, packets, packets_in, ring, ring_in,
    row_own, row_send, row_recv, pack_send, pack_recv, ring_send, ring_recv, *rest,
):
    base, line, side, quarter = spot()
    rank = line * 2 + side
    tokens, width = x_ref.shape
    hidden = du_ref.shape[1]
    part = width // TEAM // QUARTERS
    block = width // TEAM
    core, chip = core_peer(quarter), chip_peer(quarter)
    reduce = Reduce(tokens // 4, *rest[:5], rest[5:REDUCE])
    rest = rest[REDUCE:]
    qkvs = Quarters(*rest[:8])

    def place(source, slice_of, lane, lanes):
        rows = pl.ds(pl.multiple_of(slice_of * part, 16), part)
        return landed.at[source, rows, pl.ds(lane, lanes)]

    up_columns = Columns(
        lambda n: [(up_ref.at[n], 3 * HEAD, hidden)], place, 3 * HEAD, hidden, rest[8:17]
    )
    qkv_columns = Columns(
        lambda n: [(qkvs.total(n), 0, 3 * HEAD)], place, 0, 3 * HEAD, rest[17:26]
    )
    stream = Stream(ha_ref, ha_tiles, tile_load)
    loads = [
        pltpu.make_async_copy(src, dst, load_sem.at[index])
        for index, (src, dst) in enumerate(
            (
                (dqkv_in, dqkv_ref), (wq_ref, wq), (du_in, du_ref), (wu_ref, wu), (x_in, x_ref),
                (dy_in, dy_ref),
            )
        )
    ]
    for copy in loads:
        copy.start()

    def load_x(which):
        return pltpu.make_async_copy(xs_ref.at[which], xs.at[which], xs_sem.at[which])

    for other in (1 - side, side):
        for step in reversed(range(PAIRS)):
            load_x(reduce.order[step] * 2 + other).start()
    for tile in range(2):
        stream.copy(tile).start()
    greet_team(base, line, side, quarter)

    def rows_copy(which, slice_of, to):
        src = rows_ref if which < 2 else rows_out.at[slice_of]
        return send(
            src, rows_out.at[slice_of], row_send.at[which], row_recv.at[which], base + rank, to
        )

    own_rows = pltpu.make_async_copy(rows_ref, rows_out.at[quarter], row_own)
    own_rows.start()
    rows_copy(0, quarter, core).start()
    sums[...] = jnp.zeros_like(sums)
    for source in range(TEAM):
        gains[0:2, pl.ds(source * block, block)] = vec_ref[source, 0:2, :]
    for copy in loads:
        copy.wait()

    def make(which, put):
        rows = pl.ds(pl.multiple_of(which * tokens, tokens), tokens)
        load_x(which).wait()
        values = xs[which].astype(F32)
        average = jnp.mean(values, -1, keepdims=True)
        variance = jnp.mean(jnp.square(values - average), -1, keepdims=True)
        inverse = lax.rsqrt(variance + EPSILON)
        for start in range(0, width, 512):
            span = pl.ds(start, 512)
            attn = contract_last(dqkv_ref[rows, :], wq[span, :])
            mlp = contract_last(du_ref[rows, :], wu[span, :])
            unit = (xs[which, :, span].astype(F32) - average) * inverse
            sums[0:1, span] += jnp.sum(attn * unit, 0, keepdims=True)
            sums[1:2, span] += jnp.sum(mlp * unit, 0, keepdims=True)
            sums[2:3, span] += jnp.sum(attn, 0, keepdims=True)
            sums[3:4, span] += jnp.sum(mlp, 0, keepdims=True)
            put(span, attn * gains[0:1, span] + mlp * gains[1:2, span])
        sums[4:5, pl.ds(0, hidden)] += jnp.sum(du_ref[rows, :].astype(F32), 0, keepdims=True)
        sums[5:6, pl.ds(0, 3 * HEAD)] += jnp.sum(
            dqkv_ref[rows, :].astype(F32), 0, keepdims=True
        )

    for step in reversed(range(PAIRS)):

        def put_out(span, value, step=step):
            reduce.side_out[step, :, span] = value.astype(BF16)

        make(reduce.order[step] * 2 + 1 - side, put_out)
        reduce.begin(step)
        if step == PAIRS - 1:
            reduce.launch()
            up_columns.start()

    def qkv_tile(tile, held):
        tile_sum[...] = contract_first(held[...], dqkv_ref[...])
        qkvs.put(tile, lambda q: tile_sum[pl.ds(pl.multiple_of(q * part, part), part), :])

    stream.run(TEAM, qkv_tile)
    qkvs.over_cores()
    rows_copy(1, quarter, chip).start()
    reduce.hop(1)
    for step in reversed(range(PAIRS)):

        def put_own(span, value, step=step):
            reduce.own[step, :, span] = value.astype(BF16)

        make(reduce.order[step] * 2 + side, put_own)
        if step == PAIRS - 1:
            reduce.advance(step)

    reduce.hop(2)

    def pack(target, _):
        span = pl.ds(pl.multiple_of(target * block, block), block)
        packets[target, pl.ds(0, 4), :] = sums[pl.ds(0, 4), span]
        packets[target, pl.ds(4, 1), :] = jnp.where(target == rank, dy_sum_ref[0:1, span], 0.0)
        for index in range(3):
            chunk = 3 * target + index
            kind = lax.div(chunk, HEADS)
            lanes = pl.ds(pl.multiple_of(kind * HEAD, HEAD), HEAD)
            packets[target, pl.ds(5 + index, 1), :] = jnp.where(
                lax.rem(chunk, HEADS) == rank, sums[5:6, lanes], 0.0
            )

    lax.fori_loop(0, TEAM, pack, None)

    def pack_copy(source, target, peer):
        return send(
            packets.at[target], packets_in.at[source], pack_send.at[target], pack_recv.at[source],
            base + peer, quarter,
        )

    def deal_packets(step, _):
        target = lax.rem(rank + step, TEAM)
        pack_copy(rank, target, target).start()

    lax.fori_loop(1, TEAM, deal_packets, None)
    packets_in[rank] = packets[rank]

    up_columns.forward()
    reduce.advance(2)
    reduce.hop(3)
    qkvs.over_chips(lambda tile: None)
    qkv_columns.start()
    reduce.advance(1)
    rows_copy(1, chip, chip).wait_recv()
    rows_copy(2, chip, core).start()
    up_columns.forward_last()

    def take_packets(step, _):
        source = lax.rem(rank + TEAM - step, TEAM)
        pack_copy(source, rank, source).wait_recv()

    lax.fori_loop(1, TEAM, take_packets, None)
    total = packets_in[0]
    for source in range(1, TEAM):
        total = total + packets_in[source]
    ring[pl.ds(0, 8), :] = total
    for index in range(hidden // block):
        ring[pl.ds(8 + index, 1), :] = sums[4:5, pl.ds(index * block, block)]

    def ring_copy(to, origin, peer):
        return send(
            ring, ring_in.at[origin], ring_send.at[to], ring_recv.at[origin], base + rank, peer
        )

    for hop in range(1, QUARTERS):
        to = lax.rem(quarter + hop, QUARTERS)
        ring_copy(to, quarter, to).start()
    ring_in[quarter] = ring[...]
    qkv_columns.forward()
    reduce.last()
    strip = 128

    def close(index, _):
        chunk = pl.ds(pl.multiple_of(index * strip, strip), strip)
        pulled = reduce.total(index, strip)
        unit, inverse = normalize(x_ref[chunk, :].astype(F32))
        pulled = (
            pulled
            - jnp.mean(pulled, -1, keepdims=True)
            - unit * jnp.mean(pulled * unit, -1, keepdims=True)
        )
        grad_ref[chunk, :] = (dy_ref[chunk, :].astype(F32) + inverse * pulled).astype(BF16)

    lax.fori_loop(0, tokens // strip, close, None)
    qkv_columns.forward_last()
    for hop in range(1, QUARTERS):
        origin = lax.rem(quarter + hop, QUARTERS)
        ring_copy(quarter, origin, origin).wait_recv()
    vector_ref[...] = (ring_in[0] + ring_in[1]) + (ring_in[2] + ring_in[3])

    reduce.finish()
    qkvs.finish()
    own_rows.wait()
    rows_copy(0, core, core).wait_recv()
    rows_copy(2, chip_peer(core), core).wait_recv()
    rows_copy(0, quarter, core).wait_send()
    rows_copy(1, quarter, chip).wait_send()
    rows_copy(2, chip, core).wait_send()
    for columns in (up_columns, qkv_columns):
        columns.arrive()
        columns.finish()

    def sent_packets(step, _):
        target = lax.rem(rank + step, TEAM)
        pack_copy(rank, target, target).wait_send()

    lax.fori_loop(1, TEAM, sent_packets, None)
    for hop in range(1, QUARTERS):
        to = lax.rem(quarter + hop, QUARTERS)
        ring_copy(to, quarter, to).wait_send()


def fourth(
    x, dy, grad_qkv, grad_up, vectors, dy_sum, everyone, w_qkv, w_up, attn_input, up_sums, row_sums
):
    tokens, width = x.shape
    hidden = grad_up.shape[-1]
    part, block = width // TEAM // QUARTERS, width // TEAM
    shapes = [
        ((tokens, width), BF16),
        ((TEAM, block, 3 * HEAD + hidden), BF16),
        ((QUARTERS, *row_sums.shape), BF16),
        ((16, block), F32),
    ]
    return pl.pallas_call(
        fourth_kernel,
        out_shape=[jax.ShapeDtypeStruct(*shape) for shape in shapes],
        in_specs=[VMEM] * 2 + [ANY] * 10,
        out_specs=[VMEM, ANY, ANY, VMEM],
        scratch_shapes=[
            pltpu.VMEM(x.shape, BF16),
            pltpu.VMEM(dy.shape, BF16),
            pltpu.VMEM(grad_qkv.shape, BF16),
            pltpu.VMEM(grad_up.shape, BF16),
            pltpu.VMEM(w_qkv.shape, BF16),
            pltpu.VMEM(w_up.shape, BF16),
            pltpu.VMEM(everyone.shape, BF16),
            pltpu.VMEM((8, width), F32),
            DMA((6,)),
            DMA((TEAM,)),
            DMA((2,)),
            pltpu.VMEM((2, TEAM * tokens, block), BF16),
            pltpu.VMEM((block, 3 * HEAD), F32),
            pltpu.VMEM((8, width), F32),
            pltpu.VMEM((TEAM, 8, block), F32),
            pltpu.VMEM((TEAM, 8, block), F32),
            pltpu.VMEM((16, block), F32),
            pltpu.VMEM((QUARTERS, 16, block), F32),
            DMA,
            DMA((3,)),
            DMA((3,)),
            DMA((TEAM,)),
            DMA((TEAM,)),
            DMA((QUARTERS,)),
            DMA((QUARTERS,)),
        ]
        + reduce_scratch(tokens, width, PAIRS, BF16, tokens // 4)
        + quarters_scratch(TEAM, part, 3 * HEAD)
        + column_sems(1) * 2,
        compiler_params=pltpu.CompilerParams(
            collective_id=3, has_side_effects=True, vmem_limit_bytes=LIMIT
        ),
        name="scatter_grad",
    )(
        vectors, dy_sum, x, dy, grad_qkv, grad_up, everyone, w_qkv, w_up, attn_input, up_sums,
        row_sums,
    )


def settle_kernel(
    vector_ref, columns_ref, rows_ref, result_ref, grad_ref,
    gain_out, shift_out, bias_out, bias_again, qkv_bias_out, up_bias_out,
    qkv_out, up_out, down_out, out_out, result_out, grad_out,
    low, wide, low_rows, wide_rows, passing, load_sem, store_sem, rows_load, rows_store, copy_sem,
):
    team, block, span = columns_ref.shape
    quarters, tall, share = rows_ref.shape
    width = team * HEAD
    hidden = span - 3 * HEAD
    plain = [
        (
            pltpu.make_async_copy(src, passing.at[index], copy_sem.at[index, 0]),
            pltpu.make_async_copy(passing.at[index], dst, copy_sem.at[index, 1]),
        )
        for index, (src, dst) in enumerate(((result_ref, result_out), (grad_ref, grad_out)))
    ]
    for load_in, _ in plain:
        load_in.start()
    size = vector_ref.shape[1]
    gain_out[...] = vector_ref[0:2, :]
    shift_out[...] = vector_ref[2:4, :]
    bias_out[...] = vector_ref[4:5, :].reshape(size)
    bias_again[...] = vector_ref[4:5, :].reshape(size)
    for index in range(3):
        row = vector_ref[5 + index : 6 + index, :]
        qkv_bias_out[pl.ds(index * size, size)] = row.reshape(size)
    for index in range(hidden // size):
        row = vector_ref[8 + index : 9 + index, :]
        up_bias_out[pl.ds(index * size, size)] = row.reshape(size)

    def load(source):
        slot = lax.rem(source, 2)
        return pltpu.make_async_copy(columns_ref.at[source], low.at[slot], load_sem.at[slot])

    def stores(source):
        slot = lax.rem(source, 2)
        pairs = []
        for kind in range(3):
            start = pl.multiple_of(kind * width + source * HEAD, HEAD)
            pairs.append((pl.ds(kind * HEAD, HEAD), qkv_out.at[:, pl.ds(start, HEAD)]))
        start = pl.multiple_of(source * hidden, hidden)
        pairs.append((pl.ds(3 * HEAD, hidden), up_out.at[:, pl.ds(start, hidden)]))
        return [
            pltpu.make_async_copy(wide.at[slot, :, lanes], dst, store_sem.at[slot, index])
            for index, (lanes, dst) in enumerate(pairs)
        ]

    def load_rows(quarter):
        slot = lax.rem(quarter, 2)
        return pltpu.make_async_copy(rows_ref.at[quarter], low_rows.at[slot], rows_load.at[slot])

    def stores_rows(quarter):
        slot = lax.rem(quarter, 2)
        lanes = pl.ds(pl.multiple_of(quarter * share, share), share)
        size = tall - HEAD
        return [
            pltpu.make_async_copy(
                wide_rows.at[slot, pl.ds(0, size), :], down_out.at[:, lanes], rows_store.at[slot, 0]
            ),
            pltpu.make_async_copy(
                wide_rows.at[slot, pl.ds(size, HEAD), :], out_out.at[:, lanes],
                rows_store.at[slot, 1],
            ),
        ]

    def run(count, load, stores, low, wide, strip):
        def one(index, _):
            slot = lax.rem(index, 2)
            load(index).wait()

            @pl.when(index >= 2)
            def _():
                for copy in stores(index - 2):
                    copy.wait()

            def widen(step, _):
                chunk = pl.ds(pl.multiple_of(step * strip, strip), strip)
                wide[slot, chunk, :] = low[slot, chunk, :].astype(F32)

            lax.fori_loop(0, low.shape[1] // strip, widen, None)
            for copy in stores(index):
                copy.start()
            pl.when(index + 2 < count)(lambda: load(index + 2).start())

        lax.fori_loop(0, count, one, None)

    for index in range(2):
        load_rows(index).start()
        load(index).start()
    for load_in, store_out in plain:
        load_in.wait()
        store_out.start()
    run(quarters, load_rows, stores_rows, low_rows, wide_rows, 256)
    run(team, load, stores, low, wide, min(128, block))
    for index in (quarters - 2, quarters - 1):
        for copy in stores_rows(index):
            copy.wait()
    for index in (team - 2, team - 1):
        for copy in stores(index):
            copy.wait()
    for _, store_out in plain:
        store_out.wait()


def settle(vector, columns, row_sums, result, grad_inputs):
    team, block, span = columns.shape
    quarters, tall, share = row_sums.shape
    size = vector.shape[1]
    shapes = [
        ((2, size), F32),
        ((2, size), F32),
        ((size,), F32),
        ((size,), F32),
        ((3 * size,), F32),
        ((tall - HEAD,), F32),
        ((block, team * 3 * HEAD), F32),
        ((block, team * (span - 3 * HEAD)), F32),
        ((tall - HEAD, quarters * share), F32),
        ((HEAD, quarters * share), F32),
        (result.shape, BF16),
        (grad_inputs.shape, BF16),
    ]
    return pl.pallas_call(
        settle_kernel,
        out_shape=[jax.ShapeDtypeStruct(*shape) for shape in shapes],
        in_specs=[VMEM] + [ANY] * 4,
        out_specs=[VMEM] * 6 + [ANY] * 6,
        scratch_shapes=[
            pltpu.VMEM((2, block, span), BF16),
            pltpu.VMEM((2, block, span), F32),
            pltpu.VMEM((2, tall, share), BF16),
            pltpu.VMEM((2, tall, share), F32),
            pltpu.VMEM((2, *result.shape), BF16),
            DMA((2,)),
            DMA((2, 4)),
            DMA((2,)),
            DMA((2, 2)),
            DMA((2, 2)),
        ],
        compiler_params=pltpu.CompilerParams(vmem_limit_bytes=LIMIT),
        name="settle",
    )(vector, columns, row_sums, result, grad_inputs)


def on_device(
    dp,
    ctx,
    inputs,
    segments,
    ln_gain,
    ln_bias,
    qkv_weight,
    qkv_bias,
    out_weight,
    out_bias,
    up_weight,
    up_bias,
    down_weight,
    down_bias,
    cotangent,
):
    assert dp % TEAM == 0 and ctx == QUARTERS
    teams = dp // TEAM
    together = None if teams == 1 else [[g * TEAM + i for i in range(TEAM)] for g in range(teams)]
    across = None if teams == 1 else [[g * TEAM + i for g in range(teams)] for i in range(TEAM)]
    place = lax.axis_index("dp")
    rank = place % TEAM
    _, tokens, width = inputs.shape
    hidden = up_weight.shape[1] // TEAM
    shard = width // dp

    def team_order(values):
        if teams == 1:
            return values
        lead = values.shape[:-1]
        return values.reshape(*lead, teams, TEAM, shard).swapaxes(-3, -2).reshape(*lead, width)

    def plain_order(values):
        if teams == 1:
            return values
        lead = values.shape[:-1]
        return values.reshape(*lead, TEAM, teams, shard).swapaxes(-3, -2).reshape(*lead, width)

    if teams == 1:
        w_qkv, w_up, w_out, w_down = qkv_weight, up_weight, out_weight, down_weight
        gain, shift, b_qkv, b_up = ln_gain, ln_bias, qkv_bias, up_bias
        b_rows = [out_bias, down_bias]
    else:
        line_up = partial(lax.all_gather, axis_name="dp", axis_index_groups=across, tiled=True)
        whole = partial(lax.all_gather, axis_name="dp", axis=0, tiled=True)

        def cut(values):
            size = values.shape[0] // TEAM
            return lax.dynamic_slice_in_dim(values, rank * size, size, 0)

        w_qkv, w_up = line_up(qkv_weight, axis=0), line_up(up_weight, axis=0)
        gain, shift = line_up(ln_gain, axis=1), line_up(ln_bias, axis=1)
        w_out, w_down = cut(whole(out_weight)), cut(whole(down_weight))
        b_qkv, b_up = cut(whole(qkv_bias)), cut(whole(up_bias))
        b_rows = [cut(whole(out_bias)), cut(whole(down_bias))]
    rows = w_qkv.shape[0]
    mine = inputs.reshape(tokens, width)
    grad_mine = cotangent.reshape(tokens, width)
    mine_team = team_order(mine)
    tables = rotary_tables(ctx * tokens)
    (
        everyone, attn_input, mlp_input, w_head, w_units, qkv, marks, vectors,
        grad_rows, activated, grad_up, grad_attended, attended, dy_sum,
    ) = gather(
        mine_team, grad_mine, (gain, shift, *b_rows, b_qkv, b_up, segments), w_out, w_down, tables,
        w_qkv, w_up,
    )
    grads = attend_back(qkv, grad_attended, marks, tables)
    flat = (TEAM * tokens, -1)
    attn_input, mlp_input, grad_rows, activated, grad_up, attended = (
        values.reshape(flat)
        for values in (attn_input, mlp_input, grad_rows, activated, grad_up, attended)
    )
    result, grad_qkv, up_sums, row_sums = third(
        mine, attended, activated, w_out, w_down, vectors, grad_up, grads, mlp_input, grad_rows
    )
    grad_inputs, columns, row_sums, vector = fourth(
        mine_team, team_order(grad_mine), grad_qkv.reshape(flat), grad_up, vectors, dy_sum, everyone,
        w_head, w_units, attn_input, up_sums, row_sums,
    )
    grad_inputs = plain_order(grad_inputs)
    if teams > 1:
        columns = lax.psum_scatter(
            columns, "dp", scatter_dimension=1, axis_index_groups=across, tiled=True
        )
    (
        grad_gain, grad_shift, grad_out_b, grad_down_b, grad_qkv_b, grad_up_b,
        grad_qkv_w, grad_up_w, grad_down_w, grad_out_w, result, grad_inputs,
    ) = settle(vector, columns, row_sums, result, grad_inputs)
    if teams > 1:
        near = partial(lax.all_gather, axis_name="dp", axis_index_groups=together, tiled=True)

        def own(values):
            size = values.shape[0] // dp
            total = lax.psum(near(values, axis=0), "dp", axis_index_groups=across)
            return lax.dynamic_slice_in_dim(total, place * (TEAM * size), TEAM * size, 0)

        def own_end(values):
            return lax.psum_scatter(
                values, "dp", scatter_dimension=1, axis_index_groups=across, tiled=True
            )

        def scatter_rows(term):
            size = term.shape[0]
            full = jnp.zeros((TEAM, size, width), BF16)
            full = lax.dynamic_update_slice_in_dim(full, term.astype(BF16)[None], rank, 0)
            return lax.psum_scatter(
                full.reshape(TEAM * size, width), "dp", scatter_dimension=0, tiled=True
            ).astype(F32)

        grad_gain, grad_shift = own_end(grad_gain), own_end(grad_shift)
        grad_out_b, grad_down_b = own(grad_out_b), own(grad_down_b)
        grad_qkv_b, grad_up_b = own(grad_qkv_b), own(grad_up_b)
        grad_out_w, grad_down_w = scatter_rows(grad_out_w), scatter_rows(grad_down_w)
    return (
        result.reshape(inputs.shape),
        grad_inputs.reshape(inputs.shape),
        grad_gain,
        grad_shift,
        grad_qkv_w,
        grad_qkv_b,
        grad_out_w,
        grad_out_b,
        grad_up_w,
        grad_up_b,
        grad_down_w,
        grad_down_b,
    )


def solution(mesh):
    placed = (
        P("dp", "ctx", None),
        P("dp", "ctx"),
        P(None, "dp"),
        P(None, "dp"),
        P("dp", None),
        P("dp"),
        P("dp", None),
        P("dp"),
        P("dp", None),
        P("dp"),
        P("dp", None),
        P("dp"),
        P("dp", "ctx", None),
    )
    return jax.shard_map(
        partial(on_device, mesh.shape["dp"], mesh.shape["ctx"]),
        mesh=mesh,
        in_specs=placed,
        out_specs=(
            P("dp", "ctx", None),
            P("dp", "ctx", None),
            P(None, "dp"),
            P(None, "dp"),
            P("dp", None),
            P("dp"),
            P("dp", None),
            P("dp"),
            P("dp", None),
            P("dp"),
            P("dp", None),
            P("dp"),
        ),
        check_vma=False,
    )
```
